32 devices in a mesh: ens: 2 (over y), sub: 4 (over x, core), hor: 4 (over z).
Axes of the slice: x: 2, y: 2, z: 4, core: 2. Of those that a mesh axis runs over, the one named last changes fastest.
Arguments:
- adjoint_state: float32 [8, 2, 48, 16, 768], P(('ens', 'sub'), None, 'hor'), parts along dimension 0, may hold values from -6 to 6
- courant_east: float32 [8, 48, 16, 768], P(('ens', 'sub'), 'hor'), parts along dimension 0, may hold values from -0.47 to 0.47
- courant_north: float32 [8, 48, 16, 768], P(('ens', 'sub'), 'hor'), parts along dimension 0, may hold values from -0.47 to 0.47
- parent_cell: int32 [2, 2, 48], P(None, None, 'hor'), may hold values from 1 to 29, as said below
- stencil_offset: int32 [4, 2, 2, 48], P(None, None, None, 'hor'), may hold values from -1 to 2
- stencil_weight: float32 [4, 2, 2, 48], P(None, None, None, 'hor'), may hold values from 0.05 to 0.35
- owner_slot: int32 [32], replicated, may hold values from 0 to 31, each once
Outputs:
- adjoint_result: float32 [8, 2, 48, 16, 768], P(('ens', 'sub'), None, 'hor'), parts along dimension 0
- boundary_gradient: float32 [4, 16, 32], P('ens', 'sub', 'hor'), parts along dimension 0
The draws below stay inside these ranges and needn't reach their ends.
There are 2 independent parts, one for each index of `ens`. The reference program is written for one: setup_inputs(seed, part) draws one part's arguments, and reference() takes and returns one part's arrays. A program takes and returns all parts, laid end to end along the dimension named above; an argument that names none is the same for every part. Nothing has to cross between parts.
Inputs may be any that keep to these rules, and one draw needn't show every extreme that they name: `parent_cell`: on side s the parent cell lies between s * 16 + 1 and s * 16 + 13, so every interpolation point stays on its own side.
All inputs are finite; a program needn't handle non-finite values.
Results may differ from the reference program's by a relative error of at most 0.000084.
Values sent between devices are 32-bit elements; how exact they have to be, the bound alone decides.
No kernel may reach another device: no remote copies, remote signals or barrier semaphores. Data moves between devices by JAX's collectives and lax.ppermute only.
A program may use at most 384 MiB of HBM per device.

```python
import jax
import jax.numpy as jnp
from jax import lax

SUBS = 4
NY = 768
LEV = 16
STEPS = 4
RATIO = 3
NX = 48
PX = 16
NPAR = 32


def draw_courant_east(key, part):
    key = jax.random.fold_in(key, 11)
    shape = (SUBS, NX, LEV, NY)
    return jax.random.uniform(key, shape, jnp.float32, -0.47, 0.47)


def draw_courant_north(key, part):
    key = jax.random.fold_in(key, 23)
    shape = (SUBS, NX, LEV, NY)
    return jax.random.uniform(key, shape, jnp.float32, -0.47, 0.47)


def draw_parent_cell(key, part):
    key = jax.random.fold_in(key, 37)
    stagger = jax.random.randint(key, (2, 2, 1), 0, 3, jnp.int32)
    rows = jnp.arange(NX, dtype=jnp.int32)[None, None, :]
    sides = jnp.arange(2, dtype=jnp.int32)[None, :, None]
    cells = jnp.clip((rows + stagger) // RATIO, 1, PX - 3)
    return (cells + sides * PX).astype(jnp.int32)


def place_ends(array, stream_key, least, largest):
    index_at = [jax.random.randint(jax.random.fold_in(stream_key, axis), (), 0, length) for axis, length in enumerate(array.shape)]
    longest = array.shape.index(max(array.shape))
    beside = index_at[:longest] + [(index_at[longest] + 1) % array.shape[longest]] + index_at[longest + 1:]
    return array.at[tuple(index_at)].set(least).at[tuple(beside)].set(largest)


def steps_of(rng, shape, cuts, least, top_value):
    loudness, own = 1.0, jax.random.fold_in(rng, 6)
    for axis_at, parts in cuts:
        heights = jnp.exp(jax.random.uniform(jax.random.fold_in(own, axis_at), (parts,), jnp.float32, least / len(cuts), top_value / len(cuts)))
        loudness = loudness * jnp.repeat(heights, shape[axis_at] // parts).reshape([-1 if axis == axis_at else 1 for axis in range(len(shape))])
    return loudness


def scatter_about(rng, dims, scale, reach, split=(), kind=jnp.bfloat16):
    gain = steps_of(rng, dims, split, -0.22, 0.18) if split else 1.0
    values = jax.random.normal(rng, dims, jnp.float32) * scale * gain
    return jnp.minimum(jnp.maximum(values, -reach), reach).astype(kind)


def setup_inputs(seed: int = 0, part: int = 0) -> dict:
    seeds = jax.random.split(jax.random.key(seed), 8)
    part_keys = jax.random.split(jax.random.fold_in(seeds[7], part), 8)
    adjoint_state = scatter_about(part_keys[0], (SUBS, 2, NX, LEV, NY), 1.0, 6.0, ((0, 4), (2, 4)), jnp.float32)
    courant_east = draw_courant_east(jax.random.fold_in(jax.random.fold_in(seeds[7], part), 71), part)
    courant_north = draw_courant_north(jax.random.fold_in(jax.random.fold_in(seeds[7], part), 71), part)
    parent_cell = draw_parent_cell(jax.random.fold_in(seeds[7], 71), part)
    stencil_offset = place_ends(jax.random.randint(seeds[4], (4, 2, 2, NX), -1, 3), jax.random.fold_in(seeds[4], 1), -1, 2).astype(jnp.int32)
    stencil_weight = jnp.clip(0.05 + 0.29999999 * jax.random.uniform(seeds[5], (4, 2, 2, NX), jnp.float32) ** steps_of(seeds[5], (4, 2, 2, NX), ((3, 4),), -0.2, 0.2), 0.05, 0.35)
    owner_slot = jax.random.permutation(seeds[6], NPAR).astype(jnp.int32)
    return {"adjoint_state": adjoint_state, "courant_east": courant_east, "courant_north": courant_north, "parent_cell": parent_cell, "stencil_offset": stencil_offset, "stencil_weight": stencil_weight, "owner_slot": owner_slot}


def coefficients(east_rate, north_rate):
    return (jnp.maximum(east_rate, 0.0), jnp.maximum(-east_rate, 0.0),
            jnp.maximum(north_rate, 0.0), jnp.maximum(-north_rate, 0.0),
            1.0 - jnp.abs(east_rate) - jnp.abs(north_rate))


def northward(adjoint, north_plus, north_minus):
    upper = jnp.pad((north_plus * adjoint)[..., 1:], ((0, 0), (0, 0), (0, 0), (0, 1)))
    lower = jnp.pad((north_minus * adjoint)[..., :-1], ((0, 0), (0, 0), (0, 0), (1, 0)))
    return upper + lower


def local_substep(adjoint, terms):
    east_plus, east_minus, north_plus, north_minus, centre = terms
    from_east = jnp.pad((east_plus * adjoint)[:, 1:], ((0, 0), (0, 1), (0, 0), (0, 0)))
    from_west = jnp.pad((east_minus * adjoint)[:, :-1], ((0, 0), (1, 0), (0, 0), (0, 0)))
    return centre * adjoint + from_east + from_west + northward(adjoint, north_plus, north_minus)


def reference(adjoint_state, courant_east, courant_north, parent_cell, stencil_offset, stencil_weight, owner_slot):
    end_states = []
    south_total = jnp.zeros((2, NX, LEV), jnp.float32)
    north_total = jnp.zeros((2, NX, LEV), jnp.float32)
    for window in range(SUBS):
        terms = coefficients(courant_east[window], courant_north[window])
        adjoint = adjoint_state[window]
        for substep in range(STEPS):
            south_total = south_total + terms[2][:, :, 0] * adjoint[..., 0]
            north_total = north_total + terms[3][:, :, -1] * adjoint[..., -1]
            adjoint = local_substep(adjoint, terms)
        end_states.append(adjoint)
    later = jnp.stack(end_states[1:] + [jnp.zeros_like(end_states[0])], 0)
    adjoint_result = adjoint_state - later
    ghost = jnp.stack([south_total, north_total], 1)
    target = parent_cell[None] + stencil_offset
    slots = jnp.arange(NPAR, dtype=jnp.int32)
    onehot = (target[..., None] == slots).astype(jnp.float32)
    mixing = jnp.sum(stencil_weight[..., None] * onehot, 0)
    parent_grad = jnp.einsum("csil,csip->clp", ghost, mixing, precision=lax.Precision.HIGHEST)
    boundary_gradient = jnp.zeros_like(parent_grad).at[:, :, owner_slot].set(parent_grad)
    return adjoint_result, boundary_gradient
```

```python
import functools

import jax
import jax.numpy as jnp
from jax import lax
from jax.experimental import pallas as pl
from jax.experimental.pallas import tpu as pltpu
from jax.sharding import PartitionSpec as P

STEPS = 4
HALF = 8
FLUX_ROWS = 2 * STEPS
PACK_ROWS = FLUX_ROWS + 3


def from_behind(value, axis, by):
    peers = lax.axis_size(axis)
    pairs = [(i, i + by) for i in range(peers) if 0 <= i + by < peers]
    return lax.ppermute(value, axis, pairs)


def north_rates(north_rate):
    width = north_rate.shape[-1]
    column = lax.broadcasted_iota(jnp.int32, north_rate.shape, len(north_rate.shape) - 1)
    plus = jnp.where(column == 0, 0.0, jnp.maximum(north_rate, 0.0))
    minus = jnp.where(column == width - 1, 0.0, jnp.maximum(-north_rate, 0.0))
    return plus, minus


def shifted(flux_plus, flux_minus):
    width = flux_plus.shape[-1]
    axis = len(flux_plus.shape) - 1
    return pltpu.roll(flux_plus, width - 1, axis) + pltpu.roll(flux_minus, 1, axis)


class Row:
    def __init__(self, east_rate, north_rate=None, flip=False):
        self.outward = jnp.maximum(-east_rate if flip else east_rate, 0.0)
        self.inward = jnp.maximum(east_rate if flip else -east_rate, 0.0)
        if north_rate is not None:
            self.centre = 1.0 - jnp.abs(east_rate) - jnp.abs(north_rate)
            self.plus, self.minus = north_rates(north_rate)

    def stay(self, value):
        return self.centre * value + shifted(self.plus * value, self.minus * value)


def edge_kernel(state_ref, east_ref, north_ref, low_ref, high_ref):
    def one_side(flip, pack_ref):
        def half(h, carry):
            levels = pl.ds(pl.multiple_of(h * HALF, HALF), HALF)
            place = (lambda r: STEPS - 1 - r) if flip else (lambda r: r)
            rows = [
                Row(east_ref[0, place(r), levels, :], north_ref[0, place(r), levels, :], flip)
                for r in range(STEPS)
            ]
            pack_ref[FLUX_ROWS, levels, :] = east_ref[0, place(0), levels, :]
            pack_ref[FLUX_ROWS + 1, levels, :] = north_ref[0, place(0), levels, :]
            pack_ref[FLUX_ROWS + 2, levels, :] = east_ref[0, place(1), levels, :]
            for c in range(2):
                field = [state_ref[0, c, place(r), levels, :] for r in range(STEPS)]
                for k in range(STEPS):
                    pack_ref[2 * k + c, levels, :] = rows[0].outward * field[0]
                    after = []
                    for r in range(STEPS - 1 - k):
                        value = rows[r].stay(field[r]) + rows[r + 1].outward * field[r + 1]
                        if r > 0:
                            value = value + rows[r - 1].inward * field[r - 1]
                        after.append(value)
                    field = after
            return carry

        lax.fori_loop(0, pack_ref.shape[1] // HALF, half, 0)

    @pl.when(pl.program_id(0) == 0)
    def _():
        one_side(False, low_ref)

    @pl.when(pl.program_id(0) == 1)
    def _():
        one_side(True, high_ref)


def main_kernel(
    cell_ref, offset_ref, weight_ref, owner_ref,
    state_ref, east_ref, north_ref,
    middle_ref, ends_ref, spread_ref, partial_ref,
    field, plus_ref, minus_ref, centre_ref, ghost_ref,
):
    rows = east_ref.shape[1]
    slots = spread_ref.shape[-1]

    @pl.when(pl.program_id(0) == 0)
    def _():
        slot_ids = lax.broadcasted_iota(jnp.int32, (1, slots), 1)

        def one_row(i, carry):
            for c in range(2):
                for s in range(2):
                    total = jnp.zeros((1, slots), jnp.float32)
                    for point in range(offset_ref.shape[0]):
                        slot = owner_ref[cell_ref[c, s, i] + offset_ref[point, c, s, i]]
                        total = total + jnp.where(slot_ids == slot, weight_ref[point, c, s, i], 0.0)
                    spread_ref[c, s, pl.ds(i, 1), :] = total
            return carry

        lax.fori_loop(0, rows, one_row, 0)

    for i in range(rows):
        east_rate = east_ref[0, i]
        north_rate = north_ref[0, i]
        centre_ref[i] = 1.0 - jnp.abs(east_rate) - jnp.abs(north_rate)
        plus_ref[i] = jnp.maximum(north_rate, 0.0)
        minus_ref[i] = jnp.maximum(-north_rate, 0.0)

    width = east_ref.shape[-1]
    column = lax.broadcasted_iota(jnp.int32, (HALF, width), 1)
    first = column == 0
    last = column == width - 1

    for k in range(STEPS):
        read = (lambda c, i: state_ref[0, c, i]) if k == 0 else (lambda c, i, s=(k - 1) % 2: field[s, c, i])
        prior = [read(c, 0) for c in range(2)]
        here_flux = None
        west = [None, None]
        here = prior
        for i in range(rows):
            east_here = east_ref[0, i]
            after = [read(c, i + 1) for c in range(2)] if i + 1 < rows else None
            east_after = jnp.maximum(east_ref[0, i + 1], 0.0) if i + 1 < rows else None
            leave_west = jnp.maximum(-east_here, 0.0)
            centre = centre_ref[i]
            plus = plus_ref[i]
            minus = minus_ref[i]
            for c in range(2):
                value = here[c]
                up = plus * value
                down = minus * value
                if k == 0:
                    ghost_ref[c, 0, i] = up[:, :128]
                    ghost_ref[c, 1, i] = down[:, width - 128:]
                else:
                    ghost_ref[c, 0, i] += up[:, :128]
                    ghost_ref[c, 1, i] += down[:, width - 128:]
                up = jnp.where(first, 0.0, up)
                down = jnp.where(last, 0.0, down)
                total = centre * value + shifted(up, down)
                if after is not None:
                    total = total + east_after * after[c]
                if west[c] is not None:
                    total = total + west[c]
                west[c] = leave_west * value
                if k < STEPS - 1:
                    field[k % 2, c, i] = total
                elif i < STEPS:
                    ends_ref[c, i] = total
                elif i >= rows - STEPS:
                    ends_ref[c, i - rows + 2 * STEPS] = total
                else:
                    middle_ref[c, i - STEPS] = total
            here = after

    for c in range(2):
        total = jnp.zeros((HALF, slots), jnp.float32)
        for s in range(2):
            lane = 0 if s == 0 else 127
            for i in range(rows):
                total = total + ghost_ref[c, s, i, :, lane:lane + 1] * spread_ref[c, s, i:i + 1, :]
        partial_ref[c] = total


def mend_kernel(
    east_ref, north_ref, low_ref, high_ref, below_ref, above_ref, ends_ref, spread_ref, partial_ref,
    out_ref, sum_ref,
):
    levels_all = sum_ref.shape[1]
    rows = spread_ref.shape[2]
    width = east_ref.shape[-1]

    def one_side(flip, mine_ref, other_ref):
        place = (lambda r: STEPS - 1 - r) if flip else (lambda r: r)

        def half(h, carry):
            levels = pl.ds(pl.multiple_of(h * HALF, HALF), HALF)
            own = [
                Row(east_ref[0, place(r), levels, :], north_ref[0, place(r), levels, :], flip)
                for r in range(STEPS - 1)
            ]
            near = Row(other_ref[FLUX_ROWS, levels, :], other_ref[FLUX_ROWS + 1, levels, :], flip)
            far = Row(other_ref[FLUX_ROWS + 2, levels, :], None, flip)
            for c in range(2):
                mine = lambda k: mine_ref[2 * k + c, levels, :]
                theirs = lambda k: other_ref[2 * k + c, levels, :]
                a0 = theirs(0)
                n1 = mine(0)
                b0 = own[0].stay(a0) + near.inward * n1 + theirs(1)
                b1 = own[0].inward * a0
                bn1 = near.stay(n1) + own[0].outward * a0 + mine(1)
                bn2 = near.outward * n1
                c0 = own[0].stay(b0) + near.inward * bn1 + own[1].outward * b1 + theirs(2)
                c1 = own[1].stay(b1) + own[0].inward * b0
                c2 = own[1].inward * b1
                cn1 = near.stay(bn1) + own[0].outward * b0 + far.inward * bn2 + mine(2)
                d0 = own[0].stay(c0) + near.inward * cn1 + own[1].outward * c1 + theirs(3)
                d1 = own[1].stay(c1) + own[0].inward * c0 + own[2].outward * c2
                d2 = own[2].stay(c2) + own[1].inward * c1
                d3 = own[2].inward * c2
                for r, value in enumerate((d0, d1, d2, d3)):
                    out_ref[c, place(r), levels, :] = ends_ref[c, place(r), levels, :] + value
                total = sum_ref[c, levels, :]
                for r, value in enumerate((a0 + b0 + c0, b1 + c1, c2)):
                    i = rows - 1 - r if flip else r
                    rate = north_ref[0, place(r), levels, :]
                    south = jnp.maximum(rate[:, :1], 0.0) * value[:, :1]
                    north = jnp.maximum(-rate[:, width - 1:], 0.0) * value[:, width - 1:]
                    total = total + south * spread_ref[c, 0, i:i + 1, :]
                    total = total + north * spread_ref[c, 1, i:i + 1, :]
                sum_ref[c, levels, :] = total
            return carry

        lax.fori_loop(0, levels_all // HALF, half, 0)

    @pl.when(pl.program_id(0) == 0)
    def _():
        sum_ref[...] = partial_ref[...]
        one_side(False, low_ref, below_ref)

    @pl.when(pl.program_id(0) == 1)
    def _():
        one_side(True, high_ref, above_ref)


def subtract_middle(state_ref, other_ref, out_ref):
    out_ref[0] = state_ref[0] - other_ref[...]


def subtract_ends(begun_ref, state_ref, other_ref, out_ref):
    out_ref[0] = state_ref[0] - other_ref[...]


def cost(flops, moved):
    return pl.CostEstimate(flops=flops, bytes_accessed=moved, transcendentals=0)


PARAMS = pltpu.CompilerParams(vmem_limit_bytes=40 * 1024 * 1024)


def local(
    adjoint_state,
    courant_east,
    courant_north,
    parent_cell,
    stencil_offset,
    stencil_weight,
    owner_slot,
):
    _, parts, rows, levels, width = adjoint_state.shape
    slots = owner_slot.shape[0]
    blocks = rows // STEPS
    inner = rows - 2 * STEPS
    row_bytes = levels * width * 4
    f32 = functools.partial(jax.ShapeDtypeStruct, dtype=jnp.float32)
    at_end = lambda s: (0, 0, s * (blocks - 1), 0, 0)
    at_end4 = lambda s: (0, s * (blocks - 1), 0, 0)
    whole = lambda *dims: pl.BlockSpec(dims, lambda s: (0,) * len(dims))
    state_end = pl.BlockSpec((1, parts, STEPS, levels, width), at_end)
    rate_end = pl.BlockSpec((1, STEPS, levels, width), at_end4)
    pack_spec = whole(PACK_ROWS, levels, width)

    low, high = pl.pallas_call(
        edge_kernel,
        grid=(2,),
        in_specs=[state_end, rate_end, rate_end],
        out_specs=[pack_spec, pack_spec],
        out_shape=[f32((PACK_ROWS, levels, width))] * 2,
        compiler_params=PARAMS,
        cost_estimate=cost(24 * levels * width * 13, 54 * row_bytes),
        name="edge_fluxes",
    )(adjoint_state, courant_east, courant_north)
    below = from_behind(high, "hor", 1)
    above = from_behind(low, "hor", -1)

    smem = pl.BlockSpec(memory_space=pltpu.SMEM)
    by_half = pl.BlockSpec((1, rows, HALF, width), lambda h: (0, 0, h, 0))
    middle, ends, spread, partial = pl.pallas_call(
        main_kernel,
        grid=(levels // HALF,),
        in_specs=[
            smem, smem, smem, smem,
            pl.BlockSpec((1, parts, rows, HALF, width), lambda h: (0, 0, 0, h, 0)),
            by_half, by_half,
        ],
        out_specs=[
            pl.BlockSpec((parts, inner, HALF, width), lambda h: (0, 0, h, 0)),
            pl.BlockSpec((parts, 2 * STEPS, HALF, width), lambda h: (0, 0, h, 0)),
            whole(parts, 2, rows, slots),
            pl.BlockSpec((parts, HALF, slots), lambda h: (0, h, 0)),
        ],
        out_shape=[
            f32((parts, inner, levels, width)),
            f32((parts, 2 * STEPS, levels, width)),
            f32((parts, 2, rows, slots)),
            f32((parts, levels, slots)),
        ],
        scratch_shapes=[
            pltpu.VMEM((2, parts, rows, HALF, width), jnp.float32),
            pltpu.VMEM((rows, HALF, width), jnp.float32),
            pltpu.VMEM((rows, HALF, width), jnp.float32),
            pltpu.VMEM((rows, HALF, width), jnp.float32),
            pltpu.VMEM((parts, 2, rows, HALF, 128), jnp.float32),
        ],
        compiler_params=PARAMS,
        cost_estimate=cost(8 * rows * levels * width * 13, 6 * rows * row_bytes),
        name="inner_sweep",
    )(parent_cell, stencil_offset, stencil_weight, owner_slot, adjoint_state, courant_east, courant_north)
    middle_next = from_behind(middle, "sub", -1)

    ends, partial = pl.pallas_call(
        mend_kernel,
        grid=(2,),
        in_specs=[
            rate_end, rate_end, pack_spec, pack_spec, pack_spec, pack_spec,
            pl.BlockSpec((parts, STEPS, levels, width), lambda s: (0, s, 0, 0)),
            whole(parts, 2, rows, slots),
            whole(parts, levels, slots),
        ],
        out_specs=[
            pl.BlockSpec((parts, STEPS, levels, width), lambda s: (0, s, 0, 0)),
            whole(parts, levels, slots),
        ],
        out_shape=[f32((parts, 2 * STEPS, levels, width)), f32((parts, levels, slots))],
        compiler_params=PARAMS,
        cost_estimate=cost(32 * levels * width * 13, 92 * row_bytes),
        name="mend_ends",
    )(courant_east, courant_north, low, high, below, above, ends, spread, partial)
    ends_next = from_behind(ends, "sub", -1)

    subs, hors = lax.axis_size("sub"), lax.axis_size("hor")
    pieces = partial.reshape(parts, subs, levels // subs, hors, slots // hors)
    pieces = pieces.transpose(1, 3, 0, 2, 4).reshape(subs * hors, parts, levels // subs, slots // hors)
    boundary_gradient = jnp.sum(lax.all_to_all(pieces, ("sub", "hor"), 0, 0, tiled=True), 0)

    state_block = lambda pick: pl.BlockSpec((1, parts, STEPS, levels, width), lambda s: (0, 0, pick(s), 0, 0))
    other_block = pl.BlockSpec((parts, STEPS, levels, width), lambda s: (0, s, 0, 0))
    begun = pl.pallas_call(
        subtract_middle,
        grid=(inner // STEPS,),
        in_specs=[state_block(lambda s: s + 1), other_block],
        out_specs=state_block(lambda s: s + 1),
        out_shape=f32(adjoint_state.shape),
        compiler_params=PARAMS,
        cost_estimate=cost(parts * inner * levels * width, 3 * parts * inner * row_bytes),
        name="subtract_middle",
    )(adjoint_state, middle_next)
    adjoint_result = pl.pallas_call(
        subtract_ends,
        grid=(2,),
        in_specs=[
            pl.BlockSpec(memory_space=pl.ANY),
            state_block(lambda s: s * (blocks - 1)),
            other_block,
        ],
        out_specs=state_block(lambda s: s * (blocks - 1)),
        out_shape=f32(adjoint_state.shape),
        input_output_aliases={0: 0},
        compiler_params=PARAMS,
        cost_estimate=cost(parts * 2 * STEPS * levels * width, 6 * parts * STEPS * row_bytes),
        name="subtract_ends",
    )(begun, adjoint_state, ends_next)
    return (adjoint_result, boundary_gradient)


def solution(mesh):
    in_specs = (
        P(("ens", "sub"), None, "hor", None, None),
        P(("ens", "sub"), "hor", None, None),
        P(("ens", "sub"), "hor", None, None),
        P(None, None, "hor"),
        P(None, None, None, "hor"),
        P(None, None, None, "hor"),
        P(),
    )
    out_specs = (P(("ens", "sub"), None, "hor", None, None), P("ens", "sub", "hor"))
    return jax.shard_map(local, mesh=mesh, in_specs=in_specs, out_specs=out_specs, check_vma=False)
```

```python
import functools

import jax
import jax.numpy as jnp
from jax import lax
from jax.experimental import pallas as pl
from jax.experimental.pallas import tpu as pltpu
from jax.sharding import PartitionSpec as P

STEPS = 4
HALF = 8
FLUX_ROWS = 2 * STEPS
PACK_ROWS = FLUX_ROWS + 3
LANES = 128


def along(value, axis, step_of):
    peers = lax.axis_size(axis)
    pairs = [(i, i + step_of) for i in range(peers) if 0 <= i + step_of < peers]
    return lax.ppermute(value, axis, pairs)


def alternating(value, sign):
    subs, hors = lax.axis_size("sub"), lax.axis_size("hor")
    pairs = []
    for s in range(subs):
        step = sign if s % 2 == 0 else -sign
        pairs += [(s * hors + h, s * hors + h + step) for h in range(hors) if 0 <= h + step < hors]
    return lax.ppermute(value, ("sub", "hor"), pairs)


def parity():
    return lax.rem(lax.axis_index("sub"), 2)


def sign_of(flip):
    return jnp.where(flip == 1, jnp.float32(-1.0), jnp.float32(1.0))


def north_rates(north_rate):
    width = north_rate.shape[-1]
    column = lax.broadcasted_iota(jnp.int32, north_rate.shape, len(north_rate.shape) - 1)
    plus = jnp.where(column == 0, 0.0, jnp.maximum(north_rate, 0.0))
    minus = jnp.where(column == width - 1, 0.0, jnp.maximum(-north_rate, 0.0))
    return plus, minus


def shifted(flux_plus, flux_minus):
    width = flux_plus.shape[-1]
    axis = len(flux_plus.shape) - 1
    return pltpu.roll(flux_plus, width - 1, axis) + pltpu.roll(flux_minus, 1, axis)


class Row:
    def __init__(self, east_rate, north_rate=None):
        self.outward = jnp.maximum(east_rate, 0.0)
        self.inward = jnp.maximum(-east_rate, 0.0)
        if north_rate is not None:
            self.centre = 1.0 - jnp.abs(east_rate) - jnp.abs(north_rate)
            self.plus, self.minus = north_rates(north_rate)

    def stay(self, value):
        return self.centre * value + shifted(self.plus * value, self.minus * value)


def level_halves(levels, body):
    def step(h, carry):
        body(pl.ds(pl.multiple_of(h * HALF, HALF), HALF))
        return carry

    lax.fori_loop(0, levels // HALF, step, 0)


def first_kernel(
    state_hbm, east_hbm, north_hbm, pack_ref, state_ref, east_ref, north_ref, early_sems, late_sems
):
    parts, rows, levels = state_ref.shape[1:4]
    flip = parity()
    sign = sign_of(flip)
    start = flip * (rows - STEPS)
    place = lambda r: start + r + flip * (STEPS - 1 - 2 * r)

    def copies(first_row, count, sems):
        at = pl.ds(first_row, count)
        made = [
            pltpu.make_async_copy(state_hbm.at[0, c, at], state_ref.at[0, c, at], sems.at[c])
            for c in range(parts)
        ]
        made.append(pltpu.make_async_copy(east_hbm.at[0, at], east_ref.at[0, at], sems.at[parts]))
        made.append(pltpu.make_async_copy(north_hbm.at[0, at], north_ref.at[0, at], sems.at[parts + 1]))
        return made

    early = copies(start, STEPS, early_sems)
    late = copies(STEPS * (1 - flip), rows - STEPS, late_sems)
    for copy in early + late:
        copy.start()
    for copy in early:
        copy.wait()

    def half(at):
        row = [
            Row(east_ref[0, place(r), at, :] * sign, north_ref[0, place(r), at, :])
            for r in range(STEPS)
        ]
        pack_ref[FLUX_ROWS, at, :] = east_ref[0, place(0), at, :]
        pack_ref[FLUX_ROWS + 1, at, :] = north_ref[0, place(0), at, :]
        pack_ref[FLUX_ROWS + 2, at, :] = east_ref[0, place(1), at, :]
        for c in range(parts):
            field = [state_ref[0, c, place(r), at, :] for r in range(STEPS)]
            for k in range(STEPS):
                pack_ref[2 * k + c, at, :] = row[0].outward * field[0]
                after = []
                for r in range(STEPS - 1 - k):
                    value = row[r].stay(field[r]) + row[r + 1].outward * field[r + 1]
                    if r > 0:
                        value = value + row[r - 1].inward * field[r - 1]
                    after.append(value)
                field = after

    level_halves(levels, half)
    for copy in late:
        copy.wait()


def sweep_kernel(
    cell_ref, offset_ref, weight_ref, owner_ref, state_ref, east_ref, north_ref,
    pack_ref, middle_ref, ends_ref, spread_ref, partial_ref,
    field, plus_ref, minus_ref, centre_ref, ghost_ref,
):
    parts, rows, levels, width = state_ref.shape[1:]
    slots = spread_ref.shape[-1]
    slot_ids = lax.broadcasted_iota(jnp.int32, (1, slots), 1)
    flip = 1 - parity()
    sign = sign_of(flip)
    end_row = flip * (rows - 1)
    next_row = end_row + 1 - 2 * flip

    def one_row(i, carry):
        for c in range(2):
            for s in range(2):
                total = jnp.zeros((1, slots), jnp.float32)
                for point in range(offset_ref.shape[0]):
                    slot = owner_ref[cell_ref[c, s, i] + offset_ref[point, c, s, i]]
                    total = total + jnp.where(slot_ids == slot, weight_ref[point, c, s, i], 0.0)
                spread_ref[c, s, pl.ds(i, 1), :] = total
        return carry

    lax.fori_loop(0, rows, one_row, 0)

    def half(at):
        pack_ref[FLUX_ROWS, at, :] = east_ref[0, end_row, at, :]
        pack_ref[FLUX_ROWS + 1, at, :] = north_ref[0, end_row, at, :]
        pack_ref[FLUX_ROWS + 2, at, :] = east_ref[0, next_row, at, :]
        leaving = jnp.maximum(east_ref[0, end_row, at, :] * sign, 0.0)

        def coefficients(i, carry):
            east_rate = east_ref[0, i, at, :]
            north_rate = north_ref[0, i, at, :]
            centre_ref[i] = 1.0 - jnp.abs(east_rate) - jnp.abs(north_rate)
            plus_ref[i], minus_ref[i] = north_rates(north_rate)
            return carry

        lax.fori_loop(0, rows, coefficients, 0)

        for k in range(STEPS):
            if k == 0:
                read = lambda c, i: state_ref[0, c, i, at, :]
            else:
                read = lambda c, i, slot=(k - 1) % 2: field[slot, c, i]
            for c in range(parts):
                pack_ref[2 * k + c, at, :] = leaving * read(c, end_row)
            west = [None] * parts
            here = [read(c, 0) for c in range(parts)]
            for i in range(rows):
                east_here = east_ref[0, i, at, :]
                leave_west = jnp.maximum(-east_here, 0.0)
                if i + 1 < rows:
                    after = [read(c, i + 1) for c in range(parts)]
                    east_after = jnp.maximum(east_ref[0, i + 1, at, :], 0.0)
                centre, plus, minus = centre_ref[i], plus_ref[i], minus_ref[i]
                south_rate = jnp.maximum(north_ref[0, i, at, :LANES], 0.0)
                north_rate = jnp.maximum(-north_ref[0, i, at, width - LANES:], 0.0)
                for c in range(parts):
                    value = here[c]
                    south = south_rate * value[:, :LANES]
                    north = north_rate * value[:, width - LANES:]
                    if k == 0:
                        ghost_ref[c, 0, i] = south
                        ghost_ref[c, 1, i] = north
                    else:
                        ghost_ref[c, 0, i] += south
                        ghost_ref[c, 1, i] += north
                    total = centre * value + shifted(plus * value, minus * value)
                    if i + 1 < rows:
                        total = total + east_after * after[c]
                    if i > 0:
                        total = total + west[c]
                    west[c] = leave_west * value
                    if k < STEPS - 1:
                        field[k % 2, c, i] = total
                    elif i < STEPS:
                        ends_ref[c, i, at, :] = total
                    elif i >= rows - STEPS:
                        ends_ref[c, i - rows + 2 * STEPS, at, :] = total
                    else:
                        middle_ref[c, i - STEPS, at, :] = total
                here = after

        for c in range(parts):
            total = jnp.zeros((HALF, slots), jnp.float32)
            for s in range(2):
                lane = 0 if s == 0 else LANES - 1
                for i in range(rows):
                    total = total + ghost_ref[c, s, i, :, lane:lane + 1] * spread_ref[c, s, i:i + 1, :]
            partial_ref[c, at, :] = total

    level_halves(levels, half)


def mend_kernel(
    which, east_ref, north_ref, mine_ref, other_ref, ends_ref, spread_ref, partial_ref, out_ref, sum_ref
):
    parts, levels = sum_ref.shape[:2]
    rows = spread_ref.shape[2]
    width = east_ref.shape[-1]
    flip = 1 - parity() if which == 0 else parity()
    sign = sign_of(flip)
    turn = lambda r: r + flip * (STEPS - 1 - 2 * r)
    place = lambda r: flip * (rows - STEPS) + turn(r)

    def half(at):
        own = [Row(east_ref[0, place(r), at, :] * sign, north_ref[0, place(r), at, :]) for r in range(STEPS - 1)]
        near = Row(other_ref[FLUX_ROWS, at, :] * sign, other_ref[FLUX_ROWS + 1, at, :])
        far = Row(other_ref[FLUX_ROWS + 2, at, :] * sign)
        for c in range(parts):
            mine = lambda k: mine_ref[2 * k + c, at, :]
            theirs = lambda k: other_ref[2 * k + c, at, :]
            a0 = theirs(0)
            n1 = mine(0)
            b0 = own[0].stay(a0) + near.inward * n1 + theirs(1)
            b1 = own[0].inward * a0
            bn1 = near.stay(n1) + own[0].outward * a0 + mine(1)
            bn2 = near.outward * n1
            c0 = own[0].stay(b0) + near.inward * bn1 + own[1].outward * b1 + theirs(2)
            c1 = own[1].stay(b1) + own[0].inward * b0
            c2 = own[1].inward * b1
            cn1 = near.stay(bn1) + own[0].outward * b0 + far.inward * bn2 + mine(2)
            d0 = own[0].stay(c0) + near.inward * cn1 + own[1].outward * c1 + theirs(3)
            d1 = own[1].stay(c1) + own[0].inward * c0 + own[2].outward * c2
            d2 = own[2].stay(c2) + own[1].inward * c1
            d3 = own[2].inward * c2
            for r, value in enumerate((d0, d1, d2, d3)):
                out_ref[c, turn(r), at, :] = ends_ref[c, flip * STEPS + turn(r), at, :] + value
            total = partial_ref[c, at, :]
            for r, value in enumerate((a0 + b0 + c0, b1 + c1, c2)):
                i = place(r)
                rate = north_ref[0, i, at, :]
                south = jnp.maximum(rate[:, :1], 0.0) * value[:, :1]
                north = jnp.maximum(-rate[:, width - 1:], 0.0) * value[:, width - 1:]
                total = total + south * spread_ref[c, 0, pl.ds(i, 1), :]
                total = total + north * spread_ref[c, 1, pl.ds(i, 1), :]
            sum_ref[c, at, :] = total

    level_halves(levels, half)


def subtract_most(state_ref, middle_ref, side_ref, out_hbm, buffer, sems):
    parts, inner = middle_ref.shape[:2]
    rows = state_ref.shape[2]
    flip = parity()
    start = flip * (rows - STEPS)
    copies = []
    for c in range(parts):
        buffer[c, :inner] = state_ref[0, c, STEPS:STEPS + inner] - middle_ref[c]
        copies.append(
            pltpu.make_async_copy(buffer.at[c, pl.ds(0, inner)], out_hbm.at[0, c, pl.ds(STEPS, inner)], sems.at[2 * c])
        )
        copies[-1].start()
        for r in range(STEPS):
            buffer[c, inner + r] = state_ref[0, c, start + r] - side_ref[c, r]
        copies.append(
            pltpu.make_async_copy(
                buffer.at[c, pl.ds(inner, STEPS)], out_hbm.at[0, c, pl.ds(start, STEPS)], sems.at[2 * c + 1]
            )
        )
        copies[-1].start()
    for copy in copies:
        copy.wait()


def subtract_last(begun_hbm, state_ref, side_ref, out_hbm, buffer, sems):
    parts = side_ref.shape[0]
    rows = state_ref.shape[2]
    start = (1 - parity()) * (rows - STEPS)
    copies = []
    for c in range(parts):
        for r in range(STEPS):
            buffer[c, r] = state_ref[0, c, start + r] - side_ref[c, r]
        copies.append(pltpu.make_async_copy(buffer.at[c], out_hbm.at[0, c, pl.ds(start, STEPS)], sems.at[c]))
        copies[-1].start()
    for copy in copies:
        copy.wait()


def cost(flops, moved):
    return pl.CostEstimate(flops=flops, bytes_accessed=moved, transcendentals=0)


PARAMS = pltpu.CompilerParams(vmem_limit_bytes=24 * 1024 * 1024)


def local(
    adjoint_state,
    courant_east,
    courant_north,
    parent_cell,
    stencil_offset,
    stencil_weight,
    owner_slot,
):
    _, parts, rows, levels, width = adjoint_state.shape
    slots = owner_slot.shape[0]
    inner = rows - 2 * STEPS
    row_bytes = levels * width * 4
    f32 = lambda *shape: jax.ShapeDtypeStruct(shape, jnp.float32)
    vmem = pl.BlockSpec(memory_space=pltpu.VMEM)
    smem = pl.BlockSpec(memory_space=pltpu.SMEM)
    hbm = pl.BlockSpec(memory_space=pltpu.HBM)
    in_hbm = lambda value: pltpu.with_memory_space_constraint(value, pltpu.HBM)

    first_pack, state, east, north = pl.pallas_call(
        first_kernel,
        in_specs=[hbm] * 3,
        out_specs=[vmem] * 4,
        out_shape=[
            f32(PACK_ROWS, levels, width),
            f32(*adjoint_state.shape), f32(*courant_east.shape), f32(*courant_north.shape),
        ],
        scratch_shapes=[pltpu.SemaphoreType.DMA((parts + 2,)), pltpu.SemaphoreType.DMA((parts + 2,))],
        compiler_params=PARAMS,
        cost_estimate=cost(12 * levels * width * 13, 48 * row_bytes),
        name="first_pack",
    )(in_hbm(adjoint_state), in_hbm(courant_east), in_hbm(courant_north))
    first_came = alternating(first_pack, -1)

    second_pack, middle, ends, spread, partial = pl.pallas_call(
        sweep_kernel,
        in_specs=[smem] * 4 + [vmem] * 3,
        out_specs=[vmem] * 5,
        out_shape=[
            f32(PACK_ROWS, levels, width),
            f32(parts, inner, levels, width),
            f32(parts, 2 * STEPS, levels, width),
            f32(parts, 2, rows, slots),
            f32(parts, levels, slots),
        ],
        scratch_shapes=[
            pltpu.VMEM((2, parts, rows, HALF, width), jnp.float32),
            pltpu.VMEM((rows, HALF, width), jnp.float32),
            pltpu.VMEM((rows, HALF, width), jnp.float32),
            pltpu.VMEM((rows, HALF, width), jnp.float32),
            pltpu.VMEM((parts, 2, rows, HALF, LANES), jnp.float32),
        ],
        compiler_params=PARAMS,
        cost_estimate=cost(8 * rows * levels * width * 13, 6 * rows * row_bytes),
        name="sweep",
    )(parent_cell, stencil_offset, stencil_weight, owner_slot, state, east, north)
    middle_came = along(middle, "sub", -1)
    second_came = alternating(second_pack, 1)

    def mend(which, mine, other, so_far):
        return pl.pallas_call(
            functools.partial(mend_kernel, which),
            in_specs=[vmem] * 7,
            out_specs=[vmem] * 2,
            out_shape=[f32(parts, STEPS, levels, width), f32(parts, levels, slots)],
            compiler_params=PARAMS,
            cost_estimate=cost(16 * levels * width * 13, 46 * row_bytes),
            name="mend_" + "ab"[which],
        )(east, north, mine, other, ends, spread, so_far)

    side_a, partial = mend(0, second_pack, first_came, partial)
    a_came = along(side_a, "sub", -1)
    side_b, partial = mend(1, first_pack, second_came, partial)
    b_came = along(side_b, "sub", -1)

    subs, hors = lax.axis_size("sub"), lax.axis_size("hor")
    gathered = lax.all_gather(partial, ("sub", "hor"))
    mine_part = lax.dynamic_slice(
        gathered,
        (0, 0, lax.axis_index("sub") * (levels // subs), lax.axis_index("hor") * (slots // hors)),
        (subs * hors, parts, levels // subs, slots // hors),
    )
    boundary_gradient = jnp.sum(mine_part, 0)

    begun = pl.pallas_call(
        subtract_most,
        in_specs=[vmem] * 3,
        out_specs=hbm,
        out_shape=f32(*adjoint_state.shape),
        scratch_shapes=[
            pltpu.VMEM((parts, inner + STEPS, levels, width), jnp.float32),
            pltpu.SemaphoreType.DMA((2 * parts,)),
        ],
        compiler_params=PARAMS,
        cost_estimate=cost(parts * 8 * levels * width, 48 * row_bytes),
        name="subtract_most",
    )(state, middle_came, a_came)
    adjoint_result = pl.pallas_call(
        subtract_last,
        in_specs=[hbm, vmem, vmem],
        out_specs=hbm,
        out_shape=f32(*adjoint_state.shape),
        input_output_aliases={0: 0},
        scratch_shapes=[
            pltpu.VMEM((parts, STEPS, levels, width), jnp.float32),
            pltpu.SemaphoreType.DMA((parts,)),
        ],
        compiler_params=PARAMS,
        cost_estimate=cost(parts * 4 * levels * width, 24 * row_bytes),
        name="subtract_last",
    )(begun, state, b_came)
    return (adjoint_result, boundary_gradient)


def solution(mesh):
    in_specs = (
        P(("ens", "sub"), None, "hor", None, None),
        P(("ens", "sub"), "hor", None, None),
        P(("ens", "sub"), "hor", None, None),
        P(None, None, "hor"),
        P(None, None, None, "hor"),
        P(None, None, None, "hor"),
        P(),
    )
    out_specs = (P(("ens", "sub"), None, "hor", None, None), P("ens", "sub", "hor"))
    return jax.shard_map(local, mesh=mesh, in_specs=in_specs, out_specs=out_specs, check_vma=False)
```

```python
import functools

import jax
import jax.numpy as jnp
from jax import lax
from jax.experimental import pallas as pl
from jax.experimental.pallas import tpu as pltpu
from jax.sharding import PartitionSpec as P

STEPS = 4
HALF = 8
FLUX_ROWS = 2 * STEPS
PACK_ROWS = FLUX_ROWS + 3
LANES = 128


def along(value, axis, step_of):
    peers = lax.axis_size(axis)
    pairs = [(i, i + step_of) for i in range(peers) if 0 <= i + step_of < peers]
    return lax.ppermute(value, axis, pairs)


def alternating(value, sign):
    subs, hors = lax.axis_size("sub"), lax.axis_size("hor")
    pairs = []
    for s in range(subs):
        step = sign if s % 2 == 0 else -sign
        pairs += [(s * hors + h, s * hors + h + step) for h in range(hors) if 0 <= h + step < hors]
    return lax.ppermute(value, ("sub", "hor"), pairs)


def parity():
    return lax.rem(lax.axis_index("sub"), 2)


def sign_of(flip):
    return jnp.where(flip == 1, jnp.float32(-1.0), jnp.float32(1.0))


def north_rates(north_rate):
    width = north_rate.shape[-1]
    column = lax.broadcasted_iota(jnp.int32, north_rate.shape, len(north_rate.shape) - 1)
    plus = jnp.where(column == 0, 0.0, jnp.maximum(north_rate, 0.0))
    minus = jnp.where(column == width - 1, 0.0, jnp.maximum(-north_rate, 0.0))
    return plus, minus


def shifted(flux_plus, flux_minus):
    width = flux_plus.shape[-1]
    axis = len(flux_plus.shape) - 1
    return pltpu.roll(flux_plus, width - 1, axis) + pltpu.roll(flux_minus, 1, axis)


class Row:
    def __init__(self, east_rate, north_rate=None):
        self.outward = jnp.maximum(east_rate, 0.0)
        self.inward = jnp.maximum(-east_rate, 0.0)
        if north_rate is not None:
            self.centre = 1.0 - jnp.abs(east_rate) - jnp.abs(north_rate)
            self.plus, self.minus = north_rates(north_rate)

    def stay(self, value):
        return self.centre * value + shifted(self.plus * value, self.minus * value)


def level_halves(levels, body):
    def step(h, carry):
        body(pl.ds(pl.multiple_of(h * HALF, HALF), HALF))
        return carry

    lax.fori_loop(0, levels // HALF, step, 0)


def first_kernel(state_hbm, east_hbm, north_hbm, pack_ref, state_ref, east_ref, north_ref, sems):
    parts, rows, levels = state_hbm.shape[1:4]
    flip = parity()
    sign = sign_of(flip)
    at_end = pl.ds(flip * (rows - STEPS), STEPS)
    place = lambda r: r + flip * (STEPS - 1 - 2 * r)
    copies = [
        pltpu.make_async_copy(state_hbm.at[0, c, at_end], state_ref.at[c], sems.at[c]) for c in range(parts)
    ]
    copies.append(pltpu.make_async_copy(east_hbm.at[0, at_end], east_ref, sems.at[parts]))
    copies.append(pltpu.make_async_copy(north_hbm.at[0, at_end], north_ref, sems.at[parts + 1]))
    for copy in copies:
        copy.start()
    for copy in copies:
        copy.wait()

    def half(at):
        row = [Row(east_ref[place(r), at, :] * sign, north_ref[place(r), at, :]) for r in range(STEPS)]
        pack_ref[FLUX_ROWS, at, :] = east_ref[place(0), at, :]
        pack_ref[FLUX_ROWS + 1, at, :] = north_ref[place(0), at, :]
        pack_ref[FLUX_ROWS + 2, at, :] = east_ref[place(1), at, :]
        for c in range(parts):
            field = [state_ref[c, place(r), at, :] for r in range(STEPS)]
            for k in range(STEPS):
                pack_ref[2 * k + c, at, :] = row[0].outward * field[0]
                after = []
                for r in range(STEPS - 1 - k):
                    value = row[r].stay(field[r]) + row[r + 1].outward * field[r + 1]
                    if r > 0:
                        value = value + row[r - 1].inward * field[r - 1]
                    after.append(value)
                field = after

    level_halves(levels, half)


def as_column(row):
    count = row.shape[1]
    here = lax.broadcasted_iota(jnp.int32, (count, count), 0)
    there = lax.broadcasted_iota(jnp.int32, (count, count), 1)
    return jnp.sum(jnp.where(here == there, row, 0), axis=1, keepdims=True)


def sweep_kernel(
    cell_ref, offset_ref, weight_ref, owner_ref, state_ref, east_ref, north_ref,
    pack_ref, middle_ref, ends_ref, spread_ref, partial_ref,
    field, to_east, to_west, plus_ref, minus_ref, centre_ref,
):
    parts, rows, levels, width = state_ref.shape[1:]
    slots = spread_ref.shape[-1]
    flip = 1 - parity()
    sign = sign_of(flip)
    end_row = flip * (rows - 1)
    next_row = end_row + 1 - 2 * flip

    nothing = jnp.zeros((levels, width), jnp.float32)
    for edge in (0, rows + 1):
        to_east[edge] = nothing
        to_west[edge] = nothing
        for slot in range(STEPS):
            for c in range(parts):
                field[slot, c, edge] = nothing

    def prepare(i, carry):
        east_rate = east_ref[0, i]
        north_rate = north_ref[0, i]
        to_west[i + 1] = jnp.maximum(east_rate, 0.0)
        to_east[i + 1] = jnp.maximum(-east_rate, 0.0)
        centre_ref[i] = 1.0 - jnp.abs(east_rate) - jnp.abs(north_rate)
        plus_ref[i], minus_ref[i] = north_rates(north_rate)
        for c in range(parts):
            field[0, c, i + 1] = state_ref[0, c, i]
        return carry

    lax.fori_loop(0, rows, prepare, 0, unroll=2)

    pack_ref[FLUX_ROWS] = east_ref[0, end_row]
    pack_ref[FLUX_ROWS + 1] = north_ref[0, end_row]
    pack_ref[FLUX_ROWS + 2] = east_ref[0, next_row]

    def advance(k, i, c, at):
        value = field[k, c, i + 1, at, :]
        total = centre_ref[i, at, :] * value + shifted(plus_ref[i, at, :] * value, minus_ref[i, at, :] * value)
        total = total + to_west[i + 2, at, :] * field[k, c, i + 2, at, :]
        return total + to_east[i, at, :] * field[k, c, i, at, :]

    halves = [pl.ds(h * HALF, HALF) for h in range(levels // HALF)]
    for k in range(STEPS):
        leaving = jnp.maximum(east_ref[0, end_row] * sign, 0.0)
        for c in range(parts):
            pack_ref[2 * k + c] = leaving * field[k, c, end_row + 1]

        if k < STEPS - 1:

            def one_row(i, carry, k=k):
                for at in halves:
                    for c in range(parts):
                        field[k + 1, c, i + 1, at, :] = advance(k, i, c, at)
                return carry

            lax.fori_loop(0, rows, one_row, 0, unroll=2)
        else:

            def end_rows(i, carry, k=k):
                for at in halves:
                    for c in range(parts):
                        ends_ref[c, i, at, :] = advance(k, i, c, at)
                        ends_ref[c, i + STEPS, at, :] = advance(k, i + rows - STEPS, c, at)
                return carry

            def middle_row(i, carry, k=k):
                for at in halves:
                    for c in range(parts):
                        middle_ref[c, i, at, :] = advance(k, i + STEPS, c, at)
                return carry

            lax.fori_loop(0, STEPS, end_rows, 0)
            lax.fori_loop(0, rows - 2 * STEPS, middle_row, 0, unroll=2)

    here = lax.broadcasted_iota(jnp.int32, (slots, slots), 1)
    placing = jnp.where(as_column(owner_ref[...]) == here, 1.0, 0.0)
    cells = lax.broadcasted_iota(jnp.int32, (rows, slots), 1)
    for c in range(parts):
        for s in range(2):
            mixing = jnp.zeros((rows, slots), jnp.float32)
            for point in range(offset_ref.shape[0]):
                target = as_column(cell_ref[c, s:s + 1, :] + offset_ref[point, c, s:s + 1, :])
                mixing = mixing + jnp.where(target == cells, as_column(weight_ref[point, c, s:s + 1, :]), 0.0)
            spread_ref[c, s] = jnp.dot(
                mixing, placing, precision=lax.Precision.HIGHEST, preferred_element_type=jnp.float32
            )

    for c in range(parts):
        total = jnp.zeros((levels, slots), jnp.float32)
        for i in range(rows):
            rate = north_ref[0, i]
            iterates = [field[k, c, i + 1] for k in range(STEPS)]
            first = sum(value[:, :1] for value in iterates)
            last = sum(value[:, width - 1:] for value in iterates)
            total = total + (jnp.maximum(rate[:, :1], 0.0) * first) * spread_ref[c, 0, i:i + 1, :]
            total = total + (jnp.maximum(-rate[:, width - 1:], 0.0) * last) * spread_ref[c, 1, i:i + 1, :]
        partial_ref[c] = total


def mend_kernel(
    which, east_ref, north_ref, mine_ref, other_ref, ends_ref, spread_ref, partial_ref, out_ref, sum_ref
):
    parts, levels, slots = partial_ref.shape
    rows = spread_ref.shape[2]
    width = east_ref.shape[-1]
    flip = 1 - parity() if which == 0 else parity()
    sign = sign_of(flip)
    turn = lambda r: r + flip * (STEPS - 1 - 2 * r)
    place = lambda r: flip * (rows - STEPS) + turn(r)

    def half(at):
        own = [Row(east_ref[0, place(r), at, :] * sign, north_ref[0, place(r), at, :]) for r in range(STEPS - 1)]
        near = Row(other_ref[FLUX_ROWS, at, :] * sign, other_ref[FLUX_ROWS + 1, at, :])
        far = Row(other_ref[FLUX_ROWS + 2, at, :] * sign)
        for c in range(parts):
            mine = lambda k: mine_ref[2 * k + c, at, :]
            theirs = lambda k: other_ref[2 * k + c, at, :]
            a0 = theirs(0)
            n1 = mine(0)
            b0 = own[0].stay(a0) + near.inward * n1 + theirs(1)
            b1 = own[0].inward * a0
            bn1 = near.stay(n1) + own[0].outward * a0 + mine(1)
            bn2 = near.outward * n1
            c0 = own[0].stay(b0) + near.inward * bn1 + own[1].outward * b1 + theirs(2)
            c1 = own[1].stay(b1) + own[0].inward * b0
            c2 = own[1].inward * b1
            cn1 = near.stay(bn1) + own[0].outward * b0 + far.inward * bn2 + mine(2)
            d0 = own[0].stay(c0) + near.inward * cn1 + own[1].outward * c1 + theirs(3)
            d1 = own[1].stay(c1) + own[0].inward * c0 + own[2].outward * c2
            d2 = own[2].stay(c2) + own[1].inward * c1
            d3 = own[2].inward * c2
            for r, value in enumerate((d0, d1, d2, d3)):
                out_ref[c, turn(r), at, :] = ends_ref[c, flip * STEPS + turn(r), at, :] + value
            total = partial_ref[c, at, :]
            for r, value in enumerate((a0 + b0 + c0, b1 + c1, c2)):
                i = place(r)
                rate = north_ref[0, i, at, :]
                south = jnp.maximum(rate[:, :1], 0.0) * value[:, :1]
                north = jnp.maximum(-rate[:, width - 1:], 0.0) * value[:, width - 1:]
                total = total + south * spread_ref[c, 0, pl.ds(i, 1), :]
                total = total + north * spread_ref[c, 1, pl.ds(i, 1), :]
            if which == 0:
                sum_ref[c, at, :] = total
            else:
                share = sum_ref.shape[-1]
                for p in range(slots // share):
                    sum_ref[p, c, at, :] = total[:, p * share:(p + 1) * share]

    level_halves(levels, half)


def join_hor(came_ref, out_ref):
    subs, parts, share = out_ref.shape[:3]
    total = jnp.sum(came_ref[...], 0)
    for s in range(subs):
        for c in range(parts):
            out_ref[s, c] = total[c, s * share:(s + 1) * share]


def join_sub(came_ref, out_ref):
    out_ref[...] = jnp.sum(came_ref[...], 0)


def subtract_most(state_ref, middle_ref, side_ref, out_hbm, buffer, sems):
    parts, inner = middle_ref.shape[:2]
    rows = state_ref.shape[2]
    flip = parity()
    start = flip * (rows - STEPS)
    copies = []
    for c in range(parts):
        buffer[c, :inner] = state_ref[0, c, STEPS:STEPS + inner] - middle_ref[c]
        copies.append(
            pltpu.make_async_copy(buffer.at[c, pl.ds(0, inner)], out_hbm.at[0, c, pl.ds(STEPS, inner)], sems.at[2 * c])
        )
        copies[-1].start()
        for r in range(STEPS):
            buffer[c, inner + r] = state_ref[0, c, start + r] - side_ref[c, r]
        copies.append(
            pltpu.make_async_copy(
                buffer.at[c, pl.ds(inner, STEPS)], out_hbm.at[0, c, pl.ds(start, STEPS)], sems.at[2 * c + 1]
            )
        )
        copies[-1].start()
    for copy in copies:
        copy.wait()


def subtract_last(begun_hbm, state_ref, side_ref, out_hbm, buffer, sems):
    parts = side_ref.shape[0]
    rows = state_ref.shape[2]
    start = (1 - parity()) * (rows - STEPS)
    copies = []
    for c in range(parts):
        for r in range(STEPS):
            buffer[c, r] = state_ref[0, c, start + r] - side_ref[c, r]
        copies.append(pltpu.make_async_copy(buffer.at[c], out_hbm.at[0, c, pl.ds(start, STEPS)], sems.at[c]))
        copies[-1].start()
    for copy in copies:
        copy.wait()


def cost(flops, moved):
    return pl.CostEstimate(flops=flops, bytes_accessed=moved, transcendentals=0)


PARAMS = pltpu.CompilerParams(vmem_limit_bytes=24 * 1024 * 1024)


def local(
    adjoint_state,
    courant_east,
    courant_north,
    parent_cell,
    stencil_offset,
    stencil_weight,
    owner_slot,
):
    _, parts, rows, levels, width = adjoint_state.shape
    slots = owner_slot.shape[0]
    inner = rows - 2 * STEPS
    row_bytes = levels * width * 4
    f32 = lambda *shape: jax.ShapeDtypeStruct(shape, jnp.float32)
    vmem = pl.BlockSpec(memory_space=pltpu.VMEM)
    smem = pl.BlockSpec(memory_space=pltpu.SMEM)
    hbm = pl.BlockSpec(memory_space=pltpu.HBM)
    in_hbm = lambda value: pltpu.with_memory_space_constraint(value, pltpu.HBM)

    first_pack = pl.pallas_call(
        first_kernel,
        in_specs=[hbm] * 3,
        out_specs=vmem,
        out_shape=f32(PACK_ROWS, levels, width),
        scratch_shapes=[
            pltpu.VMEM((parts, STEPS, levels, width), jnp.float32),
            pltpu.VMEM((STEPS, levels, width), jnp.float32),
            pltpu.VMEM((STEPS, levels, width), jnp.float32),
            pltpu.SemaphoreType.DMA((parts + 2,)),
        ],
        compiler_params=PARAMS,
        cost_estimate=cost(12 * levels * width * 13, 27 * row_bytes),
        name="first_pack",
    )(in_hbm(adjoint_state), in_hbm(courant_east), in_hbm(courant_north))
    first_came = alternating(first_pack, -1)

    state, east, north = adjoint_state, courant_east, courant_north
    second_pack, middle, ends, spread, partial = pl.pallas_call(
        sweep_kernel,
        in_specs=[vmem] * 7,
        out_specs=[vmem] * 5,
        out_shape=[
            f32(PACK_ROWS, levels, width),
            f32(parts, inner, levels, width),
            f32(parts, 2 * STEPS, levels, width),
            f32(parts, 2, rows, slots),
            f32(parts, levels, slots),
        ],
        scratch_shapes=[
            pltpu.VMEM((STEPS, parts, rows + 2, levels, width), jnp.float32),
            pltpu.VMEM((rows + 2, levels, width), jnp.float32),
            pltpu.VMEM((rows + 2, levels, width), jnp.float32),
            pltpu.VMEM((rows, levels, width), jnp.float32),
            pltpu.VMEM((rows, levels, width), jnp.float32),
            pltpu.VMEM((rows, levels, width), jnp.float32),
        ],
        compiler_params=PARAMS,
        cost_estimate=cost(8 * rows * levels * width * 13, 6 * rows * row_bytes),
        name="sweep",
    )(parent_cell, stencil_offset, stencil_weight, owner_slot[None], state, east, north)
    middle_came = along(middle, "sub", -1)
    second_came = alternating(second_pack, 1)

    subs, hors = lax.axis_size("sub"), lax.axis_size("hor")

    def mend(which, mine, other, so_far):
        summed = f32(parts, levels, slots) if which == 0 else f32(hors, parts, levels, slots // hors)
        return pl.pallas_call(
            functools.partial(mend_kernel, which),
            in_specs=[vmem] * 7,
            out_specs=[vmem] * 2,
            out_shape=[f32(parts, STEPS, levels, width), summed],
            compiler_params=PARAMS,
            cost_estimate=cost(16 * levels * width * 13, 46 * row_bytes),
            name="mend_" + "ab"[which],
        )(east, north, mine, other, ends, spread, so_far)

    side_a, partial = mend(0, second_pack, first_came, partial)
    a_came = along(side_a, "sub", -1)
    side_b, pieces = mend(1, first_pack, second_came, partial)
    b_came = along(side_b, "sub", -1)

    pieces = lax.all_to_all(pieces, "hor", 0, 0, tiled=True)
    pieces = pl.pallas_call(
        join_hor,
        in_specs=[vmem],
        out_specs=vmem,
        out_shape=f32(subs, parts, levels // subs, slots // hors),
        compiler_params=PARAMS,
        name="join_hor",
    )(pieces)
    pieces = lax.all_to_all(pieces, "sub", 0, 0, tiled=True)
    boundary_gradient = pl.pallas_call(
        join_sub,
        in_specs=[vmem],
        out_specs=vmem,
        out_shape=f32(parts, levels // subs, slots // hors),
        compiler_params=PARAMS,
        name="join_sub",
    )(pieces)

    begun = pl.pallas_call(
        subtract_most,
        in_specs=[vmem] * 3,
        out_specs=hbm,
        out_shape=f32(*adjoint_state.shape),
        scratch_shapes=[
            pltpu.VMEM((parts, inner + STEPS, levels, width), jnp.float32),
            pltpu.SemaphoreType.DMA((2 * parts,)),
        ],
        compiler_params=PARAMS,
        cost_estimate=cost(parts * 8 * levels * width, 48 * row_bytes),
        name="subtract_most",
    )(state, middle_came, a_came)
    adjoint_result = pl.pallas_call(
        subtract_last,
        in_specs=[hbm, vmem, vmem],
        out_specs=hbm,
        out_shape=f32(*adjoint_state.shape),
        input_output_aliases={0: 0},
        scratch_shapes=[
            pltpu.VMEM((parts, STEPS, levels, width), jnp.float32),
            pltpu.SemaphoreType.DMA((parts,)),
        ],
        compiler_params=PARAMS,
        cost_estimate=cost(parts * 4 * levels * width, 24 * row_bytes),
        name="subtract_last",
    )(begun, state, b_came)
    return (adjoint_result, boundary_gradient)


def solution(mesh):
    in_specs = (
        P(("ens", "sub"), None, "hor", None, None),
        P(("ens", "sub"), "hor", None, None),
        P(("ens", "sub"), "hor", None, None),
        P(None, None, "hor"),
        P(None, None, None, "hor"),
        P(None, None, None, "hor"),
        P(),
    )
    out_specs = (P(("ens", "sub"), None, "hor", None, None), P("ens", "sub", "hor"))
    return jax.shard_map(local, mesh=mesh, in_specs=in_specs, out_specs=out_specs, check_vma=False)
```

```python
import functools

import jax
import jax.numpy as jnp
from jax import lax
from jax.experimental import pallas as pl
from jax.experimental.pallas import tpu as pltpu
from jax.sharding import PartitionSpec as P

STEPS = 4
HALF = 8
FLUX_ROWS = 2 * STEPS
PACK_ROWS = FLUX_ROWS + 3
LANES = 128


def along(value, axis, step_of):
    peers = lax.axis_size(axis)
    pairs = [(i, i + step_of) for i in range(peers) if 0 <= i + step_of < peers]
    return lax.ppermute(value, axis, pairs)


def alternating(value, sign):
    subs, hors = lax.axis_size("sub"), lax.axis_size("hor")
    pairs = []
    for s in range(subs):
        step = sign if s % 2 == 0 else -sign
        pairs += [(s * hors + h, s * hors + h + step) for h in range(hors) if 0 <= h + step < hors]
    return lax.ppermute(value, ("sub", "hor"), pairs)


def parity():
    return lax.rem(lax.axis_index("sub"), 2)


def sign_of(flip):
    return jnp.where(flip == 1, jnp.float32(-1.0), jnp.float32(1.0))


def north_rates(north_rate):
    width = north_rate.shape[-1]
    column = lax.broadcasted_iota(jnp.int32, north_rate.shape, len(north_rate.shape) - 1)
    plus = jnp.where(column == 0, 0.0, jnp.maximum(north_rate, 0.0))
    minus = jnp.where(column == width - 1, 0.0, jnp.maximum(-north_rate, 0.0))
    return plus, minus


def shifted(flux_plus, flux_minus):
    width = flux_plus.shape[-1]
    axis = len(flux_plus.shape) - 1
    return pltpu.roll(flux_plus, width - 1, axis) + pltpu.roll(flux_minus, 1, axis)


class Row:
    def __init__(self, east_rate, north_rate=None):
        self.outward = jnp.maximum(east_rate, 0.0)
        self.inward = jnp.maximum(-east_rate, 0.0)
        if north_rate is not None:
            self.centre = 1.0 - jnp.abs(east_rate) - jnp.abs(north_rate)
            self.plus, self.minus = north_rates(north_rate)

    def stay(self, value):
        return self.centre * value + shifted(self.plus * value, self.minus * value)


def level_halves(levels, body):
    def step(h, carry):
        body(pl.ds(pl.multiple_of(h * HALF, HALF), HALF))
        return carry

    lax.fori_loop(0, levels // HALF, step, 0)


def first_kernel(state_hbm, east_hbm, north_hbm, pack_ref, state_ref, east_ref, north_ref, sems):
    parts, rows, levels = state_hbm.shape[1:4]
    flip = parity()
    sign = sign_of(flip)
    at_end = pl.ds(flip * (rows - STEPS), STEPS)
    place = lambda r: r + flip * (STEPS - 1 - 2 * r)
    halves = levels // HALF
    copies = []
    for h in range(halves):
        at = pl.ds(h * HALF, HALF)
        sem = sems.at[h]
        batch = [
            pltpu.make_async_copy(state_hbm.at[0, c, at_end, at], state_ref.at[c, :, at], sem.at[c])
            for c in range(parts)
        ]
        batch.append(pltpu.make_async_copy(east_hbm.at[0, at_end, at], east_ref.at[:, at], sem.at[parts]))
        batch.append(pltpu.make_async_copy(north_hbm.at[0, at_end, at], north_ref.at[:, at], sem.at[parts + 1]))
        copies.append(batch)
        for copy in batch:
            copy.start()

    def half(at):
        row = [Row(east_ref[place(r), at, :] * sign, north_ref[place(r), at, :]) for r in range(STEPS)]
        pack_ref[FLUX_ROWS, at, :] = east_ref[place(0), at, :]
        pack_ref[FLUX_ROWS + 1, at, :] = north_ref[place(0), at, :]
        pack_ref[FLUX_ROWS + 2, at, :] = east_ref[place(1), at, :]
        for c in range(parts):
            field = [state_ref[c, place(r), at, :] for r in range(STEPS)]
            for k in range(STEPS):
                pack_ref[2 * k + c, at, :] = row[0].outward * field[0]
                after = []
                for r in range(STEPS - 1 - k):
                    value = row[r].stay(field[r]) + row[r + 1].outward * field[r + 1]
                    if r > 0:
                        value = value + row[r - 1].inward * field[r - 1]
                    after.append(value)
                field = after

    for h in range(halves):
        for copy in copies[h]:
            copy.wait()
        half(pl.ds(h * HALF, HALF))


def as_column(row):
    count = row.shape[1]
    here = lax.broadcasted_iota(jnp.int32, (count, count), 0)
    there = lax.broadcasted_iota(jnp.int32, (count, count), 1)
    return jnp.sum(jnp.where(here == there, row, 0), axis=1, keepdims=True)


def sweep_kernel(
    state_ref, east_ref, north_ref, pack_ref, middle_ref, ends_ref, column_ref,
    field, plus_ref, minus_ref, centre_ref,
):
    parts, rows, levels, width = state_ref.shape[1:]
    flip = 1 - parity()
    sign = sign_of(flip)
    end_row = flip * (rows - 1)
    next_row = end_row + 1 - 2 * flip

    def half(at):
        pack_ref[FLUX_ROWS, at, :] = east_ref[0, end_row, at, :]
        pack_ref[FLUX_ROWS + 1, at, :] = north_ref[0, end_row, at, :]
        pack_ref[FLUX_ROWS + 2, at, :] = east_ref[0, next_row, at, :]

        for k in range(STEPS):
            if k == 0:
                read = lambda c, i: state_ref[0, c, i, at, :]
            else:
                read = lambda c, i, slot=k - 1: field[slot, c, i]
            leaving = jnp.maximum(east_ref[0, end_row, at, :] * sign, 0.0)
            for c in range(parts):
                pack_ref[2 * k + c, at, :] = leaving * read(c, end_row)
            west = [None] * parts
            here = [read(c, 0) for c in range(parts)]
            east_here = east_ref[0, 0, at, :]
            for i in range(rows):
                leave_west = jnp.maximum(-east_here, 0.0)
                if k == 0:
                    north_rate = north_ref[0, i, at, :]
                    centre = 1.0 - jnp.abs(east_here) - jnp.abs(north_rate)
                    plus, minus = north_rates(north_rate)
                    centre_ref[i], plus_ref[i], minus_ref[i] = centre, plus, minus
                else:
                    centre, plus, minus = centre_ref[i], plus_ref[i], minus_ref[i]
                if i + 1 < rows:
                    east_here = east_ref[0, i + 1, at, :]
                    east_after = jnp.maximum(east_here, 0.0)
                for c in range(parts):
                    value = here[c]
                    total = centre * value + shifted(plus * value, minus * value)
                    if i > 0:
                        total = total + west[c]
                    if i + 1 < rows:
                        west[c] = leave_west * value
                        here[c] = read(c, i + 1)
                        total = total + east_after * here[c]
                    if k < STEPS - 1:
                        field[k, c, i] = total
                    elif i < STEPS:
                        ends_ref[c, i, at, :] = total
                    elif i >= rows - STEPS:
                        ends_ref[c, i - rows + 2 * STEPS, at, :] = total
                    else:
                        middle_ref[c, i - STEPS, at, :] = total

        def columns(i, carry):
            for c in range(parts):
                value = state_ref[0, c, i, at, :]
                first, last = value[:, :LANES], value[:, width - LANES:]
                for slot in range(STEPS - 1):
                    first = first + field[slot, c, i, :, :LANES]
                    last = last + field[slot, c, i, :, width - LANES:]
                column_ref[c, 0, i, at, :] = first
                column_ref[c, 1, i, at, :] = last
            return carry

        lax.fori_loop(0, rows, columns, 0, unroll=2)

    level_halves(levels, half)


def ghost_kernel(
    cell_ref, offset_ref, weight_ref, owner_ref, column_ref, north_hbm, spread_ref, partial_ref, first_rate, last_rate, sems
):
    parts, _, rows, levels, _ = column_ref.shape
    slots = spread_ref.shape[-1]
    width = north_hbm.shape[-1]
    copies = [
        pltpu.make_async_copy(north_hbm.at[0, :, :, pl.ds(0, LANES)], first_rate, sems.at[0]),
        pltpu.make_async_copy(north_hbm.at[0, :, :, pl.ds(width - LANES, LANES)], last_rate, sems.at[1]),
    ]
    for copy in copies:
        copy.start()

    here = lax.broadcasted_iota(jnp.int32, (slots, slots), 1)
    placing = jnp.where(as_column(owner_ref[...]) == here, 1.0, 0.0)
    cells = lax.broadcasted_iota(jnp.int32, (rows, slots), 1)
    for c in range(parts):
        for s in range(2):
            mixing = jnp.zeros((rows, slots), jnp.float32)
            for point in range(offset_ref.shape[0]):
                target = as_column(cell_ref[c, s:s + 1, :] + offset_ref[point, c, s:s + 1, :])
                mixing = mixing + jnp.where(target == cells, as_column(weight_ref[point, c, s:s + 1, :]), 0.0)
            spread_ref[c, s] = jnp.dot(
                mixing, placing, precision=lax.Precision.HIGHEST, preferred_element_type=jnp.float32
            )

    for copy in copies:
        copy.wait()
    for c in range(parts):
        total = jnp.zeros((levels, slots), jnp.float32)
        for i in range(rows):
            south = jnp.maximum(first_rate[i, :, :1], 0.0) * column_ref[c, 0, i, :, :1]
            north = jnp.maximum(-last_rate[i, :, LANES - 1:], 0.0) * column_ref[c, 1, i, :, LANES - 1:]
            total = total + south * spread_ref[c, 0, i:i + 1, :]
            total = total + north * spread_ref[c, 1, i:i + 1, :]
        partial_ref[c] = total


def mend_kernel(
    which, east_ref, north_ref, mine_ref, other_ref, ends_ref, spread_ref, partial_ref, out_ref, sum_ref
):
    parts, levels, slots = partial_ref.shape
    rows = spread_ref.shape[2]
    width = east_ref.shape[-1]
    flip = 1 - parity() if which == 0 else parity()
    sign = sign_of(flip)
    turn = lambda r: r + flip * (STEPS - 1 - 2 * r)
    place = lambda r: flip * (rows - STEPS) + turn(r)

    def half(at):
        own = [Row(east_ref[0, place(r), at, :] * sign, north_ref[0, place(r), at, :]) for r in range(STEPS - 1)]
        near = Row(other_ref[FLUX_ROWS, at, :] * sign, other_ref[FLUX_ROWS + 1, at, :])
        far = Row(other_ref[FLUX_ROWS + 2, at, :] * sign)
        for c in range(parts):
            mine = lambda k: mine_ref[2 * k + c, at, :]
            theirs = lambda k: other_ref[2 * k + c, at, :]
            a0 = theirs(0)
            n1 = mine(0)
            b0 = own[0].stay(a0) + near.inward * n1 + theirs(1)
            b1 = own[0].inward * a0
            bn1 = near.stay(n1) + own[0].outward * a0 + mine(1)
            bn2 = near.outward * n1
            c0 = own[0].stay(b0) + near.inward * bn1 + own[1].outward * b1 + theirs(2)
            c1 = own[1].stay(b1) + own[0].inward * b0
            c2 = own[1].inward * b1
            cn1 = near.stay(bn1) + own[0].outward * b0 + far.inward * bn2 + mine(2)
            d0 = own[0].stay(c0) + near.inward * cn1 + own[1].outward * c1 + theirs(3)
            d1 = own[1].stay(c1) + own[0].inward * c0 + own[2].outward * c2
            d2 = own[2].stay(c2) + own[1].inward * c1
            d3 = own[2].inward * c2
            for r, value in enumerate((d0, d1, d2, d3)):
                out_ref[c, turn(r), at, :] = ends_ref[c, flip * STEPS + turn(r), at, :] + value
            total = partial_ref[c, at, :]
            for r, value in enumerate((a0 + b0 + c0, b1 + c1, c2)):
                i = place(r)
                rate = north_ref[0, i, at, :]
                south = jnp.maximum(rate[:, :1], 0.0) * value[:, :1]
                north = jnp.maximum(-rate[:, width - 1:], 0.0) * value[:, width - 1:]
                total = total + south * spread_ref[c, 0, pl.ds(i, 1), :]
                total = total + north * spread_ref[c, 1, pl.ds(i, 1), :]
            sum_ref[c, at, :] = total

    level_halves(levels, half)


def pieces_kernel(total_ref, out_hbm, buffer, sem):
    parts, levels, slots = total_ref.shape
    peers, height, lanes = buffer.shape
    share = height // parts
    subs = levels // share
    each = peers // subs
    for s in range(subs):
        block = jnp.concatenate([total_ref[c, s * share:(s + 1) * share, :] for c in range(parts)], 0)
        if lanes > slots:
            block = jnp.concatenate([block, jnp.zeros((height, lanes - slots), jnp.float32)], 1)

        def give(p, carry, s=s, block=block):
            buffer[s * each + p] = block
            return carry

        lax.fori_loop(0, each, give, 0, unroll=4)
    copy = pltpu.make_async_copy(buffer, out_hbm, sem)
    copy.start()
    copy.wait()


def join_kernel(came_ref, out_ref):
    parts, share, mine = out_ref.shape
    lanes = came_ref.shape[-1]
    start = lax.axis_index("hor") * mine
    from_slot = lax.broadcasted_iota(jnp.int32, (lanes, mine), 0)
    to_slot = lax.broadcasted_iota(jnp.int32, (lanes, mine), 1)
    pick = jnp.where(from_slot == to_slot + start, 1.0, 0.0)
    total = jnp.sum(came_ref[...], 0)
    total = jnp.dot(total, pick, precision=lax.Precision.HIGHEST, preferred_element_type=jnp.float32)
    for c in range(parts):
        out_ref[c] = total[c * share:(c + 1) * share]


def subtract_kernel(state_ref, middle_ref, a_ref, b_ref, out_hbm, buffer, sems):
    parts, inner = middle_ref.shape[:2]
    rows = state_ref.shape[2]
    a_start = parity() * (rows - STEPS)
    b_start = (1 - parity()) * (rows - STEPS)
    copies = []
    for start, other in ((STEPS, middle_ref), (a_start, a_ref), (b_start, b_ref)):
        for c in range(parts):
            count = other.shape[1]
            for r in range(count):
                buffer[c, start + r] = state_ref[0, c, start + r] - other[c, r]
            at = pl.ds(start, count)
            copy = pltpu.make_async_copy(buffer.at[c, at], out_hbm.at[0, c, at], sems.at[len(copies)])
            copy.start()
            copies.append(copy)
    for copy in copies:
        copy.wait()


def cost(flops, moved):
    return pl.CostEstimate(flops=flops, bytes_accessed=moved, transcendentals=0)


PARAMS = pltpu.CompilerParams(vmem_limit_bytes=24 * 1024 * 1024)


def local(
    adjoint_state,
    courant_east,
    courant_north,
    parent_cell,
    stencil_offset,
    stencil_weight,
    owner_slot,
):
    _, parts, rows, levels, width = adjoint_state.shape
    slots = owner_slot.shape[0]
    inner = rows - 2 * STEPS
    row_bytes = levels * width * 4
    f32 = lambda *shape: jax.ShapeDtypeStruct(shape, jnp.float32)
    vmem = pl.BlockSpec(memory_space=pltpu.VMEM)
    smem = pl.BlockSpec(memory_space=pltpu.SMEM)
    hbm = pl.BlockSpec(memory_space=pltpu.HBM)
    in_hbm = lambda value: pltpu.with_memory_space_constraint(value, pltpu.HBM)

    first_pack = pl.pallas_call(
        first_kernel,
        in_specs=[hbm] * 3,
        out_specs=vmem,
        out_shape=f32(PACK_ROWS, levels, width),
        scratch_shapes=[
            pltpu.VMEM((parts, STEPS, levels, width), jnp.float32),
            pltpu.VMEM((STEPS, levels, width), jnp.float32),
            pltpu.VMEM((STEPS, levels, width), jnp.float32),
            pltpu.SemaphoreType.DMA((levels // HALF, parts + 2)),
        ],
        compiler_params=PARAMS,
        cost_estimate=cost(12 * levels * width * 13, 27 * row_bytes),
        name="first_pack",
    )(in_hbm(adjoint_state), in_hbm(courant_east), in_hbm(courant_north))
    first_came = alternating(first_pack, -1)

    state, east, north = adjoint_state, courant_east, courant_north
    second_pack, middle, ends, columns = pl.pallas_call(
        sweep_kernel,
        in_specs=[vmem] * 3,
        out_specs=[vmem] * 4,
        out_shape=[
            f32(PACK_ROWS, levels, width),
            f32(parts, inner, levels, width),
            f32(parts, 2 * STEPS, levels, width),
            f32(parts, 2, rows, levels, LANES),
        ],
        scratch_shapes=[
            pltpu.VMEM((STEPS - 1, parts, rows, HALF, width), jnp.float32),
            pltpu.VMEM((rows, HALF, width), jnp.float32),
            pltpu.VMEM((rows, HALF, width), jnp.float32),
            pltpu.VMEM((rows, HALF, width), jnp.float32),
        ],
        compiler_params=PARAMS,
        cost_estimate=cost(8 * rows * levels * width * 13, 6 * rows * row_bytes),
        name="sweep",
    )(state, east, north)
    middle_came = along(middle, "sub", -1)
    second_came = alternating(second_pack, 1)

    spread, partial = pl.pallas_call(
        ghost_kernel,
        in_specs=[vmem] * 5 + [hbm],
        out_specs=[vmem] * 2,
        out_shape=[f32(parts, 2, rows, slots), f32(parts, levels, slots)],
        scratch_shapes=[
            pltpu.VMEM((rows, levels, LANES), jnp.float32),
            pltpu.VMEM((rows, levels, LANES), jnp.float32),
            pltpu.SemaphoreType.DMA((2,)),
        ],
        compiler_params=PARAMS,
        cost_estimate=cost(parts * rows * levels * slots * 8, 4 * rows * levels * LANES * 8),
        name="ghost_sums",
    )(parent_cell, stencil_offset, stencil_weight, owner_slot[None], columns, in_hbm(courant_north))

    subs, hors = lax.axis_size("sub"), lax.axis_size("hor")

    def mend(which, mine, other, so_far):
        return pl.pallas_call(
            functools.partial(mend_kernel, which),
            in_specs=[vmem] * 7,
            out_specs=[vmem] * 2,
            out_shape=[f32(parts, STEPS, levels, width), f32(parts, levels, slots)],
            compiler_params=PARAMS,
            cost_estimate=cost(16 * levels * width * 13, 46 * row_bytes),
            name="mend_" + "ab"[which],
        )(east, north, mine, other, ends, spread, so_far)

    side_a, partial = mend(0, second_pack, first_came, partial)
    a_came = along(side_a, "sub", -1)
    side_b, partial = mend(1, first_pack, second_came, partial)
    b_came = along(side_b, "sub", -1)

    piece = (subs * hors, parts * levels // subs, -(-slots // LANES) * LANES)
    pieces = pl.pallas_call(
        pieces_kernel,
        in_specs=[vmem],
        out_specs=hbm,
        out_shape=pltpu.HBM(piece, jnp.float32),
        scratch_shapes=[pltpu.VMEM(piece, jnp.float32), pltpu.SemaphoreType.DMA],
        compiler_params=PARAMS,
        name="pieces",
    )(partial)
    pieces = lax.all_to_all(pieces, ("sub", "hor"), 0, 0, tiled=True)
    boundary_gradient = pl.pallas_call(
        join_kernel,
        in_specs=[vmem],
        out_specs=vmem,
        out_shape=f32(parts, levels // subs, slots // hors),
        compiler_params=PARAMS,
        name="join",
    )(pieces)

    adjoint_result = pl.pallas_call(
        subtract_kernel,
        in_specs=[vmem] * 4,
        out_specs=hbm,
        out_shape=f32(*adjoint_state.shape),
        scratch_shapes=[
            pltpu.VMEM((parts, rows, levels, width), jnp.float32),
            pltpu.SemaphoreType.DMA((3 * parts,)),
        ],
        compiler_params=PARAMS,
        cost_estimate=cost(parts * rows * levels * width, 6 * rows * row_bytes),
        name="subtract",
    )(state, middle_came, a_came, b_came)
    return (adjoint_result, boundary_gradient)


def solution(mesh):
    in_specs = (
        P(("ens", "sub"), None, "hor", None, None),
        P(("ens", "sub"), "hor", None, None),
        P(("ens", "sub"), "hor", None, None),
        P(None, None, "hor"),
        P(None, None, None, "hor"),
        P(None, None, None, "hor"),
        P(),
    )
    out_specs = (P(("ens", "sub"), None, "hor", None, None), P("ens", "sub", "hor"))
    return jax.shard_map(local, mesh=mesh, in_specs=in_specs, out_specs=out_specs, check_vma=False)
```

```python
import functools

import jax
import jax.numpy as jnp
from jax import lax
from jax.experimental import pallas as pl
from jax.experimental.pallas import tpu as pltpu
from jax.sharding import PartitionSpec as P

STEPS = 4
HALF = 8
FLUX_ROWS = 2 * STEPS
PACK_ROWS = FLUX_ROWS + 3
LANES = 128


def along(value, axis, step_of):
    peers = lax.axis_size(axis)
    pairs = [(i, i + step_of) for i in range(peers) if 0 <= i + step_of < peers]
    return lax.ppermute(value, axis, pairs)


def alternating(value, sign):
    subs, hors = lax.axis_size("sub"), lax.axis_size("hor")
    pairs = []
    for s in range(subs):
        step = sign if s % 2 == 0 else -sign
        pairs += [(s * hors + h, s * hors + h + step) for h in range(hors) if 0 <= h + step < hors]
    return lax.ppermute(value, ("sub", "hor"), pairs)


def parity():
    return lax.rem(lax.axis_index("sub"), 2)


def sign_of(flip):
    return jnp.where(flip == 1, jnp.float32(-1.0), jnp.float32(1.0))


def north_rates(north_rate):
    width = north_rate.shape[-1]
    column = lax.broadcasted_iota(jnp.int32, north_rate.shape, len(north_rate.shape) - 1)
    plus = jnp.where(column == 0, 0.0, jnp.maximum(north_rate, 0.0))
    minus = jnp.where(column == width - 1, 0.0, jnp.maximum(-north_rate, 0.0))
    return plus, minus


def shifted(flux_plus, flux_minus):
    width = flux_plus.shape[-1]
    axis = len(flux_plus.shape) - 1
    return pltpu.roll(flux_plus, width - 1, axis) + pltpu.roll(flux_minus, 1, axis)


class Row:
    def __init__(self, east_rate, north_rate=None):
        self.outward = jnp.maximum(east_rate, 0.0)
        self.inward = jnp.maximum(-east_rate, 0.0)
        if north_rate is not None:
            self.centre = 1.0 - jnp.abs(east_rate) - jnp.abs(north_rate)
            self.plus, self.minus = north_rates(north_rate)

    def stay(self, value):
        return self.centre * value + shifted(self.plus * value, self.minus * value)


def level_halves(levels, body):
    def step(h, carry):
        body(pl.ds(pl.multiple_of(h * HALF, HALF), HALF))
        return carry

    lax.fori_loop(0, levels // HALF, step, 0)


def first_kernel(state_hbm, east_hbm, north_hbm, pack_ref, state_ref, east_ref, north_ref, sems):
    parts, rows, levels = state_hbm.shape[1:4]
    flip = parity()
    sign = sign_of(flip)
    at_end = pl.ds(flip * (rows - STEPS), STEPS)
    place = lambda r: r + flip * (STEPS - 1 - 2 * r)
    halves = levels // HALF
    copies = []
    for h in range(halves):
        at = pl.ds(h * HALF, HALF)
        sem = sems.at[h]
        batch = [
            pltpu.make_async_copy(state_hbm.at[0, c, at_end, at], state_ref.at[c, :, at], sem.at[c])
            for c in range(parts)
        ]
        batch.append(pltpu.make_async_copy(east_hbm.at[0, at_end, at], east_ref.at[:, at], sem.at[parts]))
        batch.append(pltpu.make_async_copy(north_hbm.at[0, at_end, at], north_ref.at[:, at], sem.at[parts + 1]))
        copies.append(batch)
        for copy in batch:
            copy.start()

    def half(at):
        row = [Row(east_ref[place(r), at, :] * sign, north_ref[place(r), at, :]) for r in range(STEPS)]
        pack_ref[FLUX_ROWS, at, :] = east_ref[place(0), at, :]
        pack_ref[FLUX_ROWS + 1, at, :] = north_ref[place(0), at, :]
        pack_ref[FLUX_ROWS + 2, at, :] = east_ref[place(1), at, :]
        for c in range(parts):
            field = [state_ref[c, place(r), at, :] for r in range(STEPS)]
            for k in range(STEPS):
                pack_ref[2 * k + c, at, :] = row[0].outward * field[0]
                after = []
                for r in range(STEPS - 1 - k):
                    value = row[r].stay(field[r]) + row[r + 1].outward * field[r + 1]
                    if r > 0:
                        value = value + row[r - 1].inward * field[r - 1]
                    after.append(value)
                field = after

    for h in range(halves):
        for copy in copies[h]:
            copy.wait()
        half(pl.ds(h * HALF, HALF))


def as_column(row):
    count = row.shape[1]
    here = lax.broadcasted_iota(jnp.int32, (count, count), 0)
    there = lax.broadcasted_iota(jnp.int32, (count, count), 1)
    return jnp.sum(jnp.where(here == there, row, 0), axis=1, keepdims=True)


def sweep_kernel(
    state_ref, east_ref, north_ref, pack_ref, middle_ref, ends_ref, column_ref,
    field, plus_ref, minus_ref, centre_ref,
):
    parts, rows, levels, width = state_ref.shape[1:]
    flip = 1 - parity()
    sign = sign_of(flip)
    end_row = flip * (rows - 1)
    next_row = end_row + 1 - 2 * flip

    def half(at):
        pack_ref[FLUX_ROWS, at, :] = east_ref[0, end_row, at, :]
        pack_ref[FLUX_ROWS + 1, at, :] = north_ref[0, end_row, at, :]
        pack_ref[FLUX_ROWS + 2, at, :] = east_ref[0, next_row, at, :]

        for k in range(STEPS):
            if k == 0:
                read = lambda c, i: state_ref[0, c, i, at, :]
            else:
                read = lambda c, i, slot=k - 1: field[slot, c, i]
            leaving = jnp.maximum(east_ref[0, end_row, at, :] * sign, 0.0)
            for c in range(parts):
                pack_ref[2 * k + c, at, :] = leaving * read(c, end_row)
            west = [None] * parts
            here = [read(c, 0) for c in range(parts)]
            east_here = east_ref[0, 0, at, :]
            for i in range(rows):
                leave_west = jnp.maximum(-east_here, 0.0)
                if k == 0:
                    north_rate = north_ref[0, i, at, :]
                    centre = 1.0 - jnp.abs(east_here) - jnp.abs(north_rate)
                    plus, minus = north_rates(north_rate)
                    centre_ref[i], plus_ref[i], minus_ref[i] = centre, plus, minus
                else:
                    centre, plus, minus = centre_ref[i], plus_ref[i], minus_ref[i]
                if i + 1 < rows:
                    east_here = east_ref[0, i + 1, at, :]
                    east_after = jnp.maximum(east_here, 0.0)
                for c in range(parts):
                    value = here[c]
                    total = centre * value + shifted(plus * value, minus * value)
                    if i > 0:
                        total = total + west[c]
                    if i + 1 < rows:
                        west[c] = leave_west * value
                        here[c] = read(c, i + 1)
                        total = total + east_after * here[c]
                    if k < STEPS - 1:
                        field[k, c, i] = total
                    elif i < STEPS:
                        ends_ref[c, i, at, :] = total
                    elif i >= rows - STEPS:
                        ends_ref[c, i - rows + 2 * STEPS, at, :] = total
                    else:
                        middle_ref[c, i - STEPS, at, :] = total

        def columns(i, carry):
            for c in range(parts):
                value = state_ref[0, c, i, at, :]
                first, last = value[:, :LANES], value[:, width - LANES:]
                for slot in range(STEPS - 1):
                    first = first + field[slot, c, i, :, :LANES]
                    last = last + field[slot, c, i, :, width - LANES:]
                column_ref[c, 0, i, at, :] = first
                column_ref[c, 1, i, at, :] = last
            return carry

        lax.fori_loop(0, rows, columns, 0, unroll=2)

    level_halves(levels, half)


def ghost_kernel(
    cell_ref, offset_ref, weight_ref, owner_ref, column_ref, north_hbm, spread_ref, partial_ref, first_rate, last_rate, sems
):
    parts, _, rows, levels, _ = column_ref.shape
    slots = spread_ref.shape[-1]
    width = north_hbm.shape[-1]
    copies = [
        pltpu.make_async_copy(north_hbm.at[0, :, :, pl.ds(0, LANES)], first_rate, sems.at[0]),
        pltpu.make_async_copy(north_hbm.at[0, :, :, pl.ds(width - LANES, LANES)], last_rate, sems.at[1]),
    ]
    for copy in copies:
        copy.start()

    here = lax.broadcasted_iota(jnp.int32, (slots, slots), 1)
    placing = jnp.where(as_column(owner_ref[...]) == here, 1.0, 0.0)
    cells = lax.broadcasted_iota(jnp.int32, (rows, slots), 1)
    for c in range(parts):
        for s in range(2):
            mixing = jnp.zeros((rows, slots), jnp.float32)
            for point in range(offset_ref.shape[0]):
                target = as_column(cell_ref[c, s:s + 1, :] + offset_ref[point, c, s:s + 1, :])
                mixing = mixing + jnp.where(target == cells, as_column(weight_ref[point, c, s:s + 1, :]), 0.0)
            spread_ref[c, s] = jnp.dot(
                mixing, placing, precision=lax.Precision.HIGHEST, preferred_element_type=jnp.float32
            )

    for copy in copies:
        copy.wait()
    for c in range(parts):
        total = jnp.zeros((levels, slots), jnp.float32)
        for i in range(rows):
            south = jnp.maximum(first_rate[i, :, :1], 0.0) * column_ref[c, 0, i, :, :1]
            north = jnp.maximum(-last_rate[i, :, LANES - 1:], 0.0) * column_ref[c, 1, i, :, LANES - 1:]
            total = total + south * spread_ref[c, 0, i:i + 1, :]
            total = total + north * spread_ref[c, 1, i:i + 1, :]
        partial_ref[c] = total


def mend_kernel(
    which, east_ref, north_ref, mine_ref, other_ref, ends_ref, spread_ref, partial_ref, out_ref, sum_ref
):
    parts, levels, slots = partial_ref.shape
    rows = spread_ref.shape[2]
    width = east_ref.shape[-1]
    flip = 1 - parity() if which == 0 else parity()
    sign = sign_of(flip)
    turn = lambda r: r + flip * (STEPS - 1 - 2 * r)
    place = lambda r: flip * (rows - STEPS) + turn(r)

    def half(at):
        own = [Row(east_ref[0, place(r), at, :] * sign, north_ref[0, place(r), at, :]) for r in range(STEPS - 1)]
        near = Row(other_ref[FLUX_ROWS, at, :] * sign, other_ref[FLUX_ROWS + 1, at, :])
        far = Row(other_ref[FLUX_ROWS + 2, at, :] * sign)
        for c in range(parts):
            mine = lambda k: mine_ref[2 * k + c, at, :]
            theirs = lambda k: other_ref[2 * k + c, at, :]
            a0 = theirs(0)
            n1 = mine(0)
            b0 = own[0].stay(a0) + near.inward * n1 + theirs(1)
            b1 = own[0].inward * a0
            bn1 = near.stay(n1) + own[0].outward * a0 + mine(1)
            bn2 = near.outward * n1
            c0 = own[0].stay(b0) + near.inward * bn1 + own[1].outward * b1 + theirs(2)
            c1 = own[1].stay(b1) + own[0].inward * b0
            c2 = own[1].inward * b1
            cn1 = near.stay(bn1) + own[0].outward * b0 + far.inward * bn2 + mine(2)
            d0 = own[0].stay(c0) + near.inward * cn1 + own[1].outward * c1 + theirs(3)
            d1 = own[1].stay(c1) + own[0].inward * c0 + own[2].outward * c2
            d2 = own[2].stay(c2) + own[1].inward * c1
            d3 = own[2].inward * c2
            for r, value in enumerate((d0, d1, d2, d3)):
                out_ref[c, turn(r), at, :] = ends_ref[c, flip * STEPS + turn(r), at, :] + value
            total = partial_ref[c, at, :]
            for r, value in enumerate((a0 + b0 + c0, b1 + c1, c2)):
                i = place(r)
                rate = north_ref[0, i, at, :]
                south = jnp.maximum(rate[:, :1], 0.0) * value[:, :1]
                north = jnp.maximum(-rate[:, width - 1:], 0.0) * value[:, width - 1:]
                total = total + south * spread_ref[c, 0, pl.ds(i, 1), :]
                total = total + north * spread_ref[c, 1, pl.ds(i, 1), :]
            sum_ref[c, at, :] = total

    level_halves(levels, half)


def widen_kernel(total_ref, out_hbm, buffer, sem):
    parts, levels, slots = total_ref.shape
    lanes = buffer.shape[-1]
    for c in range(parts):
        block = total_ref[c]
        if lanes > slots:
            block = jnp.concatenate([block, jnp.zeros((levels, lanes - slots), jnp.float32)], 1)
        buffer[c * levels:(c + 1) * levels] = block
    copy = pltpu.make_async_copy(buffer, out_hbm, sem)
    copy.start()
    copy.wait()


def join_kernel(came_ref, out_ref):
    parts, share, mine = out_ref.shape
    peers, height, lanes = came_ref.shape
    levels = height // parts
    from_slot = lax.broadcasted_iota(jnp.int32, (lanes, mine), 0)
    to_slot = lax.broadcasted_iota(jnp.int32, (lanes, mine), 1)
    pick = jnp.where(from_slot == to_slot + lax.axis_index("hor") * mine, 1.0, 0.0)
    total = jnp.sum(came_ref[...], 0)
    total = jnp.dot(total, pick, precision=lax.Precision.HIGHEST, preferred_element_type=jnp.float32)
    for c in range(parts):
        chosen = jnp.zeros((share, mine), jnp.float32)
        for s in range(levels // share):
            block = total[c * levels + s * share:c * levels + (s + 1) * share]
            chosen = jnp.where(lax.axis_index("sub") == s, block, chosen)
        out_ref[c] = chosen


def subtract_kernel(state_ref, middle_ref, a_ref, b_ref, out_hbm, buffer, sems):
    parts, inner = middle_ref.shape[:2]
    rows = state_ref.shape[2]
    a_start = parity() * (rows - STEPS)
    b_start = (1 - parity()) * (rows - STEPS)
    copies = []
    for start, other in ((STEPS, middle_ref), (a_start, a_ref), (b_start, b_ref)):
        for c in range(parts):
            count = other.shape[1]
            for r in range(count):
                buffer[c, start + r] = state_ref[0, c, start + r] - other[c, r]
            at = pl.ds(start, count)
            copy = pltpu.make_async_copy(buffer.at[c, at], out_hbm.at[0, c, at], sems.at[len(copies)])
            copy.start()
            copies.append(copy)
    for copy in copies:
        copy.wait()


def cost(flops, moved):
    return pl.CostEstimate(flops=flops, bytes_accessed=moved, transcendentals=0)


PARAMS = pltpu.CompilerParams(vmem_limit_bytes=24 * 1024 * 1024)


def local(
    adjoint_state,
    courant_east,
    courant_north,
    parent_cell,
    stencil_offset,
    stencil_weight,
    owner_slot,
):
    _, parts, rows, levels, width = adjoint_state.shape
    slots = owner_slot.shape[0]
    inner = rows - 2 * STEPS
    row_bytes = levels * width * 4
    f32 = lambda *shape: jax.ShapeDtypeStruct(shape, jnp.float32)
    vmem = pl.BlockSpec(memory_space=pltpu.VMEM)
    smem = pl.BlockSpec(memory_space=pltpu.SMEM)
    hbm = pl.BlockSpec(memory_space=pltpu.HBM)
    in_hbm = lambda value: pltpu.with_memory_space_constraint(value, pltpu.HBM)

    first_pack = pl.pallas_call(
        first_kernel,
        in_specs=[hbm] * 3,
        out_specs=vmem,
        out_shape=f32(PACK_ROWS, levels, width),
        scratch_shapes=[
            pltpu.VMEM((parts, STEPS, levels, width), jnp.float32),
            pltpu.VMEM((STEPS, levels, width), jnp.float32),
            pltpu.VMEM((STEPS, levels, width), jnp.float32),
            pltpu.SemaphoreType.DMA((levels // HALF, parts + 2)),
        ],
        compiler_params=PARAMS,
        cost_estimate=cost(12 * levels * width * 13, 27 * row_bytes),
        name="first_pack",
    )(in_hbm(adjoint_state), in_hbm(courant_east), in_hbm(courant_north))
    first_came = alternating(first_pack, -1)

    state, east, north = adjoint_state, courant_east, courant_north
    second_pack, middle, ends, columns = pl.pallas_call(
        sweep_kernel,
        in_specs=[vmem] * 3,
        out_specs=[vmem] * 4,
        out_shape=[
            f32(PACK_ROWS, levels, width),
            f32(parts, inner, levels, width),
            f32(parts, 2 * STEPS, levels, width),
            f32(parts, 2, rows, levels, LANES),
        ],
        scratch_shapes=[
            pltpu.VMEM((STEPS - 1, parts, rows, HALF, width), jnp.float32),
            pltpu.VMEM((rows, HALF, width), jnp.float32),
            pltpu.VMEM((rows, HALF, width), jnp.float32),
            pltpu.VMEM((rows, HALF, width), jnp.float32),
        ],
        compiler_params=PARAMS,
        cost_estimate=cost(8 * rows * levels * width * 13, 6 * rows * row_bytes),
        name="sweep",
    )(state, east, north)
    middle_came = along(middle, "sub", -1)
    second_came = alternating(second_pack, 1)

    spread, partial = pl.pallas_call(
        ghost_kernel,
        in_specs=[vmem] * 5 + [hbm],
        out_specs=[vmem] * 2,
        out_shape=[f32(parts, 2, rows, slots), f32(parts, levels, slots)],
        scratch_shapes=[
            pltpu.VMEM((rows, levels, LANES), jnp.float32),
            pltpu.VMEM((rows, levels, LANES), jnp.float32),
            pltpu.SemaphoreType.DMA((2,)),
        ],
        compiler_params=PARAMS,
        cost_estimate=cost(parts * rows * levels * slots * 8, 4 * rows * levels * LANES * 8),
        name="ghost_sums",
    )(parent_cell, stencil_offset, stencil_weight, owner_slot[None], columns, in_hbm(courant_north))

    subs, hors = lax.axis_size("sub"), lax.axis_size("hor")

    def mend(which, mine, other, so_far):
        return pl.pallas_call(
            functools.partial(mend_kernel, which),
            in_specs=[vmem] * 7,
            out_specs=[vmem] * 2,
            out_shape=[f32(parts, STEPS, levels, width), f32(parts, levels, slots)],
            compiler_params=PARAMS,
            cost_estimate=cost(16 * levels * width * 13, 46 * row_bytes),
            name="mend_" + "ab"[which],
        )(east, north, mine, other, ends, spread, so_far)

    side_a, partial = mend(0, second_pack, first_came, partial)
    a_came = along(side_a, "sub", -1)
    side_b, partial = mend(1, first_pack, second_came, partial)
    b_came = along(side_b, "sub", -1)

    piece = (parts * levels, -(-slots // LANES) * LANES)
    piece = pl.pallas_call(
        widen_kernel,
        in_specs=[vmem],
        out_specs=hbm,
        out_shape=pltpu.HBM(piece, jnp.float32),
        scratch_shapes=[pltpu.VMEM(piece, jnp.float32), pltpu.SemaphoreType.DMA],
        compiler_params=PARAMS,
        name="widen",
    )(partial)
    pieces = lax.all_gather(piece, ("sub", "hor"))
    boundary_gradient = pl.pallas_call(
        join_kernel,
        in_specs=[vmem],
        out_specs=vmem,
        out_shape=f32(parts, levels // subs, slots // hors),
        compiler_params=PARAMS,
        name="join",
    )(pieces)

    adjoint_result = pl.pallas_call(
        subtract_kernel,
        in_specs=[vmem] * 4,
        out_specs=hbm,
        out_shape=f32(*adjoint_state.shape),
        scratch_shapes=[
            pltpu.VMEM((parts, rows, levels, width), jnp.float32),
            pltpu.SemaphoreType.DMA((3 * parts,)),
        ],
        compiler_params=PARAMS,
        cost_estimate=cost(parts * rows * levels * width, 6 * rows * row_bytes),
        name="subtract",
    )(state, middle_came, a_came, b_came)
    return (adjoint_result, boundary_gradient)


def solution(mesh):
    in_specs = (
        P(("ens", "sub"), None, "hor", None, None),
        P(("ens", "sub"), "hor", None, None),
        P(("ens", "sub"), "hor", None, None),
        P(None, None, "hor"),
        P(None, None, None, "hor"),
        P(None, None, None, "hor"),
        P(),
    )
    out_specs = (P(("ens", "sub"), None, "hor", None, None), P("ens", "sub", "hor"))
    return jax.shard_map(local, mesh=mesh, in_specs=in_specs, out_specs=out_specs, check_vma=False)
```

```python
import functools

import jax
import jax.numpy as jnp
from jax import lax
from jax.experimental import pallas as pl
from jax.experimental.pallas import tpu as pltpu
from jax.sharding import PartitionSpec as P

STEPS = 4
HALF = 8
FLUX_ROWS = 2 * STEPS
PACK_ROWS = FLUX_ROWS + 3
LANES = 128


def along(value, axis, step_of):
    peers = lax.axis_size(axis)
    pairs = [(i, i + step_of) for i in range(peers) if 0 <= i + step_of < peers]
    return lax.ppermute(value, axis, pairs)


def alternating(value, sign):
    subs, hors = lax.axis_size("sub"), lax.axis_size("hor")
    pairs = []
    for s in range(subs):
        step = sign if s % 2 == 0 else -sign
        pairs += [(s * hors + h, s * hors + h + step) for h in range(hors) if 0 <= h + step < hors]
    return lax.ppermute(value, ("sub", "hor"), pairs)


def parity():
    return lax.rem(lax.axis_index("sub"), 2)


def sign_of(flip):
    return jnp.where(flip == 1, jnp.float32(-1.0), jnp.float32(1.0))


def north_rates(north_rate):
    width = north_rate.shape[-1]
    column = lax.broadcasted_iota(jnp.int32, north_rate.shape, len(north_rate.shape) - 1)
    plus = jnp.where(column == 0, 0.0, jnp.maximum(north_rate, 0.0))
    minus = jnp.where(column == width - 1, 0.0, jnp.maximum(-north_rate, 0.0))
    return plus, minus


def shifted(flux_plus, flux_minus):
    width = flux_plus.shape[-1]
    axis = len(flux_plus.shape) - 1
    return pltpu.roll(flux_plus, width - 1, axis) + pltpu.roll(flux_minus, 1, axis)


class Row:
    def __init__(self, east_rate, north_rate=None):
        self.outward = jnp.maximum(east_rate, 0.0)
        self.inward = jnp.maximum(-east_rate, 0.0)
        if north_rate is not None:
            self.centre = 1.0 - jnp.abs(east_rate) - jnp.abs(north_rate)
            self.plus, self.minus = north_rates(north_rate)

    def stay(self, value):
        return self.centre * value + shifted(self.plus * value, self.minus * value)


def level_halves(levels, body):
    def step(h, carry):
        body(pl.ds(pl.multiple_of(h * HALF, HALF), HALF))
        return carry

    lax.fori_loop(0, levels // HALF, step, 0)


def first_kernel(state_hbm, east_hbm, north_hbm, pack_ref, state_ref, east_ref, north_ref, sems):
    parts, rows, levels = state_hbm.shape[1:4]
    flip = parity()
    sign = sign_of(flip)
    at_end = pl.ds(flip * (rows - STEPS), STEPS)
    place = lambda r: r + flip * (STEPS - 1 - 2 * r)
    halves = levels // HALF
    copies = []
    for h in range(halves):
        at = pl.ds(h * HALF, HALF)
        sem = sems.at[h]
        batch = [
            pltpu.make_async_copy(state_hbm.at[0, c, at_end, at], state_ref.at[c, :, at], sem.at[c])
            for c in range(parts)
        ]
        batch.append(pltpu.make_async_copy(east_hbm.at[0, at_end, at], east_ref.at[:, at], sem.at[parts]))
        batch.append(pltpu.make_async_copy(north_hbm.at[0, at_end, at], north_ref.at[:, at], sem.at[parts + 1]))
        copies.append(batch)
        for copy in batch:
            copy.start()

    def half(at):
        row = [Row(east_ref[place(r), at, :] * sign, north_ref[place(r), at, :]) for r in range(STEPS)]
        pack_ref[FLUX_ROWS, at, :] = east_ref[place(0), at, :]
        pack_ref[FLUX_ROWS + 1, at, :] = north_ref[place(0), at, :]
        pack_ref[FLUX_ROWS + 2, at, :] = east_ref[place(1), at, :]
        for c in range(parts):
            field = [state_ref[c, place(r), at, :] for r in range(STEPS)]
            for k in range(STEPS):
                pack_ref[2 * k + c, at, :] = row[0].outward * field[0]
                after = []
                for r in range(STEPS - 1 - k):
                    value = row[r].stay(field[r]) + row[r + 1].outward * field[r + 1]
                    if r > 0:
                        value = value + row[r - 1].inward * field[r - 1]
                    after.append(value)
                field = after

    for h in range(halves):
        for copy in copies[h]:
            copy.wait()
        half(pl.ds(h * HALF, HALF))


def as_column(row):
    count = row.shape[1]
    here = lax.broadcasted_iota(jnp.int32, (count, count), 0)
    there = lax.broadcasted_iota(jnp.int32, (count, count), 1)
    return jnp.sum(jnp.where(here == there, row, 0), axis=1, keepdims=True)


def sweep_kernel(
    state_ref, east_ref, north_ref, pack_ref, middle_ref, ends_ref, column_ref,
    field, plus_ref, minus_ref, centre_ref,
):
    parts, rows, levels, width = state_ref.shape[1:]
    flip = 1 - parity()
    sign = sign_of(flip)
    end_row = flip * (rows - 1)
    next_row = end_row + 1 - 2 * flip

    def half(at):
        pack_ref[FLUX_ROWS, at, :] = east_ref[0, end_row, at, :]
        pack_ref[FLUX_ROWS + 1, at, :] = north_ref[0, end_row, at, :]
        pack_ref[FLUX_ROWS + 2, at, :] = east_ref[0, next_row, at, :]

        for k in range(STEPS):
            if k == 0:
                read = lambda c, i: state_ref[0, c, i, at, :]
            else:
                read = lambda c, i, slot=k - 1: field[slot, c, i]
            leaving = jnp.maximum(east_ref[0, end_row, at, :] * sign, 0.0)
            for c in range(parts):
                pack_ref[2 * k + c, at, :] = leaving * read(c, end_row)
            west = [None] * parts
            here = [read(c, 0) for c in range(parts)]
            east_here = east_ref[0, 0, at, :]
            for i in range(rows):
                leave_west = jnp.maximum(-east_here, 0.0)
                if k == 0:
                    north_rate = north_ref[0, i, at, :]
                    centre = 1.0 - jnp.abs(east_here) - jnp.abs(north_rate)
                    plus, minus = north_rates(north_rate)
                    centre_ref[i], plus_ref[i], minus_ref[i] = centre, plus, minus
                else:
                    centre, plus, minus = centre_ref[i], plus_ref[i], minus_ref[i]
                if i + 1 < rows:
                    east_here = east_ref[0, i + 1, at, :]
                    east_after = jnp.maximum(east_here, 0.0)
                for c in range(parts):
                    value = here[c]
                    total = centre * value + shifted(plus * value, minus * value)
                    if i > 0:
                        total = total + west[c]
                    if i + 1 < rows:
                        west[c] = leave_west * value
                        here[c] = read(c, i + 1)
                        total = total + east_after * here[c]
                    if k < STEPS - 1:
                        field[k, c, i] = total
                    elif i < STEPS:
                        ends_ref[c, i, at, :] = total
                    elif i >= rows - STEPS:
                        ends_ref[c, i - rows + 2 * STEPS, at, :] = total
                    else:
                        middle_ref[c, i - STEPS, at, :] = total

        def columns(i, carry):
            for c in range(parts):
                value = state_ref[0, c, i, at, :]
                first, last = value[:, :LANES], value[:, width - LANES:]
                for slot in range(STEPS - 1):
                    first = first + field[slot, c, i, :, :LANES]
                    last = last + field[slot, c, i, :, width - LANES:]
                column_ref[c, 0, i, at, :] = first
                column_ref[c, 1, i, at, :] = last
            return carry

        lax.fori_loop(0, rows, columns, 0, unroll=2)

    level_halves(levels, half)


def ghost_kernel(
    cell_ref, offset_ref, weight_ref, owner_ref, column_ref, north_hbm, spread_ref, partial_ref, first_rate, last_rate, sems
):
    parts, _, rows, levels, _ = column_ref.shape
    slots = spread_ref.shape[-1]
    width = north_hbm.shape[-1]
    copies = [
        pltpu.make_async_copy(north_hbm.at[0, :, :, pl.ds(0, LANES)], first_rate, sems.at[0]),
        pltpu.make_async_copy(north_hbm.at[0, :, :, pl.ds(width - LANES, LANES)], last_rate, sems.at[1]),
    ]
    for copy in copies:
        copy.start()

    here = lax.broadcasted_iota(jnp.int32, (slots, slots), 1)
    placing = jnp.where(as_column(owner_ref[...]) == here, 1.0, 0.0)
    cells = lax.broadcasted_iota(jnp.int32, (rows, slots), 1)
    for c in range(parts):
        for s in range(2):
            mixing = jnp.zeros((rows, slots), jnp.float32)
            for point in range(offset_ref.shape[0]):
                target = as_column(cell_ref[c, s:s + 1, :] + offset_ref[point, c, s:s + 1, :])
                mixing = mixing + jnp.where(target == cells, as_column(weight_ref[point, c, s:s + 1, :]), 0.0)
            spread_ref[c, s] = jnp.dot(
                mixing, placing, precision=lax.Precision.HIGHEST, preferred_element_type=jnp.float32
            )

    for copy in copies:
        copy.wait()
    for c in range(parts):
        total = jnp.zeros((levels, slots), jnp.float32)
        for i in range(rows):
            south = jnp.maximum(first_rate[i, :, :1], 0.0) * column_ref[c, 0, i, :, :1]
            north = jnp.maximum(-last_rate[i, :, LANES - 1:], 0.0) * column_ref[c, 1, i, :, LANES - 1:]
            total = total + south * spread_ref[c, 0, i:i + 1, :]
            total = total + north * spread_ref[c, 1, i:i + 1, :]
        partial_ref[c] = total


def mend_side(flip, east_ref, north_ref, mine_ref, other_ref, store, store_column):
    levels, width = mine_ref.shape[1:]
    rows = east_ref.shape[1]
    sign = sign_of(flip)
    place = lambda r: flip * (rows - STEPS) + r + flip * (STEPS - 1 - 2 * r)

    def half(at):
        own = [Row(east_ref[0, place(r), at, :] * sign, north_ref[0, place(r), at, :]) for r in range(STEPS - 1)]
        near = Row(other_ref[FLUX_ROWS, at, :] * sign, other_ref[FLUX_ROWS + 1, at, :])
        far = Row(other_ref[FLUX_ROWS + 2, at, :] * sign)
        for c in range(FLUX_ROWS // STEPS):
            mine = lambda k: mine_ref[2 * k + c, at, :]
            theirs = lambda k: other_ref[2 * k + c, at, :]
            a0 = theirs(0)
            n1 = mine(0)
            b0 = own[0].stay(a0) + near.inward * n1 + theirs(1)
            b1 = own[0].inward * a0
            bn1 = near.stay(n1) + own[0].outward * a0 + mine(1)
            bn2 = near.outward * n1
            c0 = own[0].stay(b0) + near.inward * bn1 + own[1].outward * b1 + theirs(2)
            c1 = own[1].stay(b1) + own[0].inward * b0
            c2 = own[1].inward * b1
            cn1 = near.stay(bn1) + own[0].outward * b0 + far.inward * bn2 + mine(2)
            d0 = own[0].stay(c0) + near.inward * cn1 + own[1].outward * c1 + theirs(3)
            d1 = own[1].stay(c1) + own[0].inward * c0 + own[2].outward * c2
            d2 = own[2].stay(c2) + own[1].inward * c1
            d3 = own[2].inward * c2
            for r, value in enumerate((d0, d1, d2, d3)):
                store(c, r, at, value)
            for r, pieces in enumerate(((a0, b0, c0), (b1, c1), (c2,))):
                store_column(c, 0, r, at, sum(value[:, :LANES] for value in pieces))
                store_column(c, 1, r, at, sum(value[:, width - LANES:] for value in pieces))

    level_halves(levels, half)


def mend_a_kernel(east_ref, north_ref, mine_ref, other_ref, ends_ref, middle_ref, out_ref, column_ref):
    parts, inner = middle_ref.shape[:2]
    flip = 1 - parity()
    turn = lambda r: r + flip * (STEPS - 1 - 2 * r)

    def store(c, r, at, value):
        out_ref[c, inner + turn(r), at, :] = ends_ref[c, flip * STEPS + turn(r), at, :] + value

    def store_column(c, s, r, at, value):
        column_ref[c, s, r, at, :] = value

    mend_side(flip, east_ref, north_ref, mine_ref, other_ref, store, store_column)
    for c in range(parts):
        for i in range(inner):
            out_ref[c, i] = middle_ref[c, i]


def mend_b_kernel(
    east_ref, north_ref, mine_ref, other_ref, ends_ref, a_column_ref, spread_ref, partial_ref,
    out_ref, sum_ref, b_column_ref,
):
    parts, levels, slots = partial_ref.shape
    rows = east_ref.shape[1]
    width = east_ref.shape[-1]
    flip = parity()
    turn = lambda r: r + flip * (STEPS - 1 - 2 * r)

    def store(c, r, at, value):
        out_ref[c, turn(r), at, :] = ends_ref[c, flip * STEPS + turn(r), at, :] + value

    def store_column(c, s, r, at, value):
        b_column_ref[c, s, r, at, :] = value

    mend_side(flip, east_ref, north_ref, mine_ref, other_ref, store, store_column)
    for c in range(parts):
        total = partial_ref[c]
        for side, column_ref in ((1 - flip, a_column_ref), (flip, b_column_ref)):
            for r in range(STEPS - 1):
                i = r + side * (rows - 1 - 2 * r)
                south = jnp.maximum(north_ref[0, i, :, :1], 0.0) * column_ref[c, 0, r, :, :1]
                north = jnp.maximum(-north_ref[0, i, :, width - 1:], 0.0) * column_ref[c, 1, r, :, LANES - 1:]
                total = total + south * spread_ref[c, 0, pl.ds(i, 1), :]
                total = total + north * spread_ref[c, 1, pl.ds(i, 1), :]
        sum_ref[c] = total


def pieces_kernel(total_ref, out_hbm, buffer, sem):
    parts, levels, slots = total_ref.shape
    peers, _, share, mine = buffer.shape
    subs = levels // share
    each = peers // subs
    from_slot = lax.broadcasted_iota(jnp.int32, (slots, mine), 0)
    to_slot = lax.broadcasted_iota(jnp.int32, (slots, mine), 1)
    total = jnp.concatenate([total_ref[c] for c in range(parts)], 0)
    for p in range(each):
        pick = jnp.where(from_slot == to_slot + p * mine, 1.0, 0.0)
        block = jnp.dot(total, pick, precision=lax.Precision.HIGHEST, preferred_element_type=jnp.float32)
        for s in range(subs):
            for c in range(parts):
                at = c * levels + s * share
                buffer[s * each + p, c] = block[at:at + share]
    copy = pltpu.make_async_copy(buffer, out_hbm, sem)
    copy.start()
    copy.wait()


def join_kernel(came_ref, out_ref):
    out_ref[...] = jnp.sum(came_ref[...], 0)


def subtract_kernel(state_ref, a_ref, b_ref, out_hbm, buffer, sems):
    parts, rows = state_ref.shape[1:3]
    inner = rows - 2 * STEPS
    a_start = parity() * (rows - STEPS)
    b_start = (1 - parity()) * (rows - STEPS)
    copies = []
    for start, other, first, count in (
        (STEPS, a_ref, 0, inner), (a_start, a_ref, inner, STEPS), (b_start, b_ref, 0, STEPS),
    ):
        for c in range(parts):
            for r in range(count):
                buffer[c, start + r] = state_ref[0, c, start + r] - other[c, first + r]
            at = pl.ds(start, count)
            copy = pltpu.make_async_copy(buffer.at[c, at], out_hbm.at[0, c, at], sems.at[len(copies)])
            copy.start()
            copies.append(copy)
    for copy in copies:
        copy.wait()


def cost(flops, moved):
    return pl.CostEstimate(flops=flops, bytes_accessed=moved, transcendentals=0)


PARAMS = pltpu.CompilerParams(vmem_limit_bytes=24 * 1024 * 1024)


def local(
    adjoint_state,
    courant_east,
    courant_north,
    parent_cell,
    stencil_offset,
    stencil_weight,
    owner_slot,
):
    _, parts, rows, levels, width = adjoint_state.shape
    slots = owner_slot.shape[0]
    inner = rows - 2 * STEPS
    row_bytes = levels * width * 4
    f32 = lambda *shape: jax.ShapeDtypeStruct(shape, jnp.float32)
    vmem = pl.BlockSpec(memory_space=pltpu.VMEM)
    smem = pl.BlockSpec(memory_space=pltpu.SMEM)
    hbm = pl.BlockSpec(memory_space=pltpu.HBM)
    in_hbm = lambda value: pltpu.with_memory_space_constraint(value, pltpu.HBM)

    first_pack = pl.pallas_call(
        first_kernel,
        in_specs=[hbm] * 3,
        out_specs=vmem,
        out_shape=f32(PACK_ROWS, levels, width),
        scratch_shapes=[
            pltpu.VMEM((parts, STEPS, levels, width), jnp.float32),
            pltpu.VMEM((STEPS, levels, width), jnp.float32),
            pltpu.VMEM((STEPS, levels, width), jnp.float32),
            pltpu.SemaphoreType.DMA((levels // HALF, parts + 2)),
        ],
        compiler_params=PARAMS,
        cost_estimate=cost(12 * levels * width * 13, 27 * row_bytes),
        name="first_pack",
    )(in_hbm(adjoint_state), in_hbm(courant_east), in_hbm(courant_north))
    first_came = alternating(first_pack, -1)

    state, east, north = adjoint_state, courant_east, courant_north
    second_pack, middle, ends, columns = pl.pallas_call(
        sweep_kernel,
        in_specs=[vmem] * 3,
        out_specs=[vmem] * 4,
        out_shape=[
            f32(PACK_ROWS, levels, width),
            f32(parts, inner, levels, width),
            f32(parts, 2 * STEPS, levels, width),
            f32(parts, 2, rows, levels, LANES),
        ],
        scratch_shapes=[
            pltpu.VMEM((STEPS - 1, parts, rows, HALF, width), jnp.float32),
            pltpu.VMEM((rows, HALF, width), jnp.float32),
            pltpu.VMEM((rows, HALF, width), jnp.float32),
            pltpu.VMEM((rows, HALF, width), jnp.float32),
        ],
        compiler_params=PARAMS,
        cost_estimate=cost(8 * rows * levels * width * 13, 6 * rows * row_bytes),
        name="sweep",
    )(state, east, north)
    second_came = alternating(second_pack, 1)

    spread, partial = pl.pallas_call(
        ghost_kernel,
        in_specs=[vmem] * 5 + [hbm],
        out_specs=[vmem] * 2,
        out_shape=[f32(parts, 2, rows, slots), f32(parts, levels, slots)],
        scratch_shapes=[
            pltpu.VMEM((rows, levels, LANES), jnp.float32),
            pltpu.VMEM((rows, levels, LANES), jnp.float32),
            pltpu.SemaphoreType.DMA((2,)),
        ],
        compiler_params=PARAMS,
        cost_estimate=cost(parts * rows * levels * slots * 8, 4 * rows * levels * LANES * 8),
        name="ghost_sums",
    )(parent_cell, stencil_offset, stencil_weight, owner_slot[None], columns, in_hbm(courant_north))

    subs, hors = lax.axis_size("sub"), lax.axis_size("hor")

    column_shape = (parts, 2, STEPS - 1, levels, LANES)
    side_a, a_columns = pl.pallas_call(
        mend_a_kernel,
        in_specs=[vmem] * 6,
        out_specs=[vmem] * 2,
        out_shape=[f32(parts, inner + STEPS, levels, width), f32(*column_shape)],
        compiler_params=PARAMS,
        cost_estimate=cost(16 * levels * width * 13, 54 * row_bytes),
        name="mend_a",
    )(east, north, second_pack, first_came, ends, middle)
    a_came = along(side_a, "sub", -1)
    side_b, partial = pl.pallas_call(
        mend_b_kernel,
        in_specs=[vmem] * 8,
        out_specs=[vmem] * 2,
        out_shape=[f32(parts, STEPS, levels, width), f32(parts, levels, slots)],
        scratch_shapes=[pltpu.VMEM(column_shape, jnp.float32)],
        compiler_params=PARAMS,
        cost_estimate=cost(16 * levels * width * 13, 46 * row_bytes),
        name="mend_b",
    )(east, north, first_pack, second_came, ends, a_columns, spread, partial)
    b_came = along(side_b, "sub", -1)

    piece = (subs * hors, parts, levels // subs, slots // hors)
    pieces = pl.pallas_call(
        pieces_kernel,
        in_specs=[vmem],
        out_specs=hbm,
        out_shape=pltpu.HBM(piece, jnp.float32),
        scratch_shapes=[pltpu.VMEM(piece, jnp.float32), pltpu.SemaphoreType.DMA],
        compiler_params=PARAMS,
        name="pieces",
    )(partial)
    pieces = lax.all_to_all(pieces, ("sub", "hor"), 0, 0, tiled=True)
    boundary_gradient = pl.pallas_call(
        join_kernel,
        in_specs=[vmem],
        out_specs=vmem,
        out_shape=f32(parts, levels // subs, slots // hors),
        compiler_params=PARAMS,
        name="join",
    )(pieces)

    adjoint_result = pl.pallas_call(
        subtract_kernel,
        in_specs=[vmem] * 3,
        out_specs=hbm,
        out_shape=f32(*adjoint_state.shape),
        scratch_shapes=[
            pltpu.VMEM((parts, rows, levels, width), jnp.float32),
            pltpu.SemaphoreType.DMA((3 * parts,)),
        ],
        compiler_params=PARAMS,
        cost_estimate=cost(parts * rows * levels * width, 6 * rows * row_bytes),
        name="subtract",
    )(state, a_came, b_came)
    return (adjoint_result, boundary_gradient)


def solution(mesh):
    in_specs = (
        P(("ens", "sub"), None, "hor", None, None),
        P(("ens", "sub"), "hor", None, None),
        P(("ens", "sub"), "hor", None, None),
        P(None, None, "hor"),
        P(None, None, None, "hor"),
        P(None, None, None, "hor"),
        P(),
    )
    out_specs = (P(("ens", "sub"), None, "hor", None, None), P("ens", "sub", "hor"))
    return jax.shard_map(local, mesh=mesh, in_specs=in_specs, out_specs=out_specs, check_vma=False)
```

```python
import functools

import jax
import jax.numpy as jnp
from jax import lax
from jax.experimental import pallas as pl
from jax.experimental.pallas import tpu as pltpu
from jax.sharding import PartitionSpec as P

STEPS = 4
HALF = 8
FLUX_ROWS = 2 * STEPS
PACK_ROWS = FLUX_ROWS + 3
LANES = 128


def along(value, axis, step_of):
    peers = lax.axis_size(axis)
    pairs = [(i, i + step_of) for i in range(peers) if 0 <= i + step_of < peers]
    return lax.ppermute(value, axis, pairs)


def alternating(value, sign):
    subs, hors = lax.axis_size("sub"), lax.axis_size("hor")
    pairs = []
    for s in range(subs):
        step = sign if s % 2 == 0 else -sign
        pairs += [(s * hors + h, s * hors + h + step) for h in range(hors) if 0 <= h + step < hors]
    return lax.ppermute(value, ("sub", "hor"), pairs)


def parity():
    return lax.rem(lax.axis_index("sub"), 2)


def sign_of(flip):
    return jnp.where(flip == 1, jnp.float32(-1.0), jnp.float32(1.0))


def north_rates(north_rate):
    width = north_rate.shape[-1]
    column = lax.broadcasted_iota(jnp.int32, north_rate.shape, len(north_rate.shape) - 1)
    plus = jnp.where(column == 0, 0.0, jnp.maximum(north_rate, 0.0))
    minus = jnp.where(column == width - 1, 0.0, jnp.maximum(-north_rate, 0.0))
    return plus, minus


def shifted(flux_plus, flux_minus):
    width = flux_plus.shape[-1]
    axis = len(flux_plus.shape) - 1
    return pltpu.roll(flux_plus, width - 1, axis) + pltpu.roll(flux_minus, 1, axis)


class Row:
    def __init__(self, east_rate, north_rate=None):
        self.outward = jnp.maximum(east_rate, 0.0)
        self.inward = jnp.maximum(-east_rate, 0.0)
        if north_rate is not None:
            self.centre = 1.0 - jnp.abs(east_rate) - jnp.abs(north_rate)
            self.plus, self.minus = north_rates(north_rate)

    def stay(self, value):
        return self.centre * value + shifted(self.plus * value, self.minus * value)


def level_halves(levels, body):
    def step(h, carry):
        body(pl.ds(pl.multiple_of(h * HALF, HALF), HALF))
        return carry

    lax.fori_loop(0, levels // HALF, step, 0)


def first_kernel(state_hbm, east_hbm, north_hbm, pack_ref, state_ref, east_ref, north_ref, sems):
    parts, rows, levels = state_hbm.shape[1:4]
    flip = parity()
    sign = sign_of(flip)
    at_end = pl.ds(flip * (rows - STEPS), STEPS)
    place = lambda r: r + flip * (STEPS - 1 - 2 * r)
    halves = levels // HALF
    copies = []
    for h in range(halves):
        at = pl.ds(h * HALF, HALF)
        sem = sems.at[h]
        batch = [
            pltpu.make_async_copy(state_hbm.at[0, c, at_end, at], state_ref.at[c, :, at], sem.at[c])
            for c in range(parts)
        ]
        batch.append(pltpu.make_async_copy(east_hbm.at[0, at_end, at], east_ref.at[:, at], sem.at[parts]))
        batch.append(pltpu.make_async_copy(north_hbm.at[0, at_end, at], north_ref.at[:, at], sem.at[parts + 1]))
        copies.append(batch)
        for copy in batch:
            copy.start()

    def half(at):
        row = [Row(east_ref[place(r), at, :] * sign, north_ref[place(r), at, :]) for r in range(STEPS)]
        pack_ref[FLUX_ROWS, at, :] = east_ref[place(0), at, :]
        pack_ref[FLUX_ROWS + 1, at, :] = north_ref[place(0), at, :]
        pack_ref[FLUX_ROWS + 2, at, :] = east_ref[place(1), at, :]
        for c in range(parts):
            field = [state_ref[c, place(r), at, :] for r in range(STEPS)]
            for k in range(STEPS):
                pack_ref[2 * k + c, at, :] = row[0].outward * field[0]
                after = []
                for r in range(STEPS - 1 - k):
                    value = row[r].stay(field[r]) + row[r + 1].outward * field[r + 1]
                    if r > 0:
                        value = value + row[r - 1].inward * field[r - 1]
                    after.append(value)
                field = after

    for h in range(halves):
        for copy in copies[h]:
            copy.wait()
        half(pl.ds(h * HALF, HALF))


def as_column(row):
    count = row.shape[1]
    here = lax.broadcasted_iota(jnp.int32, (count, count), 0)
    there = lax.broadcasted_iota(jnp.int32, (count, count), 1)
    return jnp.sum(jnp.where(here == there, row, 0), axis=1, keepdims=True)


def sweep_kernel(
    state_ref, east_ref, north_ref, pack_ref, middle_ref, ends_ref, column_ref,
    field, plus_ref, minus_ref, centre_ref,
):
    parts, rows, levels, width = state_ref.shape[1:]
    flip = 1 - parity()
    sign = sign_of(flip)
    end_row = flip * (rows - 1)
    next_row = end_row + 1 - 2 * flip

    def half(at):
        pack_ref[FLUX_ROWS, at, :] = east_ref[0, end_row, at, :]
        pack_ref[FLUX_ROWS + 1, at, :] = north_ref[0, end_row, at, :]
        pack_ref[FLUX_ROWS + 2, at, :] = east_ref[0, next_row, at, :]

        for k in range(STEPS):
            if k == 0:
                read = lambda c, i: state_ref[0, c, i, at, :]
            else:
                read = lambda c, i, slot=k - 1: field[slot, c, i]
            leaving = jnp.maximum(east_ref[0, end_row, at, :] * sign, 0.0)
            for c in range(parts):
                pack_ref[2 * k + c, at, :] = leaving * read(c, end_row)
            west = [None] * parts
            here = [read(c, 0) for c in range(parts)]
            east_here = east_ref[0, 0, at, :]
            for i in range(rows):
                leave_west = jnp.maximum(-east_here, 0.0)
                if k == 0:
                    north_rate = north_ref[0, i, at, :]
                    centre = 1.0 - jnp.abs(east_here) - jnp.abs(north_rate)
                    plus, minus = north_rates(north_rate)
                    centre_ref[i], plus_ref[i], minus_ref[i] = centre, plus, minus
                else:
                    centre, plus, minus = centre_ref[i], plus_ref[i], minus_ref[i]
                if i + 1 < rows:
                    east_here = east_ref[0, i + 1, at, :]
                    east_after = jnp.maximum(east_here, 0.0)
                for c in range(parts):
                    value = here[c]
                    total = centre * value + shifted(plus * value, minus * value)
                    if i > 0:
                        total = total + west[c]
                    if i + 1 < rows:
                        west[c] = leave_west * value
                        here[c] = read(c, i + 1)
                        total = total + east_after * here[c]
                    if k < STEPS - 1:
                        field[k, c, i] = total
                    elif i < STEPS:
                        ends_ref[c, i, at, :] = total
                    elif i >= rows - STEPS:
                        ends_ref[c, i - rows + 2 * STEPS, at, :] = total
                    else:
                        middle_ref[c, i - STEPS, at, :] = total

        def columns(i, carry):
            for c in range(parts):
                value = state_ref[0, c, i, at, :]
                first, last = value[:, :LANES], value[:, width - LANES:]
                for slot in range(STEPS - 1):
                    first = first + field[slot, c, i, :, :LANES]
                    last = last + field[slot, c, i, :, width - LANES:]
                column_ref[c, 0, i, at, :] = first
                column_ref[c, 1, i, at, :] = last
            return carry

        lax.fori_loop(0, rows, columns, 0, unroll=2)

    level_halves(levels, half)


def ghost_kernel(
    cell_ref, offset_ref, weight_ref, owner_ref, column_ref, north_hbm, spread_ref, partial_ref, first_rate, last_rate, sems
):
    parts, _, rows, levels, _ = column_ref.shape
    slots = spread_ref.shape[-1]
    width = north_hbm.shape[-1]
    copies = [
        pltpu.make_async_copy(north_hbm.at[0, :, :, pl.ds(0, LANES)], first_rate, sems.at[0]),
        pltpu.make_async_copy(north_hbm.at[0, :, :, pl.ds(width - LANES, LANES)], last_rate, sems.at[1]),
    ]
    for copy in copies:
        copy.start()

    here = lax.broadcasted_iota(jnp.int32, (slots, slots), 1)
    placing = jnp.where(as_column(owner_ref[...]) == here, 1.0, 0.0)
    cells = lax.broadcasted_iota(jnp.int32, (rows, slots), 1)
    for c in range(parts):
        for s in range(2):
            mixing = jnp.zeros((rows, slots), jnp.float32)
            for point in range(offset_ref.shape[0]):
                target = as_column(cell_ref[c, s:s + 1, :] + offset_ref[point, c, s:s + 1, :])
                mixing = mixing + jnp.where(target == cells, as_column(weight_ref[point, c, s:s + 1, :]), 0.0)
            spread_ref[c, s] = jnp.dot(
                mixing, placing, precision=lax.Precision.HIGHEST, preferred_element_type=jnp.float32
            )

    for copy in copies:
        copy.wait()
    for c in range(parts):
        total = jnp.zeros((levels, slots), jnp.float32)
        for i in range(rows):
            south = jnp.maximum(first_rate[i, :, :1], 0.0) * column_ref[c, 0, i, :, :1]
            north = jnp.maximum(-last_rate[i, :, LANES - 1:], 0.0) * column_ref[c, 1, i, :, LANES - 1:]
            total = total + south * spread_ref[c, 0, i:i + 1, :]
            total = total + north * spread_ref[c, 1, i:i + 1, :]
        partial_ref[c] = total


def mend_side(flip, east_ref, north_ref, mine_ref, other_ref, store, store_column):
    levels, width = mine_ref.shape[1:]
    rows = east_ref.shape[1]
    sign = sign_of(flip)
    place = lambda r: flip * (rows - STEPS) + r + flip * (STEPS - 1 - 2 * r)

    def half(at):
        own = [Row(east_ref[0, place(r), at, :] * sign, north_ref[0, place(r), at, :]) for r in range(STEPS - 1)]
        near = Row(other_ref[FLUX_ROWS, at, :] * sign, other_ref[FLUX_ROWS + 1, at, :])
        far = Row(other_ref[FLUX_ROWS + 2, at, :] * sign)
        for c in range(FLUX_ROWS // STEPS):
            mine = lambda k: mine_ref[2 * k + c, at, :]
            theirs = lambda k: other_ref[2 * k + c, at, :]
            a0 = theirs(0)
            n1 = mine(0)
            b0 = own[0].stay(a0) + near.inward * n1 + theirs(1)
            b1 = own[0].inward * a0
            bn1 = near.stay(n1) + own[0].outward * a0 + mine(1)
            bn2 = near.outward * n1
            c0 = own[0].stay(b0) + near.inward * bn1 + own[1].outward * b1 + theirs(2)
            c1 = own[1].stay(b1) + own[0].inward * b0
            c2 = own[1].inward * b1
            cn1 = near.stay(bn1) + own[0].outward * b0 + far.inward * bn2 + mine(2)
            d0 = own[0].stay(c0) + near.inward * cn1 + own[1].outward * c1 + theirs(3)
            d1 = own[1].stay(c1) + own[0].inward * c0 + own[2].outward * c2
            d2 = own[2].stay(c2) + own[1].inward * c1
            d3 = own[2].inward * c2
            for r, value in enumerate((d0, d1, d2, d3)):
                store(c, r, at, value)
            for r, pieces in enumerate(((a0, b0, c0), (b1, c1), (c2,))):
                store_column(c, 0, r, at, sum(value[:, :LANES] for value in pieces))
                store_column(c, 1, r, at, sum(value[:, width - LANES:] for value in pieces))

    level_halves(levels, half)


def mend_a_kernel(east_ref, north_ref, mine_ref, other_ref, ends_ref, middle_ref, out_ref, column_ref):
    parts, inner = middle_ref.shape[:2]
    flip = 1 - parity()
    turn = lambda r: r + flip * (STEPS - 1 - 2 * r)

    def store(c, r, at, value):
        out_ref[c, inner + turn(r), at, :] = ends_ref[c, flip * STEPS + turn(r), at, :] + value

    def store_column(c, s, r, at, value):
        column_ref[c, s, r, at, :] = value

    mend_side(flip, east_ref, north_ref, mine_ref, other_ref, store, store_column)
    for c in range(parts):
        for i in range(inner):
            out_ref[c, i] = middle_ref[c, i]


def mend_b_kernel(
    east_ref, north_ref, mine_ref, other_ref, ends_ref, a_column_ref, spread_ref, partial_ref,
    out_ref, sum_ref, b_column_ref,
):
    parts, levels, slots = partial_ref.shape
    rows = east_ref.shape[1]
    width = east_ref.shape[-1]
    flip = parity()
    turn = lambda r: r + flip * (STEPS - 1 - 2 * r)

    def store(c, r, at, value):
        out_ref[c, turn(r), at, :] = ends_ref[c, flip * STEPS + turn(r), at, :] + value

    def store_column(c, s, r, at, value):
        b_column_ref[c, s, r, at, :] = value

    mend_side(flip, east_ref, north_ref, mine_ref, other_ref, store, store_column)
    for c in range(parts):
        total = partial_ref[c]
        for side, column_ref in ((1 - flip, a_column_ref), (flip, b_column_ref)):
            for r in range(STEPS - 1):
                i = r + side * (rows - 1 - 2 * r)
                south = jnp.maximum(north_ref[0, i, :, :1], 0.0) * column_ref[c, 0, r, :, :1]
                north = jnp.maximum(-north_ref[0, i, :, width - 1:], 0.0) * column_ref[c, 1, r, :, LANES - 1:]
                total = total + south * spread_ref[c, 0, pl.ds(i, 1), :]
                total = total + north * spread_ref[c, 1, pl.ds(i, 1), :]
        sum_ref[c] = total


def pieces_kernel(total_ref, out_hbm, buffer, sem):
    parts, levels, slots = total_ref.shape
    peers, _, share, mine = buffer.shape
    subs = levels // share
    each = peers // subs
    from_slot = lax.broadcasted_iota(jnp.int32, (slots, mine), 0)
    to_slot = lax.broadcasted_iota(jnp.int32, (slots, mine), 1)
    total = jnp.concatenate([total_ref[c] for c in range(parts)], 0)
    for p in range(each):
        pick = jnp.where(from_slot == to_slot + p * mine, 1.0, 0.0)
        block = jnp.dot(total, pick, precision=lax.Precision.HIGHEST, preferred_element_type=jnp.float32)
        for s in range(subs):
            for c in range(parts):
                at = c * levels + s * share
                buffer[s * each + p, c] = block[at:at + share]
    copy = pltpu.make_async_copy(buffer, out_hbm, sem)
    copy.start()
    copy.wait()


def join_kernel(came_hbm, out_ref, buffer, sem):
    copy = pltpu.make_async_copy(came_hbm, buffer, sem)
    copy.start()
    copy.wait()
    out_ref[...] = jnp.sum(buffer[...], 0)


def subtract_kernel(state_ref, a_ref, b_ref, out_hbm, buffer, sems):
    parts, rows = state_ref.shape[1:3]
    inner = rows - 2 * STEPS
    a_start = parity() * (rows - STEPS)
    b_start = (1 - parity()) * (rows - STEPS)
    copies = []
    for start, other, first, count in (
        (STEPS, a_ref, 0, inner), (a_start, a_ref, inner, STEPS), (b_start, b_ref, 0, STEPS),
    ):
        for c in range(parts):
            for r in range(count):
                buffer[c, start + r] = state_ref[0, c, start + r] - other[c, first + r]
            at = pl.ds(start, count)
            copy = pltpu.make_async_copy(buffer.at[c, at], out_hbm.at[0, c, at], sems.at[len(copies)])
            copy.start()
            copies.append(copy)
    for copy in copies:
        copy.wait()


def cost(flops, moved):
    return pl.CostEstimate(flops=flops, bytes_accessed=moved, transcendentals=0)


PARAMS = pltpu.CompilerParams(vmem_limit_bytes=24 * 1024 * 1024)


def local(
    adjoint_state,
    courant_east,
    courant_north,
    parent_cell,
    stencil_offset,
    stencil_weight,
    owner_slot,
):
    _, parts, rows, levels, width = adjoint_state.shape
    slots = owner_slot.shape[0]
    inner = rows - 2 * STEPS
    row_bytes = levels * width * 4
    f32 = lambda *shape: jax.ShapeDtypeStruct(shape, jnp.float32)
    vmem = pl.BlockSpec(memory_space=pltpu.VMEM)
    smem = pl.BlockSpec(memory_space=pltpu.SMEM)
    hbm = pl.BlockSpec(memory_space=pltpu.HBM)
    in_hbm = lambda value: pltpu.with_memory_space_constraint(value, pltpu.HBM)

    first_pack = pl.pallas_call(
        first_kernel,
        in_specs=[hbm] * 3,
        out_specs=vmem,
        out_shape=f32(PACK_ROWS, levels, width),
        scratch_shapes=[
            pltpu.VMEM((parts, STEPS, levels, width), jnp.float32),
            pltpu.VMEM((STEPS, levels, width), jnp.float32),
            pltpu.VMEM((STEPS, levels, width), jnp.float32),
            pltpu.SemaphoreType.DMA((levels // HALF, parts + 2)),
        ],
        compiler_params=PARAMS,
        cost_estimate=cost(12 * levels * width * 13, 27 * row_bytes),
        name="first_pack",
    )(in_hbm(adjoint_state), in_hbm(courant_east), in_hbm(courant_north))
    first_came = alternating(first_pack, -1)

    state, east, north = adjoint_state, courant_east, courant_north
    second_pack, middle, ends, columns = pl.pallas_call(
        sweep_kernel,
        in_specs=[vmem] * 3,
        out_specs=[vmem] * 4,
        out_shape=[
            f32(PACK_ROWS, levels, width),
            f32(parts, inner, levels, width),
            f32(parts, 2 * STEPS, levels, width),
            f32(parts, 2, rows, levels, LANES),
        ],
        scratch_shapes=[
            pltpu.VMEM((STEPS - 1, parts, rows, HALF, width), jnp.float32),
            pltpu.VMEM((rows, HALF, width), jnp.float32),
            pltpu.VMEM((rows, HALF, width), jnp.float32),
            pltpu.VMEM((rows, HALF, width), jnp.float32),
        ],
        compiler_params=PARAMS,
        cost_estimate=cost(8 * rows * levels * width * 13, 6 * rows * row_bytes),
        name="sweep",
    )(state, east, north)
    second_came = alternating(second_pack, 1)

    spread, partial = pl.pallas_call(
        ghost_kernel,
        in_specs=[vmem] * 5 + [hbm],
        out_specs=[vmem] * 2,
        out_shape=[f32(parts, 2, rows, slots), f32(parts, levels, slots)],
        scratch_shapes=[
            pltpu.VMEM((rows, levels, LANES), jnp.float32),
            pltpu.VMEM((rows, levels, LANES), jnp.float32),
            pltpu.SemaphoreType.DMA((2,)),
        ],
        compiler_params=PARAMS,
        cost_estimate=cost(parts * rows * levels * slots * 8, 4 * rows * levels * LANES * 8),
        name="ghost_sums",
    )(parent_cell, stencil_offset, stencil_weight, owner_slot[None], columns, in_hbm(courant_north))

    subs, hors = lax.axis_size("sub"), lax.axis_size("hor")

    column_shape = (parts, 2, STEPS - 1, levels, LANES)
    side_a, a_columns = pl.pallas_call(
        mend_a_kernel,
        in_specs=[vmem] * 6,
        out_specs=[vmem] * 2,
        out_shape=[f32(parts, inner + STEPS, levels, width), f32(*column_shape)],
        compiler_params=PARAMS,
        cost_estimate=cost(16 * levels * width * 13, 54 * row_bytes),
        name="mend_a",
    )(east, north, second_pack, first_came, ends, middle)
    a_came = along(side_a, "sub", -1)
    side_b, partial = pl.pallas_call(
        mend_b_kernel,
        in_specs=[vmem] * 8,
        out_specs=[vmem] * 2,
        out_shape=[f32(parts, STEPS, levels, width), f32(parts, levels, slots)],
        scratch_shapes=[pltpu.VMEM(column_shape, jnp.float32)],
        compiler_params=PARAMS,
        cost_estimate=cost(16 * levels * width * 13, 46 * row_bytes),
        name="mend_b",
    )(east, north, first_pack, second_came, ends, a_columns, spread, partial)
    b_came = along(side_b, "sub", -1)

    piece = (subs * hors, parts, levels // subs, slots // hors)
    pieces = pl.pallas_call(
        pieces_kernel,
        in_specs=[vmem],
        out_specs=hbm,
        out_shape=pltpu.HBM(piece, jnp.float32),
        scratch_shapes=[pltpu.VMEM(piece, jnp.float32), pltpu.SemaphoreType.DMA],
        compiler_params=PARAMS,
        name="pieces",
    )(partial)
    pieces = lax.all_to_all(pieces, ("sub", "hor"), 0, 0, tiled=True)
    boundary_gradient = pl.pallas_call(
        join_kernel,
        in_specs=[hbm],
        out_specs=vmem,
        out_shape=f32(parts, levels // subs, slots // hors),
        scratch_shapes=[pltpu.VMEM(piece, jnp.float32), pltpu.SemaphoreType.DMA],
        compiler_params=PARAMS,
        name="join",
    )(in_hbm(pieces))

    adjoint_result = pl.pallas_call(
        subtract_kernel,
        in_specs=[vmem] * 3,
        out_specs=hbm,
        out_shape=f32(*adjoint_state.shape),
        scratch_shapes=[
            pltpu.VMEM((parts, rows, levels, width), jnp.float32),
            pltpu.SemaphoreType.DMA((3 * parts,)),
        ],
        compiler_params=PARAMS,
        cost_estimate=cost(parts * rows * levels * width, 6 * rows * row_bytes),
        name="subtract",
    )(state, a_came, b_came)
    return (adjoint_result, boundary_gradient)


def solution(mesh):
    in_specs = (
        P(("ens", "sub"), None, "hor", None, None),
        P(("ens", "sub"), "hor", None, None),
        P(("ens", "sub"), "hor", None, None),
        P(None, None, "hor"),
        P(None, None, None, "hor"),
        P(None, None, None, "hor"),
        P(),
    )
    out_specs = (P(("ens", "sub"), None, "hor", None, None), P("ens", "sub", "hor"))
    return jax.shard_map(local, mesh=mesh, in_specs=in_specs, out_specs=out_specs, check_vma=False)
```

```python
import functools

import jax
import jax.numpy as jnp
from jax import lax
from jax.experimental import pallas as pl
from jax.experimental.pallas import tpu as pltpu
from jax.sharding import PartitionSpec as P

STEPS = 4
HALF = 8
FLUX_ROWS = 2 * STEPS
PACK_ROWS = FLUX_ROWS + 3
LANES = 128
EXTRA = PACK_ROWS
TARGETS = 4 * LANES
WEIGHTS = 5 * LANES


def along(value, axis, step_of):
    peers = lax.axis_size(axis)
    pairs = [(i, i + step_of) for i in range(peers) if 0 <= i + step_of < peers]
    return lax.ppermute(value, axis, pairs)


def alternating(value, sign):
    subs, hors = lax.axis_size("sub"), lax.axis_size("hor")
    pairs = []
    for s in range(subs):
        step = sign if s % 2 == 0 else -sign
        pairs += [(s * hors + h, s * hors + h + step) for h in range(hors) if 0 <= h + step < hors]
    return lax.ppermute(value, ("sub", "hor"), pairs)


def added_up(value):
    sizes = {axis: lax.axis_size(axis) for axis in ("sub", "hor")}
    if any(size & (size - 1) for size in sizes.values()):
        return lax.psum(value, ("sub", "hor"))
    steps = {axis: [1 << n for n in range(size.bit_length() - 1)] for axis, size in sizes.items()}
    order = [("sub", step) for step in steps["sub"][:1]]
    order += [("hor", step) for step in steps["hor"]]
    order += [("sub", step) for step in steps["sub"][1:]]
    for axis, step in order:
        value = value + lax.ppermute(value, axis, [(i, i ^ step) for i in range(sizes[axis])])
    return value


def parity():
    return lax.rem(lax.axis_index("sub"), 2)


def sign_of(flip):
    return jnp.where(flip == 1, jnp.float32(-1.0), jnp.float32(1.0))


def north_rates(north_rate):
    width = north_rate.shape[-1]
    column = lax.broadcasted_iota(jnp.int32, north_rate.shape, len(north_rate.shape) - 1)
    plus = jnp.where(column == 0, 0.0, jnp.maximum(north_rate, 0.0))
    minus = jnp.where(column == width - 1, 0.0, jnp.maximum(-north_rate, 0.0))
    return plus, minus


def shifted(flux_plus, flux_minus):
    width = flux_plus.shape[-1]
    axis = len(flux_plus.shape) - 1
    return pltpu.roll(flux_plus, width - 1, axis) + pltpu.roll(flux_minus, 1, axis)


class Row:
    def __init__(self, east_rate, north_rate=None):
        self.outward = jnp.maximum(east_rate, 0.0)
        self.inward = jnp.maximum(-east_rate, 0.0)
        if north_rate is not None:
            self.centre = 1.0 - jnp.abs(east_rate) - jnp.abs(north_rate)
            self.plus, self.minus = north_rates(north_rate)

    def stay(self, value):
        return self.centre * value + shifted(self.plus * value, self.minus * value)


def level_halves(levels, body):
    def step(h, carry):
        body(pl.ds(pl.multiple_of(h * HALF, HALF), HALF))
        return carry

    lax.fori_loop(0, levels // HALF, step, 0)


def pack_kernel(which, *refs):
    if which == 0:
        state_hbm, east_hbm, north_hbm, cell_hbm, offset_hbm, weight_hbm = refs[:6]
        pack_ref, state_ref, east_ref, north_ref, cell_ref, offset_ref, weight_ref, sems, small_sems = refs[6:]
    else:
        state_hbm, east_hbm, north_hbm, pack_ref, state_ref, east_ref, north_ref, sems = refs
    parts, rows, levels, width = state_hbm.shape[1:]
    flip = parity() if which == 0 else 1 - parity()
    sign = sign_of(flip)
    at_end = pl.ds(flip * (rows - STEPS), STEPS)
    place = lambda r: r + flip * (STEPS - 1 - 2 * r)
    halves = levels // HALF
    copies = []
    for h in range(halves):
        at = pl.ds(h * HALF, HALF)
        sem = sems.at[h]
        batch = [
            pltpu.make_async_copy(state_hbm.at[0, c, at_end, at], state_ref.at[c, :, at], sem.at[c])
            for c in range(parts)
        ]
        batch.append(pltpu.make_async_copy(east_hbm.at[0, at_end, at], east_ref.at[:, at], sem.at[parts]))
        batch.append(pltpu.make_async_copy(north_hbm.at[0, at_end, at], north_ref.at[:, at], sem.at[parts + 1]))
        copies.append(batch)
        for copy in batch:
            copy.start()
    if which == 0:
        small = [
            pltpu.make_async_copy(source, target, small_sems.at[n])
            for n, (source, target) in enumerate(
                ((cell_hbm, cell_ref), (offset_hbm, offset_ref), (weight_hbm, weight_ref))
            )
        ]
        for copy in small:
            copy.start()

    def half(at):
        row = [Row(east_ref[place(r), at, :] * sign, north_ref[place(r), at, :]) for r in range(STEPS)]
        pack_ref[FLUX_ROWS, at, :] = east_ref[place(0), at, :]
        pack_ref[FLUX_ROWS + 1, at, :] = north_ref[place(0), at, :]
        pack_ref[FLUX_ROWS + 2, at, :] = east_ref[place(1), at, :]
        if which == 0:
            for r in (1, 2):
                lanes = (2 * r - 2) * LANES
                pack_ref[EXTRA, at, lanes:lanes + LANES] = north_ref[place(r), at, :LANES]
                pack_ref[EXTRA, at, lanes + LANES:lanes + 2 * LANES] = north_ref[place(r), at, width - LANES:]
        for c in range(parts):
            field = [state_ref[c, place(r), at, :] for r in range(STEPS)]
            for k in range(STEPS):
                pack_ref[2 * k + c, at, :] = row[0].outward * field[0]
                after = []
                for r in range(STEPS - 1 - k):
                    value = row[r].stay(field[r]) + row[r + 1].outward * field[r + 1]
                    if r > 0:
                        value = value + row[r - 1].inward * field[r - 1]
                    after.append(value)
                field = after

    for h in range(halves):
        for copy in copies[h]:
            copy.wait()
        half(pl.ds(h * HALF, HALF))

    if which == 0:
        for copy in small:
            copy.wait()
        n = 0
        for point in range(offset_ref.shape[0]):
            for c in range(parts):
                target = (cell_ref[c] + offset_ref[point, c]).astype(jnp.float32)
                pack_ref[EXTRA, n:n + 2, TARGETS:TARGETS + rows] = target
                pack_ref[EXTRA, n:n + 2, WEIGHTS:WEIGHTS + rows] = weight_ref[point, c]
                n += 2


def as_column(row):
    count = row.shape[1]
    here = lax.broadcasted_iota(jnp.int32, (count, count), 0)
    there = lax.broadcasted_iota(jnp.int32, (count, count), 1)
    return jnp.sum(jnp.where(here == there, row, 0), axis=1, keepdims=True)


def sweep_kernel(
    state_ref, east_ref, north_ref, middle_ref, ends_ref, column_ref,
    field, plus_ref, minus_ref, centre_ref,
):
    parts, rows, levels, width = state_ref.shape[1:]

    def half(at):
        for k in range(STEPS):
            if k == 0:
                read = lambda c, i: state_ref[0, c, i, at, :]
            else:
                read = lambda c, i, slot=k - 1: field[slot, c, i]
            west = [None] * parts
            here = [read(c, 0) for c in range(parts)]
            east_here = east_ref[0, 0, at, :]
            for i in range(rows):
                leave_west = jnp.maximum(-east_here, 0.0)
                if k == 0:
                    north_rate = north_ref[0, i, at, :]
                    centre = 1.0 - jnp.abs(east_here) - jnp.abs(north_rate)
                    plus, minus = north_rates(north_rate)
                    centre_ref[i], plus_ref[i], minus_ref[i] = centre, plus, minus
                else:
                    centre, plus, minus = centre_ref[i], plus_ref[i], minus_ref[i]
                if i + 1 < rows:
                    east_here = east_ref[0, i + 1, at, :]
                    east_after = jnp.maximum(east_here, 0.0)
                for c in range(parts):
                    value = here[c]
                    total = centre * value + shifted(plus * value, minus * value)
                    if i > 0:
                        total = total + west[c]
                    if i + 1 < rows:
                        west[c] = leave_west * value
                        here[c] = read(c, i + 1)
                        total = total + east_after * here[c]
                    if k < STEPS - 1:
                        field[k, c, i] = total
                    elif i < STEPS:
                        ends_ref[c, i, at, :] = total
                    elif i >= rows - STEPS:
                        ends_ref[c, i - rows + 2 * STEPS, at, :] = total
                    else:
                        middle_ref[c, i - STEPS, at, :] = total

        def columns(i, carry):
            for c in range(parts):
                value = state_ref[0, c, i, at, :]
                first, last = value[:, :LANES], value[:, width - LANES:]
                for slot in range(STEPS - 1):
                    first = first + field[slot, c, i, :, :LANES]
                    last = last + field[slot, c, i, :, width - LANES:]
                column_ref[c, 0, i, at, :] = first
                column_ref[c, 1, i, at, :] = last
            return carry

        lax.fori_loop(0, rows, columns, 0, unroll=2)

    level_halves(levels, half)


def mix(targets, weights, cells, total):
    for target, weight in zip(targets, weights):
        total = total + jnp.where(as_column(target) == cells, as_column(weight), 0.0)
    return total


def ghost_base_kernel(
    cell_ref, offset_ref, weight_ref, column_ref, north_ref, mixing_ref, partial_ref
):
    parts, _, rows, levels, _ = column_ref.shape
    slots = mixing_ref.shape[-1]
    width = north_ref.shape[-1]
    points = range(offset_ref.shape[0])
    cells = lax.broadcasted_iota(jnp.int32, (rows, slots), 1)
    for c in range(parts):
        for s in range(2):
            mixing_ref[c, s] = mix(
                [cell_ref[c, s:s + 1, :] + offset_ref[point, c, s:s + 1, :] for point in points],
                [weight_ref[point, c, s:s + 1, :] for point in points],
                cells, jnp.zeros((rows, slots), jnp.float32),
            )

    for c in range(parts):
        total = jnp.zeros((levels, slots), jnp.float32)
        for i in range(rows):
            south = jnp.maximum(north_ref[0, i, :, :1], 0.0) * column_ref[c, 0, i, :, :1]
            north = jnp.maximum(-north_ref[0, i, :, width - 1:], 0.0) * column_ref[c, 1, i, :, LANES - 1:]
            total = total + south * mixing_ref[c, 0, i:i + 1, :]
            total = total + north * mixing_ref[c, 1, i:i + 1, :]
        partial_ref[c] = total


def ghost_kernel(north_ref, other_ref, column_ref, mixing_ref, partial_ref, sum_ref, near_mixing):
    parts, levels, slots = partial_ref.shape
    rows = mixing_ref.shape[2]
    width = north_ref.shape[-1]
    flip = 1 - parity()
    cells = lax.broadcasted_iota(jnp.int32, (rows, slots), 1).astype(jnp.float32)
    points = (WEIGHTS - TARGETS) // LANES * 4
    for c in range(parts):
        for s in range(2):
            at = [(point * parts + c) * 2 + s for point in range(points)]
            near_mixing[c, s] = mix(
                [other_ref[EXTRA, n:n + 1, TARGETS:TARGETS + rows] for n in at],
                [other_ref[EXTRA, n:n + 1, WEIGHTS:WEIGHTS + rows] for n in at],
                cells, jnp.zeros((rows, slots), jnp.float32),
            )
    for c in range(parts):
        total = partial_ref[c]
        for r in range(STEPS - 1):
            i = r + flip * (rows - 1 - 2 * r)
            south = jnp.maximum(north_ref[0, i, :, :1], 0.0) * column_ref[c, 0, r, :, :1]
            north = jnp.maximum(-north_ref[0, i, :, width - 1:], 0.0) * column_ref[c, 1, r, :, LANES - 1:]
            total = total + south * mixing_ref[c, 0, pl.ds(i, 1), :]
            total = total + north * mixing_ref[c, 1, pl.ds(i, 1), :]
            i = r + (1 - flip) * (rows - 1 - 2 * r)
            if r == 0:
                first_rate = other_ref[FLUX_ROWS + 1, :, :LANES]
                last_rate = other_ref[FLUX_ROWS + 1, :, width - LANES:]
            else:
                lanes = (2 * r - 2) * LANES
                first_rate = other_ref[EXTRA, :, lanes:lanes + LANES]
                last_rate = other_ref[EXTRA, :, lanes + LANES:lanes + 2 * LANES]
            south = jnp.maximum(first_rate[:, :1], 0.0) * column_ref[c, 0, STEPS - 1 + r, :, :1]
            north = jnp.maximum(-last_rate[:, LANES - 1:], 0.0) * column_ref[c, 1, STEPS - 1 + r, :, LANES - 1:]
            total = total + south * near_mixing[c, 0, pl.ds(i, 1), :]
            total = total + north * near_mixing[c, 1, pl.ds(i, 1), :]
        sum_ref[c] = total


def mend_side(flip, east_ref, north_ref, mine_ref, other_ref, store, store_column):
    levels, width = mine_ref.shape[1:]
    rows = east_ref.shape[1]
    sign = sign_of(flip)
    place = lambda r: flip * (rows - STEPS) + r + flip * (STEPS - 1 - 2 * r)

    def half(at):
        own = [Row(east_ref[0, place(r), at, :] * sign, north_ref[0, place(r), at, :]) for r in range(STEPS - 1)]
        near = Row(other_ref[FLUX_ROWS, at, :] * sign, other_ref[FLUX_ROWS + 1, at, :])
        far = Row(other_ref[FLUX_ROWS + 2, at, :] * sign)
        for c in range(FLUX_ROWS // STEPS):
            mine = lambda k: mine_ref[2 * k + c, at, :]
            theirs = lambda k: other_ref[2 * k + c, at, :]
            a0 = theirs(0)
            n1 = mine(0)
            b0 = own[0].stay(a0) + near.inward * n1 + theirs(1)
            b1 = own[0].inward * a0
            bn1 = near.stay(n1) + own[0].outward * a0 + mine(1)
            bn2 = near.outward * n1
            c0 = own[0].stay(b0) + near.inward * bn1 + own[1].outward * b1 + theirs(2)
            c1 = own[1].stay(b1) + own[0].inward * b0
            c2 = own[1].inward * b1
            cn1 = near.stay(bn1) + own[0].outward * b0 + far.inward * bn2 + mine(2)
            d0 = own[0].stay(c0) + near.inward * cn1 + own[1].outward * c1 + theirs(3)
            d1 = own[1].stay(c1) + own[0].inward * c0 + own[2].outward * c2
            d2 = own[2].stay(c2) + own[1].inward * c1
            d3 = own[2].inward * c2
            for r, value in enumerate((d0, d1, d2, d3)):
                store(c, r, at, value)
            if store_column is not None:
                tiles = (slice(0, LANES), slice(width - LANES, width))
                for s, lanes in enumerate(tiles):
                    tile = lambda value: value[:, lanes]
                    rate = other_ref[EXTRA, at, s * LANES:(s + 1) * LANES]
                    stays = 1.0 - jnp.abs(other_ref[FLUX_ROWS + 2, at, lanes]) - jnp.abs(rate)
                    drift = jnp.maximum(rate if s == 0 else -rate, 0.0) * tile(bn2)
                    cn2 = stays * tile(bn2) + pltpu.roll(drift, LANES - 1 if s == 0 else 1, 1)
                    cn2 = cn2 + tile(near.outward) * tile(bn1)
                    cn3 = tile(far.outward) * tile(bn2)
                    sums = (
                        tile(a0) + tile(b0) + tile(c0), tile(b1) + tile(c1), tile(c2),
                        tile(n1) + tile(bn1) + tile(cn1), tile(bn2) + cn2, cn3,
                    )
                    for r, value in enumerate(sums):
                        store_column(c, s, r, at, value)

    level_halves(levels, half)


def mend_a_kernel(east_ref, north_ref, mine_ref, other_ref, ends_ref, middle_ref, base_ref, out_ref, column_ref):
    parts, inner = middle_ref.shape[:2]
    flip = 1 - parity()
    turn = lambda r: r + flip * (STEPS - 1 - 2 * r)

    def store(c, r, at, value):
        out_ref[c, inner + turn(r), at, :] = ends_ref[c, flip * STEPS + turn(r), at, :] + value

    def store_column(c, s, r, at, value):
        column_ref[c, s, r, at, :] = value

    mend_side(flip, east_ref, north_ref, mine_ref, other_ref, store, store_column)
    for c in range(parts):
        for i in range(inner):
            out_ref[c, i] = middle_ref[c, i]


def mend_b_kernel(east_ref, north_ref, mine_ref, other_ref, ends_ref, out_ref):
    flip = parity()
    turn = lambda r: r + flip * (STEPS - 1 - 2 * r)

    def store(c, r, at, value):
        out_ref[c, turn(r), at, :] = ends_ref[c, flip * STEPS + turn(r), at, :] + value

    mend_side(flip, east_ref, north_ref, mine_ref, other_ref, store, None)


def pick_kernel(total_ref, owner_ref, out_ref):
    parts, share, mine = out_ref.shape
    slots = owner_ref.shape[-1]
    to_slot = lax.broadcasted_iota(jnp.int32, (slots, mine), 1) + lax.axis_index("hor") * mine
    pick = jnp.where(as_column(owner_ref[...]) == to_slot, 1.0, 0.0)
    for c in range(parts):
        chosen = jnp.zeros((share, slots), jnp.float32)
        for s in range(total_ref.shape[1] // share):
            block = total_ref[c, s * share:(s + 1) * share, :]
            chosen = jnp.where(lax.axis_index("sub") == s, block, chosen)
        out_ref[c] = jnp.dot(chosen, pick, precision=lax.Precision.HIGHEST, preferred_element_type=jnp.float32)


def subtract_kernel(state_ref, a_ref, b_ref, out_hbm, buffer, sems):
    parts, rows = state_ref.shape[1:3]
    inner = rows - 2 * STEPS
    a_start = parity() * (rows - STEPS)
    b_start = (1 - parity()) * (rows - STEPS)
    copies = []
    for start, other, first, count in (
        (STEPS, a_ref, 0, inner), (a_start, a_ref, inner, STEPS), (b_start, b_ref, 0, STEPS),
    ):
        for c in range(parts):
            for r in range(count):
                buffer[c, start + r] = state_ref[0, c, start + r] - other[c, first + r]
            at = pl.ds(start, count)
            copy = pltpu.make_async_copy(buffer.at[c, at], out_hbm.at[0, c, at], sems.at[len(copies)])
            copy.start()
            copies.append(copy)
    for copy in copies:
        copy.wait()


def cost(flops, moved):
    return pl.CostEstimate(flops=flops, bytes_accessed=moved, transcendentals=0)


PARAMS = pltpu.CompilerParams(vmem_limit_bytes=24 * 1024 * 1024)


def local(
    adjoint_state,
    courant_east,
    courant_north,
    parent_cell,
    stencil_offset,
    stencil_weight,
    owner_slot,
):
    _, parts, rows, levels, width = adjoint_state.shape
    slots = owner_slot.shape[0]
    inner = rows - 2 * STEPS
    row_bytes = levels * width * 4
    f32 = lambda *shape: jax.ShapeDtypeStruct(shape, jnp.float32)
    vmem = pl.BlockSpec(memory_space=pltpu.VMEM)
    smem = pl.BlockSpec(memory_space=pltpu.SMEM)
    hbm = pl.BlockSpec(memory_space=pltpu.HBM)
    in_hbm = lambda value: pltpu.with_memory_space_constraint(value, pltpu.HBM)

    subs, hors = lax.axis_size("sub"), lax.axis_size("hor")
    small = [parent_cell, stencil_offset, stencil_weight]

    def pack(which):
        extra = small if which == 0 else []
        return pl.pallas_call(
            functools.partial(pack_kernel, which),
            in_specs=[hbm] * (3 + len(extra)),
            out_specs=vmem,
            out_shape=f32(PACK_ROWS + 1 - which, levels, width),
            scratch_shapes=[
                pltpu.VMEM((parts, STEPS, levels, width), jnp.float32),
                pltpu.VMEM((STEPS, levels, width), jnp.float32),
                pltpu.VMEM((STEPS, levels, width), jnp.float32),
            ]
            + [pltpu.VMEM(value.shape, value.dtype) for value in extra]
            + [pltpu.SemaphoreType.DMA((levels // HALF, parts + 2))]
            + [pltpu.SemaphoreType.DMA((3,)) for _ in extra[:1]],
            compiler_params=PARAMS,
            cost_estimate=cost(12 * levels * width * 13, 28 * row_bytes),
            name="pack_" + "ab"[which],
        )(*[in_hbm(value) for value in [adjoint_state, courant_east, courant_north] + extra])

    first_pack = pack(0)
    first_came = alternating(first_pack, -1)
    second_pack = pack(1)
    second_came = alternating(second_pack, 1)

    state, east, north = adjoint_state, courant_east, courant_north
    middle, ends, columns = pl.pallas_call(
        sweep_kernel,
        in_specs=[vmem] * 3,
        out_specs=[vmem] * 3,
        out_shape=[
            f32(parts, inner, levels, width),
            f32(parts, 2 * STEPS, levels, width),
            f32(parts, 2, rows, levels, LANES),
        ],
        scratch_shapes=[
            pltpu.VMEM((STEPS - 1, parts, rows, HALF, width), jnp.float32),
            pltpu.VMEM((rows, HALF, width), jnp.float32),
            pltpu.VMEM((rows, HALF, width), jnp.float32),
            pltpu.VMEM((rows, HALF, width), jnp.float32),
        ],
        compiler_params=PARAMS,
        cost_estimate=cost(8 * rows * levels * width * 13, 6 * rows * row_bytes),
        name="sweep",
    )(state, east, north)

    mixing, base = pl.pallas_call(
        ghost_base_kernel,
        in_specs=[vmem] * 5,
        out_specs=[vmem] * 2,
        out_shape=[f32(parts, 2, rows, slots), f32(parts, levels, slots)],
        compiler_params=PARAMS,
        cost_estimate=cost(parts * rows * levels * slots * 8, 4 * rows * levels * LANES * 8),
        name="ghost_base",
    )(*small, columns, north)

    column_shape = (parts, 2, 2 * (STEPS - 1), levels, LANES)
    side_a, a_columns = pl.pallas_call(
        mend_a_kernel,
        in_specs=[vmem] * 7,
        out_specs=[vmem] * 2,
        out_shape=[f32(parts, inner + STEPS, levels, width), f32(*column_shape)],
        compiler_params=PARAMS,
        cost_estimate=cost(16 * levels * width * 13, 54 * row_bytes),
        name="mend_a",
    )(east, north, second_pack, first_came, ends, middle, base)
    a_came = along(side_a, "sub", -1)
    total = pl.pallas_call(
        ghost_kernel,
        in_specs=[vmem] * 5,
        out_specs=vmem,
        out_shape=f32(parts, levels, slots),
        scratch_shapes=[pltpu.VMEM((parts, 2, rows, slots), jnp.float32)],
        compiler_params=PARAMS,
        cost_estimate=cost(parts * levels * slots * 64, 8 * row_bytes),
        name="ghost",
    )(north, first_came, a_columns, mixing, base)
    side_b = pl.pallas_call(
        mend_b_kernel,
        in_specs=[vmem] * 5,
        out_specs=vmem,
        out_shape=f32(parts, STEPS, levels, width),
        compiler_params=PARAMS,
        cost_estimate=cost(16 * levels * width * 13, 46 * row_bytes),
        name="mend_b",
    )(east, north, first_pack, second_came, ends)
    b_came = along(side_b, "sub", -1)

    total = added_up(total)
    boundary_gradient = pl.pallas_call(
        pick_kernel,
        in_specs=[vmem] * 2,
        out_specs=vmem,
        out_shape=f32(parts, levels // subs, slots // hors),
        compiler_params=PARAMS,
        name="pick",
    )(total, owner_slot[None])

    adjoint_result = pl.pallas_call(
        subtract_kernel,
        in_specs=[vmem] * 3,
        out_specs=hbm,
        out_shape=f32(*adjoint_state.shape),
        scratch_shapes=[
            pltpu.VMEM((parts, rows, levels, width), jnp.float32),
            pltpu.SemaphoreType.DMA((3 * parts,)),
        ],
        compiler_params=PARAMS,
        cost_estimate=cost(parts * rows * levels * width, 6 * rows * row_bytes),
        name="subtract",
    )(state, a_came, b_came)
    return (adjoint_result, boundary_gradient)


def solution(mesh):
    in_specs = (
        P(("ens", "sub"), None, "hor", None, None),
        P(("ens", "sub"), "hor", None, None),
        P(("ens", "sub"), "hor", None, None),
        P(None, None, "hor"),
        P(None, None, None, "hor"),
        P(None, None, None, "hor"),
        P(),
    )
    out_specs = (P(("ens", "sub"), None, "hor", None, None), P("ens", "sub", "hor"))
    return jax.shard_map(local, mesh=mesh, in_specs=in_specs, out_specs=out_specs, check_vma=False)
```

```python
import functools

import jax
import jax.numpy as jnp
from jax import lax
from jax.experimental import pallas as pl
from jax.experimental.pallas import tpu as pltpu
from jax.sharding import PartitionSpec as P

STEPS = 4
HALF = 8
FLUX_ROWS = 2 * STEPS
PACK_ROWS = FLUX_ROWS + 3
LANES = 128
EXTRA = PACK_ROWS
TARGETS = 4 * LANES
WEIGHTS = 5 * LANES


def along(value, axis, step_of):
    peers = lax.axis_size(axis)
    pairs = [(i, i + step_of) for i in range(peers) if 0 <= i + step_of < peers]
    return lax.ppermute(value, axis, pairs)


def alternating(value, sign):
    subs, hors = lax.axis_size("sub"), lax.axis_size("hor")
    pairs = []
    for s in range(subs):
        step = sign if s % 2 == 0 else -sign
        pairs += [(s * hors + h, s * hors + h + step) for h in range(hors) if 0 <= h + step < hors]
    return lax.ppermute(value, ("sub", "hor"), pairs)


def added_up(value):
    sizes = {axis: lax.axis_size(axis) for axis in ("hor", "sub")}
    if any(size & (size - 1) for size in sizes.values()):
        return lax.psum(value, ("sub", "hor"))
    for axis, size in sizes.items():
        step = 1
        while step < size:
            group = min(4, size // step)
            came = [
                lax.ppermute(value, axis, [(i, i ^ (step * j)) for i in range(size)])
                for j in range(1, group)
            ]
            value = sum(came, value)
            step *= group
    return value


def parity():
    return lax.rem(lax.axis_index("sub"), 2)


def sign_of(flip):
    return jnp.where(flip == 1, jnp.float32(-1.0), jnp.float32(1.0))


def north_rates(north_rate):
    width = north_rate.shape[-1]
    column = lax.broadcasted_iota(jnp.int32, north_rate.shape, len(north_rate.shape) - 1)
    plus = jnp.where(column == 0, 0.0, jnp.maximum(north_rate, 0.0))
    minus = jnp.where(column == width - 1, 0.0, jnp.maximum(-north_rate, 0.0))
    return plus, minus


def shifted(flux_plus, flux_minus):
    width = flux_plus.shape[-1]
    axis = len(flux_plus.shape) - 1
    return pltpu.roll(flux_plus, width - 1, axis) + pltpu.roll(flux_minus, 1, axis)


class Row:
    def __init__(self, east_rate, north_rate=None):
        self.outward = jnp.maximum(east_rate, 0.0)
        self.inward = jnp.maximum(-east_rate, 0.0)
        if north_rate is not None:
            self.centre = 1.0 - jnp.abs(east_rate) - jnp.abs(north_rate)
            self.plus, self.minus = north_rates(north_rate)

    def stay(self, value):
        return self.centre * value + shifted(self.plus * value, self.minus * value)


def level_halves(levels, body):
    def step(h, carry):
        body(pl.ds(pl.multiple_of(h * HALF, HALF), HALF))
        return carry

    lax.fori_loop(0, levels // HALF, step, 0)


def pack_kernel(which, *refs):
    if which == 0:
        state_hbm, east_hbm, north_hbm, cell_hbm, offset_hbm, weight_hbm = refs[:6]
        pack_ref, state_ref, east_ref, north_ref, cell_ref, offset_ref, weight_ref, sems, small_sems = refs[6:]
        parts, rows, levels, width = state_hbm.shape[1:]
    else:
        state_ref, east_ref, north_ref, pack_ref = refs
        parts, rows, levels, width = state_ref.shape[1:]
        state_ref, east_ref, north_ref = state_ref.at[0], east_ref.at[0], north_ref.at[0]
    flip = parity() if which == 0 else 1 - parity()
    sign = sign_of(flip)
    at_end = pl.ds(flip * (rows - STEPS), STEPS)
    before = 0 if which == 0 else flip * (rows - STEPS)
    place = lambda r: before + r + flip * (STEPS - 1 - 2 * r)
    halves = levels // HALF
    copies = [[]] * halves
    for h in range(halves if which == 0 else 0):
        at = pl.ds(h * HALF, HALF)
        sem = sems.at[h]
        batch = [
            pltpu.make_async_copy(state_hbm.at[0, c, at_end, at], state_ref.at[c, :, at], sem.at[c])
            for c in range(parts)
        ]
        batch.append(pltpu.make_async_copy(east_hbm.at[0, at_end, at], east_ref.at[:, at], sem.at[parts]))
        batch.append(pltpu.make_async_copy(north_hbm.at[0, at_end, at], north_ref.at[:, at], sem.at[parts + 1]))
        copies[h] = batch
        for copy in batch:
            copy.start()
    if which == 0:
        small = [
            pltpu.make_async_copy(source, target, small_sems.at[n])
            for n, (source, target) in enumerate(
                ((cell_hbm, cell_ref), (offset_hbm, offset_ref), (weight_hbm, weight_ref))
            )
        ]
        for copy in small:
            copy.start()

    def half(at):
        row = [Row(east_ref[place(r), at, :] * sign, north_ref[place(r), at, :]) for r in range(STEPS)]
        pack_ref[FLUX_ROWS, at, :] = east_ref[place(0), at, :]
        pack_ref[FLUX_ROWS + 1, at, :] = north_ref[place(0), at, :]
        pack_ref[FLUX_ROWS + 2, at, :] = east_ref[place(1), at, :]
        if which == 0:
            for r in (1, 2):
                lanes = (2 * r - 2) * LANES
                pack_ref[EXTRA, at, lanes:lanes + LANES] = north_ref[place(r), at, :LANES]
                pack_ref[EXTRA, at, lanes + LANES:lanes + 2 * LANES] = north_ref[place(r), at, width - LANES:]
        for c in range(parts):
            field = [state_ref[c, place(r), at, :] for r in range(STEPS)]
            for k in range(STEPS):
                pack_ref[2 * k + c, at, :] = row[0].outward * field[0]
                after = []
                for r in range(STEPS - 1 - k):
                    value = row[r].stay(field[r]) + row[r + 1].outward * field[r + 1]
                    if r > 0:
                        value = value + row[r - 1].inward * field[r - 1]
                    after.append(value)
                field = after

    for h in range(halves):
        for copy in copies[h]:
            copy.wait()
        half(pl.ds(h * HALF, HALF))

    if which == 0:
        for copy in small:
            copy.wait()
        n = 0
        for point in range(offset_ref.shape[0]):
            for c in range(parts):
                target = (cell_ref[c] + offset_ref[point, c]).astype(jnp.float32)
                pack_ref[EXTRA, n:n + 2, TARGETS:TARGETS + rows] = target
                pack_ref[EXTRA, n:n + 2, WEIGHTS:WEIGHTS + rows] = weight_ref[point, c]
                n += 2


def as_column(row):
    count = row.shape[1]
    here = lax.broadcasted_iota(jnp.int32, (count, count), 0)
    there = lax.broadcasted_iota(jnp.int32, (count, count), 1)
    return jnp.sum(jnp.where(here == there, row, 0), axis=1, keepdims=True)


def sweep_kernel(
    state_ref, east_ref, north_ref, middle_ref, ends_ref, column_ref,
    field, plus_ref, minus_ref, centre_ref,
):
    parts, rows, levels, width = state_ref.shape[1:]

    def half(at):
        for k in range(STEPS):
            if k == 0:
                read = lambda c, i: state_ref[0, c, i, at, :]
            else:
                read = lambda c, i, slot=k - 1: field[slot, c, i]
            west = [None] * parts
            here = [read(c, 0) for c in range(parts)]
            east_here = east_ref[0, 0, at, :]
            for i in range(rows):
                leave_west = jnp.maximum(-east_here, 0.0)
                if k == 0:
                    north_rate = north_ref[0, i, at, :]
                    centre = 1.0 - jnp.abs(east_here) - jnp.abs(north_rate)
                    plus, minus = north_rates(north_rate)
                    centre_ref[i], plus_ref[i], minus_ref[i] = centre, plus, minus
                else:
                    centre, plus, minus = centre_ref[i], plus_ref[i], minus_ref[i]
                if i + 1 < rows:
                    east_here = east_ref[0, i + 1, at, :]
                    east_after = jnp.maximum(east_here, 0.0)
                for c in range(parts):
                    value = here[c]
                    total = centre * value + shifted(plus * value, minus * value)
                    if i > 0:
                        total = total + west[c]
                    if i + 1 < rows:
                        west[c] = leave_west * value
                        here[c] = read(c, i + 1)
                        total = total + east_after * here[c]
                    if k < STEPS - 1:
                        field[k, c, i] = total
                    elif i < STEPS:
                        ends_ref[c, i, at, :] = total
                    elif i >= rows - STEPS:
                        ends_ref[c, i - rows + 2 * STEPS, at, :] = total
                    else:
                        middle_ref[c, i - STEPS, at, :] = total

        def columns(i, carry):
            for c in range(parts):
                value = state_ref[0, c, i, at, :]
                first, last = value[:, :LANES], value[:, width - LANES:]
                for slot in range(STEPS - 1):
                    first = first + field[slot, c, i, :, :LANES]
                    last = last + field[slot, c, i, :, width - LANES:]
                column_ref[c, 0, i, at, :] = first
                column_ref[c, 1, i, at, :] = last
            return carry

        lax.fori_loop(0, rows, columns, 0, unroll=2)

    level_halves(levels, half)


def mix(targets, weights, cells, total):
    for target, weight in zip(targets, weights):
        total = total + jnp.where(as_column(target) == cells, as_column(weight), 0.0)
    return total


def ghost_base_kernel(
    cell_ref, offset_ref, weight_ref, column_ref, north_ref, mixing_ref, partial_ref
):
    parts, _, rows, levels, _ = column_ref.shape
    slots = mixing_ref.shape[-1]
    width = north_ref.shape[-1]
    points = range(offset_ref.shape[0])
    cells = lax.broadcasted_iota(jnp.int32, (rows, slots), 1)
    for c in range(parts):
        for s in range(2):
            mixing_ref[c, s] = mix(
                [cell_ref[c, s:s + 1, :] + offset_ref[point, c, s:s + 1, :] for point in points],
                [weight_ref[point, c, s:s + 1, :] for point in points],
                cells, jnp.zeros((rows, slots), jnp.float32),
            )

    for c in range(parts):
        total = jnp.zeros((levels, slots), jnp.float32)
        for i in range(rows):
            south = jnp.maximum(north_ref[0, i, :, :1], 0.0) * column_ref[c, 0, i, :, :1]
            north = jnp.maximum(-north_ref[0, i, :, width - 1:], 0.0) * column_ref[c, 1, i, :, LANES - 1:]
            total = total + south * mixing_ref[c, 0, i:i + 1, :]
            total = total + north * mixing_ref[c, 1, i:i + 1, :]
        partial_ref[c] = total


def ghost_kernel(north_ref, other_ref, column_ref, mixing_ref, partial_ref, sum_ref, near_mixing):
    parts, levels, slots = partial_ref.shape
    rows = mixing_ref.shape[2]
    width = north_ref.shape[-1]
    flip = 1 - parity()
    cells = lax.broadcasted_iota(jnp.int32, (rows, slots), 1).astype(jnp.float32)
    points = (WEIGHTS - TARGETS) // LANES * 4
    for c in range(parts):
        for s in range(2):
            at = [(point * parts + c) * 2 + s for point in range(points)]
            near_mixing[c, s] = mix(
                [other_ref[EXTRA, n:n + 1, TARGETS:TARGETS + rows] for n in at],
                [other_ref[EXTRA, n:n + 1, WEIGHTS:WEIGHTS + rows] for n in at],
                cells, jnp.zeros((rows, slots), jnp.float32),
            )
    for c in range(parts):
        total = partial_ref[c]
        for r in range(STEPS - 1):
            i = r + flip * (rows - 1 - 2 * r)
            south = jnp.maximum(north_ref[0, i, :, :1], 0.0) * column_ref[c, 0, r, :, :1]
            north = jnp.maximum(-north_ref[0, i, :, width - 1:], 0.0) * column_ref[c, 1, r, :, LANES - 1:]
            total = total + south * mixing_ref[c, 0, pl.ds(i, 1), :]
            total = total + north * mixing_ref[c, 1, pl.ds(i, 1), :]
            i = r + (1 - flip) * (rows - 1 - 2 * r)
            if r == 0:
                first_rate = other_ref[FLUX_ROWS + 1, :, :LANES]
                last_rate = other_ref[FLUX_ROWS + 1, :, width - LANES:]
            else:
                lanes = (2 * r - 2) * LANES
                first_rate = other_ref[EXTRA, :, lanes:lanes + LANES]
                last_rate = other_ref[EXTRA, :, lanes + LANES:lanes + 2 * LANES]
            south = jnp.maximum(first_rate[:, :1], 0.0) * column_ref[c, 0, STEPS - 1 + r, :, :1]
            north = jnp.maximum(-last_rate[:, LANES - 1:], 0.0) * column_ref[c, 1, STEPS - 1 + r, :, LANES - 1:]
            total = total + south * near_mixing[c, 0, pl.ds(i, 1), :]
            total = total + north * near_mixing[c, 1, pl.ds(i, 1), :]
        sum_ref[c] = total


def mend_side(flip, east_ref, north_ref, mine_ref, other_ref, store, store_column):
    levels, width = mine_ref.shape[1:]
    rows = east_ref.shape[1]
    sign = sign_of(flip)
    place = lambda r: flip * (rows - STEPS) + r + flip * (STEPS - 1 - 2 * r)

    def half(at):
        own = [Row(east_ref[0, place(r), at, :] * sign, north_ref[0, place(r), at, :]) for r in range(STEPS - 1)]
        near = Row(other_ref[FLUX_ROWS, at, :] * sign, other_ref[FLUX_ROWS + 1, at, :])
        far = Row(other_ref[FLUX_ROWS + 2, at, :] * sign)
        for c in range(FLUX_ROWS // STEPS):
            mine = lambda k: mine_ref[2 * k + c, at, :]
            theirs = lambda k: other_ref[2 * k + c, at, :]
            a0 = theirs(0)
            n1 = mine(0)
            b0 = own[0].stay(a0) + near.inward * n1 + theirs(1)
            b1 = own[0].inward * a0
            bn1 = near.stay(n1) + own[0].outward * a0 + mine(1)
            bn2 = near.outward * n1
            c0 = own[0].stay(b0) + near.inward * bn1 + own[1].outward * b1 + theirs(2)
            c1 = own[1].stay(b1) + own[0].inward * b0
            c2 = own[1].inward * b1
            cn1 = near.stay(bn1) + own[0].outward * b0 + far.inward * bn2 + mine(2)
            d0 = own[0].stay(c0) + near.inward * cn1 + own[1].outward * c1 + theirs(3)
            d1 = own[1].stay(c1) + own[0].inward * c0 + own[2].outward * c2
            d2 = own[2].stay(c2) + own[1].inward * c1
            d3 = own[2].inward * c2
            for r, value in enumerate((d0, d1, d2, d3)):
                store(c, r, at, value)
            if store_column is not None:
                tiles = (slice(0, LANES), slice(width - LANES, width))
                for s, lanes in enumerate(tiles):
                    tile = lambda value: value[:, lanes]
                    rate = other_ref[EXTRA, at, s * LANES:(s + 1) * LANES]
                    stays = 1.0 - jnp.abs(other_ref[FLUX_ROWS + 2, at, lanes]) - jnp.abs(rate)
                    drift = jnp.maximum(rate if s == 0 else -rate, 0.0) * tile(bn2)
                    cn2 = stays * tile(bn2) + pltpu.roll(drift, LANES - 1 if s == 0 else 1, 1)
                    cn2 = cn2 + tile(near.outward) * tile(bn1)
                    cn3 = tile(far.outward) * tile(bn2)
                    sums = (
                        tile(a0) + tile(b0) + tile(c0), tile(b1) + tile(c1), tile(c2),
                        tile(n1) + tile(bn1) + tile(cn1), tile(bn2) + cn2, cn3,
                    )
                    for r, value in enumerate(sums):
                        store_column(c, s, r, at, value)

    level_halves(levels, half)


def mend_a_kernel(east_ref, north_ref, mine_ref, other_ref, ends_ref, base_ref, out_ref, column_ref):
    flip = 1 - parity()
    turn = lambda r: r + flip * (STEPS - 1 - 2 * r)

    def store(c, r, at, value):
        out_ref[c, turn(r), at, :] = ends_ref[c, flip * STEPS + turn(r), at, :] + value

    def store_column(c, s, r, at, value):
        column_ref[c, s, r, at, :] = value

    mend_side(flip, east_ref, north_ref, mine_ref, other_ref, store, store_column)


def mend_b_kernel(east_ref, north_ref, mine_ref, other_ref, ends_ref, out_ref):
    flip = parity()
    turn = lambda r: r + flip * (STEPS - 1 - 2 * r)

    def store(c, r, at, value):
        out_ref[c, turn(r), at, :] = ends_ref[c, flip * STEPS + turn(r), at, :] + value

    mend_side(flip, east_ref, north_ref, mine_ref, other_ref, store, None)


def finish_kernel(
    total_ref, owner_ref, state_ref, middle_ref, a_ref, b_ref, out_hbm, gradient_ref, buffer, sems
):
    parts, rows = state_ref.shape[1:3]
    inner = rows - 2 * STEPS
    a_start = parity() * (rows - STEPS)
    b_start = (1 - parity()) * (rows - STEPS)
    copies = []
    for start, other in ((STEPS, middle_ref), (a_start, a_ref), (b_start, b_ref)):
        for c in range(parts):
            count = other.shape[1]
            for r in range(count):
                buffer[c, start + r] = state_ref[0, c, start + r] - other[c, r]
            at = pl.ds(start, count)
            copy = pltpu.make_async_copy(buffer.at[c, at], out_hbm.at[0, c, at], sems.at[len(copies)])
            copy.start()
            copies.append(copy)

    share, mine = gradient_ref.shape[1:]
    slots = owner_ref.shape[-1]
    to_slot = lax.broadcasted_iota(jnp.int32, (slots, mine), 1) + lax.axis_index("hor") * mine
    pick = jnp.where(as_column(owner_ref[...]) == to_slot, 1.0, 0.0)
    for c in range(parts):
        chosen = jnp.zeros((share, slots), jnp.float32)
        for s in range(total_ref.shape[1] // share):
            block = total_ref[c, s * share:(s + 1) * share, :]
            chosen = jnp.where(lax.axis_index("sub") == s, block, chosen)
        gradient_ref[c] = jnp.dot(chosen, pick, precision=lax.Precision.HIGHEST, preferred_element_type=jnp.float32)
    for copy in copies:
        copy.wait()


def cost(flops, moved):
    return pl.CostEstimate(flops=flops, bytes_accessed=moved, transcendentals=0)


PARAMS = pltpu.CompilerParams(vmem_limit_bytes=24 * 1024 * 1024)


def local(
    adjoint_state,
    courant_east,
    courant_north,
    parent_cell,
    stencil_offset,
    stencil_weight,
    owner_slot,
):
    _, parts, rows, levels, width = adjoint_state.shape
    slots = owner_slot.shape[0]
    inner = rows - 2 * STEPS
    row_bytes = levels * width * 4
    f32 = lambda *shape: jax.ShapeDtypeStruct(shape, jnp.float32)
    vmem = pl.BlockSpec(memory_space=pltpu.VMEM)
    smem = pl.BlockSpec(memory_space=pltpu.SMEM)
    hbm = pl.BlockSpec(memory_space=pltpu.HBM)
    in_hbm = lambda value: pltpu.with_memory_space_constraint(value, pltpu.HBM)

    subs, hors = lax.axis_size("sub"), lax.axis_size("hor")
    small = [parent_cell, stencil_offset, stencil_weight]

    packing = dict(
        out_specs=vmem, compiler_params=PARAMS, cost_estimate=cost(12 * levels * width * 13, 28 * row_bytes)
    )
    first_pack = pl.pallas_call(
        functools.partial(pack_kernel, 0),
        in_specs=[hbm] * 6,
        out_shape=f32(PACK_ROWS + 1, levels, width),
        scratch_shapes=[
            pltpu.VMEM((parts, STEPS, levels, width), jnp.float32),
            pltpu.VMEM((STEPS, levels, width), jnp.float32),
            pltpu.VMEM((STEPS, levels, width), jnp.float32),
        ]
        + [pltpu.VMEM(value.shape, value.dtype) for value in small]
        + [pltpu.SemaphoreType.DMA((levels // HALF, parts + 2)), pltpu.SemaphoreType.DMA((3,))],
        name="pack_a",
        **packing,
    )(*[in_hbm(value) for value in [adjoint_state, courant_east, courant_north] + small])
    second_pack = pl.pallas_call(
        functools.partial(pack_kernel, 1),
        in_specs=[vmem] * 3,
        out_shape=f32(PACK_ROWS, levels, width),
        name="pack_b",
        **packing,
    )(adjoint_state, courant_east, courant_north)
    first_came = alternating(first_pack, -1)
    second_came = alternating(second_pack, 1)

    state, east, north = adjoint_state, courant_east, courant_north
    middle, ends, columns = pl.pallas_call(
        sweep_kernel,
        in_specs=[vmem] * 3,
        out_specs=[vmem] * 3,
        out_shape=[
            f32(parts, inner, levels, width),
            f32(parts, 2 * STEPS, levels, width),
            f32(parts, 2, rows, levels, LANES),
        ],
        scratch_shapes=[
            pltpu.VMEM((STEPS - 1, parts, rows, HALF, width), jnp.float32),
            pltpu.VMEM((rows, HALF, width), jnp.float32),
            pltpu.VMEM((rows, HALF, width), jnp.float32),
            pltpu.VMEM((rows, HALF, width), jnp.float32),
        ],
        compiler_params=PARAMS,
        cost_estimate=cost(8 * rows * levels * width * 13, 6 * rows * row_bytes),
        name="sweep",
    )(state, east, north)
    middle_came = along(middle, "sub", -1)

    mixing, base = pl.pallas_call(
        ghost_base_kernel,
        in_specs=[vmem] * 5,
        out_specs=[vmem] * 2,
        out_shape=[f32(parts, 2, rows, slots), f32(parts, levels, slots)],
        compiler_params=PARAMS,
        cost_estimate=cost(parts * rows * levels * slots * 8, 4 * rows * levels * LANES * 8),
        name="ghost_base",
    )(*small, columns, north)

    column_shape = (parts, 2, 2 * (STEPS - 1), levels, LANES)
    side_a, a_columns = pl.pallas_call(
        mend_a_kernel,
        in_specs=[vmem] * 6,
        out_specs=[vmem] * 2,
        out_shape=[f32(parts, STEPS, levels, width), f32(*column_shape)],
        compiler_params=PARAMS,
        cost_estimate=cost(16 * levels * width * 13, 54 * row_bytes),
        name="mend_a",
    )(east, north, second_pack, first_came, ends, base)
    a_came = along(side_a, "sub", -1)
    total = pl.pallas_call(
        ghost_kernel,
        in_specs=[vmem] * 5,
        out_specs=vmem,
        out_shape=f32(parts, levels, slots),
        scratch_shapes=[pltpu.VMEM((parts, 2, rows, slots), jnp.float32)],
        compiler_params=PARAMS,
        cost_estimate=cost(parts * levels * slots * 64, 8 * row_bytes),
        name="ghost",
    )(north, first_came, a_columns, mixing, base)
    side_b = pl.pallas_call(
        mend_b_kernel,
        in_specs=[vmem] * 5,
        out_specs=vmem,
        out_shape=f32(parts, STEPS, levels, width),
        compiler_params=PARAMS,
        cost_estimate=cost(16 * levels * width * 13, 46 * row_bytes),
        name="mend_b",
    )(east, north, first_pack, second_came, ends)
    b_came = along(side_b, "sub", -1)

    total = added_up(total)
    adjoint_result, boundary_gradient = pl.pallas_call(
        finish_kernel,
        in_specs=[vmem] * 6,
        out_specs=[hbm, vmem],
        out_shape=[f32(*adjoint_state.shape), f32(parts, levels // subs, slots // hors)],
        scratch_shapes=[
            pltpu.VMEM((parts, rows, levels, width), jnp.float32),
            pltpu.SemaphoreType.DMA((3 * parts,)),
        ],
        compiler_params=PARAMS,
        cost_estimate=cost(parts * rows * levels * width, 6 * rows * row_bytes),
        name="finish",
    )(total, owner_slot[None], state, middle_came, a_came, b_came)
    return (adjoint_result, boundary_gradient)


def solution(mesh):
    in_specs = (
        P(("ens", "sub"), None, "hor", None, None),
        P(("ens", "sub"), "hor", None, None),
        P(("ens", "sub"), "hor", None, None),
        P(None, None, "hor"),
        P(None, None, None, "hor"),
        P(None, None, None, "hor"),
        P(),
    )
    out_specs = (P(("ens", "sub"), None, "hor", None, None), P("ens", "sub", "hor"))
    return jax.shard_map(local, mesh=mesh, in_specs=in_specs, out_specs=out_specs, check_vma=False)
```

```python
import functools

import jax
import jax.numpy as jnp
from jax import lax
from jax.experimental import pallas as pl
from jax.experimental.pallas import tpu as pltpu
from jax.sharding import PartitionSpec as P

STEPS = 4
HALF = 8
FLUX_ROWS = 2 * STEPS
PACK_ROWS = FLUX_ROWS + 3
LANES = 128
EXTRA = PACK_ROWS
TARGETS = 4 * LANES
WEIGHTS = 5 * LANES


def along(value, axis, step_of):
    peers = lax.axis_size(axis)
    pairs = [(i, i + step_of) for i in range(peers) if 0 <= i + step_of < peers]
    return lax.ppermute(value, axis, pairs)


def alternating(value, sign):
    subs, hors = lax.axis_size("sub"), lax.axis_size("hor")
    pairs = []
    for s in range(subs):
        step = sign if s % 2 == 0 else -sign
        pairs += [(s * hors + h, s * hors + h + step) for h in range(hors) if 0 <= h + step < hors]
    return lax.ppermute(value, ("sub", "hor"), pairs)


def peers_along(axis, step, group):
    size = lax.axis_size(axis)
    return [[(i, i ^ (step * j)) for i in range(size)] for j in range(1, group)]


def rounds():
    subs, hors = lax.axis_size("sub"), lax.axis_size("hor")
    assert not subs & (subs - 1) and not hors & (hors - 1)
    order = []
    step = 2
    while step < subs:
        order.append(("sub", step, 2))
        step *= 2
    if subs > 1:
        order.append(("sub", 1, 2))
    step = 1
    while step < hors:
        group = min(4, hors // step)
        order.append(("hor", step, group))
        step *= group
    return order


def exchange(value, axis, step, group):
    return [lax.ppermute(value, axis, pairs) for pairs in peers_along(axis, step, group)]


def parity():
    return lax.rem(lax.axis_index("sub"), 2)


def sign_of(flip):
    return jnp.where(flip == 1, jnp.float32(-1.0), jnp.float32(1.0))


def north_rates(north_rate):
    width = north_rate.shape[-1]
    column = lax.broadcasted_iota(jnp.int32, north_rate.shape, len(north_rate.shape) - 1)
    plus = jnp.where(column == 0, 0.0, jnp.maximum(north_rate, 0.0))
    minus = jnp.where(column == width - 1, 0.0, jnp.maximum(-north_rate, 0.0))
    return plus, minus


def shifted(flux_plus, flux_minus):
    width = flux_plus.shape[-1]
    axis = len(flux_plus.shape) - 1
    return pltpu.roll(flux_plus, width - 1, axis) + pltpu.roll(flux_minus, 1, axis)


class Row:
    def __init__(self, east_rate, north_rate=None):
        self.outward = jnp.maximum(east_rate, 0.0)
        self.inward = jnp.maximum(-east_rate, 0.0)
        if north_rate is not None:
            self.centre = 1.0 - jnp.abs(east_rate) - jnp.abs(north_rate)
            self.plus, self.minus = north_rates(north_rate)

    def stay(self, value):
        return self.centre * value + shifted(self.plus * value, self.minus * value)


def level_halves(levels, body):
    def step(h, carry):
        body(pl.ds(pl.multiple_of(h * HALF, HALF), HALF))
        return carry

    lax.fori_loop(0, levels // HALF, step, 0)


def pack_kernel(
    state_hbm, east_hbm, north_hbm, cell_hbm, offset_hbm, weight_hbm,
    pack_ref, state_ref, east_ref, north_ref, cell_ref, offset_ref, weight_ref, sems, small_sems,
):
    parts, rows, levels, width = state_hbm.shape[1:]
    flip = parity()
    sign = sign_of(flip)
    at_end = pl.ds(flip * (rows - STEPS), STEPS)
    place = lambda r: r + flip * (STEPS - 1 - 2 * r)
    halves = levels // HALF
    copies = []
    for h in range(halves):
        at = pl.ds(h * HALF, HALF)
        sem = sems.at[h]
        batch = [
            pltpu.make_async_copy(state_hbm.at[0, c, at_end, at], state_ref.at[c, :, at], sem.at[c])
            for c in range(parts)
        ]
        batch.append(pltpu.make_async_copy(east_hbm.at[0, at_end, at], east_ref.at[:, at], sem.at[parts]))
        batch.append(pltpu.make_async_copy(north_hbm.at[0, at_end, at], north_ref.at[:, at], sem.at[parts + 1]))
        copies.append(batch)
        for copy in batch:
            copy.start()
    small = [
        pltpu.make_async_copy(source, target, small_sems.at[n])
        for n, (source, target) in enumerate(
            ((cell_hbm, cell_ref), (offset_hbm, offset_ref), (weight_hbm, weight_ref))
        )
    ]
    for copy in small:
        copy.start()

    def half(at):
        row = [Row(east_ref[place(r), at, :] * sign, north_ref[place(r), at, :]) for r in range(STEPS)]
        pack_ref[FLUX_ROWS, at, :] = east_ref[place(0), at, :]
        pack_ref[FLUX_ROWS + 1, at, :] = north_ref[place(0), at, :]
        pack_ref[FLUX_ROWS + 2, at, :] = east_ref[place(1), at, :]
        for r in (1, 2):
            lanes = (2 * r - 2) * LANES
            pack_ref[EXTRA, at, lanes:lanes + LANES] = north_ref[place(r), at, :LANES]
            pack_ref[EXTRA, at, lanes + LANES:lanes + 2 * LANES] = north_ref[place(r), at, width - LANES:]
        for c in range(parts):
            field = [state_ref[c, place(r), at, :] for r in range(STEPS)]
            for k in range(STEPS):
                pack_ref[2 * k + c, at, :] = row[0].outward * field[0]
                after = []
                for r in range(STEPS - 1 - k):
                    value = row[r].stay(field[r]) + row[r + 1].outward * field[r + 1]
                    if r > 0:
                        value = value + row[r - 1].inward * field[r - 1]
                    after.append(value)
                field = after

    for h in range(halves):
        for copy in copies[h]:
            copy.wait()
        half(pl.ds(h * HALF, HALF))

    for copy in small:
        copy.wait()
    n = 0
    for point in range(offset_ref.shape[0]):
        for c in range(parts):
            target = (cell_ref[c] + offset_ref[point, c]).astype(jnp.float32)
            pack_ref[EXTRA, n:n + 2, TARGETS:TARGETS + rows] = target
            pack_ref[EXTRA, n:n + 2, WEIGHTS:WEIGHTS + rows] = weight_ref[point, c]
            n += 2


def as_column(row):
    count = row.shape[1]
    here = lax.broadcasted_iota(jnp.int32, (count, count), 0)
    there = lax.broadcasted_iota(jnp.int32, (count, count), 1)
    return jnp.sum(jnp.where(here == there, row, 0), axis=1, keepdims=True)


def sweep_kernel(
    state_ref, east_ref, north_ref, pack_ref, middle_ref, ends_ref, column_ref,
    field, plus_ref, minus_ref, centre_ref,
):
    parts, rows, levels, width = state_ref.shape[1:]
    flip = 1 - parity()
    sign = sign_of(flip)
    end_row = flip * (rows - 1)
    next_row = end_row + 1 - 2 * flip

    def half(at):
        pack_ref[FLUX_ROWS, at, :] = east_ref[0, end_row, at, :]
        pack_ref[FLUX_ROWS + 1, at, :] = north_ref[0, end_row, at, :]
        pack_ref[FLUX_ROWS + 2, at, :] = east_ref[0, next_row, at, :]

        for k in range(STEPS):
            if k == 0:
                read = lambda c, i: state_ref[0, c, i, at, :]
            else:
                read = lambda c, i, slot=k - 1: field[slot, c, i]
            leaving = jnp.maximum(east_ref[0, end_row, at, :] * sign, 0.0)
            for c in range(parts):
                pack_ref[2 * k + c, at, :] = leaving * read(c, end_row)
            west = [None] * parts
            here = [read(c, 0) for c in range(parts)]
            east_here = east_ref[0, 0, at, :]
            for i in range(rows):
                leave_west = jnp.maximum(-east_here, 0.0)
                if k == 0:
                    north_rate = north_ref[0, i, at, :]
                    centre = 1.0 - jnp.abs(east_here) - jnp.abs(north_rate)
                    plus, minus = north_rates(north_rate)
                    centre_ref[i], plus_ref[i], minus_ref[i] = centre, plus, minus
                else:
                    centre, plus, minus = centre_ref[i], plus_ref[i], minus_ref[i]
                if i + 1 < rows:
                    east_here = east_ref[0, i + 1, at, :]
                    east_after = jnp.maximum(east_here, 0.0)
                for c in range(parts):
                    value = here[c]
                    total = centre * value + shifted(plus * value, minus * value)
                    if i > 0:
                        total = total + west[c]
                    if i + 1 < rows:
                        west[c] = leave_west * value
                        here[c] = read(c, i + 1)
                        total = total + east_after * here[c]
                    if k < STEPS - 1:
                        field[k, c, i] = total
                    elif i < STEPS:
                        ends_ref[c, i, at, :] = total
                    elif i >= rows - STEPS:
                        ends_ref[c, i - rows + 2 * STEPS, at, :] = total
                    else:
                        middle_ref[c, i - STEPS, at, :] = total

        def columns(i, carry):
            for c in range(parts):
                value = state_ref[0, c, i, at, :]
                first, last = value[:, :LANES], value[:, width - LANES:]
                for slot in range(STEPS - 1):
                    first = first + field[slot, c, i, :, :LANES]
                    last = last + field[slot, c, i, :, width - LANES:]
                column_ref[c, 0, i, at, :] = first
                column_ref[c, 1, i, at, :] = last
            return carry

        lax.fori_loop(0, rows, columns, 0, unroll=2)

    level_halves(levels, half)


def mix(targets, weights, cells, total):
    for target, weight in zip(targets, weights):
        total = total + jnp.where(as_column(target) == cells, as_column(weight), 0.0)
    return total


def ghost_base_kernel(
    cell_ref, offset_ref, weight_ref, column_ref, north_ref, mixing_ref, partial_ref
):
    parts, _, rows, levels, _ = column_ref.shape
    slots = mixing_ref.shape[-1]
    width = north_ref.shape[-1]
    points = range(offset_ref.shape[0])
    cells = lax.broadcasted_iota(jnp.int32, (rows, slots), 1)
    for c in range(parts):
        for s in range(2):
            mixing_ref[c, s] = mix(
                [cell_ref[c, s:s + 1, :] + offset_ref[point, c, s:s + 1, :] for point in points],
                [weight_ref[point, c, s:s + 1, :] for point in points],
                cells, jnp.zeros((rows, slots), jnp.float32),
            )

    for c in range(parts):
        total = jnp.zeros((levels, slots), jnp.float32)
        for i in range(rows):
            south = jnp.maximum(north_ref[0, i, :, :1], 0.0) * column_ref[c, 0, i, :, :1]
            north = jnp.maximum(-north_ref[0, i, :, width - 1:], 0.0) * column_ref[c, 1, i, :, LANES - 1:]
            total = total + south * mixing_ref[c, 0, i:i + 1, :]
            total = total + north * mixing_ref[c, 1, i:i + 1, :]
        partial_ref[c] = total


def ghost_kernel(north_ref, other_ref, column_ref, mixing_ref, partial_ref, sum_ref, near_mixing):
    parts, levels, slots = partial_ref.shape
    rows = mixing_ref.shape[2]
    width = north_ref.shape[-1]
    flip = 1 - parity()
    cells = lax.broadcasted_iota(jnp.int32, (rows, slots), 1).astype(jnp.float32)
    points = (WEIGHTS - TARGETS) // LANES * 4
    for c in range(parts):
        for s in range(2):
            at = [(point * parts + c) * 2 + s for point in range(points)]
            near_mixing[c, s] = mix(
                [other_ref[EXTRA, n:n + 1, TARGETS:TARGETS + rows] for n in at],
                [other_ref[EXTRA, n:n + 1, WEIGHTS:WEIGHTS + rows] for n in at],
                cells, jnp.zeros((rows, slots), jnp.float32),
            )
    for c in range(parts):
        total = partial_ref[c]
        for r in range(STEPS - 1):
            i = r + flip * (rows - 1 - 2 * r)
            south = jnp.maximum(north_ref[0, i, :, :1], 0.0) * column_ref[c, 0, r, :, :1]
            north = jnp.maximum(-north_ref[0, i, :, width - 1:], 0.0) * column_ref[c, 1, r, :, LANES - 1:]
            total = total + south * mixing_ref[c, 0, pl.ds(i, 1), :]
            total = total + north * mixing_ref[c, 1, pl.ds(i, 1), :]
            i = r + (1 - flip) * (rows - 1 - 2 * r)
            if r == 0:
                first_rate = other_ref[FLUX_ROWS + 1, :, :LANES]
                last_rate = other_ref[FLUX_ROWS + 1, :, width - LANES:]
            else:
                lanes = (2 * r - 2) * LANES
                first_rate = other_ref[EXTRA, :, lanes:lanes + LANES]
                last_rate = other_ref[EXTRA, :, lanes + LANES:lanes + 2 * LANES]
            south = jnp.maximum(first_rate[:, :1], 0.0) * column_ref[c, 0, STEPS - 1 + r, :, :1]
            north = jnp.maximum(-last_rate[:, LANES - 1:], 0.0) * column_ref[c, 1, STEPS - 1 + r, :, LANES - 1:]
            total = total + south * near_mixing[c, 0, pl.ds(i, 1), :]
            total = total + north * near_mixing[c, 1, pl.ds(i, 1), :]
        sum_ref[c] = total


def mend_side(flip, east_ref, north_ref, mine_ref, other_ref, store, store_column):
    levels, width = mine_ref.shape[1:]
    rows = east_ref.shape[1]
    sign = sign_of(flip)
    place = lambda r: flip * (rows - STEPS) + r + flip * (STEPS - 1 - 2 * r)

    def half(at):
        own = [Row(east_ref[0, place(r), at, :] * sign, north_ref[0, place(r), at, :]) for r in range(STEPS - 1)]
        near = Row(other_ref[FLUX_ROWS, at, :] * sign, other_ref[FLUX_ROWS + 1, at, :])
        far = Row(other_ref[FLUX_ROWS + 2, at, :] * sign)
        for c in range(FLUX_ROWS // STEPS):
            mine = lambda k: mine_ref[2 * k + c, at, :]
            theirs = lambda k: other_ref[2 * k + c, at, :]
            a0 = theirs(0)
            n1 = mine(0)
            b0 = own[0].stay(a0) + near.inward * n1 + theirs(1)
            b1 = own[0].inward * a0
            bn1 = near.stay(n1) + own[0].outward * a0 + mine(1)
            bn2 = near.outward * n1
            c0 = own[0].stay(b0) + near.inward * bn1 + own[1].outward * b1 + theirs(2)
            c1 = own[1].stay(b1) + own[0].inward * b0
            c2 = own[1].inward * b1
            cn1 = near.stay(bn1) + own[0].outward * b0 + far.inward * bn2 + mine(2)
            d0 = own[0].stay(c0) + near.inward * cn1 + own[1].outward * c1 + theirs(3)
            d1 = own[1].stay(c1) + own[0].inward * c0 + own[2].outward * c2
            d2 = own[2].stay(c2) + own[1].inward * c1
            d3 = own[2].inward * c2
            for r, value in enumerate((d0, d1, d2, d3)):
                store(c, r, at, value)
            if store_column is not None:
                tiles = (slice(0, LANES), slice(width - LANES, width))
                for s, lanes in enumerate(tiles):
                    tile = lambda value: value[:, lanes]
                    rate = other_ref[EXTRA, at, s * LANES:(s + 1) * LANES]
                    stays = 1.0 - jnp.abs(other_ref[FLUX_ROWS + 2, at, lanes]) - jnp.abs(rate)
                    drift = jnp.maximum(rate if s == 0 else -rate, 0.0) * tile(bn2)
                    cn2 = stays * tile(bn2) + pltpu.roll(drift, LANES - 1 if s == 0 else 1, 1)
                    cn2 = cn2 + tile(near.outward) * tile(bn1)
                    cn3 = tile(far.outward) * tile(bn2)
                    sums = (
                        tile(a0) + tile(b0) + tile(c0), tile(b1) + tile(c1), tile(c2),
                        tile(n1) + tile(bn1) + tile(cn1), tile(bn2) + cn2, cn3,
                    )
                    for r, value in enumerate(sums):
                        store_column(c, s, r, at, value)

    level_halves(levels, half)


def mend_a_kernel(east_ref, north_ref, mine_ref, other_ref, ends_ref, base_ref, out_ref, column_ref):
    flip = 1 - parity()
    turn = lambda r: r + flip * (STEPS - 1 - 2 * r)

    def store(c, r, at, value):
        out_ref[c, turn(r), at, :] = ends_ref[c, flip * STEPS + turn(r), at, :] + value

    def store_column(c, s, r, at, value):
        column_ref[c, s, r, at, :] = value

    mend_side(flip, east_ref, north_ref, mine_ref, other_ref, store, store_column)


def mend_b_kernel(*refs):
    east_ref, north_ref, mine_ref, other_ref, ends_ref, _ = refs[:6]
    out_ref, sum_ref = refs[-2:]
    flip = parity()
    turn = lambda r: r + flip * (STEPS - 1 - 2 * r)

    def store(c, r, at, value):
        out_ref[c, turn(r), at, :] = ends_ref[c, flip * STEPS + turn(r), at, :] + value

    mend_side(flip, east_ref, north_ref, mine_ref, other_ref, store, None)
    sum_ref[...] = sum((ref[...] for ref in refs[7:-2]), refs[6][...])


def finish_kernel(
    total_ref, owner_ref, state_ref, middle_ref, a_ref, b_ref, out_hbm, gradient_ref, buffer, sems
):
    parts, rows = state_ref.shape[1:3]
    inner = rows - 2 * STEPS
    a_start = parity() * (rows - STEPS)
    b_start = (1 - parity()) * (rows - STEPS)
    share, mine = gradient_ref.shape[1:]
    start = lax.axis_index("hor") * mine
    chosen = []
    for c in range(parts):
        block = total_ref[c, :share, :]
        for s in range(1, total_ref.shape[1] // share):
            block = jnp.where(lax.axis_index("sub") == s, total_ref[c, s * share:(s + 1) * share, :], block)
        chosen.append(block)
    chosen = jnp.concatenate(chosen, 0)
    column = lax.broadcasted_iota(jnp.int32, (parts * share, mine), 1)
    picked = jnp.zeros((parts * share, mine), jnp.float32)
    for q in range(mine):
        value = jnp.sum(jnp.where(owner_ref[...] == start + q, chosen, 0.0), axis=1, keepdims=True)
        picked = jnp.where(column == q, value, picked)
    for c in range(parts):
        gradient_ref[c] = picked[c * share:(c + 1) * share]

    copies = []
    for start, other in ((STEPS, middle_ref), (a_start, a_ref), (b_start, b_ref)):
        for c in range(parts):
            count = other.shape[1]
            for r in range(count):
                buffer[c, start + r] = state_ref[0, c, start + r] - other[c, r]
            at = pl.ds(start, count)
            copy = pltpu.make_async_copy(buffer.at[c, at], out_hbm.at[0, c, at], sems.at[len(copies)])
            copy.start()
            copies.append(copy)

    for copy in copies:
        copy.wait()


BRIEF = pl.CostEstimate(flops=1, bytes_accessed=1, transcendentals=0)
PARAMS = pltpu.CompilerParams(vmem_limit_bytes=24 * 1024 * 1024)


def local(
    adjoint_state,
    courant_east,
    courant_north,
    parent_cell,
    stencil_offset,
    stencil_weight,
    owner_slot,
):
    _, parts, rows, levels, width = adjoint_state.shape
    slots = owner_slot.shape[0]
    inner = rows - 2 * STEPS
    row_bytes = levels * width * 4
    f32 = lambda *shape: jax.ShapeDtypeStruct(shape, jnp.float32)
    vmem = pl.BlockSpec(memory_space=pltpu.VMEM)
    smem = pl.BlockSpec(memory_space=pltpu.SMEM)
    hbm = pl.BlockSpec(memory_space=pltpu.HBM)
    in_hbm = lambda value: pltpu.with_memory_space_constraint(value, pltpu.HBM)

    subs, hors = lax.axis_size("sub"), lax.axis_size("hor")
    small = [parent_cell, stencil_offset, stencil_weight]

    first_pack = pl.pallas_call(
        pack_kernel,
        in_specs=[hbm] * 6,
        out_specs=vmem,
        out_shape=f32(PACK_ROWS + 1, levels, width),
        scratch_shapes=[
            pltpu.VMEM((parts, STEPS, levels, width), jnp.float32),
            pltpu.VMEM((STEPS, levels, width), jnp.float32),
            pltpu.VMEM((STEPS, levels, width), jnp.float32),
        ]
        + [pltpu.VMEM(value.shape, value.dtype) for value in small]
        + [pltpu.SemaphoreType.DMA((levels // HALF, parts + 2)), pltpu.SemaphoreType.DMA((3,))],
        compiler_params=PARAMS,
        cost_estimate=BRIEF,
        name="pack",
    )(*[in_hbm(value) for value in [adjoint_state, courant_east, courant_north] + small])
    first_came = alternating(first_pack, -1)

    state, east, north = adjoint_state, courant_east, courant_north
    second_pack, middle, ends, columns = pl.pallas_call(
        sweep_kernel,
        in_specs=[vmem] * 3,
        out_specs=[vmem] * 4,
        out_shape=[
            f32(PACK_ROWS, levels, width),
            f32(parts, inner, levels, width),
            f32(parts, 2 * STEPS, levels, width),
            f32(parts, 2, rows, levels, LANES),
        ],
        scratch_shapes=[
            pltpu.VMEM((STEPS - 1, parts, rows, HALF, width), jnp.float32),
            pltpu.VMEM((rows, HALF, width), jnp.float32),
            pltpu.VMEM((rows, HALF, width), jnp.float32),
            pltpu.VMEM((rows, HALF, width), jnp.float32),
        ],
        compiler_params=PARAMS,
        cost_estimate=BRIEF,
        name="sweep",
    )(state, east, north)
    second_came = alternating(second_pack, 1)
    middle_came = along(middle, "sub", -1)

    mixing, base = pl.pallas_call(
        ghost_base_kernel,
        in_specs=[vmem] * 5,
        out_specs=[vmem] * 2,
        out_shape=[f32(parts, 2, rows, slots), f32(parts, levels, slots)],
        compiler_params=PARAMS,
        cost_estimate=BRIEF,
        name="ghost_base",
    )(*small, columns, north)

    column_shape = (parts, 2, 2 * (STEPS - 1), levels, LANES)
    side_a, a_columns = pl.pallas_call(
        mend_a_kernel,
        in_specs=[vmem] * 6,
        out_specs=[vmem] * 2,
        out_shape=[f32(parts, STEPS, levels, width), f32(*column_shape)],
        compiler_params=PARAMS,
        cost_estimate=BRIEF,
        name="mend_a",
    )(east, north, second_pack, first_came, ends, base)
    a_came = along(side_a, "sub", -1)
    total = pl.pallas_call(
        ghost_kernel,
        in_specs=[vmem] * 5,
        out_specs=vmem,
        out_shape=f32(parts, levels, slots),
        scratch_shapes=[pltpu.VMEM((parts, 2, rows, slots), jnp.float32)],
        compiler_params=PARAMS,
        cost_estimate=BRIEF,
        name="ghost",
    )(north, first_came, a_columns, mixing, base)
    order = rounds()
    came = exchange(total, *order[0])
    side_b, total = pl.pallas_call(
        mend_b_kernel,
        in_specs=[vmem] * 5 + [pl.BlockSpec(memory_space=pl.ANY)] + [vmem] * (1 + len(came)),
        out_specs=[vmem] * 2,
        out_shape=[f32(parts, STEPS, levels, width), f32(parts, levels, slots)],
        compiler_params=PARAMS,
        cost_estimate=BRIEF,
        name="mend_b",
    )(east, north, first_pack, second_came, ends, middle_came, total, *came)
    b_came = along(side_b, "sub", -1)

    for each in order[1:]:
        total = sum(exchange(total, *each), total)
    adjoint_result, boundary_gradient = pl.pallas_call(
        finish_kernel,
        in_specs=[vmem] * 6,
        out_specs=[hbm, vmem],
        out_shape=[f32(*adjoint_state.shape), f32(parts, levels // subs, slots // hors)],
        scratch_shapes=[
            pltpu.VMEM((parts, rows, levels, width), jnp.float32),
            pltpu.SemaphoreType.DMA((3 * parts,)),
        ],
        compiler_params=PARAMS,
        cost_estimate=BRIEF,
        name="finish",
    )(total, owner_slot[None], state, middle_came, a_came, b_came)
    return (adjoint_result, boundary_gradient)


def solution(mesh):
    in_specs = (
        P(("ens", "sub"), None, "hor", None, None),
        P(("ens", "sub"), "hor", None, None),
        P(("ens", "sub"), "hor", None, None),
        P(None, None, "hor"),
        P(None, None, None, "hor"),
        P(None, None, None, "hor"),
        P(),
    )
    out_specs = (P(("ens", "sub"), None, "hor", None, None), P("ens", "sub", "hor"))
    return jax.shard_map(local, mesh=mesh, in_specs=in_specs, out_specs=out_specs, check_vma=False)
```

```python
import functools

import jax
import jax.numpy as jnp
from jax import lax
from jax.experimental import pallas as pl
from jax.experimental.pallas import tpu as pltpu
from jax.sharding import PartitionSpec as P

STEPS = 4
HALF = 8
FLUX_ROWS = 2 * STEPS
PACK_ROWS = FLUX_ROWS + 3
LANES = 128
EXTRA = PACK_ROWS
TARGETS = 4 * LANES
WEIGHTS = 5 * LANES


def along(value, axis, step_of):
    peers = lax.axis_size(axis)
    pairs = [(i, i + step_of) for i in range(peers) if 0 <= i + step_of < peers]
    return lax.ppermute(value, axis, pairs)


def alternating(value, sign):
    subs, hors = lax.axis_size("sub"), lax.axis_size("hor")
    pairs = []
    for s in range(subs):
        step = sign if s % 2 == 0 else -sign
        pairs += [(s * hors + h, s * hors + h + step) for h in range(hors) if 0 <= h + step < hors]
    return lax.ppermute(value, ("sub", "hor"), pairs)


def rounds():
    subs, hors = lax.axis_size("sub"), lax.axis_size("hor")
    assert not subs & (subs - 1) and not hors & (hors - 1)
    order = [("sub", 1 << n) for n in reversed(range(subs.bit_length() - 1))]
    return order + [("hor", 1 << n) for n in range(hors.bit_length() - 1)]


def exchanged(value, axis, distance):
    return lax.ppermute(value, axis, [(i, i ^ distance) for i in range(lax.axis_size(axis))])


def parity():
    return lax.rem(lax.axis_index("sub"), 2)


def sign_of(flip):
    return jnp.where(flip == 1, jnp.float32(-1.0), jnp.float32(1.0))


def north_rates(north_rate):
    width = north_rate.shape[-1]
    column = lax.broadcasted_iota(jnp.int32, north_rate.shape, len(north_rate.shape) - 1)
    plus = jnp.where(column == 0, 0.0, jnp.maximum(north_rate, 0.0))
    minus = jnp.where(column == width - 1, 0.0, jnp.maximum(-north_rate, 0.0))
    return plus, minus


def shifted(flux_plus, flux_minus):
    width = flux_plus.shape[-1]
    axis = len(flux_plus.shape) - 1
    return pltpu.roll(flux_plus, width - 1, axis) + pltpu.roll(flux_minus, 1, axis)


class Row:
    def __init__(self, east_rate, north_rate=None):
        self.outward = jnp.maximum(east_rate, 0.0)
        self.inward = jnp.maximum(-east_rate, 0.0)
        if north_rate is not None:
            self.centre = 1.0 - jnp.abs(east_rate) - jnp.abs(north_rate)
            self.plus, self.minus = north_rates(north_rate)

    def stay(self, value):
        return self.centre * value + shifted(self.plus * value, self.minus * value)


def level_halves(levels, body):
    def step(h, carry):
        body(pl.ds(pl.multiple_of(h * HALF, HALF), HALF))
        return carry

    lax.fori_loop(0, levels // HALF, step, 0)


def pack_kernel(
    state_hbm, east_hbm, north_hbm, cell_hbm, offset_hbm, weight_hbm,
    pack_ref, state_ref, east_ref, north_ref, cell_ref, offset_ref, weight_ref, sems, small_sems,
):
    parts, rows, levels, width = state_hbm.shape[1:]
    flip = parity()
    sign = sign_of(flip)
    at_end = pl.ds(flip * (rows - STEPS), STEPS)
    place = lambda r: r + flip * (STEPS - 1 - 2 * r)
    halves = levels // HALF
    copies = []
    for h in range(halves):
        at = pl.ds(h * HALF, HALF)
        sem = sems.at[h]
        batch = [
            pltpu.make_async_copy(state_hbm.at[0, c, at_end, at], state_ref.at[c, :, at], sem.at[c])
            for c in range(parts)
        ]
        batch.append(pltpu.make_async_copy(east_hbm.at[0, at_end, at], east_ref.at[:, at], sem.at[parts]))
        batch.append(pltpu.make_async_copy(north_hbm.at[0, at_end, at], north_ref.at[:, at], sem.at[parts + 1]))
        copies.append(batch)
        for copy in batch:
            copy.start()
    small = [
        pltpu.make_async_copy(source, target, small_sems.at[n])
        for n, (source, target) in enumerate(
            ((cell_hbm, cell_ref), (offset_hbm, offset_ref), (weight_hbm, weight_ref))
        )
    ]
    for copy in small:
        copy.start()

    def half(at):
        row = [Row(east_ref[place(r), at, :] * sign, north_ref[place(r), at, :]) for r in range(STEPS)]
        pack_ref[FLUX_ROWS, at, :] = east_ref[place(0), at, :]
        pack_ref[FLUX_ROWS + 1, at, :] = north_ref[place(0), at, :]
        pack_ref[FLUX_ROWS + 2, at, :] = east_ref[place(1), at, :]
        for r in (1, 2):
            lanes = (2 * r - 2) * LANES
            pack_ref[EXTRA, at, lanes:lanes + LANES] = north_ref[place(r), at, :LANES]
            pack_ref[EXTRA, at, lanes + LANES:lanes + 2 * LANES] = north_ref[place(r), at, width - LANES:]
        for c in range(parts):
            field = [state_ref[c, place(r), at, :] for r in range(STEPS)]
            for k in range(STEPS):
                pack_ref[2 * k + c, at, :] = row[0].outward * field[0]
                after = []
                for r in range(STEPS - 1 - k):
                    value = row[r].stay(field[r]) + row[r + 1].outward * field[r + 1]
                    if r > 0:
                        value = value + row[r - 1].inward * field[r - 1]
                    after.append(value)
                field = after

    for h in range(halves):
        for copy in copies[h]:
            copy.wait()
        half(pl.ds(h * HALF, HALF))

    for copy in small:
        copy.wait()
    n = 0
    for point in range(offset_ref.shape[0]):
        for c in range(parts):
            target = (cell_ref[c] + offset_ref[point, c]).astype(jnp.float32)
            pack_ref[EXTRA, n:n + 2, TARGETS:TARGETS + rows] = target
            pack_ref[EXTRA, n:n + 2, WEIGHTS:WEIGHTS + rows] = weight_ref[point, c]
            n += 2


def as_column(row):
    count = row.shape[1]
    here = lax.broadcasted_iota(jnp.int32, (count, count), 0)
    there = lax.broadcasted_iota(jnp.int32, (count, count), 1)
    return jnp.sum(jnp.where(here == there, row, 0), axis=1, keepdims=True)


def sweep_kernel(
    state_ref, east_ref, north_ref, pack_ref, middle_ref, ends_ref, column_ref,
    field, plus_ref, minus_ref, centre_ref,
):
    parts, rows, levels, width = state_ref.shape[1:]
    flip = 1 - parity()
    sign = sign_of(flip)
    end_row = flip * (rows - 1)
    next_row = end_row + 1 - 2 * flip

    def half(at):
        pack_ref[FLUX_ROWS, at, :] = east_ref[0, end_row, at, :]
        pack_ref[FLUX_ROWS + 1, at, :] = north_ref[0, end_row, at, :]
        pack_ref[FLUX_ROWS + 2, at, :] = east_ref[0, next_row, at, :]

        for k in range(STEPS):
            if k == 0:
                read = lambda c, i: state_ref[0, c, i, at, :]
            else:
                read = lambda c, i, slot=k - 1: field[slot, c, i]
            leaving = jnp.maximum(east_ref[0, end_row, at, :] * sign, 0.0)
            for c in range(parts):
                pack_ref[2 * k + c, at, :] = leaving * read(c, end_row)
            west = [None] * parts
            here = [read(c, 0) for c in range(parts)]
            east_here = east_ref[0, 0, at, :]
            for i in range(rows):
                leave_west = jnp.maximum(-east_here, 0.0)
                if k == 0:
                    north_rate = north_ref[0, i, at, :]
                    centre = 1.0 - jnp.abs(east_here) - jnp.abs(north_rate)
                    plus, minus = north_rates(north_rate)
                    centre_ref[i], plus_ref[i], minus_ref[i] = centre, plus, minus
                else:
                    centre, plus, minus = centre_ref[i], plus_ref[i], minus_ref[i]
                if i + 1 < rows:
                    east_here = east_ref[0, i + 1, at, :]
                    east_after = jnp.maximum(east_here, 0.0)
                for c in range(parts):
                    value = here[c]
                    total = centre * value + shifted(plus * value, minus * value)
                    if i > 0:
                        total = total + west[c]
                    if i + 1 < rows:
                        west[c] = leave_west * value
                        here[c] = read(c, i + 1)
                        total = total + east_after * here[c]
                    if k < STEPS - 1:
                        field[k, c, i] = total
                    elif i < STEPS:
                        ends_ref[c, i, at, :] = total
                    elif i >= rows - STEPS:
                        ends_ref[c, i - rows + 2 * STEPS, at, :] = total
                    else:
                        middle_ref[c, i - STEPS, at, :] = total

        def columns(i, carry):
            for c in range(parts):
                value = state_ref[0, c, i, at, :]
                first, last = value[:, :LANES], value[:, width - LANES:]
                for slot in range(STEPS - 1):
                    first = first + field[slot, c, i, :, :LANES]
                    last = last + field[slot, c, i, :, width - LANES:]
                column_ref[c, 0, i, at, :] = first
                column_ref[c, 1, i, at, :] = last
            return carry

        lax.fori_loop(0, rows, columns, 0, unroll=2)

    level_halves(levels, half)


def mix(targets, weights, cells, total):
    for target, weight in zip(targets, weights):
        total = total + jnp.where(as_column(target) == cells, as_column(weight), 0.0)
    return total


def ghost_base_kernel(
    cell_ref, offset_ref, weight_ref, column_ref, north_ref, mixing_ref, partial_ref
):
    parts, _, rows, levels, _ = column_ref.shape
    slots = mixing_ref.shape[-1]
    width = north_ref.shape[-1]
    points = range(offset_ref.shape[0])
    cells = lax.broadcasted_iota(jnp.int32, (rows, slots), 1)
    for c in range(parts):
        for s in range(2):
            mixing_ref[c, s] = mix(
                [cell_ref[c, s:s + 1, :] + offset_ref[point, c, s:s + 1, :] for point in points],
                [weight_ref[point, c, s:s + 1, :] for point in points],
                cells, jnp.zeros((rows, slots), jnp.float32),
            )

    for c in range(parts):
        total = jnp.zeros((levels, slots), jnp.float32)
        for i in range(rows):
            south = jnp.maximum(north_ref[0, i, :, :1], 0.0) * column_ref[c, 0, i, :, :1]
            north = jnp.maximum(-north_ref[0, i, :, width - 1:], 0.0) * column_ref[c, 1, i, :, LANES - 1:]
            total = total + south * mixing_ref[c, 0, i:i + 1, :]
            total = total + north * mixing_ref[c, 1, i:i + 1, :]
        partial_ref[c] = total


def ghost_kernel(north_ref, other_ref, column_ref, mixing_ref, partial_ref, sum_ref, near_mixing):
    parts, levels, slots = partial_ref.shape
    rows = mixing_ref.shape[2]
    width = north_ref.shape[-1]
    flip = 1 - parity()
    cells = lax.broadcasted_iota(jnp.int32, (rows, slots), 1).astype(jnp.float32)
    points = (WEIGHTS - TARGETS) // LANES * 4
    for c in range(parts):
        for s in range(2):
            at = [(point * parts + c) * 2 + s for point in range(points)]
            near_mixing[c, s] = mix(
                [other_ref[EXTRA, n:n + 1, TARGETS:TARGETS + rows] for n in at],
                [other_ref[EXTRA, n:n + 1, WEIGHTS:WEIGHTS + rows] for n in at],
                cells, jnp.zeros((rows, slots), jnp.float32),
            )
    for c in range(parts):
        total = partial_ref[c]
        for r in range(STEPS - 1):
            i = r + flip * (rows - 1 - 2 * r)
            south = jnp.maximum(north_ref[0, i, :, :1], 0.0) * column_ref[c, 0, r, :, :1]
            north = jnp.maximum(-north_ref[0, i, :, width - 1:], 0.0) * column_ref[c, 1, r, :, LANES - 1:]
            total = total + south * mixing_ref[c, 0, pl.ds(i, 1), :]
            total = total + north * mixing_ref[c, 1, pl.ds(i, 1), :]
            i = r + (1 - flip) * (rows - 1 - 2 * r)
            if r == 0:
                first_rate = other_ref[FLUX_ROWS + 1, :, :LANES]
                last_rate = other_ref[FLUX_ROWS + 1, :, width - LANES:]
            else:
                lanes = (2 * r - 2) * LANES
                first_rate = other_ref[EXTRA, :, lanes:lanes + LANES]
                last_rate = other_ref[EXTRA, :, lanes + LANES:lanes + 2 * LANES]
            south = jnp.maximum(first_rate[:, :1], 0.0) * column_ref[c, 0, STEPS - 1 + r, :, :1]
            north = jnp.maximum(-last_rate[:, LANES - 1:], 0.0) * column_ref[c, 1, STEPS - 1 + r, :, LANES - 1:]
            total = total + south * near_mixing[c, 0, pl.ds(i, 1), :]
            total = total + north * near_mixing[c, 1, pl.ds(i, 1), :]
        sum_ref[c] = total


def mend_side(flip, east_ref, north_ref, mine_ref, other_ref, store, store_column):
    levels, width = mine_ref.shape[1:]
    rows = east_ref.shape[1]
    sign = sign_of(flip)
    place = lambda r: flip * (rows - STEPS) + r + flip * (STEPS - 1 - 2 * r)

    def half(at):
        own = [Row(east_ref[0, place(r), at, :] * sign, north_ref[0, place(r), at, :]) for r in range(STEPS - 1)]
        near = Row(other_ref[FLUX_ROWS, at, :] * sign, other_ref[FLUX_ROWS + 1, at, :])
        far = Row(other_ref[FLUX_ROWS + 2, at, :] * sign)
        for c in range(FLUX_ROWS // STEPS):
            mine = lambda k: mine_ref[2 * k + c, at, :]
            theirs = lambda k: other_ref[2 * k + c, at, :]
            a0 = theirs(0)
            n1 = mine(0)
            b0 = own[0].stay(a0) + near.inward * n1 + theirs(1)
            b1 = own[0].inward * a0
            bn1 = near.stay(n1) + own[0].outward * a0 + mine(1)
            bn2 = near.outward * n1
            c0 = own[0].stay(b0) + near.inward * bn1 + own[1].outward * b1 + theirs(2)
            c1 = own[1].stay(b1) + own[0].inward * b0
            c2 = own[1].inward * b1
            cn1 = near.stay(bn1) + own[0].outward * b0 + far.inward * bn2 + mine(2)
            d0 = own[0].stay(c0) + near.inward * cn1 + own[1].outward * c1 + theirs(3)
            d1 = own[1].stay(c1) + own[0].inward * c0 + own[2].outward * c2
            d2 = own[2].stay(c2) + own[1].inward * c1
            d3 = own[2].inward * c2
            for r, value in enumerate((d0, d1, d2, d3)):
                store(c, r, at, value)
            if store_column is not None:
                tiles = (slice(0, LANES), slice(width - LANES, width))
                for s, lanes in enumerate(tiles):
                    tile = lambda value: value[:, lanes]
                    rate = other_ref[EXTRA, at, s * LANES:(s + 1) * LANES]
                    stays = 1.0 - jnp.abs(other_ref[FLUX_ROWS + 2, at, lanes]) - jnp.abs(rate)
                    drift = jnp.maximum(rate if s == 0 else -rate, 0.0) * tile(bn2)
                    cn2 = stays * tile(bn2) + pltpu.roll(drift, LANES - 1 if s == 0 else 1, 1)
                    cn2 = cn2 + tile(near.outward) * tile(bn1)
                    cn3 = tile(far.outward) * tile(bn2)
                    sums = (
                        tile(a0) + tile(b0) + tile(c0), tile(b1) + tile(c1), tile(c2),
                        tile(n1) + tile(bn1) + tile(cn1), tile(bn2) + cn2, cn3,
                    )
                    for r, value in enumerate(sums):
                        store_column(c, s, r, at, value)

    level_halves(levels, half)


def mend_a_kernel(east_ref, north_ref, mine_ref, other_ref, ends_ref, base_ref, out_ref, column_ref):
    flip = 1 - parity()
    turn = lambda r: r + flip * (STEPS - 1 - 2 * r)

    def store(c, r, at, value):
        out_ref[c, turn(r), at, :] = ends_ref[c, flip * STEPS + turn(r), at, :] + value

    def store_column(c, s, r, at, value):
        column_ref[c, s, r, at, :] = value

    mend_side(flip, east_ref, north_ref, mine_ref, other_ref, store, store_column)


def mend_b_kernel(east_ref, north_ref, mine_ref, other_ref, ends_ref, _, __, out_ref):
    flip = parity()
    turn = lambda r: r + flip * (STEPS - 1 - 2 * r)

    def store(c, r, at, value):
        out_ref[c, turn(r), at, :] = ends_ref[c, flip * STEPS + turn(r), at, :] + value

    mend_side(flip, east_ref, north_ref, mine_ref, other_ref, store, None)


def subtract_rows(state_ref, out_hbm, buffer, sems, jobs):
    copies = []
    for start, other in jobs:
        for c in range(other.shape[0]):
            count = other.shape[1]
            for r in range(count):
                buffer[c, start + r] = state_ref[0, c, start + r] - other[c, r]
            at = pl.ds(start, count)
            copy = pltpu.make_async_copy(buffer.at[c, at], out_hbm.at[0, c, at], sems.at[len(copies)])
            copy.start()
            copies.append(copy)
    return copies


def begin_kernel(state_ref, middle_ref, a_ref, out_hbm, buffer, sems):
    start = parity() * (state_ref.shape[2] - STEPS)
    for copy in subtract_rows(state_ref, out_hbm, buffer, sems, ((STEPS, middle_ref), (start, a_ref))):
        copy.wait()


def finish_kernel(
    begun_hbm, state_ref, b_ref, owner_ref, total_ref, came_ref, out_hbm, gradient_ref, buffer, sems
):
    parts = b_ref.shape[0]
    start = (1 - parity()) * (state_ref.shape[2] - STEPS)
    copies = subtract_rows(state_ref, out_hbm, buffer, sems, ((start, b_ref),))

    share, mine = gradient_ref.shape[1:]
    start = lax.axis_index("hor") * mine
    chosen = []
    for c in range(parts):
        total = total_ref[c] + came_ref[c]
        block = total[:share]
        for s in range(1, total.shape[0] // share):
            block = jnp.where(lax.axis_index("sub") == s, total[s * share:(s + 1) * share], block)
        chosen.append(block)
    chosen = jnp.concatenate(chosen, 0)
    column = lax.broadcasted_iota(jnp.int32, (parts * share, mine), 1)
    picked = jnp.zeros((parts * share, mine), jnp.float32)
    for q in range(mine):
        value = jnp.sum(jnp.where(owner_ref[...] == start + q, chosen, 0.0), axis=1, keepdims=True)
        picked = jnp.where(column == q, value, picked)
    for c in range(parts):
        gradient_ref[c] = picked[c * share:(c + 1) * share]
    for copy in copies:
        copy.wait()


BRIEF = pl.CostEstimate(flops=1, bytes_accessed=1, transcendentals=0)
PARAMS = pltpu.CompilerParams(vmem_limit_bytes=24 * 1024 * 1024)


def local(
    adjoint_state,
    courant_east,
    courant_north,
    parent_cell,
    stencil_offset,
    stencil_weight,
    owner_slot,
):
    _, parts, rows, levels, width = adjoint_state.shape
    slots = owner_slot.shape[0]
    inner = rows - 2 * STEPS
    row_bytes = levels * width * 4
    f32 = lambda *shape: jax.ShapeDtypeStruct(shape, jnp.float32)
    vmem = pl.BlockSpec(memory_space=pltpu.VMEM)
    smem = pl.BlockSpec(memory_space=pltpu.SMEM)
    hbm = pl.BlockSpec(memory_space=pltpu.HBM)
    in_hbm = lambda value: pltpu.with_memory_space_constraint(value, pltpu.HBM)

    subs, hors = lax.axis_size("sub"), lax.axis_size("hor")
    small = [parent_cell, stencil_offset, stencil_weight]

    first_pack = pl.pallas_call(
        pack_kernel,
        in_specs=[hbm] * 6,
        out_specs=vmem,
        out_shape=f32(PACK_ROWS + 1, levels, width),
        scratch_shapes=[
            pltpu.VMEM((parts, STEPS, levels, width), jnp.float32),
            pltpu.VMEM((STEPS, levels, width), jnp.float32),
            pltpu.VMEM((STEPS, levels, width), jnp.float32),
        ]
        + [pltpu.VMEM(value.shape, value.dtype) for value in small]
        + [pltpu.SemaphoreType.DMA((levels // HALF, parts + 2)), pltpu.SemaphoreType.DMA((3,))],
        compiler_params=PARAMS,
        cost_estimate=BRIEF,
        name="pack",
    )(*[in_hbm(value) for value in [adjoint_state, courant_east, courant_north] + small])
    first_came = alternating(first_pack, -1)

    state, east, north = adjoint_state, courant_east, courant_north
    second_pack, middle, ends, columns = pl.pallas_call(
        sweep_kernel,
        in_specs=[vmem] * 3,
        out_specs=[vmem] * 4,
        out_shape=[
            f32(PACK_ROWS, levels, width),
            f32(parts, inner, levels, width),
            f32(parts, 2 * STEPS, levels, width),
            f32(parts, 2, rows, levels, LANES),
        ],
        scratch_shapes=[
            pltpu.VMEM((STEPS - 1, parts, rows, HALF, width), jnp.float32),
            pltpu.VMEM((rows, HALF, width), jnp.float32),
            pltpu.VMEM((rows, HALF, width), jnp.float32),
            pltpu.VMEM((rows, HALF, width), jnp.float32),
        ],
        compiler_params=PARAMS,
        cost_estimate=BRIEF,
        name="sweep",
    )(state, east, north)
    second_came = alternating(second_pack, 1)
    middle_came = along(middle, "sub", -1)

    mixing, base = pl.pallas_call(
        ghost_base_kernel,
        in_specs=[vmem] * 5,
        out_specs=[vmem] * 2,
        out_shape=[f32(parts, 2, rows, slots), f32(parts, levels, slots)],
        compiler_params=PARAMS,
        cost_estimate=BRIEF,
        name="ghost_base",
    )(*small, columns, north)

    column_shape = (parts, 2, 2 * (STEPS - 1), levels, LANES)
    side_a, a_columns = pl.pallas_call(
        mend_a_kernel,
        in_specs=[vmem] * 6,
        out_specs=[vmem] * 2,
        out_shape=[f32(parts, STEPS, levels, width), f32(*column_shape)],
        compiler_params=PARAMS,
        cost_estimate=BRIEF,
        name="mend_a",
    )(east, north, second_pack, first_came, ends, base)
    a_came = along(side_a, "sub", -1)
    total = pl.pallas_call(
        ghost_kernel,
        in_specs=[vmem] * 5,
        out_specs=vmem,
        out_shape=f32(parts, levels, slots),
        scratch_shapes=[pltpu.VMEM((parts, 2, rows, slots), jnp.float32)],
        compiler_params=PARAMS,
        cost_estimate=BRIEF,
        name="ghost",
    )(north, first_came, a_columns, mixing, base)
    order = rounds()
    total = total + exchanged(total, *order[0])
    side_b = pl.pallas_call(
        mend_b_kernel,
        in_specs=[vmem] * 5 + [pl.BlockSpec(memory_space=pl.ANY)] * 2,
        out_specs=vmem,
        out_shape=f32(parts, STEPS, levels, width),
        compiler_params=PARAMS,
        cost_estimate=BRIEF,
        name="mend_b",
    )(east, north, first_pack, second_came, ends, middle_came, total)
    b_came = along(side_b, "sub", -1)

    for each in order[1:-1]:
        total = total + exchanged(total, *each)
    came = exchanged(total, *order[-1])

    result = f32(*adjoint_state.shape)
    buffer = pltpu.VMEM((parts, rows, levels, width), jnp.float32)
    begun = pl.pallas_call(
        begin_kernel,
        in_specs=[vmem] * 3,
        out_specs=hbm,
        out_shape=result,
        scratch_shapes=[buffer, pltpu.SemaphoreType.DMA((2 * parts,))],
        compiler_params=PARAMS,
        cost_estimate=BRIEF,
        name="begin",
    )(state, middle_came, a_came)
    adjoint_result, boundary_gradient = pl.pallas_call(
        finish_kernel,
        in_specs=[hbm] + [vmem] * 5,
        out_specs=[hbm, vmem],
        out_shape=[result, f32(parts, levels // subs, slots // hors)],
        scratch_shapes=[buffer, pltpu.SemaphoreType.DMA((parts,))],
        input_output_aliases={0: 0},
        compiler_params=PARAMS,
        cost_estimate=BRIEF,
        name="finish",
    )(begun, state, b_came, owner_slot[None], total, came)
    return (adjoint_result, boundary_gradient)


def solution(mesh):
    in_specs = (
        P(("ens", "sub"), None, "hor", None, None),
        P(("ens", "sub"), "hor", None, None),
        P(("ens", "sub"), "hor", None, None),
        P(None, None, "hor"),
        P(None, None, None, "hor"),
        P(None, None, None, "hor"),
        P(),
    )
    out_specs = (P(("ens", "sub"), None, "hor", None, None), P("ens", "sub", "hor"))
    return jax.shard_map(local, mesh=mesh, in_specs=in_specs, out_specs=out_specs, check_vma=False)
```

```python
import functools

import jax
import jax.numpy as jnp
from jax import lax
from jax.experimental import pallas as pl
from jax.experimental.pallas import tpu as pltpu
from jax.sharding import PartitionSpec as P

STEPS = 4
HALF = 8
FLUX_ROWS = 2 * STEPS
PACK_ROWS = FLUX_ROWS + 3
LANES = 128
EXTRA = PACK_ROWS
TARGETS = 4 * LANES
WEIGHTS = 5 * LANES


def along(value, axis, step_of):
    peers = lax.axis_size(axis)
    pairs = [(i, i + step_of) for i in range(peers) if 0 <= i + step_of < peers]
    return lax.ppermute(value, axis, pairs)


def alternating(value, sign):
    subs, hors = lax.axis_size("sub"), lax.axis_size("hor")
    pairs = []
    for s in range(subs):
        step = sign if s % 2 == 0 else -sign
        pairs += [(s * hors + h, s * hors + h + step) for h in range(hors) if 0 <= h + step < hors]
    return lax.ppermute(value, ("sub", "hor"), pairs)


def rounds():
    subs, hors = lax.axis_size("sub"), lax.axis_size("hor")
    assert not subs & (subs - 1) and not hors & (hors - 1)
    order = [("sub", range(1, min(subs, 4)))]
    order += [("sub", [1 << n]) for n in range(2, subs.bit_length() - 1)]
    return order + [("hor", [1 << n]) for n in range(hors.bit_length() - 1)]


def exchanged(value, axis, distances):
    size = lax.axis_size(axis)
    return sum(lax.ppermute(value, axis, [(i, i ^ distance) for i in range(size)]) for distance in distances)


def parity():
    return lax.rem(lax.axis_index("sub"), 2)


def sign_of(flip):
    return jnp.where(flip == 1, jnp.float32(-1.0), jnp.float32(1.0))


def north_rates(north_rate):
    width = north_rate.shape[-1]
    column = lax.broadcasted_iota(jnp.int32, north_rate.shape, len(north_rate.shape) - 1)
    plus = jnp.where(column == 0, 0.0, jnp.maximum(north_rate, 0.0))
    minus = jnp.where(column == width - 1, 0.0, jnp.maximum(-north_rate, 0.0))
    return plus, minus


def shifted(flux_plus, flux_minus):
    width = flux_plus.shape[-1]
    axis = len(flux_plus.shape) - 1
    return pltpu.roll(flux_plus, width - 1, axis) + pltpu.roll(flux_minus, 1, axis)


class Row:
    def __init__(self, east_rate, north_rate=None):
        self.outward = jnp.maximum(east_rate, 0.0)
        self.inward = jnp.maximum(-east_rate, 0.0)
        if north_rate is not None:
            self.centre = 1.0 - jnp.abs(east_rate) - jnp.abs(north_rate)
            self.plus, self.minus = north_rates(north_rate)

    def stay(self, value):
        return self.centre * value + shifted(self.plus * value, self.minus * value)


def level_halves(levels, body):
    def step(h, carry):
        body(pl.ds(pl.multiple_of(h * HALF, HALF), HALF))
        return carry

    lax.fori_loop(0, levels // HALF, step, 0)


def pack_kernel(
    state_hbm, east_hbm, north_hbm, cell_hbm, offset_hbm, weight_hbm,
    pack_ref, state_ref, east_ref, north_ref, cell_ref, offset_ref, weight_ref, sems, small_sems,
):
    parts, rows, levels, width = state_hbm.shape[1:]
    flip = parity()
    sign = sign_of(flip)
    at_end = pl.ds(flip * (rows - STEPS), STEPS)
    place = lambda r: r + flip * (STEPS - 1 - 2 * r)
    halves = levels // HALF
    copies = []
    for h in range(halves):
        at = pl.ds(h * HALF, HALF)
        sem = sems.at[h]
        batch = [
            pltpu.make_async_copy(state_hbm.at[0, c, at_end, at], state_ref.at[c, :, at], sem.at[c])
            for c in range(parts)
        ]
        batch.append(pltpu.make_async_copy(east_hbm.at[0, at_end, at], east_ref.at[:, at], sem.at[parts]))
        batch.append(pltpu.make_async_copy(north_hbm.at[0, at_end, at], north_ref.at[:, at], sem.at[parts + 1]))
        copies.append(batch)
        for copy in batch:
            copy.start()
    small = [
        pltpu.make_async_copy(source, target, small_sems.at[n])
        for n, (source, target) in enumerate(
            ((cell_hbm, cell_ref), (offset_hbm, offset_ref), (weight_hbm, weight_ref))
        )
    ]
    for copy in small:
        copy.start()

    def half(at):
        row = [Row(east_ref[place(r), at, :] * sign, north_ref[place(r), at, :]) for r in range(STEPS)]
        pack_ref[FLUX_ROWS, at, :] = east_ref[place(0), at, :]
        pack_ref[FLUX_ROWS + 1, at, :] = north_ref[place(0), at, :]
        pack_ref[FLUX_ROWS + 2, at, :] = east_ref[place(1), at, :]
        for r in (1, 2):
            lanes = (2 * r - 2) * LANES
            pack_ref[EXTRA, at, lanes:lanes + LANES] = north_ref[place(r), at, :LANES]
            pack_ref[EXTRA, at, lanes + LANES:lanes + 2 * LANES] = north_ref[place(r), at, width - LANES:]
        for c in range(parts):
            field = [state_ref[c, place(r), at, :] for r in range(STEPS)]
            for k in range(STEPS):
                pack_ref[2 * k + c, at, :] = row[0].outward * field[0]
                after = []
                for r in range(STEPS - 1 - k):
                    value = row[r].stay(field[r]) + row[r + 1].outward * field[r + 1]
                    if r > 0:
                        value = value + row[r - 1].inward * field[r - 1]
                    after.append(value)
                field = after

    for h in range(halves):
        for copy in copies[h]:
            copy.wait()
        half(pl.ds(h * HALF, HALF))

    for copy in small:
        copy.wait()
    n = 0
    for point in range(offset_ref.shape[0]):
        for c in range(parts):
            target = (cell_ref[c] + offset_ref[point, c]).astype(jnp.float32)
            pack_ref[EXTRA, n:n + 2, TARGETS:TARGETS + rows] = target
            pack_ref[EXTRA, n:n + 2, WEIGHTS:WEIGHTS + rows] = weight_ref[point, c]
            n += 2


def as_column(row):
    count = row.shape[1]
    here = lax.broadcasted_iota(jnp.int32, (count, count), 0)
    there = lax.broadcasted_iota(jnp.int32, (count, count), 1)
    return jnp.sum(jnp.where(here == there, row, 0), axis=1, keepdims=True)


def sweep_kernel(
    state_ref, east_ref, north_ref, pack_ref, middle_ref, ends_ref, column_ref,
    field, plus_ref, minus_ref, centre_ref,
):
    parts, rows, levels, width = state_ref.shape[1:]
    flip = 1 - parity()
    sign = sign_of(flip)
    end_row = flip * (rows - 1)
    next_row = end_row + 1 - 2 * flip

    def half(at):
        pack_ref[FLUX_ROWS, at, :] = east_ref[0, end_row, at, :]
        pack_ref[FLUX_ROWS + 1, at, :] = north_ref[0, end_row, at, :]
        pack_ref[FLUX_ROWS + 2, at, :] = east_ref[0, next_row, at, :]

        for k in range(STEPS):
            if k == 0:
                read = lambda c, i: state_ref[0, c, i, at, :]
            else:
                read = lambda c, i, slot=k - 1: field[slot, c, i]
            leaving = jnp.maximum(east_ref[0, end_row, at, :] * sign, 0.0)
            for c in range(parts):
                pack_ref[2 * k + c, at, :] = leaving * read(c, end_row)
            west = [None] * parts
            here = [read(c, 0) for c in range(parts)]
            east_here = east_ref[0, 0, at, :]
            for i in range(rows):
                leave_west = jnp.maximum(-east_here, 0.0)
                if k == 0:
                    north_rate = north_ref[0, i, at, :]
                    centre = 1.0 - jnp.abs(east_here) - jnp.abs(north_rate)
                    plus, minus = north_rates(north_rate)
                    centre_ref[i], plus_ref[i], minus_ref[i] = centre, plus, minus
                else:
                    centre, plus, minus = centre_ref[i], plus_ref[i], minus_ref[i]
                if i + 1 < rows:
                    east_here = east_ref[0, i + 1, at, :]
                    east_after = jnp.maximum(east_here, 0.0)
                for c in range(parts):
                    value = here[c]
                    total = centre * value + shifted(plus * value, minus * value)
                    if i > 0:
                        total = total + west[c]
                    if i + 1 < rows:
                        west[c] = leave_west * value
                        here[c] = read(c, i + 1)
                        total = total + east_after * here[c]
                    if k < STEPS - 1:
                        field[k, c, i] = total
                    elif i < STEPS:
                        ends_ref[c, i, at, :] = total
                    elif i >= rows - STEPS:
                        ends_ref[c, i - rows + 2 * STEPS, at, :] = total
                    else:
                        middle_ref[c, i - STEPS, at, :] = total

        def columns(i, carry):
            for c in range(parts):
                value = state_ref[0, c, i, at, :]
                first, last = value[:, :LANES], value[:, width - LANES:]
                for slot in range(STEPS - 1):
                    first = first + field[slot, c, i, :, :LANES]
                    last = last + field[slot, c, i, :, width - LANES:]
                column_ref[c, 0, i, at, :] = first
                column_ref[c, 1, i, at, :] = last
            return carry

        lax.fori_loop(0, rows, columns, 0, unroll=2)

    level_halves(levels, half)


def mix(targets, weights, cells, total):
    for target, weight in zip(targets, weights):
        total = total + jnp.where(as_column(target) == cells, as_column(weight), 0.0)
    return total


def ghost_base_kernel(
    cell_ref, offset_ref, weight_ref, column_ref, north_ref, mixing_ref, partial_ref
):
    parts, _, rows, levels, _ = column_ref.shape
    slots = mixing_ref.shape[-1]
    width = north_ref.shape[-1]
    points = range(offset_ref.shape[0])
    cells = lax.broadcasted_iota(jnp.int32, (rows, slots), 1)
    for c in range(parts):
        for s in range(2):
            mixing_ref[c, s] = mix(
                [cell_ref[c, s:s + 1, :] + offset_ref[point, c, s:s + 1, :] for point in points],
                [weight_ref[point, c, s:s + 1, :] for point in points],
                cells, jnp.zeros((rows, slots), jnp.float32),
            )

    for c in range(parts):
        total = jnp.zeros((levels, slots), jnp.float32)
        for i in range(rows):
            south = jnp.maximum(north_ref[0, i, :, :1], 0.0) * column_ref[c, 0, i, :, :1]
            north = jnp.maximum(-north_ref[0, i, :, width - 1:], 0.0) * column_ref[c, 1, i, :, LANES - 1:]
            total = total + south * mixing_ref[c, 0, i:i + 1, :]
            total = total + north * mixing_ref[c, 1, i:i + 1, :]
        partial_ref[c] = total


def ghost_kernel(north_ref, other_ref, column_ref, mixing_ref, partial_ref, sum_ref, near_mixing):
    parts, levels, slots = partial_ref.shape
    rows = mixing_ref.shape[2]
    width = north_ref.shape[-1]
    flip = 1 - parity()
    cells = lax.broadcasted_iota(jnp.int32, (rows, slots), 1).astype(jnp.float32)
    points = (WEIGHTS - TARGETS) // LANES * 4
    for c in range(parts):
        for s in range(2):
            at = [(point * parts + c) * 2 + s for point in range(points)]
            near_mixing[c, s] = mix(
                [other_ref[EXTRA, n:n + 1, TARGETS:TARGETS + rows] for n in at],
                [other_ref[EXTRA, n:n + 1, WEIGHTS:WEIGHTS + rows] for n in at],
                cells, jnp.zeros((rows, slots), jnp.float32),
            )
    for c in range(parts):
        total = partial_ref[c]
        for r in range(STEPS - 1):
            i = r + flip * (rows - 1 - 2 * r)
            south = jnp.maximum(north_ref[0, i, :, :1], 0.0) * column_ref[c, 0, r, :, :1]
            north = jnp.maximum(-north_ref[0, i, :, width - 1:], 0.0) * column_ref[c, 1, r, :, LANES - 1:]
            total = total + south * mixing_ref[c, 0, pl.ds(i, 1), :]
            total = total + north * mixing_ref[c, 1, pl.ds(i, 1), :]
            i = r + (1 - flip) * (rows - 1 - 2 * r)
            if r == 0:
                first_rate = other_ref[FLUX_ROWS + 1, :, :LANES]
                last_rate = other_ref[FLUX_ROWS + 1, :, width - LANES:]
            else:
                lanes = (2 * r - 2) * LANES
                first_rate = other_ref[EXTRA, :, lanes:lanes + LANES]
                last_rate = other_ref[EXTRA, :, lanes + LANES:lanes + 2 * LANES]
            south = jnp.maximum(first_rate[:, :1], 0.0) * column_ref[c, 0, STEPS - 1 + r, :, :1]
            north = jnp.maximum(-last_rate[:, LANES - 1:], 0.0) * column_ref[c, 1, STEPS - 1 + r, :, LANES - 1:]
            total = total + south * near_mixing[c, 0, pl.ds(i, 1), :]
            total = total + north * near_mixing[c, 1, pl.ds(i, 1), :]
        sum_ref[c] = total


def mend_side(flip, east_ref, north_ref, mine_ref, other_ref, store, store_column):
    levels, width = mine_ref.shape[1:]
    rows = east_ref.shape[1]
    sign = sign_of(flip)
    place = lambda r: flip * (rows - STEPS) + r + flip * (STEPS - 1 - 2 * r)

    def half(at):
        own = [Row(east_ref[0, place(r), at, :] * sign, north_ref[0, place(r), at, :]) for r in range(STEPS - 1)]
        near = Row(other_ref[FLUX_ROWS, at, :] * sign, other_ref[FLUX_ROWS + 1, at, :])
        far = Row(other_ref[FLUX_ROWS + 2, at, :] * sign)
        for c in range(FLUX_ROWS // STEPS):
            mine = lambda k: mine_ref[2 * k + c, at, :]
            theirs = lambda k: other_ref[2 * k + c, at, :]
            a0 = theirs(0)
            n1 = mine(0)
            b0 = own[0].stay(a0) + near.inward * n1 + theirs(1)
            b1 = own[0].inward * a0
            bn1 = near.stay(n1) + own[0].outward * a0 + mine(1)
            bn2 = near.outward * n1
            c0 = own[0].stay(b0) + near.inward * bn1 + own[1].outward * b1 + theirs(2)
            c1 = own[1].stay(b1) + own[0].inward * b0
            c2 = own[1].inward * b1
            cn1 = near.stay(bn1) + own[0].outward * b0 + far.inward * bn2 + mine(2)
            d0 = own[0].stay(c0) + near.inward * cn1 + own[1].outward * c1 + theirs(3)
            d1 = own[1].stay(c1) + own[0].inward * c0 + own[2].outward * c2
            d2 = own[2].stay(c2) + own[1].inward * c1
            d3 = own[2].inward * c2
            for r, value in enumerate((d0, d1, d2, d3)):
                store(c, r, at, value)
            if store_column is not None:
                tiles = (slice(0, LANES), slice(width - LANES, width))
                for s, lanes in enumerate(tiles):
                    tile = lambda value: value[:, lanes]
                    rate = other_ref[EXTRA, at, s * LANES:(s + 1) * LANES]
                    stays = 1.0 - jnp.abs(other_ref[FLUX_ROWS + 2, at, lanes]) - jnp.abs(rate)
                    drift = jnp.maximum(rate if s == 0 else -rate, 0.0) * tile(bn2)
                    cn2 = stays * tile(bn2) + pltpu.roll(drift, LANES - 1 if s == 0 else 1, 1)
                    cn2 = cn2 + tile(near.outward) * tile(bn1)
                    cn3 = tile(far.outward) * tile(bn2)
                    sums = (
                        tile(a0) + tile(b0) + tile(c0), tile(b1) + tile(c1), tile(c2),
                        tile(n1) + tile(bn1) + tile(cn1), tile(bn2) + cn2, cn3,
                    )
                    for r, value in enumerate(sums):
                        store_column(c, s, r, at, value)

    level_halves(levels, half)


def mend_a_kernel(east_ref, north_ref, mine_ref, other_ref, ends_ref, base_ref, out_ref, column_ref):
    flip = 1 - parity()
    turn = lambda r: r + flip * (STEPS - 1 - 2 * r)

    def store(c, r, at, value):
        out_ref[c, turn(r), at, :] = ends_ref[c, flip * STEPS + turn(r), at, :] + value

    def store_column(c, s, r, at, value):
        column_ref[c, s, r, at, :] = value

    mend_side(flip, east_ref, north_ref, mine_ref, other_ref, store, store_column)


def mend_b_kernel(east_ref, north_ref, mine_ref, other_ref, ends_ref, _, __, out_ref):
    flip = parity()
    turn = lambda r: r + flip * (STEPS - 1 - 2 * r)

    def store(c, r, at, value):
        out_ref[c, turn(r), at, :] = ends_ref[c, flip * STEPS + turn(r), at, :] + value

    mend_side(flip, east_ref, north_ref, mine_ref, other_ref, store, None)


def subtract_rows(state_ref, out_hbm, buffer, sems, jobs):
    copies = []
    for start, other in jobs:
        for c in range(other.shape[0]):
            count = other.shape[1]
            for r in range(count):
                buffer[c, start + r] = state_ref[0, c, start + r] - other[c, r]
            at = pl.ds(start, count)
            copy = pltpu.make_async_copy(buffer.at[c, at], out_hbm.at[0, c, at], sems.at[len(copies)])
            copy.start()
            copies.append(copy)
    return copies


def begin_kernel(state_ref, middle_ref, a_ref, out_hbm, buffer, sems):
    start = parity() * (state_ref.shape[2] - STEPS)
    for copy in subtract_rows(state_ref, out_hbm, buffer, sems, ((STEPS, middle_ref), (start, a_ref))):
        copy.wait()


def finish_kernel(
    begun_hbm, state_ref, b_ref, owner_ref, total_ref, came_ref, out_hbm, gradient_ref, buffer, sems
):
    parts = b_ref.shape[0]
    start = (1 - parity()) * (state_ref.shape[2] - STEPS)
    copies = subtract_rows(state_ref, out_hbm, buffer, sems, ((start, b_ref),))

    share, mine = gradient_ref.shape[1:]
    start = lax.axis_index("hor") * mine
    chosen = []
    for c in range(parts):
        total = total_ref[c] + came_ref[c]
        block = total[:share]
        for s in range(1, total.shape[0] // share):
            block = jnp.where(lax.axis_index("sub") == s, total[s * share:(s + 1) * share], block)
        chosen.append(block)
    chosen = jnp.concatenate(chosen, 0)
    column = lax.broadcasted_iota(jnp.int32, (parts * share, mine), 1)
    picked = jnp.zeros((parts * share, mine), jnp.float32)
    for q in range(mine):
        value = jnp.sum(jnp.where(owner_ref[...] == start + q, chosen, 0.0), axis=1, keepdims=True)
        picked = jnp.where(column == q, value, picked)
    for c in range(parts):
        gradient_ref[c] = picked[c * share:(c + 1) * share]
    for copy in copies:
        copy.wait()


BRIEF = pl.CostEstimate(flops=1, bytes_accessed=1, transcendentals=0)
PARAMS = pltpu.CompilerParams(vmem_limit_bytes=24 * 1024 * 1024)


def local(
    adjoint_state,
    courant_east,
    courant_north,
    parent_cell,
    stencil_offset,
    stencil_weight,
    owner_slot,
):
    _, parts, rows, levels, width = adjoint_state.shape
    slots = owner_slot.shape[0]
    inner = rows - 2 * STEPS
    row_bytes = levels * width * 4
    f32 = lambda *shape: jax.ShapeDtypeStruct(shape, jnp.float32)
    vmem = pl.BlockSpec(memory_space=pltpu.VMEM)
    smem = pl.BlockSpec(memory_space=pltpu.SMEM)
    hbm = pl.BlockSpec(memory_space=pltpu.HBM)
    in_hbm = lambda value: pltpu.with_memory_space_constraint(value, pltpu.HBM)

    subs, hors = lax.axis_size("sub"), lax.axis_size("hor")
    small = [parent_cell, stencil_offset, stencil_weight]

    first_pack = pl.pallas_call(
        pack_kernel,
        in_specs=[hbm] * 6,
        out_specs=vmem,
        out_shape=f32(PACK_ROWS + 1, levels, width),
        scratch_shapes=[
            pltpu.VMEM((parts, STEPS, levels, width), jnp.float32),
            pltpu.VMEM((STEPS, levels, width), jnp.float32),
            pltpu.VMEM((STEPS, levels, width), jnp.float32),
        ]
        + [pltpu.VMEM(value.shape, value.dtype) for value in small]
        + [pltpu.SemaphoreType.DMA((levels // HALF, parts + 2)), pltpu.SemaphoreType.DMA((3,))],
        compiler_params=PARAMS,
        cost_estimate=BRIEF,
        name="pack",
    )(*[in_hbm(value) for value in [adjoint_state, courant_east, courant_north] + small])
    first_came = alternating(first_pack, -1)

    state, east, north = adjoint_state, courant_east, courant_north
    second_pack, middle, ends, columns = pl.pallas_call(
        sweep_kernel,
        in_specs=[vmem] * 3,
        out_specs=[vmem] * 4,
        out_shape=[
            f32(PACK_ROWS, levels, width),
            f32(parts, inner, levels, width),
            f32(parts, 2 * STEPS, levels, width),
            f32(parts, 2, rows, levels, LANES),
        ],
        scratch_shapes=[
            pltpu.VMEM((STEPS - 1, parts, rows, HALF, width), jnp.float32),
            pltpu.VMEM((rows, HALF, width), jnp.float32),
            pltpu.VMEM((rows, HALF, width), jnp.float32),
            pltpu.VMEM((rows, HALF, width), jnp.float32),
        ],
        compiler_params=PARAMS,
        cost_estimate=BRIEF,
        name="sweep",
    )(state, east, north)
    second_came = alternating(second_pack, 1)
    middle_came = along(middle, "sub", -1)

    mixing, base = pl.pallas_call(
        ghost_base_kernel,
        in_specs=[vmem] * 5,
        out_specs=[vmem] * 2,
        out_shape=[f32(parts, 2, rows, slots), f32(parts, levels, slots)],
        compiler_params=PARAMS,
        cost_estimate=BRIEF,
        name="ghost_base",
    )(*small, columns, north)

    column_shape = (parts, 2, 2 * (STEPS - 1), levels, LANES)
    side_a, a_columns = pl.pallas_call(
        mend_a_kernel,
        in_specs=[vmem] * 6,
        out_specs=[vmem] * 2,
        out_shape=[f32(parts, STEPS, levels, width), f32(*column_shape)],
        compiler_params=PARAMS,
        cost_estimate=BRIEF,
        name="mend_a",
    )(east, north, second_pack, first_came, ends, base)
    a_came = along(side_a, "sub", -1)
    total = pl.pallas_call(
        ghost_kernel,
        in_specs=[vmem] * 5,
        out_specs=vmem,
        out_shape=f32(parts, levels, slots),
        scratch_shapes=[pltpu.VMEM((parts, 2, rows, slots), jnp.float32)],
        compiler_params=PARAMS,
        cost_estimate=BRIEF,
        name="ghost",
    )(north, first_came, a_columns, mixing, base)
    order = rounds()
    total = total + exchanged(total, *order[0])
    side_b = pl.pallas_call(
        mend_b_kernel,
        in_specs=[vmem] * 5 + [pl.BlockSpec(memory_space=pl.ANY)] * 2,
        out_specs=vmem,
        out_shape=f32(parts, STEPS, levels, width),
        compiler_params=PARAMS,
        cost_estimate=BRIEF,
        name="mend_b",
    )(east, north, first_pack, second_came, ends, middle_came, total)
    b_came = along(side_b, "sub", -1)

    for each in order[1:-1]:
        total = total + exchanged(total, *each)
    came = exchanged(total, *order[-1])

    result = f32(*adjoint_state.shape)
    buffer = pltpu.VMEM((parts, rows, levels, width), jnp.float32)
    begun = pl.pallas_call(
        begin_kernel,
        in_specs=[vmem] * 3,
        out_specs=hbm,
        out_shape=result,
        scratch_shapes=[buffer, pltpu.SemaphoreType.DMA((2 * parts,))],
        compiler_params=PARAMS,
        cost_estimate=BRIEF,
        name="begin",
    )(state, middle_came, a_came)
    adjoint_result, boundary_gradient = pl.pallas_call(
        finish_kernel,
        in_specs=[hbm] + [vmem] * 5,
        out_specs=[hbm, vmem],
        out_shape=[result, f32(parts, levels // subs, slots // hors)],
        scratch_shapes=[buffer, pltpu.SemaphoreType.DMA((parts,))],
        input_output_aliases={0: 0},
        compiler_params=PARAMS,
        cost_estimate=BRIEF,
        name="finish",
    )(begun, state, b_came, owner_slot[None], total, came)
    return (adjoint_result, boundary_gradient)


def solution(mesh):
    in_specs = (
        P(("ens", "sub"), None, "hor", None, None),
        P(("ens", "sub"), "hor", None, None),
        P(("ens", "sub"), "hor", None, None),
        P(None, None, "hor"),
        P(None, None, None, "hor"),
        P(None, None, None, "hor"),
        P(),
    )
    out_specs = (P(("ens", "sub"), None, "hor", None, None), P("ens", "sub", "hor"))
    return jax.shard_map(local, mesh=mesh, in_specs=in_specs, out_specs=out_specs, check_vma=False)
```

```python
import functools

import jax
import jax.numpy as jnp
from jax import lax
from jax.experimental import pallas as pl
from jax.experimental.pallas import tpu as pltpu
from jax.sharding import PartitionSpec as P

STEPS = 4
HALF = 8
FLUX_ROWS = 2 * STEPS
PACK_ROWS = FLUX_ROWS + 3
LANES = 128
EXTRA = PACK_ROWS
TARGETS = 4 * LANES
WEIGHTS = 5 * LANES


def to_previous(value):
    peers = lax.axis_size("sub")
    return lax.ppermute(value, "sub", [(i, (i - 1) % peers) for i in range(peers)])


def alternating(value, sign):
    subs, hors = lax.axis_size("sub"), lax.axis_size("hor")
    pairs = []
    for s in range(subs):
        step = sign if s % 2 == 0 else -sign
        pairs += [(s * hors + h, s * hors + h + step) for h in range(hors) if 0 <= h + step < hors]
    return lax.ppermute(value, ("sub", "hor"), pairs)


def rounds():
    subs, hors = lax.axis_size("sub"), lax.axis_size("hor")
    assert not subs & (subs - 1) and not hors & (hors - 1)
    order = [("sub", range(1, min(subs, 4)))]
    order += [("sub", [1 << n]) for n in range(2, subs.bit_length() - 1)]
    return order + [("hor", [1 << n]) for n in range(hors.bit_length() - 1)]


def exchanged(value, axis, distances):
    size = lax.axis_size(axis)
    return sum(lax.ppermute(value, axis, [(i, i ^ distance) for i in range(size)]) for distance in distances)


def parity():
    return lax.rem(lax.axis_index("sub"), 2)


def sign_of(flip):
    return jnp.where(flip == 1, jnp.float32(-1.0), jnp.float32(1.0))


def north_rates(north_rate):
    width = north_rate.shape[-1]
    column = lax.broadcasted_iota(jnp.int32, north_rate.shape, len(north_rate.shape) - 1)
    plus = jnp.where(column == 0, 0.0, jnp.maximum(north_rate, 0.0))
    minus = jnp.where(column == width - 1, 0.0, jnp.maximum(-north_rate, 0.0))
    return plus, minus


def shifted(flux_plus, flux_minus):
    width = flux_plus.shape[-1]
    axis = len(flux_plus.shape) - 1
    return pltpu.roll(flux_plus, width - 1, axis) + pltpu.roll(flux_minus, 1, axis)


class Row:
    def __init__(self, east_rate, north_rate=None):
        self.outward = jnp.maximum(east_rate, 0.0)
        self.inward = jnp.maximum(-east_rate, 0.0)
        if north_rate is not None:
            self.centre = 1.0 - jnp.abs(east_rate) - jnp.abs(north_rate)
            self.plus, self.minus = north_rates(north_rate)

    def stay(self, value):
        return self.centre * value + shifted(self.plus * value, self.minus * value)


def level_halves(levels, body):
    def step(h, carry):
        body(pl.ds(pl.multiple_of(h * HALF, HALF), HALF))
        return carry

    lax.fori_loop(0, levels // HALF, step, 0)


def pack_kernel(
    state_hbm, east_hbm, north_hbm, cell_hbm, offset_hbm, weight_hbm,
    pack_ref, state_ref, east_ref, north_ref, cell_ref, offset_ref, weight_ref, sems, small_sems,
):
    parts, rows, levels, width = state_hbm.shape[1:]
    flip = parity()
    sign = sign_of(flip)
    at_end = pl.ds(flip * (rows - STEPS), STEPS)
    place = lambda r: r + flip * (STEPS - 1 - 2 * r)
    halves = levels // HALF
    copies = []
    for h in range(halves):
        at = pl.ds(h * HALF, HALF)
        sem = sems.at[h]
        batch = [
            pltpu.make_async_copy(state_hbm.at[0, c, at_end, at], state_ref.at[c, :, at], sem.at[c])
            for c in range(parts)
        ]
        batch.append(pltpu.make_async_copy(east_hbm.at[0, at_end, at], east_ref.at[:, at], sem.at[parts]))
        batch.append(pltpu.make_async_copy(north_hbm.at[0, at_end, at], north_ref.at[:, at], sem.at[parts + 1]))
        copies.append(batch)
        for copy in batch:
            copy.start()
    small = [
        pltpu.make_async_copy(source, target, small_sems.at[n])
        for n, (source, target) in enumerate(
            ((cell_hbm, cell_ref), (offset_hbm, offset_ref), (weight_hbm, weight_ref))
        )
    ]
    for copy in small:
        copy.start()

    def half(at):
        row = [Row(east_ref[place(r), at, :] * sign, north_ref[place(r), at, :]) for r in range(STEPS)]
        pack_ref[FLUX_ROWS, at, :] = east_ref[place(0), at, :]
        pack_ref[FLUX_ROWS + 1, at, :] = north_ref[place(0), at, :]
        pack_ref[FLUX_ROWS + 2, at, :] = east_ref[place(1), at, :]
        for r in (1, 2):
            lanes = (2 * r - 2) * LANES
            pack_ref[EXTRA, at, lanes:lanes + LANES] = north_ref[place(r), at, :LANES]
            pack_ref[EXTRA, at, lanes + LANES:lanes + 2 * LANES] = north_ref[place(r), at, width - LANES:]
        for c in range(parts):
            field = [state_ref[c, place(r), at, :] for r in range(STEPS)]
            for k in range(STEPS):
                pack_ref[2 * k + c, at, :] = row[0].outward * field[0]
                after = []
                for r in range(STEPS - 1 - k):
                    value = row[r].stay(field[r]) + row[r + 1].outward * field[r + 1]
                    if r > 0:
                        value = value + row[r - 1].inward * field[r - 1]
                    after.append(value)
                field = after

    for h in range(halves):
        for copy in copies[h]:
            copy.wait()
        half(pl.ds(h * HALF, HALF))

    for copy in small:
        copy.wait()
    n = 0
    for point in range(offset_ref.shape[0]):
        for c in range(parts):
            target = (cell_ref[c] + offset_ref[point, c]).astype(jnp.float32)
            pack_ref[EXTRA, n:n + 2, TARGETS:TARGETS + rows] = target
            pack_ref[EXTRA, n:n + 2, WEIGHTS:WEIGHTS + rows] = weight_ref[point, c]
            n += 2


def as_column(row):
    count = row.shape[1]
    here = lax.broadcasted_iota(jnp.int32, (count, count), 0)
    there = lax.broadcasted_iota(jnp.int32, (count, count), 1)
    return jnp.sum(jnp.where(here == there, row, 0), axis=1, keepdims=True)


def sweep_kernel(
    state_ref, east_ref, north_ref, pack_ref, middle_ref, ends_ref, column_ref,
    field, plus_ref, minus_ref, centre_ref,
):
    parts, rows, levels, width = state_ref.shape[1:]
    flip = 1 - parity()
    sign = sign_of(flip)
    end_row = flip * (rows - 1)
    next_row = end_row + 1 - 2 * flip

    def half(at):
        pack_ref[FLUX_ROWS, at, :] = east_ref[0, end_row, at, :]
        pack_ref[FLUX_ROWS + 1, at, :] = north_ref[0, end_row, at, :]
        pack_ref[FLUX_ROWS + 2, at, :] = east_ref[0, next_row, at, :]

        for k in range(STEPS):
            if k == 0:
                read = lambda c, i: state_ref[0, c, i, at, :]
            else:
                read = lambda c, i, slot=k - 1: field[slot, c, i]
            leaving = jnp.maximum(east_ref[0, end_row, at, :] * sign, 0.0)
            for c in range(parts):
                pack_ref[2 * k + c, at, :] = leaving * read(c, end_row)
            west = [None] * parts
            here = [read(c, 0) for c in range(parts)]
            east_here = east_ref[0, 0, at, :]
            for i in range(rows):
                leave_west = jnp.maximum(-east_here, 0.0)
                if k == 0:
                    north_rate = north_ref[0, i, at, :]
                    centre = 1.0 - jnp.abs(east_here) - jnp.abs(north_rate)
                    plus, minus = north_rates(north_rate)
                    centre_ref[i], plus_ref[i], minus_ref[i] = centre, plus, minus
                else:
                    centre, plus, minus = centre_ref[i], plus_ref[i], minus_ref[i]
                if i + 1 < rows:
                    east_here = east_ref[0, i + 1, at, :]
                    east_after = jnp.maximum(east_here, 0.0)
                for c in range(parts):
                    value = here[c]
                    total = centre * value + shifted(plus * value, minus * value)
                    if i > 0:
                        total = total + west[c]
                    if i + 1 < rows:
                        west[c] = leave_west * value
                        here[c] = read(c, i + 1)
                        total = total + east_after * here[c]
                    if k < STEPS - 1:
                        field[k, c, i] = total
                    elif i < STEPS:
                        ends_ref[c, i, at, :] = total
                    elif i >= rows - STEPS:
                        ends_ref[c, i - rows + 2 * STEPS, at, :] = total
                    else:
                        middle_ref[c, i - STEPS, at, :] = total

        def columns(i, carry):
            for c in range(parts):
                value = state_ref[0, c, i, at, :]
                first, last = value[:, :LANES], value[:, width - LANES:]
                for slot in range(STEPS - 1):
                    first = first + field[slot, c, i, :, :LANES]
                    last = last + field[slot, c, i, :, width - LANES:]
                column_ref[c, 0, i, at, :] = first
                column_ref[c, 1, i, at, :] = last
            return carry

        lax.fori_loop(0, rows, columns, 0, unroll=2)

    level_halves(levels, half)


def mix(targets, weights, cells, total):
    for target, weight in zip(targets, weights):
        total = total + jnp.where(as_column(target) == cells, as_column(weight), 0.0)
    return total


def ghost_base_kernel(
    cell_ref, offset_ref, weight_ref, column_ref, north_ref, mixing_ref, partial_ref
):
    parts, _, rows, levels, _ = column_ref.shape
    slots = mixing_ref.shape[-1]
    width = north_ref.shape[-1]
    points = range(offset_ref.shape[0])
    cells = lax.broadcasted_iota(jnp.int32, (rows, slots), 1)
    for c in range(parts):
        for s in range(2):
            mixing_ref[c, s] = mix(
                [cell_ref[c, s:s + 1, :] + offset_ref[point, c, s:s + 1, :] for point in points],
                [weight_ref[point, c, s:s + 1, :] for point in points],
                cells, jnp.zeros((rows, slots), jnp.float32),
            )

    for c in range(parts):
        total = jnp.zeros((levels, slots), jnp.float32)
        for i in range(rows):
            south = jnp.maximum(north_ref[0, i, :, :1], 0.0) * column_ref[c, 0, i, :, :1]
            north = jnp.maximum(-north_ref[0, i, :, width - 1:], 0.0) * column_ref[c, 1, i, :, LANES - 1:]
            total = total + south * mixing_ref[c, 0, i:i + 1, :]
            total = total + north * mixing_ref[c, 1, i:i + 1, :]
        partial_ref[c] = total


def ghost_kernel(north_ref, other_ref, column_ref, mixing_ref, partial_ref, sum_ref, near_mixing):
    parts, levels, slots = partial_ref.shape
    rows = mixing_ref.shape[2]
    width = north_ref.shape[-1]
    flip = 1 - parity()
    cells = lax.broadcasted_iota(jnp.int32, (rows, slots), 1).astype(jnp.float32)
    points = (WEIGHTS - TARGETS) // LANES * 4
    for c in range(parts):
        for s in range(2):
            at = [(point * parts + c) * 2 + s for point in range(points)]
            near_mixing[c, s] = mix(
                [other_ref[EXTRA, n:n + 1, TARGETS:TARGETS + rows] for n in at],
                [other_ref[EXTRA, n:n + 1, WEIGHTS:WEIGHTS + rows] for n in at],
                cells, jnp.zeros((rows, slots), jnp.float32),
            )
    for c in range(parts):
        total = partial_ref[c]
        for r in range(STEPS - 1):
            i = r + flip * (rows - 1 - 2 * r)
            south = jnp.maximum(north_ref[0, i, :, :1], 0.0) * column_ref[c, 0, r, :, :1]
            north = jnp.maximum(-north_ref[0, i, :, width - 1:], 0.0) * column_ref[c, 1, r, :, LANES - 1:]
            total = total + south * mixing_ref[c, 0, pl.ds(i, 1), :]
            total = total + north * mixing_ref[c, 1, pl.ds(i, 1), :]
            i = r + (1 - flip) * (rows - 1 - 2 * r)
            if r == 0:
                first_rate = other_ref[FLUX_ROWS + 1, :, :LANES]
                last_rate = other_ref[FLUX_ROWS + 1, :, width - LANES:]
            else:
                lanes = (2 * r - 2) * LANES
                first_rate = other_ref[EXTRA, :, lanes:lanes + LANES]
                last_rate = other_ref[EXTRA, :, lanes + LANES:lanes + 2 * LANES]
            south = jnp.maximum(first_rate[:, :1], 0.0) * column_ref[c, 0, STEPS - 1 + r, :, :1]
            north = jnp.maximum(-last_rate[:, LANES - 1:], 0.0) * column_ref[c, 1, STEPS - 1 + r, :, LANES - 1:]
            total = total + south * near_mixing[c, 0, pl.ds(i, 1), :]
            total = total + north * near_mixing[c, 1, pl.ds(i, 1), :]
        sum_ref[c] = total


def mend_side(flip, east_ref, north_ref, mine_ref, other_ref, store, store_column):
    levels, width = mine_ref.shape[1:]
    rows = east_ref.shape[1]
    sign = sign_of(flip)
    place = lambda r: flip * (rows - STEPS) + r + flip * (STEPS - 1 - 2 * r)

    def half(at):
        own = [Row(east_ref[0, place(r), at, :] * sign, north_ref[0, place(r), at, :]) for r in range(STEPS - 1)]
        near = Row(other_ref[FLUX_ROWS, at, :] * sign, other_ref[FLUX_ROWS + 1, at, :])
        far = Row(other_ref[FLUX_ROWS + 2, at, :] * sign)
        for c in range(FLUX_ROWS // STEPS):
            mine = lambda k: mine_ref[2 * k + c, at, :]
            theirs = lambda k: other_ref[2 * k + c, at, :]
            a0 = theirs(0)
            n1 = mine(0)
            b0 = own[0].stay(a0) + near.inward * n1 + theirs(1)
            b1 = own[0].inward * a0
            bn1 = near.stay(n1) + own[0].outward * a0 + mine(1)
            bn2 = near.outward * n1
            c0 = own[0].stay(b0) + near.inward * bn1 + own[1].outward * b1 + theirs(2)
            c1 = own[1].stay(b1) + own[0].inward * b0
            c2 = own[1].inward * b1
            cn1 = near.stay(bn1) + own[0].outward * b0 + far.inward * bn2 + mine(2)
            d0 = own[0].stay(c0) + near.inward * cn1 + own[1].outward * c1 + theirs(3)
            d1 = own[1].stay(c1) + own[0].inward * c0 + own[2].outward * c2
            d2 = own[2].stay(c2) + own[1].inward * c1
            d3 = own[2].inward * c2
            for r, value in enumerate((d0, d1, d2, d3)):
                store(c, r, at, value)
            if store_column is not None:
                tiles = (slice(0, LANES), slice(width - LANES, width))
                for s, lanes in enumerate(tiles):
                    tile = lambda value: value[:, lanes]
                    rate = other_ref[EXTRA, at, s * LANES:(s + 1) * LANES]
                    stays = 1.0 - jnp.abs(other_ref[FLUX_ROWS + 2, at, lanes]) - jnp.abs(rate)
                    drift = jnp.maximum(rate if s == 0 else -rate, 0.0) * tile(bn2)
                    cn2 = stays * tile(bn2) + pltpu.roll(drift, LANES - 1 if s == 0 else 1, 1)
                    cn2 = cn2 + tile(near.outward) * tile(bn1)
                    cn3 = tile(far.outward) * tile(bn2)
                    sums = (
                        tile(a0) + tile(b0) + tile(c0), tile(b1) + tile(c1), tile(c2),
                        tile(n1) + tile(bn1) + tile(cn1), tile(bn2) + cn2, cn3,
                    )
                    for r, value in enumerate(sums):
                        store_column(c, s, r, at, value)

    level_halves(levels, half)


def mend_a_kernel(east_ref, north_ref, mine_ref, other_ref, ends_ref, base_ref, out_ref, column_ref):
    flip = 1 - parity()
    turn = lambda r: r + flip * (STEPS - 1 - 2 * r)

    def store(c, r, at, value):
        out_ref[c, turn(r), at, :] = ends_ref[c, flip * STEPS + turn(r), at, :] + value

    def store_column(c, s, r, at, value):
        column_ref[c, s, r, at, :] = value

    mend_side(flip, east_ref, north_ref, mine_ref, other_ref, store, store_column)


def mend_b_kernel(east_ref, north_ref, mine_ref, other_ref, ends_ref, _, __, out_ref):
    flip = parity()
    turn = lambda r: r + flip * (STEPS - 1 - 2 * r)

    def store(c, r, at, value):
        out_ref[c, turn(r), at, :] = ends_ref[c, flip * STEPS + turn(r), at, :] + value

    mend_side(flip, east_ref, north_ref, mine_ref, other_ref, store, None)


def subtract_rows(state_ref, out_hbm, buffer, sems, jobs):
    copies = []
    is_last = lax.axis_index("sub") == lax.axis_size("sub") - 1
    for start, other in jobs:
        for c in range(other.shape[0]):
            count = other.shape[1]
            for r in range(count):
                buffer[c, start + r] = state_ref[0, c, start + r] - jnp.where(is_last, 0.0, other[c, r])
            at = pl.ds(start, count)
            copy = pltpu.make_async_copy(buffer.at[c, at], out_hbm.at[0, c, at], sems.at[len(copies)])
            copy.start()
            copies.append(copy)
    return copies


def begin_kernel(state_ref, middle_ref, a_ref, out_hbm, buffer, sems):
    start = parity() * (state_ref.shape[2] - STEPS)
    for copy in subtract_rows(state_ref, out_hbm, buffer, sems, ((STEPS, middle_ref), (start, a_ref))):
        copy.wait()


def finish_kernel(
    begun_hbm, state_ref, b_ref, owner_ref, total_ref, came_ref, out_hbm, gradient_ref, buffer, sems
):
    parts = b_ref.shape[0]
    start = (1 - parity()) * (state_ref.shape[2] - STEPS)
    copies = subtract_rows(state_ref, out_hbm, buffer, sems, ((start, b_ref),))

    share, mine = gradient_ref.shape[1:]
    start = lax.axis_index("hor") * mine
    chosen = []
    for c in range(parts):
        total = total_ref[c] + came_ref[c]
        block = total[:share]
        for s in range(1, total.shape[0] // share):
            block = jnp.where(lax.axis_index("sub") == s, total[s * share:(s + 1) * share], block)
        chosen.append(block)
    chosen = jnp.concatenate(chosen, 0)
    column = lax.broadcasted_iota(jnp.int32, (parts * share, mine), 1)
    picked = jnp.zeros((parts * share, mine), jnp.float32)
    for q in range(mine):
        value = jnp.sum(jnp.where(owner_ref[...] == start + q, chosen, 0.0), axis=1, keepdims=True)
        picked = jnp.where(column == q, value, picked)
    for c in range(parts):
        gradient_ref[c] = picked[c * share:(c + 1) * share]
    for copy in copies:
        copy.wait()


BRIEF = pl.CostEstimate(flops=1, bytes_accessed=1, transcendentals=0)
PARAMS = pltpu.CompilerParams(vmem_limit_bytes=24 * 1024 * 1024)


def local(
    adjoint_state,
    courant_east,
    courant_north,
    parent_cell,
    stencil_offset,
    stencil_weight,
    owner_slot,
):
    _, parts, rows, levels, width = adjoint_state.shape
    slots = owner_slot.shape[0]
    inner = rows - 2 * STEPS
    row_bytes = levels * width * 4
    f32 = lambda *shape: jax.ShapeDtypeStruct(shape, jnp.float32)
    vmem = pl.BlockSpec(memory_space=pltpu.VMEM)
    smem = pl.BlockSpec(memory_space=pltpu.SMEM)
    hbm = pl.BlockSpec(memory_space=pltpu.HBM)
    in_hbm = lambda value: pltpu.with_memory_space_constraint(value, pltpu.HBM)

    subs, hors = lax.axis_size("sub"), lax.axis_size("hor")
    small = [parent_cell, stencil_offset, stencil_weight]

    first_pack = pl.pallas_call(
        pack_kernel,
        in_specs=[hbm] * 6,
        out_specs=vmem,
        out_shape=f32(PACK_ROWS + 1, levels, width),
        scratch_shapes=[
            pltpu.VMEM((parts, STEPS, levels, width), jnp.float32),
            pltpu.VMEM((STEPS, levels, width), jnp.float32),
            pltpu.VMEM((STEPS, levels, width), jnp.float32),
        ]
        + [pltpu.VMEM(value.shape, value.dtype) for value in small]
        + [pltpu.SemaphoreType.DMA((levels // HALF, parts + 2)), pltpu.SemaphoreType.DMA((3,))],
        compiler_params=PARAMS,
        cost_estimate=BRIEF,
        name="pack",
    )(*[in_hbm(value) for value in [adjoint_state, courant_east, courant_north] + small])
    first_came = alternating(first_pack, -1)

    state, east, north = adjoint_state, courant_east, courant_north
    second_pack, middle, ends, columns = pl.pallas_call(
        sweep_kernel,
        in_specs=[vmem] * 3,
        out_specs=[vmem] * 4,
        out_shape=[
            f32(PACK_ROWS, levels, width),
            f32(parts, inner, levels, width),
            f32(parts, 2 * STEPS, levels, width),
            f32(parts, 2, rows, levels, LANES),
        ],
        scratch_shapes=[
            pltpu.VMEM((STEPS - 1, parts, rows, HALF, width), jnp.float32),
            pltpu.VMEM((rows, HALF, width), jnp.float32),
            pltpu.VMEM((rows, HALF, width), jnp.float32),
            pltpu.VMEM((rows, HALF, width), jnp.float32),
        ],
        compiler_params=PARAMS,
        cost_estimate=BRIEF,
        name="sweep",
    )(state, east, north)
    second_came = alternating(second_pack, 1)
    middle_came = to_previous(middle)

    mixing, base = pl.pallas_call(
        ghost_base_kernel,
        in_specs=[vmem] * 5,
        out_specs=[vmem] * 2,
        out_shape=[f32(parts, 2, rows, slots), f32(parts, levels, slots)],
        compiler_params=PARAMS,
        cost_estimate=BRIEF,
        name="ghost_base",
    )(*small, columns, north)

    column_shape = (parts, 2, 2 * (STEPS - 1), levels, LANES)
    side_a, a_columns = pl.pallas_call(
        mend_a_kernel,
        in_specs=[vmem] * 6,
        out_specs=[vmem] * 2,
        out_shape=[f32(parts, STEPS, levels, width), f32(*column_shape)],
        compiler_params=PARAMS,
        cost_estimate=BRIEF,
        name="mend_a",
    )(east, north, second_pack, first_came, ends, base)
    a_came = to_previous(side_a)
    total = pl.pallas_call(
        ghost_kernel,
        in_specs=[vmem] * 5,
        out_specs=vmem,
        out_shape=f32(parts, levels, slots),
        scratch_shapes=[pltpu.VMEM((parts, 2, rows, slots), jnp.float32)],
        compiler_params=PARAMS,
        cost_estimate=BRIEF,
        name="ghost",
    )(north, first_came, a_columns, mixing, base)
    order = rounds()
    total = total + exchanged(total, *order[0])
    side_b = pl.pallas_call(
        mend_b_kernel,
        in_specs=[vmem] * 5 + [pl.BlockSpec(memory_space=pl.ANY)] * 2,
        out_specs=vmem,
        out_shape=f32(parts, STEPS, levels, width),
        compiler_params=PARAMS,
        cost_estimate=BRIEF,
        name="mend_b",
    )(east, north, first_pack, second_came, ends, middle_came, total)
    b_came = to_previous(side_b)

    for each in order[1:-1]:
        total = total + exchanged(total, *each)
    came = exchanged(total, *order[-1])

    result = f32(*adjoint_state.shape)
    buffer = pltpu.VMEM((parts, rows, levels, width), jnp.float32)
    begun = pl.pallas_call(
        begin_kernel,
        in_specs=[vmem] * 3,
        out_specs=hbm,
        out_shape=result,
        scratch_shapes=[buffer, pltpu.SemaphoreType.DMA((2 * parts,))],
        compiler_params=PARAMS,
        cost_estimate=BRIEF,
        name="begin",
    )(state, middle_came, a_came)
    adjoint_result, boundary_gradient = pl.pallas_call(
        finish_kernel,
        in_specs=[hbm] + [vmem] * 5,
        out_specs=[hbm, vmem],
        out_shape=[result, f32(parts, levels // subs, slots // hors)],
        scratch_shapes=[buffer, pltpu.SemaphoreType.DMA((parts,))],
        input_output_aliases={0: 0},
        compiler_params=PARAMS,
        cost_estimate=BRIEF,
        name="finish",
    )(begun, state, b_came, owner_slot[None], total, came)
    return (adjoint_result, boundary_gradient)


def solution(mesh):
    in_specs = (
        P(("ens", "sub"), None, "hor", None, None),
        P(("ens", "sub"), "hor", None, None),
        P(("ens", "sub"), "hor", None, None),
        P(None, None, "hor"),
        P(None, None, None, "hor"),
        P(None, None, None, "hor"),
        P(),
    )
    out_specs = (P(("ens", "sub"), None, "hor", None, None), P("ens", "sub", "hor"))
    return jax.shard_map(local, mesh=mesh, in_specs=in_specs, out_specs=out_specs, check_vma=False)
```

```python
import functools

import jax
import jax.numpy as jnp
from jax import lax
from jax.experimental import pallas as pl
from jax.experimental.pallas import tpu as pltpu
from jax.sharding import PartitionSpec as P

STEPS = 4
HALF = 8
FLUX_ROWS = 2 * STEPS
PACK_ROWS = FLUX_ROWS + 3
LANES = 128
EXTRA = PACK_ROWS
TARGETS = 4 * LANES
WEIGHTS = 5 * LANES


def to_previous(value):
    peers = lax.axis_size("sub")
    return lax.ppermute(value, "sub", [(i, (i - 1) % peers) for i in range(peers)])


def alternating(value, sign):
    subs, hors = lax.axis_size("sub"), lax.axis_size("hor")
    assert subs % 2 == 0
    pairs = []
    for s in range(subs):
        step = sign if s % 2 == 0 else -sign
        for h in range(hors):
            inside = 0 <= h + step < hors
            pairs.append((s * hors + h, s * hors + h + step if inside else (s ^ 1) * hors + h))
    return lax.ppermute(value, ("sub", "hor"), pairs)


def has_neighbour(flip):
    hor = lax.axis_index("hor")
    return jnp.where(flip == 1, hor < lax.axis_size("hor") - 1, hor > 0)


def rounds():
    subs, hors = lax.axis_size("sub"), lax.axis_size("hor")
    assert not subs & (subs - 1) and not hors & (hors - 1)
    order = [("sub", range(1, min(subs, 4)))]
    order += [("sub", [1 << n]) for n in range(2, subs.bit_length() - 1)]
    return order + [("hor", [1 << n]) for n in range(hors.bit_length() - 1)]


def exchanged(value, axis, distances):
    size = lax.axis_size(axis)
    return sum(lax.ppermute(value, axis, [(i, i ^ distance) for i in range(size)]) for distance in distances)


def parity():
    return lax.rem(lax.axis_index("sub"), 2)


def sign_of(flip):
    return jnp.where(flip == 1, jnp.float32(-1.0), jnp.float32(1.0))


def north_rates(north_rate):
    width = north_rate.shape[-1]
    column = lax.broadcasted_iota(jnp.int32, north_rate.shape, len(north_rate.shape) - 1)
    plus = jnp.where(column == 0, 0.0, jnp.maximum(north_rate, 0.0))
    minus = jnp.where(column == width - 1, 0.0, jnp.maximum(-north_rate, 0.0))
    return plus, minus


def shifted(flux_plus, flux_minus):
    width = flux_plus.shape[-1]
    axis = len(flux_plus.shape) - 1
    return pltpu.roll(flux_plus, width - 1, axis) + pltpu.roll(flux_minus, 1, axis)


class Row:
    def __init__(self, east_rate, north_rate=None):
        self.outward = jnp.maximum(east_rate, 0.0)
        self.inward = jnp.maximum(-east_rate, 0.0)
        if north_rate is not None:
            self.centre = 1.0 - jnp.abs(east_rate) - jnp.abs(north_rate)
            self.plus, self.minus = north_rates(north_rate)

    def stay(self, value):
        return self.centre * value + shifted(self.plus * value, self.minus * value)


def level_halves(levels, body):
    def step(h, carry):
        body(pl.ds(pl.multiple_of(h * HALF, HALF), HALF))
        return carry

    lax.fori_loop(0, levels // HALF, step, 0)


def pack_kernel(
    state_hbm, east_hbm, north_hbm, cell_hbm, offset_hbm, weight_hbm,
    pack_ref, state_ref, east_ref, north_ref, cell_ref, offset_ref, weight_ref, sems, small_sems,
):
    parts, rows, levels, width = state_hbm.shape[1:]
    flip = parity()
    sign = sign_of(flip)
    at_end = pl.ds(flip * (rows - STEPS), STEPS)
    place = lambda r: r + flip * (STEPS - 1 - 2 * r)
    halves = levels // HALF
    copies = []
    for h in range(halves):
        at = pl.ds(h * HALF, HALF)
        sem = sems.at[h]
        batch = [
            pltpu.make_async_copy(state_hbm.at[0, c, at_end, at], state_ref.at[c, :, at], sem.at[c])
            for c in range(parts)
        ]
        batch.append(pltpu.make_async_copy(east_hbm.at[0, at_end, at], east_ref.at[:, at], sem.at[parts]))
        batch.append(pltpu.make_async_copy(north_hbm.at[0, at_end, at], north_ref.at[:, at], sem.at[parts + 1]))
        copies.append(batch)
        for copy in batch:
            copy.start()
    small = [
        pltpu.make_async_copy(source, target, small_sems.at[n])
        for n, (source, target) in enumerate(
            ((cell_hbm, cell_ref), (offset_hbm, offset_ref), (weight_hbm, weight_ref))
        )
    ]
    for copy in small:
        copy.start()

    def half(at):
        row = [Row(east_ref[place(r), at, :] * sign, north_ref[place(r), at, :]) for r in range(STEPS)]
        pack_ref[FLUX_ROWS, at, :] = east_ref[place(0), at, :]
        pack_ref[FLUX_ROWS + 1, at, :] = north_ref[place(0), at, :]
        pack_ref[FLUX_ROWS + 2, at, :] = east_ref[place(1), at, :]
        for r in (1, 2):
            lanes = (2 * r - 2) * LANES
            pack_ref[EXTRA, at, lanes:lanes + LANES] = north_ref[place(r), at, :LANES]
            pack_ref[EXTRA, at, lanes + LANES:lanes + 2 * LANES] = north_ref[place(r), at, width - LANES:]
        for c in range(parts):
            field = [state_ref[c, place(r), at, :] for r in range(STEPS)]
            for k in range(STEPS):
                pack_ref[2 * k + c, at, :] = row[0].outward * field[0]
                after = []
                for r in range(STEPS - 1 - k):
                    value = row[r].stay(field[r]) + row[r + 1].outward * field[r + 1]
                    if r > 0:
                        value = value + row[r - 1].inward * field[r - 1]
                    after.append(value)
                field = after

    for h in range(halves):
        for copy in copies[h]:
            copy.wait()
        half(pl.ds(h * HALF, HALF))

    for copy in small:
        copy.wait()
    n = 0
    for point in range(offset_ref.shape[0]):
        for c in range(parts):
            target = (cell_ref[c] + offset_ref[point, c]).astype(jnp.float32)
            pack_ref[EXTRA, n:n + 2, TARGETS:TARGETS + rows] = target
            pack_ref[EXTRA, n:n + 2, WEIGHTS:WEIGHTS + rows] = weight_ref[point, c]
            n += 2


def as_column(row):
    count = row.shape[1]
    here = lax.broadcasted_iota(jnp.int32, (count, count), 0)
    there = lax.broadcasted_iota(jnp.int32, (count, count), 1)
    return jnp.sum(jnp.where(here == there, row, 0), axis=1, keepdims=True)


def sweep_kernel(
    state_ref, east_ref, north_ref, pack_ref, middle_ref, ends_ref, column_ref,
    field, plus_ref, minus_ref, centre_ref,
):
    parts, rows, levels, width = state_ref.shape[1:]
    flip = 1 - parity()
    sign = sign_of(flip)
    end_row = flip * (rows - 1)
    next_row = end_row + 1 - 2 * flip

    def half(at):
        pack_ref[FLUX_ROWS, at, :] = east_ref[0, end_row, at, :]
        pack_ref[FLUX_ROWS + 1, at, :] = north_ref[0, end_row, at, :]
        pack_ref[FLUX_ROWS + 2, at, :] = east_ref[0, next_row, at, :]

        for k in range(STEPS):
            if k == 0:
                read = lambda c, i: state_ref[0, c, i, at, :]
            else:
                read = lambda c, i, slot=k - 1: field[slot, c, i]
            leaving = jnp.maximum(east_ref[0, end_row, at, :] * sign, 0.0)
            for c in range(parts):
                pack_ref[2 * k + c, at, :] = leaving * read(c, end_row)
            west = [None] * parts
            here = [read(c, 0) for c in range(parts)]
            east_here = east_ref[0, 0, at, :]
            for i in range(rows):
                leave_west = jnp.maximum(-east_here, 0.0)
                if k == 0:
                    north_rate = north_ref[0, i, at, :]
                    centre = 1.0 - jnp.abs(east_here) - jnp.abs(north_rate)
                    plus, minus = north_rates(north_rate)
                    centre_ref[i], plus_ref[i], minus_ref[i] = centre, plus, minus
                else:
                    centre, plus, minus = centre_ref[i], plus_ref[i], minus_ref[i]
                if i + 1 < rows:
                    east_here = east_ref[0, i + 1, at, :]
                    east_after = jnp.maximum(east_here, 0.0)
                for c in range(parts):
                    value = here[c]
                    total = centre * value + shifted(plus * value, minus * value)
                    if i > 0:
                        total = total + west[c]
                    if i + 1 < rows:
                        west[c] = leave_west * value
                        here[c] = read(c, i + 1)
                        total = total + east_after * here[c]
                    if k < STEPS - 1:
                        field[k, c, i] = total
                    elif i < STEPS:
                        ends_ref[c, i, at, :] = total
                    elif i >= rows - STEPS:
                        ends_ref[c, i - rows + 2 * STEPS, at, :] = total
                    else:
                        middle_ref[c, i - STEPS, at, :] = total

        def columns(i, carry):
            for c in range(parts):
                value = state_ref[0, c, i, at, :]
                first, last = value[:, :LANES], value[:, width - LANES:]
                for slot in range(STEPS - 1):
                    first = first + field[slot, c, i, :, :LANES]
                    last = last + field[slot, c, i, :, width - LANES:]
                column_ref[c, 0, i, at, :] = first
                column_ref[c, 1, i, at, :] = last
            return carry

        lax.fori_loop(0, rows, columns, 0, unroll=2)

    level_halves(levels, half)


def mix(targets, weights, cells, total):
    for target, weight in zip(targets, weights):
        total = total + jnp.where(as_column(target) == cells, as_column(weight), 0.0)
    return total


def ghost_base_kernel(
    cell_ref, offset_ref, weight_ref, column_ref, north_ref, mixing_ref, partial_ref
):
    parts, _, rows, levels, _ = column_ref.shape
    slots = mixing_ref.shape[-1]
    width = north_ref.shape[-1]
    points = range(offset_ref.shape[0])
    cells = lax.broadcasted_iota(jnp.int32, (rows, slots), 1)
    for c in range(parts):
        for s in range(2):
            mixing_ref[c, s] = mix(
                [cell_ref[c, s:s + 1, :] + offset_ref[point, c, s:s + 1, :] for point in points],
                [weight_ref[point, c, s:s + 1, :] for point in points],
                cells, jnp.zeros((rows, slots), jnp.float32),
            )

    for c in range(parts):
        total = jnp.zeros((levels, slots), jnp.float32)
        for i in range(rows):
            south = jnp.maximum(north_ref[0, i, :, :1], 0.0) * column_ref[c, 0, i, :, :1]
            north = jnp.maximum(-north_ref[0, i, :, width - 1:], 0.0) * column_ref[c, 1, i, :, LANES - 1:]
            total = total + south * mixing_ref[c, 0, i:i + 1, :]
            total = total + north * mixing_ref[c, 1, i:i + 1, :]
        partial_ref[c] = total


def ghost_kernel(north_ref, other_ref, column_ref, mixing_ref, partial_ref, sum_ref, near_mixing):
    parts, levels, slots = partial_ref.shape
    rows = mixing_ref.shape[2]
    width = north_ref.shape[-1]
    flip = 1 - parity()
    cells = lax.broadcasted_iota(jnp.int32, (rows, slots), 1).astype(jnp.float32)
    points = (WEIGHTS - TARGETS) // LANES * 4
    for c in range(parts):
        for s in range(2):
            at = [(point * parts + c) * 2 + s for point in range(points)]
            near_mixing[c, s] = mix(
                [other_ref[EXTRA, n:n + 1, TARGETS:TARGETS + rows] for n in at],
                [other_ref[EXTRA, n:n + 1, WEIGHTS:WEIGHTS + rows] for n in at],
                cells, jnp.zeros((rows, slots), jnp.float32),
            )
    for c in range(parts):
        total = partial_ref[c]
        for r in range(STEPS - 1):
            i = r + flip * (rows - 1 - 2 * r)
            south = jnp.maximum(north_ref[0, i, :, :1], 0.0) * column_ref[c, 0, r, :, :1]
            north = jnp.maximum(-north_ref[0, i, :, width - 1:], 0.0) * column_ref[c, 1, r, :, LANES - 1:]
            total = total + south * mixing_ref[c, 0, pl.ds(i, 1), :]
            total = total + north * mixing_ref[c, 1, pl.ds(i, 1), :]
            i = r + (1 - flip) * (rows - 1 - 2 * r)
            if r == 0:
                first_rate = other_ref[FLUX_ROWS + 1, :, :LANES]
                last_rate = other_ref[FLUX_ROWS + 1, :, width - LANES:]
            else:
                lanes = (2 * r - 2) * LANES
                first_rate = other_ref[EXTRA, :, lanes:lanes + LANES]
                last_rate = other_ref[EXTRA, :, lanes + LANES:lanes + 2 * LANES]
            south = jnp.maximum(first_rate[:, :1], 0.0) * column_ref[c, 0, STEPS - 1 + r, :, :1]
            north = jnp.maximum(-last_rate[:, LANES - 1:], 0.0) * column_ref[c, 1, STEPS - 1 + r, :, LANES - 1:]
            total = total + south * near_mixing[c, 0, pl.ds(i, 1), :]
            total = total + north * near_mixing[c, 1, pl.ds(i, 1), :]
        sum_ref[c] = jnp.where(has_neighbour(flip), total, partial_ref[c])


def mend_side(flip, east_ref, north_ref, mine_ref, other_ref, store, store_column):
    levels, width = mine_ref.shape[1:]
    rows = east_ref.shape[1]
    sign = sign_of(flip)
    place = lambda r: flip * (rows - STEPS) + r + flip * (STEPS - 1 - 2 * r)

    def half(at):
        own = [Row(east_ref[0, place(r), at, :] * sign, north_ref[0, place(r), at, :]) for r in range(STEPS - 1)]
        near = Row(other_ref[FLUX_ROWS, at, :] * sign, other_ref[FLUX_ROWS + 1, at, :])
        far = Row(other_ref[FLUX_ROWS + 2, at, :] * sign)
        for c in range(FLUX_ROWS // STEPS):
            mine = lambda k: mine_ref[2 * k + c, at, :]
            theirs = lambda k: other_ref[2 * k + c, at, :]
            a0 = theirs(0)
            n1 = mine(0)
            b0 = own[0].stay(a0) + near.inward * n1 + theirs(1)
            b1 = own[0].inward * a0
            bn1 = near.stay(n1) + own[0].outward * a0 + mine(1)
            bn2 = near.outward * n1
            c0 = own[0].stay(b0) + near.inward * bn1 + own[1].outward * b1 + theirs(2)
            c1 = own[1].stay(b1) + own[0].inward * b0
            c2 = own[1].inward * b1
            cn1 = near.stay(bn1) + own[0].outward * b0 + far.inward * bn2 + mine(2)
            d0 = own[0].stay(c0) + near.inward * cn1 + own[1].outward * c1 + theirs(3)
            d1 = own[1].stay(c1) + own[0].inward * c0 + own[2].outward * c2
            d2 = own[2].stay(c2) + own[1].inward * c1
            d3 = own[2].inward * c2
            for r, value in enumerate((d0, d1, d2, d3)):
                store(c, r, at, value)
            if store_column is not None:
                tiles = (slice(0, LANES), slice(width - LANES, width))
                for s, lanes in enumerate(tiles):
                    tile = lambda value: value[:, lanes]
                    rate = other_ref[EXTRA, at, s * LANES:(s + 1) * LANES]
                    stays = 1.0 - jnp.abs(other_ref[FLUX_ROWS + 2, at, lanes]) - jnp.abs(rate)
                    drift = jnp.maximum(rate if s == 0 else -rate, 0.0) * tile(bn2)
                    cn2 = stays * tile(bn2) + pltpu.roll(drift, LANES - 1 if s == 0 else 1, 1)
                    cn2 = cn2 + tile(near.outward) * tile(bn1)
                    cn3 = tile(far.outward) * tile(bn2)
                    sums = (
                        tile(a0) + tile(b0) + tile(c0), tile(b1) + tile(c1), tile(c2),
                        tile(n1) + tile(bn1) + tile(cn1), tile(bn2) + cn2, cn3,
                    )
                    for r, value in enumerate(sums):
                        store_column(c, s, r, at, value)

    level_halves(levels, half)


def copy_end(flip, ends_ref, out_ref):
    for c in range(out_ref.shape[0]):
        for r in range(STEPS):
            out_ref[c, r] = ends_ref[c, flip * STEPS + r]


def mend_a_kernel(east_ref, north_ref, mine_ref, other_ref, ends_ref, base_ref, out_ref, column_ref):
    flip = 1 - parity()
    turn = lambda r: r + flip * (STEPS - 1 - 2 * r)

    def store(c, r, at, value):
        out_ref[c, turn(r), at, :] = ends_ref[c, flip * STEPS + turn(r), at, :] + value

    def store_column(c, s, r, at, value):
        column_ref[c, s, r, at, :] = value

    @pl.when(has_neighbour(flip))
    def _():
        mend_side(flip, east_ref, north_ref, mine_ref, other_ref, store, store_column)

    @pl.when(jnp.logical_not(has_neighbour(flip)))
    def _():
        column_ref[...] = jnp.zeros_like(column_ref)
        copy_end(flip, ends_ref, out_ref)


def mend_b_kernel(east_ref, north_ref, mine_ref, other_ref, ends_ref, _, __, out_ref):
    flip = parity()
    turn = lambda r: r + flip * (STEPS - 1 - 2 * r)

    def store(c, r, at, value):
        out_ref[c, turn(r), at, :] = ends_ref[c, flip * STEPS + turn(r), at, :] + value

    @pl.when(has_neighbour(flip))
    def _():
        mend_side(flip, east_ref, north_ref, mine_ref, other_ref, store, None)

    @pl.when(jnp.logical_not(has_neighbour(flip)))
    def _():
        copy_end(flip, ends_ref, out_ref)


def subtract_rows(state_ref, out_hbm, buffer, sems, jobs):
    copies = []
    is_last = lax.axis_index("sub") == lax.axis_size("sub") - 1
    for start, other in jobs:
        for c in range(other.shape[0]):
            count = other.shape[1]
            for r in range(count):
                buffer[c, start + r] = state_ref[0, c, start + r] - jnp.where(is_last, 0.0, other[c, r])
            at = pl.ds(start, count)
            copy = pltpu.make_async_copy(buffer.at[c, at], out_hbm.at[0, c, at], sems.at[len(copies)])
            copy.start()
            copies.append(copy)
    return copies


def begin_kernel(state_ref, middle_ref, a_ref, out_hbm, buffer, sems):
    start = parity() * (state_ref.shape[2] - STEPS)
    for copy in subtract_rows(state_ref, out_hbm, buffer, sems, ((STEPS, middle_ref), (start, a_ref))):
        copy.wait()


def finish_kernel(
    begun_hbm, state_ref, b_ref, owner_ref, total_ref, came_ref, out_hbm, gradient_ref, buffer, sems
):
    parts = b_ref.shape[0]
    start = (1 - parity()) * (state_ref.shape[2] - STEPS)
    copies = subtract_rows(state_ref, out_hbm, buffer, sems, ((start, b_ref),))

    share, mine = gradient_ref.shape[1:]
    start = lax.axis_index("hor") * mine
    chosen = []
    for c in range(parts):
        total = total_ref[c] + came_ref[c]
        block = total[:share]
        for s in range(1, total.shape[0] // share):
            block = jnp.where(lax.axis_index("sub") == s, total[s * share:(s + 1) * share], block)
        chosen.append(block)
    chosen = jnp.concatenate(chosen, 0)
    column = lax.broadcasted_iota(jnp.int32, (parts * share, mine), 1)
    picked = jnp.zeros((parts * share, mine), jnp.float32)
    for q in range(mine):
        value = jnp.sum(jnp.where(owner_ref[...] == start + q, chosen, 0.0), axis=1, keepdims=True)
        picked = jnp.where(column == q, value, picked)
    for c in range(parts):
        gradient_ref[c] = picked[c * share:(c + 1) * share]
    for copy in copies:
        copy.wait()


BRIEF = pl.CostEstimate(flops=1, bytes_accessed=1, transcendentals=0)
PARAMS = pltpu.CompilerParams(vmem_limit_bytes=24 * 1024 * 1024)


def local(
    adjoint_state,
    courant_east,
    courant_north,
    parent_cell,
    stencil_offset,
    stencil_weight,
    owner_slot,
):
    _, parts, rows, levels, width = adjoint_state.shape
    slots = owner_slot.shape[0]
    inner = rows - 2 * STEPS
    row_bytes = levels * width * 4
    f32 = lambda *shape: jax.ShapeDtypeStruct(shape, jnp.float32)
    vmem = pl.BlockSpec(memory_space=pltpu.VMEM)
    smem = pl.BlockSpec(memory_space=pltpu.SMEM)
    hbm = pl.BlockSpec(memory_space=pltpu.HBM)
    in_hbm = lambda value: pltpu.with_memory_space_constraint(value, pltpu.HBM)

    subs, hors = lax.axis_size("sub"), lax.axis_size("hor")
    small = [parent_cell, stencil_offset, stencil_weight]

    first_pack = pl.pallas_call(
        pack_kernel,
        in_specs=[hbm] * 6,
        out_specs=vmem,
        out_shape=f32(PACK_ROWS + 1, levels, width),
        scratch_shapes=[
            pltpu.VMEM((parts, STEPS, levels, width), jnp.float32),
            pltpu.VMEM((STEPS, levels, width), jnp.float32),
            pltpu.VMEM((STEPS, levels, width), jnp.float32),
        ]
        + [pltpu.VMEM(value.shape, value.dtype) for value in small]
        + [pltpu.SemaphoreType.DMA((levels // HALF, parts + 2)), pltpu.SemaphoreType.DMA((3,))],
        compiler_params=PARAMS,
        cost_estimate=BRIEF,
        name="pack",
    )(*[in_hbm(value) for value in [adjoint_state, courant_east, courant_north] + small])
    first_came = alternating(first_pack, -1)

    state, east, north = adjoint_state, courant_east, courant_north
    second_pack, middle, ends, columns = pl.pallas_call(
        sweep_kernel,
        in_specs=[vmem] * 3,
        out_specs=[vmem] * 4,
        out_shape=[
            f32(PACK_ROWS, levels, width),
            f32(parts, inner, levels, width),
            f32(parts, 2 * STEPS, levels, width),
            f32(parts, 2, rows, levels, LANES),
        ],
        scratch_shapes=[
            pltpu.VMEM((STEPS - 1, parts, rows, HALF, width), jnp.float32),
            pltpu.VMEM((rows, HALF, width), jnp.float32),
            pltpu.VMEM((rows, HALF, width), jnp.float32),
            pltpu.VMEM((rows, HALF, width), jnp.float32),
        ],
        compiler_params=PARAMS,
        cost_estimate=BRIEF,
        name="sweep",
    )(state, east, north)
    second_came = alternating(second_pack, 1)
    middle_came = to_previous(middle)

    mixing, base = pl.pallas_call(
        ghost_base_kernel,
        in_specs=[vmem] * 5,
        out_specs=[vmem] * 2,
        out_shape=[f32(parts, 2, rows, slots), f32(parts, levels, slots)],
        compiler_params=PARAMS,
        cost_estimate=BRIEF,
        name="ghost_base",
    )(*small, columns, north)

    column_shape = (parts, 2, 2 * (STEPS - 1), levels, LANES)
    side_a, a_columns = pl.pallas_call(
        mend_a_kernel,
        in_specs=[vmem] * 6,
        out_specs=[vmem] * 2,
        out_shape=[f32(parts, STEPS, levels, width), f32(*column_shape)],
        compiler_params=PARAMS,
        cost_estimate=BRIEF,
        name="mend_a",
    )(east, north, second_pack, first_came, ends, base)
    a_came = to_previous(side_a)
    total = pl.pallas_call(
        ghost_kernel,
        in_specs=[vmem] * 5,
        out_specs=vmem,
        out_shape=f32(parts, levels, slots),
        scratch_shapes=[pltpu.VMEM((parts, 2, rows, slots), jnp.float32)],
        compiler_params=PARAMS,
        cost_estimate=BRIEF,
        name="ghost",
    )(north, first_came, a_columns, mixing, base)
    order = rounds()
    total = total + exchanged(total, *order[0])
    side_b = pl.pallas_call(
        mend_b_kernel,
        in_specs=[vmem] * 5 + [pl.BlockSpec(memory_space=pl.ANY)] * 2,
        out_specs=vmem,
        out_shape=f32(parts, STEPS, levels, width),
        compiler_params=PARAMS,
        cost_estimate=BRIEF,
        name="mend_b",
    )(east, north, first_pack, second_came, ends, middle_came, total)
    b_came = to_previous(side_b)

    for each in order[1:-1]:
        total = total + exchanged(total, *each)
    came = exchanged(total, *order[-1])

    result = f32(*adjoint_state.shape)
    buffer = pltpu.VMEM((parts, rows, levels, width), jnp.float32)
    begun = pl.pallas_call(
        begin_kernel,
        in_specs=[vmem] * 3,
        out_specs=hbm,
        out_shape=result,
        scratch_shapes=[buffer, pltpu.SemaphoreType.DMA((2 * parts,))],
        compiler_params=PARAMS,
        cost_estimate=BRIEF,
        name="begin",
    )(state, middle_came, a_came)
    adjoint_result, boundary_gradient = pl.pallas_call(
        finish_kernel,
        in_specs=[hbm] + [vmem] * 5,
        out_specs=[hbm, vmem],
        out_shape=[result, f32(parts, levels // subs, slots // hors)],
        scratch_shapes=[buffer, pltpu.SemaphoreType.DMA((parts,))],
        input_output_aliases={0: 0},
        compiler_params=PARAMS,
        cost_estimate=BRIEF,
        name="finish",
    )(begun, state, b_came, owner_slot[None], total, came)
    return (adjoint_result, boundary_gradient)


def solution(mesh):
    in_specs = (
        P(("ens", "sub"), None, "hor", None, None),
        P(("ens", "sub"), "hor", None, None),
        P(("ens", "sub"), "hor", None, None),
        P(None, None, "hor"),
        P(None, None, None, "hor"),
        P(None, None, None, "hor"),
        P(),
    )
    out_specs = (P(("ens", "sub"), None, "hor", None, None), P("ens", "sub", "hor"))
    return jax.shard_map(local, mesh=mesh, in_specs=in_specs, out_specs=out_specs, check_vma=False)
```

```python
import functools

import jax
import jax.numpy as jnp
from jax import lax
from jax.experimental import pallas as pl
from jax.experimental.pallas import tpu as pltpu
from jax.sharding import PartitionSpec as P

STEPS = 4
HALF = 8
FLUX_ROWS = 2 * STEPS
PACK_ROWS = FLUX_ROWS + 3
LANES = 128
PIECE_ROWS = STEPS + 2
EXTRA = STEPS + 1
TARGETS = 4 * LANES
WEIGHTS = 5 * LANES


def to_previous(value):
    peers = lax.axis_size("sub")
    return lax.ppermute(value, "sub", [(i, (i - 1) % peers) for i in range(peers)])


def alternating(value, sign):
    subs, hors = lax.axis_size("sub"), lax.axis_size("hor")
    assert subs % 2 == 0
    pairs = []
    for s in range(subs):
        step = sign if s % 2 == 0 else -sign
        for h in range(hors):
            inside = 0 <= h + step < hors
            pairs.append((s * hors + h, s * hors + h + step if inside else (s ^ 1) * hors + h))
    return lax.ppermute(value, ("sub", "hor"), pairs)


def has_neighbour(flip):
    hor = lax.axis_index("hor")
    return jnp.where(flip == 1, hor < lax.axis_size("hor") - 1, hor > 0)


def rounds():
    subs, hors = lax.axis_size("sub"), lax.axis_size("hor")
    assert not subs & (subs - 1) and not hors & (hors - 1)
    order = [("sub", range(1, min(subs, 4)))]
    order += [("sub", [1 << n]) for n in range(2, subs.bit_length() - 1)]
    return order + [("hor", [1 << n]) for n in range(hors.bit_length() - 1)]


def exchanged(value, axis, distances):
    size = lax.axis_size(axis)
    return sum(lax.ppermute(value, axis, [(i, i ^ distance) for i in range(size)]) for distance in distances)


def parity():
    return lax.rem(lax.axis_index("sub"), 2)


def sign_of(flip):
    return jnp.where(flip == 1, jnp.float32(-1.0), jnp.float32(1.0))


def north_rates(north_rate):
    width = north_rate.shape[-1]
    column = lax.broadcasted_iota(jnp.int32, north_rate.shape, len(north_rate.shape) - 1)
    plus = jnp.where(column == 0, 0.0, jnp.maximum(north_rate, 0.0))
    minus = jnp.where(column == width - 1, 0.0, jnp.maximum(-north_rate, 0.0))
    return plus, minus


def shifted(flux_plus, flux_minus):
    width = flux_plus.shape[-1]
    axis = len(flux_plus.shape) - 1
    return pltpu.roll(flux_plus, width - 1, axis) + pltpu.roll(flux_minus, 1, axis)


class Row:
    def __init__(self, east_rate, north_rate=None):
        self.outward = jnp.maximum(east_rate, 0.0)
        self.inward = jnp.maximum(-east_rate, 0.0)
        if north_rate is not None:
            self.centre = 1.0 - jnp.abs(east_rate) - jnp.abs(north_rate)
            self.plus, self.minus = north_rates(north_rate)

    def stay(self, value):
        return self.centre * value + shifted(self.plus * value, self.minus * value)


class Pack:
    def __init__(self, *refs):
        self.refs = refs

    def flux(self, c, k, at):
        return self.refs[c][k, at, :] if len(self.refs) == 2 else self.refs[0][2 * k + c, at, :]

    def east(self, r, at):
        if len(self.refs) == 2:
            return self.refs[r][STEPS, at, :]
        return self.refs[0][FLUX_ROWS + 2 * r, at, :]

    def north(self, at):
        return self.refs[0][STEPS + 1 if len(self.refs) == 2 else FLUX_ROWS + 1, at, :]


def level_halves(levels, body):
    def step(h, carry):
        body(pl.ds(pl.multiple_of(h * HALF, HALF), HALF))
        return carry

    lax.fori_loop(0, levels // HALF, step, 0)


def end_fluxes(parts, sign, state, east, north, store):
    row = [Row(east(r) * sign, north(r)) for r in range(STEPS)]
    for c in range(parts):
        field = [state(c, r) for r in range(STEPS)]
        for k in range(STEPS):
            store(c, k, row[0].outward * field[0])
            after = []
            for r in range(STEPS - 1 - k):
                value = row[r].stay(field[r]) + row[r + 1].outward * field[r + 1]
                if r > 0:
                    value = value + row[r - 1].inward * field[r - 1]
                after.append(value)
            field = after


def pack_kernel(
    state_hbm, east_hbm, north_hbm, cell_hbm, offset_hbm, weight_hbm,
    piece_0, piece_1, state_ref, east_ref, north_ref, cell_ref, offset_ref, weight_ref, sems, small_sems,
):
    parts, rows, levels, width = state_hbm.shape[1:]
    flip = parity()
    sign = sign_of(flip)
    at_end = pl.ds(flip * (rows - STEPS), STEPS)
    place = lambda r: r + flip * (STEPS - 1 - 2 * r)
    halves = levels // HALF
    copies = []
    for h in range(halves):
        at = pl.ds(h * HALF, HALF)
        sem = sems.at[h]
        batch = [
            pltpu.make_async_copy(state_hbm.at[0, c, at_end, at], state_ref.at[c, :, at], sem.at[c])
            for c in range(parts)
        ]
        batch.append(pltpu.make_async_copy(east_hbm.at[0, at_end, at], east_ref.at[:, at], sem.at[parts]))
        batch.append(pltpu.make_async_copy(north_hbm.at[0, at_end, at], north_ref.at[:, at], sem.at[parts + 1]))
        copies.append(batch)
        for copy in batch:
            copy.start()
    small = [
        pltpu.make_async_copy(source, target, small_sems.at[n])
        for n, (source, target) in enumerate(
            ((cell_hbm, cell_ref), (offset_hbm, offset_ref), (weight_hbm, weight_ref))
        )
    ]
    for copy in small:
        copy.start()

    def half(at):
        piece_0[STEPS, at, :] = east_ref[place(0), at, :]
        piece_0[STEPS + 1, at, :] = north_ref[place(0), at, :]
        piece_1[STEPS, at, :] = east_ref[place(1), at, :]
        for r in (1, 2):
            lanes = (2 * r - 2) * LANES
            piece_1[EXTRA, at, lanes:lanes + LANES] = north_ref[place(r), at, :LANES]
            piece_1[EXTRA, at, lanes + LANES:lanes + 2 * LANES] = north_ref[place(r), at, width - LANES:]

        def store(c, k, value):
            (piece_0, piece_1)[c][k, at, :] = value

        end_fluxes(
            parts, sign,
            lambda c, r: state_ref[c, place(r), at, :],
            lambda r: east_ref[place(r), at, :],
            lambda r: north_ref[place(r), at, :],
            store,
        )

    for h in range(halves):
        for copy in copies[h]:
            copy.wait()
        half(pl.ds(h * HALF, HALF))

    for copy in small:
        copy.wait()
    n = 0
    for point in range(offset_ref.shape[0]):
        for c in range(parts):
            target = (cell_ref[c] + offset_ref[point, c]).astype(jnp.float32)
            piece_1[EXTRA, n:n + 2, TARGETS:TARGETS + rows] = target
            piece_1[EXTRA, n:n + 2, WEIGHTS:WEIGHTS + rows] = weight_ref[point, c]
            n += 2


def second_pack_kernel(state_ref, east_ref, north_ref, _, pack_ref):
    parts, rows, levels = state_ref.shape[1:4]
    flip = 1 - parity()
    sign = sign_of(flip)
    place = lambda r: r + flip * (rows - 1 - 2 * r)

    def half(at):
        pack_ref[FLUX_ROWS, at, :] = east_ref[0, place(0), at, :]
        pack_ref[FLUX_ROWS + 1, at, :] = north_ref[0, place(0), at, :]
        pack_ref[FLUX_ROWS + 2, at, :] = east_ref[0, place(1), at, :]

        def store(c, k, value):
            pack_ref[2 * k + c, at, :] = value

        end_fluxes(
            parts, sign,
            lambda c, r: state_ref[0, c, place(r), at, :],
            lambda r: east_ref[0, place(r), at, :],
            lambda r: north_ref[0, place(r), at, :],
            store,
        )

    level_halves(levels, half)


def as_column(row):
    count = row.shape[1]
    here = lax.broadcasted_iota(jnp.int32, (count, count), 0)
    there = lax.broadcasted_iota(jnp.int32, (count, count), 1)
    return jnp.sum(jnp.where(here == there, row, 0), axis=1, keepdims=True)


def sweep_kernel(
    state_ref, east_ref, north_ref, _, middle_ref, ends_ref, column_ref,
    field, plus_ref, minus_ref, centre_ref,
):
    parts, rows, levels, width = state_ref.shape[1:]

    def half(at):
        for k in range(STEPS):
            if k == 0:
                read = lambda c, i: state_ref[0, c, i, at, :]
            else:
                read = lambda c, i, slot=k - 1: field[slot, c, i]
            west = [None] * parts
            here = [read(c, 0) for c in range(parts)]
            east_here = east_ref[0, 0, at, :]
            for i in range(rows):
                leave_west = jnp.maximum(-east_here, 0.0)
                if k == 0:
                    north_rate = north_ref[0, i, at, :]
                    centre = 1.0 - jnp.abs(east_here) - jnp.abs(north_rate)
                    plus, minus = north_rates(north_rate)
                    centre_ref[i], plus_ref[i], minus_ref[i] = centre, plus, minus
                else:
                    centre, plus, minus = centre_ref[i], plus_ref[i], minus_ref[i]
                if i + 1 < rows:
                    east_here = east_ref[0, i + 1, at, :]
                    east_after = jnp.maximum(east_here, 0.0)
                for c in range(parts):
                    value = here[c]
                    total = centre * value + shifted(plus * value, minus * value)
                    if i > 0:
                        total = total + west[c]
                    if i + 1 < rows:
                        west[c] = leave_west * value
                        here[c] = read(c, i + 1)
                        total = total + east_after * here[c]
                    if k < STEPS - 1:
                        field[k, c, i] = total
                    elif i < STEPS:
                        ends_ref[c, i, at, :] = total
                    elif i >= rows - STEPS:
                        ends_ref[c, i - rows + 2 * STEPS, at, :] = total
                    else:
                        middle_ref[c, i - STEPS, at, :] = total

        def columns(i, carry):
            for c in range(parts):
                value = state_ref[0, c, i, at, :]
                first, last = value[:, :LANES], value[:, width - LANES:]
                for slot in range(STEPS - 1):
                    first = first + field[slot, c, i, :, :LANES]
                    last = last + field[slot, c, i, :, width - LANES:]
                column_ref[c, 0, i, at, :] = first
                column_ref[c, 1, i, at, :] = last
            return carry

        lax.fori_loop(0, rows, columns, 0, unroll=2)

    level_halves(levels, half)


def mix(targets, weights, cells, total):
    for target, weight in zip(targets, weights):
        total = total + jnp.where(as_column(target) == cells, as_column(weight), 0.0)
    return total


def ghost_base_kernel(
    cell_ref, offset_ref, weight_ref, column_ref, north_ref, mixing_ref, partial_ref
):
    parts, _, rows, levels, _ = column_ref.shape
    slots = mixing_ref.shape[-1]
    width = north_ref.shape[-1]
    points = range(offset_ref.shape[0])
    cells = lax.broadcasted_iota(jnp.int32, (rows, slots), 1)
    for c in range(parts):
        for s in range(2):
            mixing_ref[c, s] = mix(
                [cell_ref[c, s:s + 1, :] + offset_ref[point, c, s:s + 1, :] for point in points],
                [weight_ref[point, c, s:s + 1, :] for point in points],
                cells, jnp.zeros((rows, slots), jnp.float32),
            )

    for c in range(parts):
        total = jnp.zeros((levels, slots), jnp.float32)
        for i in range(rows):
            south = jnp.maximum(north_ref[0, i, :, :1], 0.0) * column_ref[c, 0, i, :, :1]
            north = jnp.maximum(-north_ref[0, i, :, width - 1:], 0.0) * column_ref[c, 1, i, :, LANES - 1:]
            total = total + south * mixing_ref[c, 0, i:i + 1, :]
            total = total + north * mixing_ref[c, 1, i:i + 1, :]
        partial_ref[c] = total


def ghost_kernel(north_ref, other_0, other_1, column_ref, mixing_ref, partial_ref, sum_ref, near_mixing):
    parts, levels, slots = partial_ref.shape
    rows = mixing_ref.shape[2]
    width = north_ref.shape[-1]
    flip = 1 - parity()
    cells = lax.broadcasted_iota(jnp.int32, (rows, slots), 1).astype(jnp.float32)
    points = (WEIGHTS - TARGETS) // LANES * 4
    for c in range(parts):
        for s in range(2):
            at = [(point * parts + c) * 2 + s for point in range(points)]
            near_mixing[c, s] = mix(
                [other_1[EXTRA, n:n + 1, TARGETS:TARGETS + rows] for n in at],
                [other_1[EXTRA, n:n + 1, WEIGHTS:WEIGHTS + rows] for n in at],
                cells, jnp.zeros((rows, slots), jnp.float32),
            )
    for c in range(parts):
        total = partial_ref[c]
        for r in range(STEPS - 1):
            i = r + flip * (rows - 1 - 2 * r)
            south = jnp.maximum(north_ref[0, i, :, :1], 0.0) * column_ref[c, 0, r, :, :1]
            north = jnp.maximum(-north_ref[0, i, :, width - 1:], 0.0) * column_ref[c, 1, r, :, LANES - 1:]
            total = total + south * mixing_ref[c, 0, pl.ds(i, 1), :]
            total = total + north * mixing_ref[c, 1, pl.ds(i, 1), :]
            i = r + (1 - flip) * (rows - 1 - 2 * r)
            if r == 0:
                first_rate = other_0[STEPS + 1, :, :LANES]
                last_rate = other_0[STEPS + 1, :, width - LANES:]
            else:
                lanes = (2 * r - 2) * LANES
                first_rate = other_1[EXTRA, :, lanes:lanes + LANES]
                last_rate = other_1[EXTRA, :, lanes + LANES:lanes + 2 * LANES]
            south = jnp.maximum(first_rate[:, :1], 0.0) * column_ref[c, 0, STEPS - 1 + r, :, :1]
            north = jnp.maximum(-last_rate[:, LANES - 1:], 0.0) * column_ref[c, 1, STEPS - 1 + r, :, LANES - 1:]
            total = total + south * near_mixing[c, 0, pl.ds(i, 1), :]
            total = total + north * near_mixing[c, 1, pl.ds(i, 1), :]
        sum_ref[c] = jnp.where(has_neighbour(flip), total, partial_ref[c])


def mend_side(flip, east_ref, north_ref, mine_pack, other_pack, store, store_column):
    levels, width = east_ref.shape[2:]
    rows = east_ref.shape[1]
    sign = sign_of(flip)
    place = lambda r: flip * (rows - STEPS) + r + flip * (STEPS - 1 - 2 * r)

    def half(at):
        own = [Row(east_ref[0, place(r), at, :] * sign, north_ref[0, place(r), at, :]) for r in range(STEPS - 1)]
        near = Row(other_pack.east(0, at) * sign, other_pack.north(at))
        far_east = other_pack.east(1, at)
        far = Row(far_east * sign)
        for c in range(FLUX_ROWS // STEPS):
            mine = lambda k: mine_pack.flux(c, k, at)
            theirs = lambda k: other_pack.flux(c, k, at)
            a0 = theirs(0)
            n1 = mine(0)
            b0 = own[0].stay(a0) + near.inward * n1 + theirs(1)
            b1 = own[0].inward * a0
            bn1 = near.stay(n1) + own[0].outward * a0 + mine(1)
            bn2 = near.outward * n1
            c0 = own[0].stay(b0) + near.inward * bn1 + own[1].outward * b1 + theirs(2)
            c1 = own[1].stay(b1) + own[0].inward * b0
            c2 = own[1].inward * b1
            cn1 = near.stay(bn1) + own[0].outward * b0 + far.inward * bn2 + mine(2)
            d0 = own[0].stay(c0) + near.inward * cn1 + own[1].outward * c1 + theirs(3)
            d1 = own[1].stay(c1) + own[0].inward * c0 + own[2].outward * c2
            d2 = own[2].stay(c2) + own[1].inward * c1
            d3 = own[2].inward * c2
            for r, value in enumerate((d0, d1, d2, d3)):
                store(c, r, at, value)
            if store_column is not None:
                tiles = (slice(0, LANES), slice(width - LANES, width))
                for s, lanes in enumerate(tiles):
                    tile = lambda value: value[:, lanes]
                    rate = other_pack.refs[1][EXTRA, at, s * LANES:(s + 1) * LANES]
                    stays = 1.0 - jnp.abs(far_east[:, lanes]) - jnp.abs(rate)
                    drift = jnp.maximum(rate if s == 0 else -rate, 0.0) * tile(bn2)
                    cn2 = stays * tile(bn2) + pltpu.roll(drift, LANES - 1 if s == 0 else 1, 1)
                    cn2 = cn2 + tile(near.outward) * tile(bn1)
                    cn3 = tile(far.outward) * tile(bn2)
                    sums = (
                        tile(a0) + tile(b0) + tile(c0), tile(b1) + tile(c1), tile(c2),
                        tile(n1) + tile(bn1) + tile(cn1), tile(bn2) + cn2, cn3,
                    )
                    for r, value in enumerate(sums):
                        store_column(c, s, r, at, value)

    level_halves(levels, half)


def copy_end(flip, ends_ref, out_ref):
    for c in range(out_ref.shape[0]):
        for r in range(STEPS):
            out_ref[c, r] = ends_ref[c, flip * STEPS + r]


def mend_a_kernel(east_ref, north_ref, mine_ref, other_0, other_1, ends_ref, base_ref, out_ref, column_ref):
    flip = 1 - parity()
    turn = lambda r: r + flip * (STEPS - 1 - 2 * r)

    def store(c, r, at, value):
        out_ref[c, turn(r), at, :] = ends_ref[c, flip * STEPS + turn(r), at, :] + value

    def store_column(c, s, r, at, value):
        column_ref[c, s, r, at, :] = value

    @pl.when(has_neighbour(flip))
    def _():
        mend_side(flip, east_ref, north_ref, Pack(mine_ref), Pack(other_0, other_1), store, store_column)

    @pl.when(jnp.logical_not(has_neighbour(flip)))
    def _():
        column_ref[...] = jnp.zeros_like(column_ref)
        copy_end(flip, ends_ref, out_ref)


def mend_b_kernel(east_ref, north_ref, mine_0, mine_1, other_ref, ends_ref, _, __, out_ref):
    flip = parity()
    turn = lambda r: r + flip * (STEPS - 1 - 2 * r)

    def store(c, r, at, value):
        out_ref[c, turn(r), at, :] = ends_ref[c, flip * STEPS + turn(r), at, :] + value

    @pl.when(has_neighbour(flip))
    def _():
        mend_side(flip, east_ref, north_ref, Pack(mine_0, mine_1), Pack(other_ref), store, None)

    @pl.when(jnp.logical_not(has_neighbour(flip)))
    def _():
        copy_end(flip, ends_ref, out_ref)


def subtract_rows(state_ref, out_hbm, buffer, sems, jobs):
    copies = []
    is_last = lax.axis_index("sub") == lax.axis_size("sub") - 1
    for start, other in jobs:
        for c in range(other.shape[0]):
            count = other.shape[1]
            for r in range(count):
                buffer[c, start + r] = state_ref[0, c, start + r] - jnp.where(is_last, 0.0, other[c, r])
            at = pl.ds(start, count)
            copy = pltpu.make_async_copy(buffer.at[c, at], out_hbm.at[0, c, at], sems.at[len(copies)])
            copy.start()
            copies.append(copy)
    return copies


def begin_kernel(state_ref, middle_ref, a_ref, out_hbm, buffer, sems):
    start = parity() * (state_ref.shape[2] - STEPS)
    for copy in subtract_rows(state_ref, out_hbm, buffer, sems, ((STEPS, middle_ref), (start, a_ref))):
        copy.wait()


def finish_kernel(
    begun_hbm, state_ref, b_ref, owner_ref, total_ref, came_ref, out_hbm, gradient_ref, buffer, sems
):
    parts = b_ref.shape[0]
    start = (1 - parity()) * (state_ref.shape[2] - STEPS)
    copies = subtract_rows(state_ref, out_hbm, buffer, sems, ((start, b_ref),))

    share, mine = gradient_ref.shape[1:]
    start = lax.axis_index("hor") * mine
    chosen = []
    for c in range(parts):
        total = total_ref[c] + came_ref[c]
        block = total[:share]
        for s in range(1, total.shape[0] // share):
            block = jnp.where(lax.axis_index("sub") == s, total[s * share:(s + 1) * share], block)
        chosen.append(block)
    chosen = jnp.concatenate(chosen, 0)
    column = lax.broadcasted_iota(jnp.int32, (parts * share, mine), 1)
    picked = jnp.zeros((parts * share, mine), jnp.float32)
    for q in range(mine):
        value = jnp.sum(jnp.where(owner_ref[...] == start + q, chosen, 0.0), axis=1, keepdims=True)
        picked = jnp.where(column == q, value, picked)
    for c in range(parts):
        gradient_ref[c] = picked[c * share:(c + 1) * share]
    for copy in copies:
        copy.wait()


BRIEF = pl.CostEstimate(flops=1, bytes_accessed=1, transcendentals=0)
LONG = pl.CostEstimate(flops=1, bytes_accessed=1 << 26, transcendentals=0)
PARAMS = pltpu.CompilerParams(vmem_limit_bytes=24 * 1024 * 1024)


def local(
    adjoint_state,
    courant_east,
    courant_north,
    parent_cell,
    stencil_offset,
    stencil_weight,
    owner_slot,
):
    _, parts, rows, levels, width = adjoint_state.shape
    slots = owner_slot.shape[0]
    inner = rows - 2 * STEPS
    row_bytes = levels * width * 4
    f32 = lambda *shape: jax.ShapeDtypeStruct(shape, jnp.float32)
    vmem = pl.BlockSpec(memory_space=pltpu.VMEM)
    smem = pl.BlockSpec(memory_space=pltpu.SMEM)
    hbm = pl.BlockSpec(memory_space=pltpu.HBM)
    in_hbm = lambda value: pltpu.with_memory_space_constraint(value, pltpu.HBM)

    subs, hors = lax.axis_size("sub"), lax.axis_size("hor")
    small = [parent_cell, stencil_offset, stencil_weight]

    first_pack = pl.pallas_call(
        pack_kernel,
        in_specs=[hbm] * 6,
        out_specs=[vmem] * 2,
        out_shape=[f32(PIECE_ROWS, levels, width)] * 2,
        scratch_shapes=[
            pltpu.VMEM((parts, STEPS, levels, width), jnp.float32),
            pltpu.VMEM((STEPS, levels, width), jnp.float32),
            pltpu.VMEM((STEPS, levels, width), jnp.float32),
        ]
        + [pltpu.VMEM(value.shape, value.dtype) for value in small]
        + [pltpu.SemaphoreType.DMA((levels // HALF, parts + 2)), pltpu.SemaphoreType.DMA((3,))],
        compiler_params=PARAMS,
        cost_estimate=BRIEF,
        name="pack",
    )(*[in_hbm(value) for value in [adjoint_state, courant_east, courant_north] + small])
    first_came = [alternating(piece, -1) for piece in first_pack]

    state, east, north = adjoint_state, courant_east, courant_north
    after = pl.BlockSpec(memory_space=pl.ANY)
    second_pack = pl.pallas_call(
        second_pack_kernel,
        in_specs=[vmem] * 3 + [after],
        out_specs=vmem,
        out_shape=f32(PACK_ROWS, levels, width),
        compiler_params=PARAMS,
        cost_estimate=BRIEF,
        name="second_pack",
    )(state, east, north, first_pack[0])
    second_came = alternating(second_pack, 1)
    middle, ends, columns = pl.pallas_call(
        sweep_kernel,
        in_specs=[vmem] * 3 + [after],
        out_specs=[vmem] * 3,
        out_shape=[
            f32(parts, inner, levels, width),
            f32(parts, 2 * STEPS, levels, width),
            f32(parts, 2, rows, levels, LANES),
        ],
        scratch_shapes=[
            pltpu.VMEM((STEPS - 1, parts, rows, HALF, width), jnp.float32),
            pltpu.VMEM((rows, HALF, width), jnp.float32),
            pltpu.VMEM((rows, HALF, width), jnp.float32),
            pltpu.VMEM((rows, HALF, width), jnp.float32),
        ],
        compiler_params=PARAMS,
        cost_estimate=LONG,
        name="sweep",
    )(state, east, north, second_pack)
    middle_came = to_previous(middle)

    mixing, base = pl.pallas_call(
        ghost_base_kernel,
        in_specs=[vmem] * 5,
        out_specs=[vmem] * 2,
        out_shape=[f32(parts, 2, rows, slots), f32(parts, levels, slots)],
        compiler_params=PARAMS,
        cost_estimate=BRIEF,
        name="ghost_base",
    )(*small, columns, north)

    column_shape = (parts, 2, 2 * (STEPS - 1), levels, LANES)
    side_a, a_columns = pl.pallas_call(
        mend_a_kernel,
        in_specs=[vmem] * 7,
        out_specs=[vmem] * 2,
        out_shape=[f32(parts, STEPS, levels, width), f32(*column_shape)],
        compiler_params=PARAMS,
        cost_estimate=BRIEF,
        name="mend_a",
    )(east, north, second_pack, *first_came, ends, base)
    a_came = to_previous(side_a)
    total = pl.pallas_call(
        ghost_kernel,
        in_specs=[vmem] * 6,
        out_specs=vmem,
        out_shape=f32(parts, levels, slots),
        scratch_shapes=[pltpu.VMEM((parts, 2, rows, slots), jnp.float32)],
        compiler_params=PARAMS,
        cost_estimate=BRIEF,
        name="ghost",
    )(north, *first_came, a_columns, mixing, base)
    order = rounds()
    total = total + exchanged(total, *order[0])
    side_b = pl.pallas_call(
        mend_b_kernel,
        in_specs=[vmem] * 6 + [pl.BlockSpec(memory_space=pl.ANY)] * 2,
        out_specs=vmem,
        out_shape=f32(parts, STEPS, levels, width),
        compiler_params=PARAMS,
        cost_estimate=BRIEF,
        name="mend_b",
    )(east, north, *first_pack, second_came, ends, middle_came, total)
    b_came = to_previous(side_b)

    for each in order[1:-1]:
        total = total + exchanged(total, *each)
    came = exchanged(total, *order[-1])

    result = f32(*adjoint_state.shape)
    buffer = pltpu.VMEM((parts, rows, levels, width), jnp.float32)
    begun = pl.pallas_call(
        begin_kernel,
        in_specs=[vmem] * 3,
        out_specs=hbm,
        out_shape=result,
        scratch_shapes=[buffer, pltpu.SemaphoreType.DMA((2 * parts,))],
        compiler_params=PARAMS,
        cost_estimate=BRIEF,
        name="begin",
    )(state, middle_came, a_came)
    adjoint_result, boundary_gradient = pl.pallas_call(
        finish_kernel,
        in_specs=[hbm] + [vmem] * 5,
        out_specs=[hbm, vmem],
        out_shape=[result, f32(parts, levels // subs, slots // hors)],
        scratch_shapes=[buffer, pltpu.SemaphoreType.DMA((parts,))],
        input_output_aliases={0: 0},
        compiler_params=PARAMS,
        cost_estimate=BRIEF,
        name="finish",
    )(begun, state, b_came, owner_slot[None], total, came)
    return (adjoint_result, boundary_gradient)


def solution(mesh):
    in_specs = (
        P(("ens", "sub"), None, "hor", None, None),
        P(("ens", "sub"), "hor", None, None),
        P(("ens", "sub"), "hor", None, None),
        P(None, None, "hor"),
        P(None, None, None, "hor"),
        P(None, None, None, "hor"),
        P(),
    )
    out_specs = (P(("ens", "sub"), None, "hor", None, None), P("ens", "sub", "hor"))
    return jax.shard_map(local, mesh=mesh, in_specs=in_specs, out_specs=out_specs, check_vma=False)
```

```python
import functools

import jax
import jax.numpy as jnp
from jax import lax
from jax.experimental import pallas as pl
from jax.experimental.pallas import tpu as pltpu
from jax.sharding import PartitionSpec as P

STEPS = 4
HALF = 8
FLUX_ROWS = 2 * STEPS
PACK_ROWS = FLUX_ROWS + 3
LANES = 128
EXTRA = PACK_ROWS
TARGETS = 4 * LANES
WEIGHTS = 5 * LANES


def to_previous(value):
    peers = lax.axis_size("sub")
    return lax.ppermute(value, "sub", [(i, (i - 1) % peers) for i in range(peers)])


def alternating(value, sign):
    subs, hors = lax.axis_size("sub"), lax.axis_size("hor")
    assert subs % 2 == 0
    pairs = []
    for s in range(subs):
        step = sign if s % 2 == 0 else -sign
        for h in range(hors):
            inside = 0 <= h + step < hors
            pairs.append((s * hors + h, s * hors + h + step if inside else (s ^ 1) * hors + h))
    return lax.ppermute(value, ("sub", "hor"), pairs)


def has_neighbour(flip):
    hor = lax.axis_index("hor")
    return jnp.where(flip == 1, hor < lax.axis_size("hor") - 1, hor > 0)


def rounds():
    subs, hors = lax.axis_size("sub"), lax.axis_size("hor")
    assert not subs & (subs - 1) and not hors & (hors - 1)
    order = [("sub", range(1, min(subs, 4)))]
    order += [("sub", [1 << n]) for n in range(2, subs.bit_length() - 1)]
    return order + [("hor", [1 << n]) for n in range(hors.bit_length() - 1)]


def exchanged(value, axis, distances):
    size = lax.axis_size(axis)
    return sum(lax.ppermute(value, axis, [(i, i ^ distance) for i in range(size)]) for distance in distances)


def parity():
    return lax.rem(lax.axis_index("sub"), 2)


def sign_of(flip):
    return jnp.where(flip == 1, jnp.float32(-1.0), jnp.float32(1.0))


def north_rates(north_rate):
    width = north_rate.shape[-1]
    column = lax.broadcasted_iota(jnp.int32, north_rate.shape, len(north_rate.shape) - 1)
    plus = jnp.where(column == 0, 0.0, jnp.maximum(north_rate, 0.0))
    minus = jnp.where(column == width - 1, 0.0, jnp.maximum(-north_rate, 0.0))
    return plus, minus


def shifted(flux_plus, flux_minus):
    width = flux_plus.shape[-1]
    axis = len(flux_plus.shape) - 1
    return pltpu.roll(flux_plus, width - 1, axis) + pltpu.roll(flux_minus, 1, axis)


class Row:
    def __init__(self, east_rate, north_rate=None):
        self.outward = jnp.maximum(east_rate, 0.0)
        self.inward = jnp.maximum(-east_rate, 0.0)
        if north_rate is not None:
            self.centre = 1.0 - jnp.abs(east_rate) - jnp.abs(north_rate)
            self.plus, self.minus = north_rates(north_rate)

    def stay(self, value):
        return self.centre * value + shifted(self.plus * value, self.minus * value)


def level_halves(levels, body):
    def step(h, carry):
        body(pl.ds(pl.multiple_of(h * HALF, HALF), HALF))
        return carry

    lax.fori_loop(0, levels // HALF, step, 0)


def pack_kernel(
    state_hbm, east_hbm, north_hbm, cell_hbm, offset_hbm, weight_hbm,
    pack_ref, state_ref, east_ref, north_ref, cell_ref, offset_ref, weight_ref, sems, small_sems,
):
    parts, rows, levels, width = state_hbm.shape[1:]
    flip = parity()
    sign = sign_of(flip)
    at_end = pl.ds(flip * (rows - STEPS), STEPS)
    place = lambda r: r + flip * (STEPS - 1 - 2 * r)
    halves = levels // HALF
    copies = []
    for h in range(halves):
        at = pl.ds(h * HALF, HALF)
        sem = sems.at[h]
        batch = [
            pltpu.make_async_copy(state_hbm.at[0, c, at_end, at], state_ref.at[c, :, at], sem.at[c])
            for c in range(parts)
        ]
        batch.append(pltpu.make_async_copy(east_hbm.at[0, at_end, at], east_ref.at[:, at], sem.at[parts]))
        batch.append(pltpu.make_async_copy(north_hbm.at[0, at_end, at], north_ref.at[:, at], sem.at[parts + 1]))
        copies.append(batch)
        for copy in batch:
            copy.start()
    small = [
        pltpu.make_async_copy(source, target, small_sems.at[n])
        for n, (source, target) in enumerate(
            ((cell_hbm, cell_ref), (offset_hbm, offset_ref), (weight_hbm, weight_ref))
        )
    ]
    for copy in small:
        copy.start()

    def half(at):
        row = [Row(east_ref[place(r), at, :] * sign, north_ref[place(r), at, :]) for r in range(STEPS)]
        pack_ref[FLUX_ROWS, at, :] = east_ref[place(0), at, :]
        pack_ref[FLUX_ROWS + 1, at, :] = north_ref[place(0), at, :]
        pack_ref[FLUX_ROWS + 2, at, :] = east_ref[place(1), at, :]
        for r in (1, 2):
            lanes = (2 * r - 2) * LANES
            pack_ref[EXTRA, at, lanes:lanes + LANES] = north_ref[place(r), at, :LANES]
            pack_ref[EXTRA, at, lanes + LANES:lanes + 2 * LANES] = north_ref[place(r), at, width - LANES:]
        for c in range(parts):
            field = [state_ref[c, place(r), at, :] for r in range(STEPS)]
            for k in range(STEPS):
                pack_ref[2 * k + c, at, :] = row[0].outward * field[0]
                after = []
                for r in range(STEPS - 1 - k):
                    value = row[r].stay(field[r]) + row[r + 1].outward * field[r + 1]
                    if r > 0:
                        value = value + row[r - 1].inward * field[r - 1]
                    after.append(value)
                field = after

    for h in range(halves):
        for copy in copies[h]:
            copy.wait()
        half(pl.ds(h * HALF, HALF))

    for copy in small:
        copy.wait()
    n = 0
    for point in range(offset_ref.shape[0]):
        for c in range(parts):
            target = (cell_ref[c] + offset_ref[point, c]).astype(jnp.float32)
            pack_ref[EXTRA, n:n + 2, TARGETS:TARGETS + rows] = target
            pack_ref[EXTRA, n:n + 2, WEIGHTS:WEIGHTS + rows] = weight_ref[point, c]
            n += 2


def as_column(row):
    count = row.shape[1]
    here = lax.broadcasted_iota(jnp.int32, (count, count), 0)
    there = lax.broadcasted_iota(jnp.int32, (count, count), 1)
    return jnp.sum(jnp.where(here == there, row, 0), axis=1, keepdims=True)


def sweep_kernel(
    state_ref, east_ref, north_ref, pack_ref, middle_ref, ends_ref, column_ref,
    field, plus_ref, minus_ref, centre_ref,
):
    parts, rows, levels, width = state_ref.shape[1:]
    flip = 1 - parity()
    sign = sign_of(flip)
    end_row = flip * (rows - 1)
    next_row = end_row + 1 - 2 * flip

    def half(at):
        pack_ref[FLUX_ROWS, at, :] = east_ref[0, end_row, at, :]
        pack_ref[FLUX_ROWS + 1, at, :] = north_ref[0, end_row, at, :]
        pack_ref[FLUX_ROWS + 2, at, :] = east_ref[0, next_row, at, :]

        for k in range(STEPS):
            if k == 0:
                read = lambda c, i: state_ref[0, c, i, at, :]
            else:
                read = lambda c, i, slot=k - 1: field[slot, c, i]
            leaving = jnp.maximum(east_ref[0, end_row, at, :] * sign, 0.0)
            for c in range(parts):
                pack_ref[2 * k + c, at, :] = leaving * read(c, end_row)
            west = [None] * parts
            here = [read(c, 0) for c in range(parts)]
            east_here = east_ref[0, 0, at, :]
            for i in range(rows):
                leave_west = jnp.maximum(-east_here, 0.0)
                if k == 0:
                    north_rate = north_ref[0, i, at, :]
                    centre = 1.0 - jnp.abs(east_here) - jnp.abs(north_rate)
                    plus, minus = north_rates(north_rate)
                    centre_ref[i], plus_ref[i], minus_ref[i] = centre, plus, minus
                else:
                    centre, plus, minus = centre_ref[i], plus_ref[i], minus_ref[i]
                if i + 1 < rows:
                    east_here = east_ref[0, i + 1, at, :]
                    east_after = jnp.maximum(east_here, 0.0)
                for c in range(parts):
                    value = here[c]
                    total = centre * value + shifted(plus * value, minus * value)
                    if i > 0:
                        total = total + west[c]
                    if i + 1 < rows:
                        west[c] = leave_west * value
                        here[c] = read(c, i + 1)
                        total = total + east_after * here[c]
                    if k < STEPS - 1:
                        field[k, c, i] = total
                    elif i < STEPS:
                        ends_ref[c, i, at, :] = total
                    elif i >= rows - STEPS:
                        ends_ref[c, i - rows + 2 * STEPS, at, :] = total
                    else:
                        middle_ref[c, i - STEPS, at, :] = total

        def columns(i, carry):
            for c in range(parts):
                value = state_ref[0, c, i, at, :]
                first, last = value[:, :LANES], value[:, width - LANES:]
                for slot in range(STEPS - 1):
                    first = first + field[slot, c, i, :, :LANES]
                    last = last + field[slot, c, i, :, width - LANES:]
                column_ref[c, 0, i, at, :] = first
                column_ref[c, 1, i, at, :] = last
            return carry

        lax.fori_loop(0, rows, columns, 0, unroll=2)

    level_halves(levels, half)


def mix(targets, weights, cells, total):
    for target, weight in zip(targets, weights):
        total = total + jnp.where(as_column(target) == cells, as_column(weight), 0.0)
    return total


def ghost_base_kernel(
    cell_ref, offset_ref, weight_ref, column_ref, north_ref, mixing_ref, partial_ref
):
    parts, _, rows, levels, _ = column_ref.shape
    slots = mixing_ref.shape[-1]
    width = north_ref.shape[-1]
    points = range(offset_ref.shape[0])
    cells = lax.broadcasted_iota(jnp.int32, (rows, slots), 1)
    for c in range(parts):
        for s in range(2):
            mixing_ref[c, s] = mix(
                [cell_ref[c, s:s + 1, :] + offset_ref[point, c, s:s + 1, :] for point in points],
                [weight_ref[point, c, s:s + 1, :] for point in points],
                cells, jnp.zeros((rows, slots), jnp.float32),
            )

    for c in range(parts):
        total = jnp.zeros((levels, slots), jnp.float32)
        for i in range(rows):
            south = jnp.maximum(north_ref[0, i, :, :1], 0.0) * column_ref[c, 0, i, :, :1]
            north = jnp.maximum(-north_ref[0, i, :, width - 1:], 0.0) * column_ref[c, 1, i, :, LANES - 1:]
            total = total + south * mixing_ref[c, 0, i:i + 1, :]
            total = total + north * mixing_ref[c, 1, i:i + 1, :]
        partial_ref[c] = total


def ghost_kernel(north_ref, other_ref, column_ref, mixing_ref, partial_ref, sum_ref, near_mixing):
    parts, levels, slots = partial_ref.shape
    rows = mixing_ref.shape[2]
    width = north_ref.shape[-1]
    flip = 1 - parity()
    cells = lax.broadcasted_iota(jnp.int32, (rows, slots), 1).astype(jnp.float32)
    points = (WEIGHTS - TARGETS) // LANES * 4
    for c in range(parts):
        for s in range(2):
            at = [(point * parts + c) * 2 + s for point in range(points)]
            near_mixing[c, s] = mix(
                [other_ref[EXTRA, n:n + 1, TARGETS:TARGETS + rows] for n in at],
                [other_ref[EXTRA, n:n + 1, WEIGHTS:WEIGHTS + rows] for n in at],
                cells, jnp.zeros((rows, slots), jnp.float32),
            )
    for c in range(parts):
        total = partial_ref[c]
        for r in range(STEPS - 1):
            i = r + flip * (rows - 1 - 2 * r)
            south = jnp.maximum(north_ref[0, i, :, :1], 0.0) * column_ref[c, 0, r, :, :1]
            north = jnp.maximum(-north_ref[0, i, :, width - 1:], 0.0) * column_ref[c, 1, r, :, LANES - 1:]
            total = total + south * mixing_ref[c, 0, pl.ds(i, 1), :]
            total = total + north * mixing_ref[c, 1, pl.ds(i, 1), :]
            i = r + (1 - flip) * (rows - 1 - 2 * r)
            if r == 0:
                first_rate = other_ref[FLUX_ROWS + 1, :, :LANES]
                last_rate = other_ref[FLUX_ROWS + 1, :, width - LANES:]
            else:
                lanes = (2 * r - 2) * LANES
                first_rate = other_ref[EXTRA, :, lanes:lanes + LANES]
                last_rate = other_ref[EXTRA, :, lanes + LANES:lanes + 2 * LANES]
            south = jnp.maximum(first_rate[:, :1], 0.0) * column_ref[c, 0, STEPS - 1 + r, :, :1]
            north = jnp.maximum(-last_rate[:, LANES - 1:], 0.0) * column_ref[c, 1, STEPS - 1 + r, :, LANES - 1:]
            total = total + south * near_mixing[c, 0, pl.ds(i, 1), :]
            total = total + north * near_mixing[c, 1, pl.ds(i, 1), :]
        sum_ref[c] = jnp.where(has_neighbour(flip), total, partial_ref[c])


def mend_side(flip, east_ref, north_ref, mine_ref, other_ref, store, store_column):
    levels, width = mine_ref.shape[1:]
    rows = east_ref.shape[1]
    sign = sign_of(flip)
    place = lambda r: flip * (rows - STEPS) + r + flip * (STEPS - 1 - 2 * r)

    def half(at):
        own = [Row(east_ref[0, place(r), at, :] * sign, north_ref[0, place(r), at, :]) for r in range(STEPS - 1)]
        near = Row(other_ref[FLUX_ROWS, at, :] * sign, other_ref[FLUX_ROWS + 1, at, :])
        far = Row(other_ref[FLUX_ROWS + 2, at, :] * sign)
        for c in range(FLUX_ROWS // STEPS):
            mine = lambda k: mine_ref[2 * k + c, at, :]
            theirs = lambda k: other_ref[2 * k + c, at, :]
            a0 = theirs(0)
            n1 = mine(0)
            b0 = own[0].stay(a0) + near.inward * n1 + theirs(1)
            b1 = own[0].inward * a0
            bn1 = near.stay(n1) + own[0].outward * a0 + mine(1)
            bn2 = near.outward * n1
            c0 = own[0].stay(b0) + near.inward * bn1 + own[1].outward * b1 + theirs(2)
            c1 = own[1].stay(b1) + own[0].inward * b0
            c2 = own[1].inward * b1
            cn1 = near.stay(bn1) + own[0].outward * b0 + far.inward * bn2 + mine(2)
            d0 = own[0].stay(c0) + near.inward * cn1 + own[1].outward * c1 + theirs(3)
            d1 = own[1].stay(c1) + own[0].inward * c0 + own[2].outward * c2
            d2 = own[2].stay(c2) + own[1].inward * c1
            d3 = own[2].inward * c2
            for r, value in enumerate((d0, d1, d2, d3)):
                store(c, r, at, value)
            if store_column is not None:
                tiles = (slice(0, LANES), slice(width - LANES, width))
                for s, lanes in enumerate(tiles):
                    tile = lambda value: value[:, lanes]
                    rate = other_ref[EXTRA, at, s * LANES:(s + 1) * LANES]
                    stays = 1.0 - jnp.abs(other_ref[FLUX_ROWS + 2, at, lanes]) - jnp.abs(rate)
                    drift = jnp.maximum(rate if s == 0 else -rate, 0.0) * tile(bn2)
                    cn2 = stays * tile(bn2) + pltpu.roll(drift, LANES - 1 if s == 0 else 1, 1)
                    cn2 = cn2 + tile(near.outward) * tile(bn1)
                    cn3 = tile(far.outward) * tile(bn2)
                    sums = (
                        tile(a0) + tile(b0) + tile(c0), tile(b1) + tile(c1), tile(c2),
                        tile(n1) + tile(bn1) + tile(cn1), tile(bn2) + cn2, cn3,
                    )
                    for r, value in enumerate(sums):
                        store_column(c, s, r, at, value)

    level_halves(levels, half)


def copy_end(flip, ends_ref, out_ref):
    for c in range(out_ref.shape[0]):
        for r in range(STEPS):
            out_ref[c, r] = ends_ref[c, flip * STEPS + r]


def mend_a_kernel(east_ref, north_ref, mine_ref, other_ref, ends_ref, base_ref, out_ref, column_ref, passed_ref):
    passed_ref[...] = mine_ref[...]
    flip = 1 - parity()
    turn = lambda r: r + flip * (STEPS - 1 - 2 * r)

    def store(c, r, at, value):
        out_ref[c, turn(r), at, :] = ends_ref[c, flip * STEPS + turn(r), at, :] + value

    def store_column(c, s, r, at, value):
        column_ref[c, s, r, at, :] = value

    @pl.when(has_neighbour(flip))
    def _():
        mend_side(flip, east_ref, north_ref, mine_ref, other_ref, store, store_column)

    @pl.when(jnp.logical_not(has_neighbour(flip)))
    def _():
        column_ref[...] = jnp.zeros_like(column_ref)
        copy_end(flip, ends_ref, out_ref)


def mend_b_kernel(east_ref, north_ref, mine_ref, other_ref, ends_ref, _, __, out_ref):
    flip = parity()
    turn = lambda r: r + flip * (STEPS - 1 - 2 * r)

    def store(c, r, at, value):
        out_ref[c, turn(r), at, :] = ends_ref[c, flip * STEPS + turn(r), at, :] + value

    @pl.when(has_neighbour(flip))
    def _():
        mend_side(flip, east_ref, north_ref, mine_ref, other_ref, store, None)

    @pl.when(jnp.logical_not(has_neighbour(flip)))
    def _():
        copy_end(flip, ends_ref, out_ref)


def subtract_rows(state_ref, out_hbm, buffer, sems, jobs):
    copies = []
    is_last = lax.axis_index("sub") == lax.axis_size("sub") - 1
    for start, other in jobs:
        for c in range(other.shape[0]):
            count = other.shape[1]
            for r in range(count):
                buffer[c, start + r] = state_ref[0, c, start + r] - jnp.where(is_last, 0.0, other[c, r])
            at = pl.ds(start, count)
            copy = pltpu.make_async_copy(buffer.at[c, at], out_hbm.at[0, c, at], sems.at[len(copies)])
            copy.start()
            copies.append(copy)
    return copies


def begin_kernel(state_ref, middle_ref, a_ref, out_hbm, buffer, sems):
    start = parity() * (state_ref.shape[2] - STEPS)
    for copy in subtract_rows(state_ref, out_hbm, buffer, sems, ((STEPS, middle_ref), (start, a_ref))):
        copy.wait()


def finish_kernel(
    begun_hbm, state_ref, b_ref, owner_ref, total_ref, came_ref, out_hbm, gradient_ref, buffer, sems
):
    parts = b_ref.shape[0]
    start = (1 - parity()) * (state_ref.shape[2] - STEPS)
    copies = subtract_rows(state_ref, out_hbm, buffer, sems, ((start, b_ref),))

    share, mine = gradient_ref.shape[1:]
    start = lax.axis_index("hor") * mine
    chosen = []
    for c in range(parts):
        total = total_ref[c] + came_ref[c]
        block = total[:share]
        for s in range(1, total.shape[0] // share):
            block = jnp.where(lax.axis_index("sub") == s, total[s * share:(s + 1) * share], block)
        chosen.append(block)
    chosen = jnp.concatenate(chosen, 0)
    column = lax.broadcasted_iota(jnp.int32, (parts * share, mine), 1)
    picked = jnp.zeros((parts * share, mine), jnp.float32)
    for q in range(mine):
        value = jnp.sum(jnp.where(owner_ref[...] == start + q, chosen, 0.0), axis=1, keepdims=True)
        picked = jnp.where(column == q, value, picked)
    for c in range(parts):
        gradient_ref[c] = picked[c * share:(c + 1) * share]
    for copy in copies:
        copy.wait()


BRIEF = pl.CostEstimate(flops=1, bytes_accessed=1, transcendentals=0)
PARAMS = pltpu.CompilerParams(vmem_limit_bytes=24 * 1024 * 1024)


def local(
    adjoint_state,
    courant_east,
    courant_north,
    parent_cell,
    stencil_offset,
    stencil_weight,
    owner_slot,
):
    _, parts, rows, levels, width = adjoint_state.shape
    slots = owner_slot.shape[0]
    inner = rows - 2 * STEPS
    row_bytes = levels * width * 4
    f32 = lambda *shape: jax.ShapeDtypeStruct(shape, jnp.float32)
    vmem = pl.BlockSpec(memory_space=pltpu.VMEM)
    smem = pl.BlockSpec(memory_space=pltpu.SMEM)
    hbm = pl.BlockSpec(memory_space=pltpu.HBM)
    in_hbm = lambda value: pltpu.with_memory_space_constraint(value, pltpu.HBM)

    subs, hors = lax.axis_size("sub"), lax.axis_size("hor")
    small = [parent_cell, stencil_offset, stencil_weight]

    first_pack = pl.pallas_call(
        pack_kernel,
        in_specs=[hbm] * 6,
        out_specs=vmem,
        out_shape=f32(PACK_ROWS + 1, levels, width),
        scratch_shapes=[
            pltpu.VMEM((parts, STEPS, levels, width), jnp.float32),
            pltpu.VMEM((STEPS, levels, width), jnp.float32),
            pltpu.VMEM((STEPS, levels, width), jnp.float32),
        ]
        + [pltpu.VMEM(value.shape, value.dtype) for value in small]
        + [pltpu.SemaphoreType.DMA((levels // HALF, parts + 2)), pltpu.SemaphoreType.DMA((3,))],
        compiler_params=PARAMS,
        cost_estimate=BRIEF,
        name="pack",
    )(*[in_hbm(value) for value in [adjoint_state, courant_east, courant_north] + small])
    first_came = alternating(first_pack, -1)

    state, east, north = adjoint_state, courant_east, courant_north
    second_pack, middle, ends, columns = pl.pallas_call(
        sweep_kernel,
        in_specs=[vmem] * 3,
        out_specs=[vmem] * 4,
        out_shape=[
            f32(PACK_ROWS, levels, width),
            f32(parts, inner, levels, width),
            f32(parts, 2 * STEPS, levels, width),
            f32(parts, 2, rows, levels, LANES),
        ],
        scratch_shapes=[
            pltpu.VMEM((STEPS - 1, parts, rows, HALF, width), jnp.float32),
            pltpu.VMEM((rows, HALF, width), jnp.float32),
            pltpu.VMEM((rows, HALF, width), jnp.float32),
            pltpu.VMEM((rows, HALF, width), jnp.float32),
        ],
        compiler_params=PARAMS,
        cost_estimate=BRIEF,
        name="sweep",
    )(state, east, north)
    middle_came = to_previous(middle)

    mixing, base = pl.pallas_call(
        ghost_base_kernel,
        in_specs=[vmem] * 5,
        out_specs=[vmem] * 2,
        out_shape=[f32(parts, 2, rows, slots), f32(parts, levels, slots)],
        compiler_params=PARAMS,
        cost_estimate=BRIEF,
        name="ghost_base",
    )(*small, columns, north)

    column_shape = (parts, 2, 2 * (STEPS - 1), levels, LANES)
    side_a, a_columns, second_sent = pl.pallas_call(
        mend_a_kernel,
        in_specs=[vmem] * 6,
        out_specs=[vmem] * 3,
        out_shape=[
            f32(parts, STEPS, levels, width), f32(*column_shape), f32(PACK_ROWS, levels, width)
        ],
        compiler_params=PARAMS,
        cost_estimate=BRIEF,
        name="mend_a",
    )(east, north, second_pack, first_came, ends, base)
    second_came = alternating(second_sent, 1)
    a_came = to_previous(side_a)
    total = pl.pallas_call(
        ghost_kernel,
        in_specs=[vmem] * 5,
        out_specs=vmem,
        out_shape=f32(parts, levels, slots),
        scratch_shapes=[pltpu.VMEM((parts, 2, rows, slots), jnp.float32)],
        compiler_params=PARAMS,
        cost_estimate=BRIEF,
        name="ghost",
    )(north, first_came, a_columns, mixing, base)
    order = rounds()
    total = total + exchanged(total, *order[0])
    side_b = pl.pallas_call(
        mend_b_kernel,
        in_specs=[vmem] * 5 + [pl.BlockSpec(memory_space=pl.ANY)] * 2,
        out_specs=vmem,
        out_shape=f32(parts, STEPS, levels, width),
        compiler_params=PARAMS,
        cost_estimate=BRIEF,
        name="mend_b",
    )(east, north, first_pack, second_came, ends, middle_came, total)
    b_came = to_previous(side_b)

    for each in order[1:-1]:
        total = total + exchanged(total, *each)
    came = exchanged(total, *order[-1])

    result = f32(*adjoint_state.shape)
    buffer = pltpu.VMEM((parts, rows, levels, width), jnp.float32)
    begun = pl.pallas_call(
        begin_kernel,
        in_specs=[vmem] * 3,
        out_specs=hbm,
        out_shape=result,
        scratch_shapes=[buffer, pltpu.SemaphoreType.DMA((2 * parts,))],
        compiler_params=PARAMS,
        cost_estimate=BRIEF,
        name="begin",
    )(state, middle_came, a_came)
    adjoint_result, boundary_gradient = pl.pallas_call(
        finish_kernel,
        in_specs=[hbm] + [vmem] * 5,
        out_specs=[hbm, vmem],
        out_shape=[result, f32(parts, levels // subs, slots // hors)],
        scratch_shapes=[buffer, pltpu.SemaphoreType.DMA((parts,))],
        input_output_aliases={0: 0},
        compiler_params=PARAMS,
        cost_estimate=BRIEF,
        name="finish",
    )(begun, state, b_came, owner_slot[None], total, came)
    return (adjoint_result, boundary_gradient)


def solution(mesh):
    in_specs = (
        P(("ens", "sub"), None, "hor", None, None),
        P(("ens", "sub"), "hor", None, None),
        P(("ens", "sub"), "hor", None, None),
        P(None, None, "hor"),
        P(None, None, None, "hor"),
        P(None, None, None, "hor"),
        P(),
    )
    out_specs = (P(("ens", "sub"), None, "hor", None, None), P("ens", "sub", "hor"))
    return jax.shard_map(local, mesh=mesh, in_specs=in_specs, out_specs=out_specs, check_vma=False)
```

```python
import functools

import jax
import jax.numpy as jnp
from jax import lax
from jax.experimental import pallas as pl
from jax.experimental.pallas import tpu as pltpu
from jax.sharding import PartitionSpec as P

STEPS = 4
HALF = 8
FLUX_ROWS = 2 * STEPS
PACK_ROWS = FLUX_ROWS + 3
LANES = 128
EXTRA = PACK_ROWS
TARGETS = 4 * LANES
WEIGHTS = 5 * LANES


def to_previous(value):
    peers = lax.axis_size("sub")
    return lax.ppermute(value, "sub", [(i, (i - 1) % peers) for i in range(peers)])


def alternating(value, sign):
    subs, hors = lax.axis_size("sub"), lax.axis_size("hor")
    assert subs % 2 == 0
    pairs = []
    for s in range(subs):
        step = sign if s % 2 == 0 else -sign
        for h in range(hors):
            inside = 0 <= h + step < hors
            pairs.append((s * hors + h, s * hors + h + step if inside else (s ^ 1) * hors + h))
    return lax.ppermute(value, ("sub", "hor"), pairs)


def has_neighbour(flip):
    hor = lax.axis_index("hor")
    return jnp.where(flip == 1, hor < lax.axis_size("hor") - 1, hor > 0)


def rounds():
    subs, hors = lax.axis_size("sub"), lax.axis_size("hor")
    assert not subs & (subs - 1) and not hors & (hors - 1)
    order = [("sub", range(1, min(subs, 4)))]
    order += [("sub", [1 << n]) for n in range(2, subs.bit_length() - 1)]
    return order + [("hor", [1 << n]) for n in range(hors.bit_length() - 1)]


def exchanged(value, axis, distances):
    size = lax.axis_size(axis)
    return sum(lax.ppermute(value, axis, [(i, i ^ distance) for i in range(size)]) for distance in distances)


def parity():
    return lax.rem(lax.axis_index("sub"), 2)


def sign_of(flip):
    return jnp.where(flip == 1, jnp.float32(-1.0), jnp.float32(1.0))


def north_rates(north_rate):
    width = north_rate.shape[-1]
    column = lax.broadcasted_iota(jnp.int32, north_rate.shape, len(north_rate.shape) - 1)
    plus = jnp.where(column == 0, 0.0, jnp.maximum(north_rate, 0.0))
    minus = jnp.where(column == width - 1, 0.0, jnp.maximum(-north_rate, 0.0))
    return plus, minus


def shifted(flux_plus, flux_minus):
    width = flux_plus.shape[-1]
    axis = len(flux_plus.shape) - 1
    return pltpu.roll(flux_plus, width - 1, axis) + pltpu.roll(flux_minus, 1, axis)


class Row:
    def __init__(self, east_rate, north_rate=None):
        self.outward = jnp.maximum(east_rate, 0.0)
        self.inward = jnp.maximum(-east_rate, 0.0)
        if north_rate is not None:
            self.centre = 1.0 - jnp.abs(east_rate) - jnp.abs(north_rate)
            self.plus, self.minus = north_rates(north_rate)

    def stay(self, value):
        return self.centre * value + shifted(self.plus * value, self.minus * value)


def level_halves(levels, body):
    def step(h, carry):
        body(pl.ds(pl.multiple_of(h * HALF, HALF), HALF))
        return carry

    lax.fori_loop(0, levels // HALF, step, 0)


def pack_kernel(
    state_hbm, east_hbm, north_hbm, cell_hbm, offset_hbm, weight_hbm,
    pack_ref, state_ref, east_ref, north_ref, cell_ref, offset_ref, weight_ref, sems, small_sems,
):
    parts, rows, levels, width = state_hbm.shape[1:]
    flip = parity()
    sign = sign_of(flip)
    at_end = pl.ds(flip * (rows - STEPS), STEPS)
    place = lambda r: r + flip * (STEPS - 1 - 2 * r)
    halves = levels // HALF
    copies = []
    for h in range(halves):
        at = pl.ds(h * HALF, HALF)
        sem = sems.at[h]
        batch = [
            pltpu.make_async_copy(state_hbm.at[0, c, at_end, at], state_ref.at[c, :, at], sem.at[c])
            for c in range(parts)
        ]
        batch.append(pltpu.make_async_copy(east_hbm.at[0, at_end, at], east_ref.at[:, at], sem.at[parts]))
        batch.append(pltpu.make_async_copy(north_hbm.at[0, at_end, at], north_ref.at[:, at], sem.at[parts + 1]))
        copies.append(batch)
        for copy in batch:
            copy.start()
    small = [
        pltpu.make_async_copy(source, target, small_sems.at[n])
        for n, (source, target) in enumerate(
            ((cell_hbm, cell_ref), (offset_hbm, offset_ref), (weight_hbm, weight_ref))
        )
    ]
    for copy in small:
        copy.start()

    def half(at):
        row = [Row(east_ref[place(r), at, :] * sign, north_ref[place(r), at, :]) for r in range(STEPS)]
        pack_ref[FLUX_ROWS, at, :] = east_ref[place(0), at, :]
        pack_ref[FLUX_ROWS + 1, at, :] = north_ref[place(0), at, :]
        pack_ref[FLUX_ROWS + 2, at, :] = east_ref[place(1), at, :]
        for r in (1, 2):
            lanes = (2 * r - 2) * LANES
            pack_ref[EXTRA, at, lanes:lanes + LANES] = north_ref[place(r), at, :LANES]
            pack_ref[EXTRA, at, lanes + LANES:lanes + 2 * LANES] = north_ref[place(r), at, width - LANES:]
        for c in range(parts):
            field = [state_ref[c, place(r), at, :] for r in range(STEPS)]
            for k in range(STEPS):
                pack_ref[2 * k + c, at, :] = row[0].outward * field[0]
                after = []
                for r in range(STEPS - 1 - k):
                    value = row[r].stay(field[r]) + row[r + 1].outward * field[r + 1]
                    if r > 0:
                        value = value + row[r - 1].inward * field[r - 1]
                    after.append(value)
                field = after

    for h in range(halves):
        for copy in copies[h]:
            copy.wait()
        half(pl.ds(h * HALF, HALF))

    for copy in small:
        copy.wait()
    n = 0
    for point in range(offset_ref.shape[0]):
        for c in range(parts):
            target = (cell_ref[c] + offset_ref[point, c]).astype(jnp.float32)
            pack_ref[EXTRA, n:n + 2, TARGETS:TARGETS + rows] = target
            pack_ref[EXTRA, n:n + 2, WEIGHTS:WEIGHTS + rows] = weight_ref[point, c]
            n += 2


def as_column(row):
    count = row.shape[1]
    here = lax.broadcasted_iota(jnp.int32, (count, count), 0)
    there = lax.broadcasted_iota(jnp.int32, (count, count), 1)
    return jnp.sum(jnp.where(here == there, row, 0), axis=1, keepdims=True)


def sweep_kernel(
    state_ref, east_ref, north_ref, pack_ref, middle_ref, ends_ref, column_ref,
    field, plus_ref, minus_ref, centre_ref,
):
    parts, rows, levels, width = state_ref.shape[1:]
    flip = 1 - parity()
    sign = sign_of(flip)
    end_row = flip * (rows - 1)
    next_row = end_row + 1 - 2 * flip

    def half(at):
        pack_ref[FLUX_ROWS, at, :] = east_ref[0, end_row, at, :]
        pack_ref[FLUX_ROWS + 1, at, :] = north_ref[0, end_row, at, :]
        pack_ref[FLUX_ROWS + 2, at, :] = east_ref[0, next_row, at, :]

        for k in range(STEPS):
            if k == 0:
                read = lambda c, i: state_ref[0, c, i, at, :]
            else:
                read = lambda c, i, slot=k - 1: field[slot, c, i]
            leaving = jnp.maximum(east_ref[0, end_row, at, :] * sign, 0.0)
            for c in range(parts):
                pack_ref[2 * k + c, at, :] = leaving * read(c, end_row)
            west = [None] * parts
            here = [read(c, 0) for c in range(parts)]
            east_here = east_ref[0, 0, at, :]
            for i in range(rows):
                leave_west = jnp.maximum(-east_here, 0.0)
                if k == 0:
                    north_rate = north_ref[0, i, at, :]
                    centre = 1.0 - jnp.abs(east_here) - jnp.abs(north_rate)
                    plus, minus = north_rates(north_rate)
                    centre_ref[i], plus_ref[i], minus_ref[i] = centre, plus, minus
                else:
                    centre, plus, minus = centre_ref[i], plus_ref[i], minus_ref[i]
                if i + 1 < rows:
                    east_here = east_ref[0, i + 1, at, :]
                    east_after = jnp.maximum(east_here, 0.0)
                for c in range(parts):
                    value = here[c]
                    total = centre * value + shifted(plus * value, minus * value)
                    if i > 0:
                        total = total + west[c]
                    if i + 1 < rows:
                        west[c] = leave_west * value
                        here[c] = read(c, i + 1)
                        total = total + east_after * here[c]
                    if k < STEPS - 1:
                        field[k, c, i] = total
                    elif i < STEPS:
                        ends_ref[c, i, at, :] = total
                    elif i >= rows - STEPS:
                        ends_ref[c, i - rows + 2 * STEPS, at, :] = total
                    else:
                        middle_ref[c, i - STEPS, at, :] = total

        def columns(i, carry):
            for c in range(parts):
                value = state_ref[0, c, i, at, :]
                first, last = value[:, :LANES], value[:, width - LANES:]
                for slot in range(STEPS - 1):
                    first = first + field[slot, c, i, :, :LANES]
                    last = last + field[slot, c, i, :, width - LANES:]
                column_ref[c, 0, i, at, :] = first
                column_ref[c, 1, i, at, :] = last
            return carry

        lax.fori_loop(0, rows, columns, 0, unroll=2)

    level_halves(levels, half)


def mix(targets, weights, cells, total):
    for target, weight in zip(targets, weights):
        total = total + jnp.where(as_column(target) == cells, as_column(weight), 0.0)
    return total


def ghost_base_kernel(
    cell_ref, offset_ref, weight_ref, column_ref, north_ref, mixing_ref, partial_ref
):
    parts, _, rows, levels, _ = column_ref.shape
    slots = mixing_ref.shape[-1]
    width = north_ref.shape[-1]
    points = range(offset_ref.shape[0])
    cells = lax.broadcasted_iota(jnp.int32, (rows, slots), 1)
    for c in range(parts):
        for s in range(2):
            mixing_ref[c, s] = mix(
                [cell_ref[c, s:s + 1, :] + offset_ref[point, c, s:s + 1, :] for point in points],
                [weight_ref[point, c, s:s + 1, :] for point in points],
                cells, jnp.zeros((rows, slots), jnp.float32),
            )

    for c in range(parts):
        total = jnp.zeros((levels, slots), jnp.float32)
        for i in range(rows):
            south = jnp.maximum(north_ref[0, i, :, :1], 0.0) * column_ref[c, 0, i, :, :1]
            north = jnp.maximum(-north_ref[0, i, :, width - 1:], 0.0) * column_ref[c, 1, i, :, LANES - 1:]
            total = total + south * mixing_ref[c, 0, i:i + 1, :]
            total = total + north * mixing_ref[c, 1, i:i + 1, :]
        partial_ref[c] = total


def ghost_kernel(north_ref, other_ref, column_ref, mixing_ref, partial_ref, sum_ref, near_mixing):
    parts, levels, slots = partial_ref.shape
    rows = mixing_ref.shape[2]
    width = north_ref.shape[-1]
    flip = 1 - parity()
    cells = lax.broadcasted_iota(jnp.int32, (rows, slots), 1).astype(jnp.float32)
    points = (WEIGHTS - TARGETS) // LANES * 4
    for c in range(parts):
        for s in range(2):
            at = [(point * parts + c) * 2 + s for point in range(points)]
            near_mixing[c, s] = mix(
                [other_ref[EXTRA, n:n + 1, TARGETS:TARGETS + rows] for n in at],
                [other_ref[EXTRA, n:n + 1, WEIGHTS:WEIGHTS + rows] for n in at],
                cells, jnp.zeros((rows, slots), jnp.float32),
            )
    for c in range(parts):
        total = partial_ref[c]
        for r in range(STEPS - 1):
            i = r + flip * (rows - 1 - 2 * r)
            south = jnp.maximum(north_ref[0, i, :, :1], 0.0) * column_ref[c, 0, r, :, :1]
            north = jnp.maximum(-north_ref[0, i, :, width - 1:], 0.0) * column_ref[c, 1, r, :, LANES - 1:]
            total = total + south * mixing_ref[c, 0, pl.ds(i, 1), :]
            total = total + north * mixing_ref[c, 1, pl.ds(i, 1), :]
            i = r + (1 - flip) * (rows - 1 - 2 * r)
            if r == 0:
                first_rate = other_ref[FLUX_ROWS + 1, :, :LANES]
                last_rate = other_ref[FLUX_ROWS + 1, :, width - LANES:]
            else:
                lanes = (2 * r - 2) * LANES
                first_rate = other_ref[EXTRA, :, lanes:lanes + LANES]
                last_rate = other_ref[EXTRA, :, lanes + LANES:lanes + 2 * LANES]
            south = jnp.maximum(first_rate[:, :1], 0.0) * column_ref[c, 0, STEPS - 1 + r, :, :1]
            north = jnp.maximum(-last_rate[:, LANES - 1:], 0.0) * column_ref[c, 1, STEPS - 1 + r, :, LANES - 1:]
            total = total + south * near_mixing[c, 0, pl.ds(i, 1), :]
            total = total + north * near_mixing[c, 1, pl.ds(i, 1), :]
        sum_ref[c] = jnp.where(has_neighbour(flip), total, partial_ref[c])


def mend_side(flip, east_ref, north_ref, mine_ref, other_ref, store, store_column):
    levels, width = mine_ref.shape[1:]
    rows = east_ref.shape[1]
    sign = sign_of(flip)
    place = lambda r: flip * (rows - STEPS) + r + flip * (STEPS - 1 - 2 * r)

    def half(at):
        own = [Row(east_ref[0, place(r), at, :] * sign, north_ref[0, place(r), at, :]) for r in range(STEPS - 1)]
        near = Row(other_ref[FLUX_ROWS, at, :] * sign, other_ref[FLUX_ROWS + 1, at, :])
        far = Row(other_ref[FLUX_ROWS + 2, at, :] * sign)
        for c in range(FLUX_ROWS // STEPS):
            mine = lambda k: mine_ref[2 * k + c, at, :]
            theirs = lambda k: other_ref[2 * k + c, at, :]
            a0 = theirs(0)
            n1 = mine(0)
            b0 = own[0].stay(a0) + near.inward * n1 + theirs(1)
            b1 = own[0].inward * a0
            bn1 = near.stay(n1) + own[0].outward * a0 + mine(1)
            bn2 = near.outward * n1
            c0 = own[0].stay(b0) + near.inward * bn1 + own[1].outward * b1 + theirs(2)
            c1 = own[1].stay(b1) + own[0].inward * b0
            c2 = own[1].inward * b1
            cn1 = near.stay(bn1) + own[0].outward * b0 + far.inward * bn2 + mine(2)
            d0 = own[0].stay(c0) + near.inward * cn1 + own[1].outward * c1 + theirs(3)
            d1 = own[1].stay(c1) + own[0].inward * c0 + own[2].outward * c2
            d2 = own[2].stay(c2) + own[1].inward * c1
            d3 = own[2].inward * c2
            for r, value in enumerate((d0, d1, d2, d3)):
                store(c, r, at, value)
            if store_column is not None:
                tiles = (slice(0, LANES), slice(width - LANES, width))
                for s, lanes in enumerate(tiles):
                    tile = lambda value: value[:, lanes]
                    rate = other_ref[EXTRA, at, s * LANES:(s + 1) * LANES]
                    stays = 1.0 - jnp.abs(other_ref[FLUX_ROWS + 2, at, lanes]) - jnp.abs(rate)
                    drift = jnp.maximum(rate if s == 0 else -rate, 0.0) * tile(bn2)
                    cn2 = stays * tile(bn2) + pltpu.roll(drift, LANES - 1 if s == 0 else 1, 1)
                    cn2 = cn2 + tile(near.outward) * tile(bn1)
                    cn3 = tile(far.outward) * tile(bn2)
                    sums = (
                        tile(a0) + tile(b0) + tile(c0), tile(b1) + tile(c1), tile(c2),
                        tile(n1) + tile(bn1) + tile(cn1), tile(bn2) + cn2, cn3,
                    )
                    for r, value in enumerate(sums):
                        store_column(c, s, r, at, value)

    level_halves(levels, half)


def copy_end(flip, ends_ref, out_ref):
    for c in range(out_ref.shape[0]):
        for r in range(STEPS):
            out_ref[c, r] = ends_ref[c, flip * STEPS + r]


def mend_a_kernel(east_ref, north_ref, mine_ref, other_ref, ends_ref, base_ref, out_ref, column_ref):
    flip = 1 - parity()
    turn = lambda r: r + flip * (STEPS - 1 - 2 * r)

    def store(c, r, at, value):
        out_ref[c, turn(r), at, :] = ends_ref[c, flip * STEPS + turn(r), at, :] + value

    def store_column(c, s, r, at, value):
        column_ref[c, s, r, at, :] = value

    @pl.when(has_neighbour(flip))
    def _():
        mend_side(flip, east_ref, north_ref, mine_ref, other_ref, store, store_column)

    @pl.when(jnp.logical_not(has_neighbour(flip)))
    def _():
        column_ref[...] = jnp.zeros_like(column_ref)
        copy_end(flip, ends_ref, out_ref)


def mend_b_kernel(east_ref, north_ref, mine_ref, other_ref, ends_ref, _, out_ref):
    flip = parity()
    turn = lambda r: r + flip * (STEPS - 1 - 2 * r)

    def store(c, r, at, value):
        out_ref[c, turn(r), at, :] = ends_ref[c, flip * STEPS + turn(r), at, :] + value

    @pl.when(has_neighbour(flip))
    def _():
        mend_side(flip, east_ref, north_ref, mine_ref, other_ref, store, None)

    @pl.when(jnp.logical_not(has_neighbour(flip)))
    def _():
        copy_end(flip, ends_ref, out_ref)


def subtract_rows(state_ref, out_hbm, buffer, sems, jobs):
    copies = []
    is_last = lax.axis_index("sub") == lax.axis_size("sub") - 1
    for start, other in jobs:
        for c in range(other.shape[0]):
            count = other.shape[1]
            for r in range(count):
                buffer[c, start + r] = state_ref[0, c, start + r] - jnp.where(is_last, 0.0, other[c, r])
            at = pl.ds(start, count)
            copy = pltpu.make_async_copy(buffer.at[c, at], out_hbm.at[0, c, at], sems.at[len(copies)])
            copy.start()
            copies.append(copy)
    return copies


def begin_kernel(state_ref, middle_ref, a_ref, out_hbm, buffer, sems):
    start = parity() * (state_ref.shape[2] - STEPS)
    for copy in subtract_rows(state_ref, out_hbm, buffer, sems, ((STEPS, middle_ref), (start, a_ref))):
        copy.wait()


def end_kernel(begun_hbm, state_ref, b_ref, out_hbm, buffer, sems):
    start = (1 - parity()) * (state_ref.shape[2] - STEPS)
    for copy in subtract_rows(state_ref, out_hbm, buffer, sems, ((start, b_ref),)):
        copy.wait()


def pick_kernel(_, owner_ref, total_ref, came_ref, gradient_ref):
    parts = gradient_ref.shape[0]
    share, mine = gradient_ref.shape[1:]
    start = lax.axis_index("hor") * mine
    chosen = []
    for c in range(parts):
        total = total_ref[c] + came_ref[c]
        block = total[:share]
        for s in range(1, total.shape[0] // share):
            block = jnp.where(lax.axis_index("sub") == s, total[s * share:(s + 1) * share], block)
        chosen.append(block)
    chosen = jnp.concatenate(chosen, 0)
    column = lax.broadcasted_iota(jnp.int32, (parts * share, mine), 1)
    picked = jnp.zeros((parts * share, mine), jnp.float32)
    for q in range(mine):
        value = jnp.sum(jnp.where(owner_ref[...] == start + q, chosen, 0.0), axis=1, keepdims=True)
        picked = jnp.where(column == q, value, picked)
    for c in range(parts):
        gradient_ref[c] = picked[c * share:(c + 1) * share]


BRIEF = pl.CostEstimate(flops=1, bytes_accessed=1, transcendentals=0)
PARAMS = pltpu.CompilerParams(vmem_limit_bytes=24 * 1024 * 1024)


def local(
    adjoint_state,
    courant_east,
    courant_north,
    parent_cell,
    stencil_offset,
    stencil_weight,
    owner_slot,
):
    _, parts, rows, levels, width = adjoint_state.shape
    slots = owner_slot.shape[0]
    inner = rows - 2 * STEPS
    row_bytes = levels * width * 4
    f32 = lambda *shape: jax.ShapeDtypeStruct(shape, jnp.float32)
    vmem = pl.BlockSpec(memory_space=pltpu.VMEM)
    smem = pl.BlockSpec(memory_space=pltpu.SMEM)
    hbm = pl.BlockSpec(memory_space=pltpu.HBM)
    in_hbm = lambda value: pltpu.with_memory_space_constraint(value, pltpu.HBM)

    subs, hors = lax.axis_size("sub"), lax.axis_size("hor")
    small = [parent_cell, stencil_offset, stencil_weight]

    first_pack = pl.pallas_call(
        pack_kernel,
        in_specs=[hbm] * 6,
        out_specs=vmem,
        out_shape=f32(PACK_ROWS + 1, levels, width),
        scratch_shapes=[
            pltpu.VMEM((parts, STEPS, levels, width), jnp.float32),
            pltpu.VMEM((STEPS, levels, width), jnp.float32),
            pltpu.VMEM((STEPS, levels, width), jnp.float32),
        ]
        + [pltpu.VMEM(value.shape, value.dtype) for value in small]
        + [pltpu.SemaphoreType.DMA((levels // HALF, parts + 2)), pltpu.SemaphoreType.DMA((3,))],
        compiler_params=PARAMS,
        cost_estimate=BRIEF,
        name="pack",
    )(*[in_hbm(value) for value in [adjoint_state, courant_east, courant_north] + small])
    first_came = alternating(first_pack, -1)

    state, east, north = adjoint_state, courant_east, courant_north
    second_pack, middle, ends, columns = pl.pallas_call(
        sweep_kernel,
        in_specs=[vmem] * 3,
        out_specs=[vmem] * 4,
        out_shape=[
            f32(PACK_ROWS, levels, width),
            f32(parts, inner, levels, width),
            f32(parts, 2 * STEPS, levels, width),
            f32(parts, 2, rows, levels, LANES),
        ],
        scratch_shapes=[
            pltpu.VMEM((STEPS - 1, parts, rows, HALF, width), jnp.float32),
            pltpu.VMEM((rows, HALF, width), jnp.float32),
            pltpu.VMEM((rows, HALF, width), jnp.float32),
            pltpu.VMEM((rows, HALF, width), jnp.float32),
        ],
        compiler_params=PARAMS,
        cost_estimate=BRIEF,
        name="sweep",
    )(state, east, north)
    second_came = alternating(second_pack, 1)
    middle_came = to_previous(middle)

    mixing, base = pl.pallas_call(
        ghost_base_kernel,
        in_specs=[vmem] * 5,
        out_specs=[vmem] * 2,
        out_shape=[f32(parts, 2, rows, slots), f32(parts, levels, slots)],
        compiler_params=PARAMS,
        cost_estimate=BRIEF,
        name="ghost_base",
    )(*small, columns, north)

    column_shape = (parts, 2, 2 * (STEPS - 1), levels, LANES)
    side_a, a_columns = pl.pallas_call(
        mend_a_kernel,
        in_specs=[vmem] * 6,
        out_specs=[vmem] * 2,
        out_shape=[f32(parts, STEPS, levels, width), f32(*column_shape)],
        compiler_params=PARAMS,
        cost_estimate=BRIEF,
        name="mend_a",
    )(east, north, second_pack, first_came, ends, base)
    a_came = to_previous(side_a)
    total = pl.pallas_call(
        ghost_kernel,
        in_specs=[vmem] * 5,
        out_specs=vmem,
        out_shape=f32(parts, levels, slots),
        scratch_shapes=[pltpu.VMEM((parts, 2, rows, slots), jnp.float32)],
        compiler_params=PARAMS,
        cost_estimate=BRIEF,
        name="ghost",
    )(north, first_came, a_columns, mixing, base)
    order = rounds()
    total = total + exchanged(total, *order[0])
    side_b = pl.pallas_call(
        mend_b_kernel,
        in_specs=[vmem] * 5 + [pl.BlockSpec(memory_space=pl.ANY)],
        out_specs=vmem,
        out_shape=f32(parts, STEPS, levels, width),
        compiler_params=PARAMS,
        cost_estimate=BRIEF,
        name="mend_b",
    )(east, north, first_pack, second_came, ends, total)
    b_came = to_previous(side_b)

    for each in order[1:-1]:
        total = total + exchanged(total, *each)
    came = exchanged(total, *order[-1])

    result = f32(*adjoint_state.shape)
    buffer = pltpu.VMEM((parts, rows, levels, width), jnp.float32)
    begun = pl.pallas_call(
        begin_kernel,
        in_specs=[vmem] * 3,
        out_specs=hbm,
        out_shape=result,
        scratch_shapes=[buffer, pltpu.SemaphoreType.DMA((2 * parts,))],
        compiler_params=PARAMS,
        cost_estimate=BRIEF,
        name="begin",
    )(state, middle_came, a_came)
    adjoint_result = pl.pallas_call(
        end_kernel,
        in_specs=[hbm] + [vmem] * 2,
        out_specs=hbm,
        out_shape=result,
        scratch_shapes=[buffer, pltpu.SemaphoreType.DMA((parts,))],
        input_output_aliases={0: 0},
        compiler_params=PARAMS,
        cost_estimate=BRIEF,
        name="end",
    )(begun, state, b_came)
    boundary_gradient = pl.pallas_call(
        pick_kernel,
        in_specs=[pl.BlockSpec(memory_space=pl.ANY)] + [vmem] * 3,
        out_specs=vmem,
        out_shape=f32(parts, levels // subs, slots // hors),
        compiler_params=PARAMS,
        cost_estimate=BRIEF,
        name="pick",
    )(adjoint_result, owner_slot[None], total, came)
    return (adjoint_result, boundary_gradient)


def solution(mesh):
    in_specs = (
        P(("ens", "sub"), None, "hor", None, None),
        P(("ens", "sub"), "hor", None, None),
        P(("ens", "sub"), "hor", None, None),
        P(None, None, "hor"),
        P(None, None, None, "hor"),
        P(None, None, None, "hor"),
        P(),
    )
    out_specs = (P(("ens", "sub"), None, "hor", None, None), P("ens", "sub", "hor"))
    return jax.shard_map(local, mesh=mesh, in_specs=in_specs, out_specs=out_specs, check_vma=False)
```

```python
import functools

import jax
import jax.numpy as jnp
from jax import lax
from jax.experimental import pallas as pl
from jax.experimental.pallas import tpu as pltpu
from jax.sharding import PartitionSpec as P

STEPS = 4
HALF = 8
FLUX_ROWS = 2 * STEPS
PACK_ROWS = FLUX_ROWS + 3
LANES = 128
EXTRA = PACK_ROWS
TARGETS = 4 * LANES
WEIGHTS = 5 * LANES


def to_previous(value):
    peers = lax.axis_size("sub")
    return lax.ppermute(value, "sub", [(i, (i - 1) % peers) for i in range(peers)])


def alternating(value, sign):
    subs, hors = lax.axis_size("sub"), lax.axis_size("hor")
    assert subs % 2 == 0
    pairs = []
    for s in range(subs):
        step = sign if s % 2 == 0 else -sign
        for h in range(hors):
            inside = 0 <= h + step < hors
            pairs.append((s * hors + h, s * hors + h + step if inside else (s ^ 1) * hors + h))
    return lax.ppermute(value, ("sub", "hor"), pairs)


def has_neighbour(flip):
    hor = lax.axis_index("hor")
    return jnp.where(flip == 1, hor < lax.axis_size("hor") - 1, hor > 0)


def rounds():
    subs, hors = lax.axis_size("sub"), lax.axis_size("hor")
    assert not subs & (subs - 1) and not hors & (hors - 1)
    order = [("sub", range(min(subs, 4) - 1, 0, -1))]
    order += [("sub", [1 << n]) for n in range(2, subs.bit_length() - 1)]
    return order + [("hor", [1 << n]) for n in range(hors.bit_length() - 1)]


def exchanged(value, axis, distances):
    size = lax.axis_size(axis)
    return sum(lax.ppermute(value, axis, [(i, i ^ distance) for i in range(size)]) for distance in distances)


def parity():
    return lax.rem(lax.axis_index("sub"), 2)


def sign_of(flip):
    return jnp.where(flip == 1, jnp.float32(-1.0), jnp.float32(1.0))


def north_rates(north_rate):
    width = north_rate.shape[-1]
    column = lax.broadcasted_iota(jnp.int32, north_rate.shape, len(north_rate.shape) - 1)
    plus = jnp.where(column == 0, 0.0, jnp.maximum(north_rate, 0.0))
    minus = jnp.where(column == width - 1, 0.0, jnp.maximum(-north_rate, 0.0))
    return plus, minus


def shifted(flux_plus, flux_minus):
    width = flux_plus.shape[-1]
    axis = len(flux_plus.shape) - 1
    return pltpu.roll(flux_plus, width - 1, axis) + pltpu.roll(flux_minus, 1, axis)


class Row:
    def __init__(self, east_rate, north_rate=None):
        self.outward = jnp.maximum(east_rate, 0.0)
        self.inward = jnp.maximum(-east_rate, 0.0)
        if north_rate is not None:
            self.centre = 1.0 - jnp.abs(east_rate) - jnp.abs(north_rate)
            self.plus, self.minus = north_rates(north_rate)

    def stay(self, value):
        return self.centre * value + shifted(self.plus * value, self.minus * value)


def level_halves(levels, body):
    def step(h, carry):
        body(pl.ds(pl.multiple_of(h * HALF, HALF), HALF))
        return carry

    lax.fori_loop(0, levels // HALF, step, 0)


def pack_kernel(
    state_hbm, east_hbm, north_hbm, cell_hbm, offset_hbm, weight_hbm,
    pack_ref, state_ref, east_ref, north_ref, cell_ref, offset_ref, weight_ref, sems, small_sems,
):
    parts, rows, levels, width = state_hbm.shape[1:]
    flip = parity()
    sign = sign_of(flip)
    at_end = pl.ds(flip * (rows - STEPS), STEPS)
    place = lambda r: r + flip * (STEPS - 1 - 2 * r)
    halves = levels // HALF
    copies = []
    for h in range(halves):
        at = pl.ds(h * HALF, HALF)
        sem = sems.at[h]
        batch = [
            pltpu.make_async_copy(state_hbm.at[0, c, at_end, at], state_ref.at[c, :, at], sem.at[c])
            for c in range(parts)
        ]
        batch.append(pltpu.make_async_copy(east_hbm.at[0, at_end, at], east_ref.at[:, at], sem.at[parts]))
        batch.append(pltpu.make_async_copy(north_hbm.at[0, at_end, at], north_ref.at[:, at], sem.at[parts + 1]))
        copies.append(batch)
        for copy in batch:
            copy.start()
    small = [
        pltpu.make_async_copy(source, target, small_sems.at[n])
        for n, (source, target) in enumerate(
            ((cell_hbm, cell_ref), (offset_hbm, offset_ref), (weight_hbm, weight_ref))
        )
    ]
    for copy in small:
        copy.start()

    def half(at):
        row = [Row(east_ref[place(r), at, :] * sign, north_ref[place(r), at, :]) for r in range(STEPS)]
        pack_ref[FLUX_ROWS, at, :] = east_ref[place(0), at, :]
        pack_ref[FLUX_ROWS + 1, at, :] = north_ref[place(0), at, :]
        pack_ref[FLUX_ROWS + 2, at, :] = east_ref[place(1), at, :]
        for r in (1, 2):
            lanes = (2 * r - 2) * LANES
            pack_ref[EXTRA, at, lanes:lanes + LANES] = north_ref[place(r), at, :LANES]
            pack_ref[EXTRA, at, lanes + LANES:lanes + 2 * LANES] = north_ref[place(r), at, width - LANES:]
        for c in range(parts):
            field = [state_ref[c, place(r), at, :] for r in range(STEPS)]
            for k in range(STEPS):
                pack_ref[2 * k + c, at, :] = row[0].outward * field[0]
                after = []
                for r in range(STEPS - 1 - k):
                    value = row[r].stay(field[r]) + row[r + 1].outward * field[r + 1]
                    if r > 0:
                        value = value + row[r - 1].inward * field[r - 1]
                    after.append(value)
                field = after

    for h in range(halves):
        for copy in copies[h]:
            copy.wait()
        half(pl.ds(h * HALF, HALF))

    for copy in small:
        copy.wait()
    n = 0
    for point in range(offset_ref.shape[0]):
        for c in range(parts):
            target = (cell_ref[c] + offset_ref[point, c]).astype(jnp.float32)
            pack_ref[EXTRA, n:n + 2, TARGETS:TARGETS + rows] = target
            pack_ref[EXTRA, n:n + 2, WEIGHTS:WEIGHTS + rows] = weight_ref[point, c]
            n += 2


def as_column(row):
    count = row.shape[1]
    here = lax.broadcasted_iota(jnp.int32, (count, count), 0)
    there = lax.broadcasted_iota(jnp.int32, (count, count), 1)
    return jnp.sum(jnp.where(here == there, row, 0), axis=1, keepdims=True)


def sweep_kernel(
    state_ref, east_ref, north_ref, pack_ref, middle_ref, ends_ref, column_ref,
    field, plus_ref, minus_ref, centre_ref,
):
    parts, rows, levels, width = state_ref.shape[1:]
    flip = 1 - parity()
    sign = sign_of(flip)
    end_row = flip * (rows - 1)
    next_row = end_row + 1 - 2 * flip

    def half(at):
        pack_ref[FLUX_ROWS, at, :] = east_ref[0, end_row, at, :]
        pack_ref[FLUX_ROWS + 1, at, :] = north_ref[0, end_row, at, :]
        pack_ref[FLUX_ROWS + 2, at, :] = east_ref[0, next_row, at, :]

        for k in range(STEPS):
            if k == 0:
                read = lambda c, i: state_ref[0, c, i, at, :]
            else:
                read = lambda c, i, slot=k - 1: field[slot, c, i]
            leaving = jnp.maximum(east_ref[0, end_row, at, :] * sign, 0.0)
            for c in range(parts):
                pack_ref[2 * k + c, at, :] = leaving * read(c, end_row)
            west = [None] * parts
            here = [read(c, 0) for c in range(parts)]
            east_here = east_ref[0, 0, at, :]
            for i in range(rows):
                leave_west = jnp.maximum(-east_here, 0.0)
                if k == 0:
                    north_rate = north_ref[0, i, at, :]
                    centre = 1.0 - jnp.abs(east_here) - jnp.abs(north_rate)
                    plus, minus = north_rates(north_rate)
                    centre_ref[i], plus_ref[i], minus_ref[i] = centre, plus, minus
                else:
                    centre, plus, minus = centre_ref[i], plus_ref[i], minus_ref[i]
                if i + 1 < rows:
                    east_here = east_ref[0, i + 1, at, :]
                    east_after = jnp.maximum(east_here, 0.0)
                for c in range(parts):
                    value = here[c]
                    total = centre * value + shifted(plus * value, minus * value)
                    if i > 0:
                        total = total + west[c]
                    if i + 1 < rows:
                        west[c] = leave_west * value
                        here[c] = read(c, i + 1)
                        total = total + east_after * here[c]
                    if k < STEPS - 1:
                        field[k, c, i] = total
                    elif i < STEPS:
                        ends_ref[c, i, at, :] = total
                    elif i >= rows - STEPS:
                        ends_ref[c, i - rows + 2 * STEPS, at, :] = total
                    else:
                        middle_ref[c, i - STEPS, at, :] = total

        def columns(i, carry):
            for c in range(parts):
                value = state_ref[0, c, i, at, :]
                first, last = value[:, :LANES], value[:, width - LANES:]
                for slot in range(STEPS - 1):
                    first = first + field[slot, c, i, :, :LANES]
                    last = last + field[slot, c, i, :, width - LANES:]
                column_ref[c, 0, i, at, :] = first
                column_ref[c, 1, i, at, :] = last
            return carry

        lax.fori_loop(0, rows, columns, 0, unroll=2)

    level_halves(levels, half)


def mix(targets, weights, cells, total):
    for target, weight in zip(targets, weights):
        total = total + jnp.where(as_column(target) == cells, as_column(weight), 0.0)
    return total


def ghost_base_kernel(
    cell_ref, offset_ref, weight_ref, owner_ref, column_ref, north_ref, pack_ref,
    mixing_ref, partial_ref, owner_out, pack_out,
):
    owner_out[...] = owner_ref[...]
    pack_out[...] = pack_ref[...]
    parts, _, rows, levels, _ = column_ref.shape
    slots = mixing_ref.shape[-1]
    width = north_ref.shape[-1]
    points = range(offset_ref.shape[0])
    cells = lax.broadcasted_iota(jnp.int32, (rows, slots), 1)
    for c in range(parts):
        for s in range(2):
            mixing_ref[c, s] = mix(
                [cell_ref[c, s:s + 1, :] + offset_ref[point, c, s:s + 1, :] for point in points],
                [weight_ref[point, c, s:s + 1, :] for point in points],
                cells, jnp.zeros((rows, slots), jnp.float32),
            )

    for c in range(parts):
        total = jnp.zeros((levels, slots), jnp.float32)
        for i in range(rows):
            south = jnp.maximum(north_ref[0, i, :, :1], 0.0) * column_ref[c, 0, i, :, :1]
            north = jnp.maximum(-north_ref[0, i, :, width - 1:], 0.0) * column_ref[c, 1, i, :, LANES - 1:]
            total = total + south * mixing_ref[c, 0, i:i + 1, :]
            total = total + north * mixing_ref[c, 1, i:i + 1, :]
        partial_ref[c] = total


def ghost_kernel(north_ref, other_ref, column_ref, mixing_ref, partial_ref, sum_ref, near_mixing):
    parts, levels, slots = partial_ref.shape
    rows = mixing_ref.shape[2]
    width = north_ref.shape[-1]
    flip = 1 - parity()
    cells = lax.broadcasted_iota(jnp.int32, (rows, slots), 1).astype(jnp.float32)
    points = (WEIGHTS - TARGETS) // LANES * 4
    for c in range(parts):
        for s in range(2):
            at = [(point * parts + c) * 2 + s for point in range(points)]
            near_mixing[c, s] = mix(
                [other_ref[EXTRA, n:n + 1, TARGETS:TARGETS + rows] for n in at],
                [other_ref[EXTRA, n:n + 1, WEIGHTS:WEIGHTS + rows] for n in at],
                cells, jnp.zeros((rows, slots), jnp.float32),
            )
    for c in range(parts):
        total = partial_ref[c]
        for r in range(STEPS - 1):
            i = r + flip * (rows - 1 - 2 * r)
            south = jnp.maximum(north_ref[0, i, :, :1], 0.0) * column_ref[c, 0, r, :, :1]
            north = jnp.maximum(-north_ref[0, i, :, width - 1:], 0.0) * column_ref[c, 1, r, :, LANES - 1:]
            total = total + south * mixing_ref[c, 0, pl.ds(i, 1), :]
            total = total + north * mixing_ref[c, 1, pl.ds(i, 1), :]
            i = r + (1 - flip) * (rows - 1 - 2 * r)
            if r == 0:
                first_rate = other_ref[FLUX_ROWS + 1, :, :LANES]
                last_rate = other_ref[FLUX_ROWS + 1, :, width - LANES:]
            else:
                lanes = (2 * r - 2) * LANES
                first_rate = other_ref[EXTRA, :, lanes:lanes + LANES]
                last_rate = other_ref[EXTRA, :, lanes + LANES:lanes + 2 * LANES]
            south = jnp.maximum(first_rate[:, :1], 0.0) * column_ref[c, 0, STEPS - 1 + r, :, :1]
            north = jnp.maximum(-last_rate[:, LANES - 1:], 0.0) * column_ref[c, 1, STEPS - 1 + r, :, LANES - 1:]
            total = total + south * near_mixing[c, 0, pl.ds(i, 1), :]
            total = total + north * near_mixing[c, 1, pl.ds(i, 1), :]
        sum_ref[c] = jnp.where(has_neighbour(flip), total, partial_ref[c])


def mend_side(flip, east_ref, north_ref, mine_ref, other_ref, store, store_column):
    levels, width = mine_ref.shape[1:]
    rows = east_ref.shape[1]
    sign = sign_of(flip)
    place = lambda r: flip * (rows - STEPS) + r + flip * (STEPS - 1 - 2 * r)

    def half(at):
        own = [Row(east_ref[0, place(r), at, :] * sign, north_ref[0, place(r), at, :]) for r in range(STEPS - 1)]
        near = Row(other_ref[FLUX_ROWS, at, :] * sign, other_ref[FLUX_ROWS + 1, at, :])
        far = Row(other_ref[FLUX_ROWS + 2, at, :] * sign)
        for c in range(FLUX_ROWS // STEPS):
            mine = lambda k: mine_ref[2 * k + c, at, :]
            theirs = lambda k: other_ref[2 * k + c, at, :]
            a0 = theirs(0)
            n1 = mine(0)
            b0 = own[0].stay(a0) + near.inward * n1 + theirs(1)
            b1 = own[0].inward * a0
            bn1 = near.stay(n1) + own[0].outward * a0 + mine(1)
            bn2 = near.outward * n1
            c0 = own[0].stay(b0) + near.inward * bn1 + own[1].outward * b1 + theirs(2)
            c1 = own[1].stay(b1) + own[0].inward * b0
            c2 = own[1].inward * b1
            cn1 = near.stay(bn1) + own[0].outward * b0 + far.inward * bn2 + mine(2)
            d0 = own[0].stay(c0) + near.inward * cn1 + own[1].outward * c1 + theirs(3)
            d1 = own[1].stay(c1) + own[0].inward * c0 + own[2].outward * c2
            d2 = own[2].stay(c2) + own[1].inward * c1
            d3 = own[2].inward * c2
            for r, value in enumerate((d0, d1, d2, d3)):
                store(c, r, at, value)
            if store_column is not None:
                tiles = (slice(0, LANES), slice(width - LANES, width))
                for s, lanes in enumerate(tiles):
                    tile = lambda value: value[:, lanes]
                    rate = other_ref[EXTRA, at, s * LANES:(s + 1) * LANES]
                    stays = 1.0 - jnp.abs(other_ref[FLUX_ROWS + 2, at, lanes]) - jnp.abs(rate)
                    drift = jnp.maximum(rate if s == 0 else -rate, 0.0) * tile(bn2)
                    cn2 = stays * tile(bn2) + pltpu.roll(drift, LANES - 1 if s == 0 else 1, 1)
                    cn2 = cn2 + tile(near.outward) * tile(bn1)
                    cn3 = tile(far.outward) * tile(bn2)
                    sums = (
                        tile(a0) + tile(b0) + tile(c0), tile(b1) + tile(c1), tile(c2),
                        tile(n1) + tile(bn1) + tile(cn1), tile(bn2) + cn2, cn3,
                    )
                    for r, value in enumerate(sums):
                        store_column(c, s, r, at, value)

    level_halves(levels, half)


def copy_end(flip, ends_ref, out_ref):
    for c in range(out_ref.shape[0]):
        for r in range(STEPS):
            out_ref[c, r] = ends_ref[c, flip * STEPS + r]


def mend_a_kernel(east_ref, north_ref, mine_ref, other_ref, ends_ref, base_ref, out_ref, column_ref):
    flip = 1 - parity()
    turn = lambda r: r + flip * (STEPS - 1 - 2 * r)

    def store(c, r, at, value):
        out_ref[c, turn(r), at, :] = ends_ref[c, flip * STEPS + turn(r), at, :] + value

    def store_column(c, s, r, at, value):
        column_ref[c, s, r, at, :] = value

    @pl.when(has_neighbour(flip))
    def _():
        mend_side(flip, east_ref, north_ref, mine_ref, other_ref, store, store_column)

    @pl.when(jnp.logical_not(has_neighbour(flip)))
    def _():
        column_ref[...] = jnp.zeros_like(column_ref)
        copy_end(flip, ends_ref, out_ref)


def mend_b_kernel(east_ref, north_ref, mine_ref, other_ref, ends_ref, _, __, out_ref):
    flip = parity()
    turn = lambda r: r + flip * (STEPS - 1 - 2 * r)

    def store(c, r, at, value):
        out_ref[c, turn(r), at, :] = ends_ref[c, flip * STEPS + turn(r), at, :] + value

    @pl.when(has_neighbour(flip))
    def _():
        mend_side(flip, east_ref, north_ref, mine_ref, other_ref, store, None)

    @pl.when(jnp.logical_not(has_neighbour(flip)))
    def _():
        copy_end(flip, ends_ref, out_ref)


def subtract_rows(state_ref, out_hbm, buffer, sems, jobs):
    copies = []
    is_last = lax.axis_index("sub") == lax.axis_size("sub") - 1
    for start, other in jobs:
        for c in range(other.shape[0]):
            count = other.shape[1]
            for r in range(count):
                buffer[c, start + r] = state_ref[0, c, start + r] - jnp.where(is_last, 0.0, other[c, r])
            at = pl.ds(start, count)
            copy = pltpu.make_async_copy(buffer.at[c, at], out_hbm.at[0, c, at], sems.at[len(copies)])
            copy.start()
            copies.append(copy)
    return copies


def begin_kernel(state_ref, middle_ref, a_ref, out_hbm, buffer, sems):
    start = parity() * (state_ref.shape[2] - STEPS)
    for copy in subtract_rows(state_ref, out_hbm, buffer, sems, ((STEPS, middle_ref), (start, a_ref))):
        copy.wait()


def end_kernel(begun_hbm, state_ref, b_ref, out_hbm, buffer, sems):
    start = (1 - parity()) * (state_ref.shape[2] - STEPS)
    for copy in subtract_rows(state_ref, out_hbm, buffer, sems, ((start, b_ref),)):
        copy.wait()


def pick_kernel(_, owner_ref, total_ref, came_ref, gradient_ref):
    parts = gradient_ref.shape[0]
    share, mine = gradient_ref.shape[1:]
    start = lax.axis_index("hor") * mine
    chosen = []
    for c in range(parts):
        total = total_ref[c] + came_ref[c]
        block = total[:share]
        for s in range(1, total.shape[0] // share):
            block = jnp.where(lax.axis_index("sub") == s, total[s * share:(s + 1) * share], block)
        chosen.append(block)
    chosen = jnp.concatenate(chosen, 0)
    column = lax.broadcasted_iota(jnp.int32, (parts * share, mine), 1)
    picked = jnp.zeros((parts * share, mine), jnp.float32)
    for q in range(mine):
        value = jnp.sum(jnp.where(owner_ref[...] == start + q, chosen, 0.0), axis=1, keepdims=True)
        picked = jnp.where(column == q, value, picked)
    for c in range(parts):
        gradient_ref[c] = picked[c * share:(c + 1) * share]


BRIEF = pl.CostEstimate(flops=1, bytes_accessed=1, transcendentals=0)
PARAMS = pltpu.CompilerParams(vmem_limit_bytes=24 * 1024 * 1024)


def local(
    adjoint_state,
    courant_east,
    courant_north,
    parent_cell,
    stencil_offset,
    stencil_weight,
    owner_slot,
):
    _, parts, rows, levels, width = adjoint_state.shape
    slots = owner_slot.shape[0]
    inner = rows - 2 * STEPS
    row_bytes = levels * width * 4
    f32 = lambda *shape: jax.ShapeDtypeStruct(shape, jnp.float32)
    vmem = pl.BlockSpec(memory_space=pltpu.VMEM)
    smem = pl.BlockSpec(memory_space=pltpu.SMEM)
    hbm = pl.BlockSpec(memory_space=pltpu.HBM)
    in_hbm = lambda value: pltpu.with_memory_space_constraint(value, pltpu.HBM)

    subs, hors = lax.axis_size("sub"), lax.axis_size("hor")
    small = [parent_cell, stencil_offset, stencil_weight]

    first_pack = pl.pallas_call(
        pack_kernel,
        in_specs=[hbm] * 6,
        out_specs=vmem,
        out_shape=f32(PACK_ROWS + 1, levels, width),
        scratch_shapes=[
            pltpu.VMEM((parts, STEPS, levels, width), jnp.float32),
            pltpu.VMEM((STEPS, levels, width), jnp.float32),
            pltpu.VMEM((STEPS, levels, width), jnp.float32),
        ]
        + [pltpu.VMEM(value.shape, value.dtype) for value in small]
        + [pltpu.SemaphoreType.DMA((levels // HALF, parts + 2)), pltpu.SemaphoreType.DMA((3,))],
        compiler_params=PARAMS,
        cost_estimate=BRIEF,
        name="pack",
    )(*[in_hbm(value) for value in [adjoint_state, courant_east, courant_north] + small])
    first_came = alternating(first_pack, -1)

    state, east, north = adjoint_state, courant_east, courant_north
    second_pack, middle, ends, columns = pl.pallas_call(
        sweep_kernel,
        in_specs=[vmem] * 3,
        out_specs=[vmem] * 4,
        out_shape=[
            f32(PACK_ROWS, levels, width),
            f32(parts, inner, levels, width),
            f32(parts, 2 * STEPS, levels, width),
            f32(parts, 2, rows, levels, LANES),
        ],
        scratch_shapes=[
            pltpu.VMEM((STEPS - 1, parts, rows, HALF, width), jnp.float32),
            pltpu.VMEM((rows, HALF, width), jnp.float32),
            pltpu.VMEM((rows, HALF, width), jnp.float32),
            pltpu.VMEM((rows, HALF, width), jnp.float32),
        ],
        compiler_params=PARAMS,
        cost_estimate=BRIEF,
        name="sweep",
    )(state, east, north)
    middle_came = to_previous(middle)

    mixing, base, owner, second_sent = pl.pallas_call(
        ghost_base_kernel,
        in_specs=[vmem] * 7,
        out_specs=[vmem] * 4,
        out_shape=[
            f32(parts, 2, rows, slots), f32(parts, levels, slots),
            jax.ShapeDtypeStruct((1, slots), owner_slot.dtype), f32(PACK_ROWS, levels, width),
        ],
        compiler_params=PARAMS,
        cost_estimate=BRIEF,
        name="ghost_base",
    )(*small, owner_slot[None], columns, north, second_pack)
    second_came = alternating(second_sent, 1)

    column_shape = (parts, 2, 2 * (STEPS - 1), levels, LANES)
    side_a, a_columns = pl.pallas_call(
        mend_a_kernel,
        in_specs=[vmem] * 6,
        out_specs=[vmem] * 2,
        out_shape=[f32(parts, STEPS, levels, width), f32(*column_shape)],
        compiler_params=PARAMS,
        cost_estimate=BRIEF,
        name="mend_a",
    )(east, north, second_pack, first_came, ends, base)
    a_came = to_previous(side_a)
    total = pl.pallas_call(
        ghost_kernel,
        in_specs=[vmem] * 5,
        out_specs=vmem,
        out_shape=f32(parts, levels, slots),
        scratch_shapes=[pltpu.VMEM((parts, 2, rows, slots), jnp.float32)],
        compiler_params=PARAMS,
        cost_estimate=BRIEF,
        name="ghost",
    )(north, first_came, a_columns, mixing, base)
    order = rounds()
    total = total + exchanged(total, *order[0])
    side_b = pl.pallas_call(
        mend_b_kernel,
        in_specs=[vmem] * 5 + [pl.BlockSpec(memory_space=pl.ANY)] * 2,
        out_specs=vmem,
        out_shape=f32(parts, STEPS, levels, width),
        compiler_params=PARAMS,
        cost_estimate=BRIEF,
        name="mend_b",
    )(east, north, first_pack, second_came, ends, middle_came, total)
    b_came = to_previous(side_b)

    for each in order[1:-1]:
        total = total + exchanged(total, *each)
    came = exchanged(total, *order[-1])

    result = f32(*adjoint_state.shape)
    buffer = pltpu.VMEM((parts, rows, levels, width), jnp.float32)
    begun = pl.pallas_call(
        begin_kernel,
        in_specs=[vmem] * 3,
        out_specs=hbm,
        out_shape=result,
        scratch_shapes=[buffer, pltpu.SemaphoreType.DMA((2 * parts,))],
        compiler_params=PARAMS,
        cost_estimate=BRIEF,
        name="begin",
    )(state, middle_came, a_came)
    adjoint_result = pl.pallas_call(
        end_kernel,
        in_specs=[hbm] + [vmem] * 2,
        out_specs=hbm,
        out_shape=result,
        scratch_shapes=[buffer, pltpu.SemaphoreType.DMA((parts,))],
        input_output_aliases={0: 0},
        compiler_params=PARAMS,
        cost_estimate=BRIEF,
        name="end",
    )(begun, state, b_came)
    boundary_gradient = pl.pallas_call(
        pick_kernel,
        in_specs=[pl.BlockSpec(memory_space=pl.ANY)] + [vmem] * 3,
        out_specs=vmem,
        out_shape=f32(parts, levels // subs, slots // hors),
        compiler_params=PARAMS,
        cost_estimate=BRIEF,
        name="pick",
    )(adjoint_result, owner, total, came)
    return (adjoint_result, boundary_gradient)


def solution(mesh):
    in_specs = (
        P(("ens", "sub"), None, "hor", None, None),
        P(("ens", "sub"), "hor", None, None),
        P(("ens", "sub"), "hor", None, None),
        P(None, None, "hor"),
        P(None, None, None, "hor"),
        P(None, None, None, "hor"),
        P(),
    )
    out_specs = (P(("ens", "sub"), None, "hor", None, None), P("ens", "sub", "hor"))
    return jax.shard_map(local, mesh=mesh, in_specs=in_specs, out_specs=out_specs, check_vma=False)
```

```python
import functools

import jax
import jax.numpy as jnp
from jax import lax
from jax.experimental import pallas as pl
from jax.experimental.pallas import tpu as pltpu
from jax.sharding import PartitionSpec as P

STEPS = 4
HALF = 8
FLUX_ROWS = 2 * STEPS
PACK_ROWS = FLUX_ROWS + 3
LANES = 128
EXTRA = PACK_ROWS
TARGETS = 4 * LANES
WEIGHTS = 5 * LANES


def to_previous(value):
    peers = lax.axis_size("sub")
    return lax.ppermute(value, "sub", [(i, (i - 1) % peers) for i in range(peers)])


def alternating(value, sign):
    subs, hors = lax.axis_size("sub"), lax.axis_size("hor")
    assert subs % 2 == 0
    pairs = []
    for s in range(subs):
        step = sign if s % 2 == 0 else -sign
        for h in range(hors):
            inside = 0 <= h + step < hors
            pairs.append((s * hors + h, s * hors + h + step if inside else (s ^ 1) * hors + h))
    return lax.ppermute(value, ("sub", "hor"), pairs)


def has_neighbour(flip):
    hor = lax.axis_index("hor")
    return jnp.where(flip == 1, hor < lax.axis_size("hor") - 1, hor > 0)


def rounds():
    subs, hors = lax.axis_size("sub"), lax.axis_size("hor")
    assert not subs & (subs - 1) and not hors & (hors - 1)
    order = [("sub", range(min(subs, 4) - 1, 0, -1))]
    order += [("sub", [1 << n]) for n in range(2, subs.bit_length() - 1)]
    return order + [("hor", [1 << n]) for n in range(hors.bit_length() - 1)]


def exchanged(value, axis, distances):
    size = lax.axis_size(axis)
    return sum(lax.ppermute(value, axis, [(i, i ^ distance) for i in range(size)]) for distance in distances)


def parity():
    return lax.rem(lax.axis_index("sub"), 2)


def sign_of(flip):
    return jnp.where(flip == 1, jnp.float32(-1.0), jnp.float32(1.0))


def north_rates(north_rate):
    width = north_rate.shape[-1]
    column = lax.broadcasted_iota(jnp.int32, north_rate.shape, len(north_rate.shape) - 1)
    plus = jnp.where(column == 0, 0.0, jnp.maximum(north_rate, 0.0))
    minus = jnp.where(column == width - 1, 0.0, jnp.maximum(-north_rate, 0.0))
    return plus, minus


def shifted(flux_plus, flux_minus):
    width = flux_plus.shape[-1]
    axis = len(flux_plus.shape) - 1
    return pltpu.roll(flux_plus, width - 1, axis) + pltpu.roll(flux_minus, 1, axis)


class Row:
    def __init__(self, east_rate, north_rate=None):
        self.outward = jnp.maximum(east_rate, 0.0)
        self.inward = jnp.maximum(-east_rate, 0.0)
        if north_rate is not None:
            self.centre = 1.0 - jnp.abs(east_rate) - jnp.abs(north_rate)
            self.plus, self.minus = north_rates(north_rate)

    def stay(self, value):
        return self.centre * value + shifted(self.plus * value, self.minus * value)


def level_halves(levels, body):
    def step(h, carry):
        body(pl.ds(pl.multiple_of(h * HALF, HALF), HALF))
        return carry

    lax.fori_loop(0, levels // HALF, step, 0)


def pack_kernel(
    state_hbm, east_hbm, north_hbm, cell_hbm, offset_hbm, weight_hbm,
    pack_ref, state_ref, east_ref, north_ref, cell_ref, offset_ref, weight_ref, sems, small_sems,
):
    parts, rows, levels, width = state_hbm.shape[1:]
    flip = parity()
    sign = sign_of(flip)
    at_end = pl.ds(flip * (rows - STEPS), STEPS)
    place = lambda r: r + flip * (STEPS - 1 - 2 * r)
    halves = levels // HALF
    copies = []
    for h in range(halves):
        at = pl.ds(h * HALF, HALF)
        sem = sems.at[h]
        batch = [
            pltpu.make_async_copy(state_hbm.at[0, c, at_end, at], state_ref.at[c, :, at], sem.at[c])
            for c in range(parts)
        ]
        batch.append(pltpu.make_async_copy(east_hbm.at[0, at_end, at], east_ref.at[:, at], sem.at[parts]))
        batch.append(pltpu.make_async_copy(north_hbm.at[0, at_end, at], north_ref.at[:, at], sem.at[parts + 1]))
        copies.append(batch)
        for copy in batch:
            copy.start()
    small = [
        pltpu.make_async_copy(source, target, small_sems.at[n])
        for n, (source, target) in enumerate(
            ((cell_hbm, cell_ref), (offset_hbm, offset_ref), (weight_hbm, weight_ref))
        )
    ]
    for copy in small:
        copy.start()

    def half(at):
        row = [Row(east_ref[place(r), at, :] * sign, north_ref[place(r), at, :]) for r in range(STEPS)]
        pack_ref[FLUX_ROWS, at, :] = east_ref[place(0), at, :]
        pack_ref[FLUX_ROWS + 1, at, :] = north_ref[place(0), at, :]
        pack_ref[FLUX_ROWS + 2, at, :] = east_ref[place(1), at, :]
        for r in (1, 2):
            lanes = (2 * r - 2) * LANES
            pack_ref[EXTRA, at, lanes:lanes + LANES] = north_ref[place(r), at, :LANES]
            pack_ref[EXTRA, at, lanes + LANES:lanes + 2 * LANES] = north_ref[place(r), at, width - LANES:]
        for c in range(parts):
            field = [state_ref[c, place(r), at, :] for r in range(STEPS)]
            for k in range(STEPS):
                pack_ref[2 * k + c, at, :] = row[0].outward * field[0]
                after = []
                for r in range(STEPS - 1 - k):
                    value = row[r].stay(field[r]) + row[r + 1].outward * field[r + 1]
                    if r > 0:
                        value = value + row[r - 1].inward * field[r - 1]
                    after.append(value)
                field = after

    for h in range(halves):
        for copy in copies[h]:
            copy.wait()
        half(pl.ds(h * HALF, HALF))

    for copy in small:
        copy.wait()
    n = 0
    for point in range(offset_ref.shape[0]):
        for c in range(parts):
            target = (cell_ref[c] + offset_ref[point, c]).astype(jnp.float32)
            pack_ref[EXTRA, n:n + 2, TARGETS:TARGETS + rows] = target
            pack_ref[EXTRA, n:n + 2, WEIGHTS:WEIGHTS + rows] = weight_ref[point, c]
            n += 2


def as_column(row):
    count = row.shape[1]
    here = lax.broadcasted_iota(jnp.int32, (count, count), 0)
    there = lax.broadcasted_iota(jnp.int32, (count, count), 1)
    return jnp.sum(jnp.where(here == there, row, 0), axis=1, keepdims=True)


def sweep_kernel(
    state_ref, east_ref, north_ref, pack_ref, middle_ref, ends_ref, column_ref,
    field, plus_ref, minus_ref, centre_ref,
):
    parts, rows, levels, width = state_ref.shape[1:]
    flip = 1 - parity()
    sign = sign_of(flip)
    end_row = flip * (rows - 1)
    next_row = end_row + 1 - 2 * flip

    def half(at):
        pack_ref[FLUX_ROWS, at, :] = east_ref[0, end_row, at, :]
        pack_ref[FLUX_ROWS + 1, at, :] = north_ref[0, end_row, at, :]
        pack_ref[FLUX_ROWS + 2, at, :] = east_ref[0, next_row, at, :]

        for k in range(STEPS):
            if k == 0:
                read = lambda c, i: state_ref[0, c, i, at, :]
            else:
                read = lambda c, i, slot=k - 1: field[slot, c, i]
            leaving = jnp.maximum(east_ref[0, end_row, at, :] * sign, 0.0)
            for c in range(parts):
                pack_ref[2 * k + c, at, :] = leaving * read(c, end_row)
            west = [None] * parts
            here = [read(c, 0) for c in range(parts)]
            east_here = east_ref[0, 0, at, :]
            for i in range(rows):
                leave_west = jnp.maximum(-east_here, 0.0)
                if k == 0:
                    north_rate = north_ref[0, i, at, :]
                    centre = 1.0 - jnp.abs(east_here) - jnp.abs(north_rate)
                    plus, minus = north_rates(north_rate)
                    centre_ref[i], plus_ref[i], minus_ref[i] = centre, plus, minus
                else:
                    centre, plus, minus = centre_ref[i], plus_ref[i], minus_ref[i]
                if i + 1 < rows:
                    east_here = east_ref[0, i + 1, at, :]
                    east_after = jnp.maximum(east_here, 0.0)
                for c in range(parts):
                    value = here[c]
                    total = centre * value + shifted(plus * value, minus * value)
                    if i > 0:
                        total = total + west[c]
                    if i + 1 < rows:
                        west[c] = leave_west * value
                        here[c] = read(c, i + 1)
                        total = total + east_after * here[c]
                    if k < STEPS - 1:
                        field[k, c, i] = total
                    elif i < STEPS:
                        ends_ref[c, i, at, :] = total
                    elif i >= rows - STEPS:
                        ends_ref[c, i - rows + 2 * STEPS, at, :] = total
                    else:
                        middle_ref[c, i - STEPS, at, :] = total

        def columns(i, carry):
            for c in range(parts):
                value = state_ref[0, c, i, at, :]
                first, last = value[:, :LANES], value[:, width - LANES:]
                for slot in range(STEPS - 1):
                    first = first + field[slot, c, i, :, :LANES]
                    last = last + field[slot, c, i, :, width - LANES:]
                column_ref[c, 0, i, at, :] = first
                column_ref[c, 1, i, at, :] = last
            return carry

        lax.fori_loop(0, rows, columns, 0, unroll=2)

    level_halves(levels, half)


def mix(targets, weights, cells, total):
    for target, weight in zip(targets, weights):
        total = total + jnp.where(as_column(target) == cells, as_column(weight), 0.0)
    return total


def ghost_base_kernel(
    cell_ref, offset_ref, weight_ref, owner_ref, column_ref, north_ref, pack_ref,
    mixing_ref, partial_ref, owner_out, pack_out,
):
    owner_out[...] = owner_ref[...]
    pack_out[...] = pack_ref[...]
    parts, _, rows, levels, _ = column_ref.shape
    slots = mixing_ref.shape[-1]
    width = north_ref.shape[-1]
    points = range(offset_ref.shape[0])
    cells = lax.broadcasted_iota(jnp.int32, (rows, slots), 1)
    for c in range(parts):
        for s in range(2):
            mixing_ref[c, s] = mix(
                [cell_ref[c, s:s + 1, :] + offset_ref[point, c, s:s + 1, :] for point in points],
                [weight_ref[point, c, s:s + 1, :] for point in points],
                cells, jnp.zeros((rows, slots), jnp.float32),
            )

    for c in range(parts):
        total = jnp.zeros((levels, slots), jnp.float32)
        for i in range(rows):
            south = jnp.maximum(north_ref[0, i, :, :1], 0.0) * column_ref[c, 0, i, :, :1]
            north = jnp.maximum(-north_ref[0, i, :, width - 1:], 0.0) * column_ref[c, 1, i, :, LANES - 1:]
            total = total + south * mixing_ref[c, 0, i:i + 1, :]
            total = total + north * mixing_ref[c, 1, i:i + 1, :]
        partial_ref[c] = total


def ghost_kernel(north_ref, other_ref, column_ref, mixing_ref, partial_ref, sum_ref, near_mixing):
    parts, levels, slots = partial_ref.shape
    rows = mixing_ref.shape[2]
    width = north_ref.shape[-1]
    flip = 1 - parity()
    cells = lax.broadcasted_iota(jnp.int32, (rows, slots), 1).astype(jnp.float32)
    points = (WEIGHTS - TARGETS) // LANES * 4
    for c in range(parts):
        for s in range(2):
            at = [(point * parts + c) * 2 + s for point in range(points)]
            near_mixing[c, s] = mix(
                [other_ref[EXTRA, n:n + 1, TARGETS:TARGETS + rows] for n in at],
                [other_ref[EXTRA, n:n + 1, WEIGHTS:WEIGHTS + rows] for n in at],
                cells, jnp.zeros((rows, slots), jnp.float32),
            )
    for c in range(parts):
        total = partial_ref[c]
        for r in range(STEPS - 1):
            i = r + flip * (rows - 1 - 2 * r)
            south = jnp.maximum(north_ref[0, i, :, :1], 0.0) * column_ref[c, 0, r, :, :1]
            north = jnp.maximum(-north_ref[0, i, :, width - 1:], 0.0) * column_ref[c, 1, r, :, LANES - 1:]
            total = total + south * mixing_ref[c, 0, pl.ds(i, 1), :]
            total = total + north * mixing_ref[c, 1, pl.ds(i, 1), :]
            i = r + (1 - flip) * (rows - 1 - 2 * r)
            if r == 0:
                first_rate = other_ref[FLUX_ROWS + 1, :, :LANES]
                last_rate = other_ref[FLUX_ROWS + 1, :, width - LANES:]
            else:
                lanes = (2 * r - 2) * LANES
                first_rate = other_ref[EXTRA, :, lanes:lanes + LANES]
                last_rate = other_ref[EXTRA, :, lanes + LANES:lanes + 2 * LANES]
            south = jnp.maximum(first_rate[:, :1], 0.0) * column_ref[c, 0, STEPS - 1 + r, :, :1]
            north = jnp.maximum(-last_rate[:, LANES - 1:], 0.0) * column_ref[c, 1, STEPS - 1 + r, :, LANES - 1:]
            total = total + south * near_mixing[c, 0, pl.ds(i, 1), :]
            total = total + north * near_mixing[c, 1, pl.ds(i, 1), :]
        sum_ref[c] = jnp.where(has_neighbour(flip), total, partial_ref[c])


def mend_side(flip, east_ref, north_ref, mine_ref, other_ref, store, store_column):
    levels, width = mine_ref.shape[1:]
    rows = east_ref.shape[1]
    sign = sign_of(flip)
    place = lambda r: flip * (rows - STEPS) + r + flip * (STEPS - 1 - 2 * r)

    def half(at):
        own = [Row(east_ref[0, place(r), at, :] * sign, north_ref[0, place(r), at, :]) for r in range(STEPS - 1)]
        near = Row(other_ref[FLUX_ROWS, at, :] * sign, other_ref[FLUX_ROWS + 1, at, :])
        far = Row(other_ref[FLUX_ROWS + 2, at, :] * sign)
        for c in range(FLUX_ROWS // STEPS):
            mine = lambda k: mine_ref[2 * k + c, at, :]
            theirs = lambda k: other_ref[2 * k + c, at, :]
            a0 = theirs(0)
            n1 = mine(0)
            b0 = own[0].stay(a0) + near.inward * n1 + theirs(1)
            b1 = own[0].inward * a0
            bn1 = near.stay(n1) + own[0].outward * a0 + mine(1)
            bn2 = near.outward * n1
            c0 = own[0].stay(b0) + near.inward * bn1 + own[1].outward * b1 + theirs(2)
            c1 = own[1].stay(b1) + own[0].inward * b0
            c2 = own[1].inward * b1
            cn1 = near.stay(bn1) + own[0].outward * b0 + far.inward * bn2 + mine(2)
            d0 = own[0].stay(c0) + near.inward * cn1 + own[1].outward * c1 + theirs(3)
            d1 = own[1].stay(c1) + own[0].inward * c0 + own[2].outward * c2
            d2 = own[2].stay(c2) + own[1].inward * c1
            d3 = own[2].inward * c2
            for r, value in enumerate((d0, d1, d2, d3)):
                store(c, r, at, value)
            if store_column is not None:
                tiles = (slice(0, LANES), slice(width - LANES, width))
                for s, lanes in enumerate(tiles):
                    tile = lambda value: value[:, lanes]
                    rate = other_ref[EXTRA, at, s * LANES:(s + 1) * LANES]
                    stays = 1.0 - jnp.abs(other_ref[FLUX_ROWS + 2, at, lanes]) - jnp.abs(rate)
                    drift = jnp.maximum(rate if s == 0 else -rate, 0.0) * tile(bn2)
                    cn2 = stays * tile(bn2) + pltpu.roll(drift, LANES - 1 if s == 0 else 1, 1)
                    cn2 = cn2 + tile(near.outward) * tile(bn1)
                    cn3 = tile(far.outward) * tile(bn2)
                    sums = (
                        tile(a0) + tile(b0) + tile(c0), tile(b1) + tile(c1), tile(c2),
                        tile(n1) + tile(bn1) + tile(cn1), tile(bn2) + cn2, cn3,
                    )
                    for r, value in enumerate(sums):
                        store_column(c, s, r, at, value)

    level_halves(levels, half)


def copy_end(flip, ends_ref, out_ref):
    for c in range(out_ref.shape[0]):
        for r in range(STEPS):
            out_ref[c, r] = ends_ref[c, flip * STEPS + r]


def mend_a_kernel(east_ref, north_ref, mine_ref, other_ref, ends_ref, base_ref, out_ref, column_ref):
    flip = 1 - parity()
    turn = lambda r: r + flip * (STEPS - 1 - 2 * r)

    def store(c, r, at, value):
        out_ref[c, turn(r), at, :] = ends_ref[c, flip * STEPS + turn(r), at, :] + value

    def store_column(c, s, r, at, value):
        column_ref[c, s, r, at, :] = value

    @pl.when(has_neighbour(flip))
    def _():
        mend_side(flip, east_ref, north_ref, mine_ref, other_ref, store, store_column)

    @pl.when(jnp.logical_not(has_neighbour(flip)))
    def _():
        column_ref[...] = jnp.zeros_like(column_ref)
        copy_end(flip, ends_ref, out_ref)


def mend_b_kernel(east_ref, north_ref, mine_ref, other_ref, ends_ref, _, __, out_ref):
    flip = parity()
    turn = lambda r: r + flip * (STEPS - 1 - 2 * r)

    def store(c, r, at, value):
        out_ref[c, turn(r), at, :] = ends_ref[c, flip * STEPS + turn(r), at, :] + value

    @pl.when(has_neighbour(flip))
    def _():
        mend_side(flip, east_ref, north_ref, mine_ref, other_ref, store, None)

    @pl.when(jnp.logical_not(has_neighbour(flip)))
    def _():
        copy_end(flip, ends_ref, out_ref)


def subtract_rows(state_ref, out_hbm, buffer, sems, jobs):
    copies = []
    is_last = lax.axis_index("sub") == lax.axis_size("sub") - 1
    for start, other in jobs:
        for c in range(other.shape[0]):
            count = other.shape[1]
            for r in range(count):
                buffer[c, start + r] = state_ref[0, c, start + r] - jnp.where(is_last, 0.0, other[c, r])
            at = pl.ds(start, count)
            copy = pltpu.make_async_copy(buffer.at[c, at], out_hbm.at[0, c, at], sems.at[len(copies)])
            copy.start()
            copies.append(copy)
    return copies


def begin_kernel(state_ref, middle_ref, a_ref, out_hbm, buffer, sems):
    start = parity() * (state_ref.shape[2] - STEPS)
    for copy in subtract_rows(state_ref, out_hbm, buffer, sems, ((STEPS, middle_ref), (start, a_ref))):
        copy.wait()


def end_kernel(begun_hbm, state_ref, b_ref, out_hbm, buffer, sems):
    start = (1 - parity()) * (state_ref.shape[2] - STEPS)
    for copy in subtract_rows(state_ref, out_hbm, buffer, sems, ((start, b_ref),)):
        copy.wait()


def pick_kernel(_, owner_ref, total_ref, came_ref, gradient_ref):
    parts = gradient_ref.shape[0]
    share, mine = gradient_ref.shape[1:]
    start = lax.axis_index("hor") * mine
    chosen = []
    for c in range(parts):
        total = total_ref[c] + came_ref[c]
        block = total[:share]
        for s in range(1, total.shape[0] // share):
            block = jnp.where(lax.axis_index("sub") == s, total[s * share:(s + 1) * share], block)
        chosen.append(block)
    chosen = jnp.concatenate(chosen, 0)
    column = lax.broadcasted_iota(jnp.int32, (parts * share, mine), 1)
    picked = jnp.zeros((parts * share, mine), jnp.float32)
    for q in range(mine):
        value = jnp.sum(jnp.where(owner_ref[...] == start + q, chosen, 0.0), axis=1, keepdims=True)
        picked = jnp.where(column == q, value, picked)
    for c in range(parts):
        gradient_ref[c] = picked[c * share:(c + 1) * share]


BRIEF = pl.CostEstimate(flops=1, bytes_accessed=1, transcendentals=0)
PARAMS = pltpu.CompilerParams(vmem_limit_bytes=24 * 1024 * 1024)


def local(
    adjoint_state,
    courant_east,
    courant_north,
    parent_cell,
    stencil_offset,
    stencil_weight,
    owner_slot,
):
    _, parts, rows, levels, width = adjoint_state.shape
    slots = owner_slot.shape[0]
    inner = rows - 2 * STEPS
    row_bytes = levels * width * 4
    f32 = lambda *shape: jax.ShapeDtypeStruct(shape, jnp.float32)
    vmem = pl.BlockSpec(memory_space=pltpu.VMEM)
    smem = pl.BlockSpec(memory_space=pltpu.SMEM)
    hbm = pl.BlockSpec(memory_space=pltpu.HBM)
    in_hbm = lambda value: pltpu.with_memory_space_constraint(value, pltpu.HBM)

    subs, hors = lax.axis_size("sub"), lax.axis_size("hor")
    small = [parent_cell, stencil_offset, stencil_weight]

    first_pack = pl.pallas_call(
        pack_kernel,
        in_specs=[hbm] * 6,
        out_specs=vmem,
        out_shape=f32(PACK_ROWS + 1, levels, width),
        scratch_shapes=[
            pltpu.VMEM((parts, STEPS, levels, width), jnp.float32),
            pltpu.VMEM((STEPS, levels, width), jnp.float32),
            pltpu.VMEM((STEPS, levels, width), jnp.float32),
        ]
        + [pltpu.VMEM(value.shape, value.dtype) for value in small]
        + [pltpu.SemaphoreType.DMA((levels // HALF, parts + 2)), pltpu.SemaphoreType.DMA((3,))],
        compiler_params=PARAMS,
        cost_estimate=BRIEF,
        name="pack",
    )(*[in_hbm(value) for value in [adjoint_state, courant_east, courant_north] + small])
    first_came = alternating(first_pack, -1)

    state, east, north = adjoint_state, courant_east, courant_north
    second_pack, middle, ends, columns = pl.pallas_call(
        sweep_kernel,
        in_specs=[vmem] * 3,
        out_specs=[vmem] * 4,
        out_shape=[
            f32(PACK_ROWS, levels, width),
            f32(parts, inner, levels, width),
            f32(parts, 2 * STEPS, levels, width),
            f32(parts, 2, rows, levels, LANES),
        ],
        scratch_shapes=[
            pltpu.VMEM((STEPS - 1, parts, rows, HALF, width), jnp.float32),
            pltpu.VMEM((rows, HALF, width), jnp.float32),
            pltpu.VMEM((rows, HALF, width), jnp.float32),
            pltpu.VMEM((rows, HALF, width), jnp.float32),
        ],
        compiler_params=PARAMS,
        cost_estimate=BRIEF,
        name="sweep",
    )(state, east, north)
    middle_came = to_previous(middle)

    mixing, base, owner, second_sent = pl.pallas_call(
        ghost_base_kernel,
        in_specs=[vmem] * 7,
        out_specs=[vmem] * 4,
        out_shape=[
            f32(parts, 2, rows, slots), f32(parts, levels, slots),
            jax.ShapeDtypeStruct((1, slots), owner_slot.dtype), f32(PACK_ROWS, levels, width),
        ],
        compiler_params=PARAMS,
        cost_estimate=BRIEF,
        name="ghost_base",
    )(*small, owner_slot[None], columns, north, second_pack)
    second_came = alternating(second_sent, 1)

    column_shape = (parts, 2, 2 * (STEPS - 1), levels, LANES)
    side_a, a_columns = pl.pallas_call(
        mend_a_kernel,
        in_specs=[vmem] * 6,
        out_specs=[vmem] * 2,
        out_shape=[f32(parts, STEPS, levels, width), f32(*column_shape)],
        compiler_params=PARAMS,
        cost_estimate=BRIEF,
        name="mend_a",
    )(east, north, second_pack, first_came, ends, base)
    a_came = to_previous(side_a)
    total = pl.pallas_call(
        ghost_kernel,
        in_specs=[vmem] * 5,
        out_specs=vmem,
        out_shape=f32(parts, levels, slots),
        scratch_shapes=[pltpu.VMEM((parts, 2, rows, slots), jnp.float32)],
        compiler_params=PARAMS,
        cost_estimate=BRIEF,
        name="ghost",
    )(north, first_came, a_columns, mixing, base)
    order = rounds()
    total = total + exchanged(total, *order[0])
    side_b = pl.pallas_call(
        mend_b_kernel,
        in_specs=[vmem] * 5 + [pl.BlockSpec(memory_space=pl.ANY)] * 2,
        out_specs=vmem,
        out_shape=f32(parts, STEPS, levels, width),
        compiler_params=PARAMS,
        cost_estimate=BRIEF,
        name="mend_b",
    )(east, north, first_pack, second_came, ends, middle_came, total)
    b_came = to_previous(side_b)

    for each in order[1:-1]:
        total = total + exchanged(total, *each)
    came = exchanged(total, *order[-1])

    result = f32(*adjoint_state.shape)
    buffer = pltpu.VMEM((parts, rows, levels, width), jnp.float32)
    begun = pl.pallas_call(
        begin_kernel,
        in_specs=[vmem] * 3,
        out_specs=hbm,
        out_shape=result,
        scratch_shapes=[buffer, pltpu.SemaphoreType.DMA((2 * parts,))],
        compiler_params=PARAMS,
        cost_estimate=BRIEF,
        name="begin",
    )(state, middle_came, a_came)
    adjoint_result = pl.pallas_call(
        end_kernel,
        in_specs=[hbm] + [vmem] * 2,
        out_specs=hbm,
        out_shape=result,
        scratch_shapes=[buffer, pltpu.SemaphoreType.DMA((parts,))],
        input_output_aliases={0: 0},
        compiler_params=PARAMS,
        cost_estimate=BRIEF,
        name="end",
    )(begun, state, b_came)
    boundary_gradient = pl.pallas_call(
        pick_kernel,
        in_specs=[hbm] + [vmem] * 3,
        out_specs=vmem,
        out_shape=f32(parts, levels // subs, slots // hors),
        compiler_params=PARAMS,
        cost_estimate=BRIEF,
        name="pick",
    )(in_hbm(adjoint_result), owner, total, came)
    return (adjoint_result, boundary_gradient)


def solution(mesh):
    in_specs = (
        P(("ens", "sub"), None, "hor", None, None),
        P(("ens", "sub"), "hor", None, None),
        P(("ens", "sub"), "hor", None, None),
        P(None, None, "hor"),
        P(None, None, None, "hor"),
        P(None, None, None, "hor"),
        P(),
    )
    out_specs = (P(("ens", "sub"), None, "hor", None, None), P("ens", "sub", "hor"))
    return jax.shard_map(local, mesh=mesh, in_specs=in_specs, out_specs=out_specs, check_vma=False)
```

```python
import functools

import jax
import jax.numpy as jnp
from jax import lax
from jax.experimental import pallas as pl
from jax.experimental.pallas import tpu as pltpu
from jax.sharding import PartitionSpec as P

STEPS = 4
HALF = 8
FLUX_ROWS = 2 * STEPS
PACK_ROWS = FLUX_ROWS + 3
LANES = 128
EXTRA = PACK_ROWS
TARGETS = 4 * LANES
WEIGHTS = 5 * LANES


def to_previous(value):
    peers = lax.axis_size("sub")
    return lax.ppermute(value, "sub", [(i, (i - 1) % peers) for i in range(peers)])


def alternating(value, sign):
    subs, hors = lax.axis_size("sub"), lax.axis_size("hor")
    assert subs % 2 == 0
    pairs = []
    for s in range(subs):
        step = sign if s % 2 == 0 else -sign
        for h in range(hors):
            inside = 0 <= h + step < hors
            pairs.append((s * hors + h, s * hors + h + step if inside else (s ^ 1) * hors + h))
    return lax.ppermute(value, ("sub", "hor"), pairs)


def has_neighbour(flip):
    hor = lax.axis_index("hor")
    return jnp.where(flip == 1, hor < lax.axis_size("hor") - 1, hor > 0)


def rounds():
    subs, hors = lax.axis_size("sub"), lax.axis_size("hor")
    assert not subs & (subs - 1) and not hors & (hors - 1)
    order = [("sub", range(min(subs, 4) - 1, 0, -1))]
    order += [("sub", [1 << n]) for n in range(2, subs.bit_length() - 1)]
    return order + [("hor", [1 << n]) for n in range(hors.bit_length() - 1)]


def exchanged(value, axis, distances):
    size = lax.axis_size(axis)
    return sum(lax.ppermute(value, axis, [(i, i ^ distance) for i in range(size)]) for distance in distances)


def parity():
    return lax.rem(lax.axis_index("sub"), 2)


def sign_of(flip):
    return jnp.where(flip == 1, jnp.float32(-1.0), jnp.float32(1.0))


def north_rates(north_rate):
    width = north_rate.shape[-1]
    column = lax.broadcasted_iota(jnp.int32, north_rate.shape, len(north_rate.shape) - 1)
    plus = jnp.where(column == 0, 0.0, jnp.maximum(north_rate, 0.0))
    minus = jnp.where(column == width - 1, 0.0, jnp.maximum(-north_rate, 0.0))
    return plus, minus


def shifted(flux_plus, flux_minus):
    width = flux_plus.shape[-1]
    axis = len(flux_plus.shape) - 1
    return pltpu.roll(flux_plus, width - 1, axis) + pltpu.roll(flux_minus, 1, axis)


class Row:
    def __init__(self, east_rate, north_rate=None):
        self.outward = jnp.maximum(east_rate, 0.0)
        self.inward = jnp.maximum(-east_rate, 0.0)
        if north_rate is not None:
            self.centre = 1.0 - jnp.abs(east_rate) - jnp.abs(north_rate)
            self.plus, self.minus = north_rates(north_rate)

    def stay(self, value):
        return self.centre * value + shifted(self.plus * value, self.minus * value)


def level_halves(levels, body):
    def step(h, carry):
        body(pl.ds(pl.multiple_of(h * HALF, HALF), HALF))
        return carry

    lax.fori_loop(0, levels // HALF, step, 0)


def pack_kernel(
    state_hbm, east_hbm, north_hbm, cell_hbm, offset_hbm, weight_hbm,
    pack_ref, state_ref, east_ref, north_ref, cell_ref, offset_ref, weight_ref, sems, small_sems,
):
    parts, rows, levels, width = state_hbm.shape[1:]
    flip = parity()
    sign = sign_of(flip)
    at_end = pl.ds(flip * (rows - STEPS), STEPS)
    place = lambda r: r + flip * (STEPS - 1 - 2 * r)
    halves = levels // HALF
    copies = []
    for h in range(halves):
        at = pl.ds(h * HALF, HALF)
        sem = sems.at[h]
        batch = [
            pltpu.make_async_copy(state_hbm.at[0, c, at_end, at], state_ref.at[c, :, at], sem.at[c])
            for c in range(parts)
        ]
        batch.append(pltpu.make_async_copy(east_hbm.at[0, at_end, at], east_ref.at[:, at], sem.at[parts]))
        batch.append(pltpu.make_async_copy(north_hbm.at[0, at_end, at], north_ref.at[:, at], sem.at[parts + 1]))
        copies.append(batch)
        for copy in batch:
            copy.start()
    small = [
        pltpu.make_async_copy(source, target, small_sems.at[n])
        for n, (source, target) in enumerate(
            ((cell_hbm, cell_ref), (offset_hbm, offset_ref), (weight_hbm, weight_ref))
        )
    ]
    for copy in small:
        copy.start()

    def half(at):
        row = [Row(east_ref[place(r), at, :] * sign, north_ref[place(r), at, :]) for r in range(STEPS)]
        pack_ref[FLUX_ROWS, at, :] = east_ref[place(0), at, :]
        pack_ref[FLUX_ROWS + 1, at, :] = north_ref[place(0), at, :]
        pack_ref[FLUX_ROWS + 2, at, :] = east_ref[place(1), at, :]
        for r in (1, 2):
            lanes = (2 * r - 2) * LANES
            pack_ref[EXTRA, at, lanes:lanes + LANES] = north_ref[place(r), at, :LANES]
            pack_ref[EXTRA, at, lanes + LANES:lanes + 2 * LANES] = north_ref[place(r), at, width - LANES:]
        for c in range(parts):
            field = [state_ref[c, place(r), at, :] for r in range(STEPS)]
            for k in range(STEPS):
                pack_ref[2 * k + c, at, :] = row[0].outward * field[0]
                after = []
                for r in range(STEPS - 1 - k):
                    value = row[r].stay(field[r]) + row[r + 1].outward * field[r + 1]
                    if r > 0:
                        value = value + row[r - 1].inward * field[r - 1]
                    after.append(value)
                field = after

    for h in range(halves):
        for copy in copies[h]:
            copy.wait()
        half(pl.ds(h * HALF, HALF))

    for copy in small:
        copy.wait()
    n = 0
    for point in range(offset_ref.shape[0]):
        for c in range(parts):
            target = (cell_ref[c] + offset_ref[point, c]).astype(jnp.float32)
            pack_ref[EXTRA, n:n + 2, TARGETS:TARGETS + rows] = target
            pack_ref[EXTRA, n:n + 2, WEIGHTS:WEIGHTS + rows] = weight_ref[point, c]
            n += 2


def as_column(row):
    count = row.shape[1]
    here = lax.broadcasted_iota(jnp.int32, (count, count), 0)
    there = lax.broadcasted_iota(jnp.int32, (count, count), 1)
    return jnp.sum(jnp.where(here == there, row, 0), axis=1, keepdims=True)


def sweep_kernel(
    state_hbm, east_hbm, north_hbm, _,
    pack_ref, middle_ref, ends_ref, column_ref, state_ref, east_ref, north_ref,
    field, plus_ref, minus_ref, centre_ref, sems,
):
    copies = [
        pltpu.make_async_copy(source, target, sems.at[n])
        for n, (source, target) in enumerate(
            ((east_hbm, east_ref), (north_hbm, north_ref))
            + tuple((state_hbm.at[0, c], state_ref.at[0, c]) for c in range(state_hbm.shape[1]))
        )
    ]
    for copy in copies:
        copy.start()
    for copy in copies:
        copy.wait()
    parts, rows, levels, width = state_ref.shape[1:]
    flip = 1 - parity()
    sign = sign_of(flip)
    end_row = flip * (rows - 1)
    next_row = end_row + 1 - 2 * flip

    def half(at):
        pack_ref[FLUX_ROWS, at, :] = east_ref[0, end_row, at, :]
        pack_ref[FLUX_ROWS + 1, at, :] = north_ref[0, end_row, at, :]
        pack_ref[FLUX_ROWS + 2, at, :] = east_ref[0, next_row, at, :]

        for k in range(STEPS):
            if k == 0:
                read = lambda c, i: state_ref[0, c, i, at, :]
            else:
                read = lambda c, i, slot=k - 1: field[slot, c, i]
            leaving = jnp.maximum(east_ref[0, end_row, at, :] * sign, 0.0)
            for c in range(parts):
                pack_ref[2 * k + c, at, :] = leaving * read(c, end_row)
            west = [None] * parts
            here = [read(c, 0) for c in range(parts)]
            east_here = east_ref[0, 0, at, :]
            for i in range(rows):
                leave_west = jnp.maximum(-east_here, 0.0)
                if k == 0:
                    north_rate = north_ref[0, i, at, :]
                    centre = 1.0 - jnp.abs(east_here) - jnp.abs(north_rate)
                    plus, minus = north_rates(north_rate)
                    centre_ref[i], plus_ref[i], minus_ref[i] = centre, plus, minus
                else:
                    centre, plus, minus = centre_ref[i], plus_ref[i], minus_ref[i]
                if i + 1 < rows:
                    east_here = east_ref[0, i + 1, at, :]
                    east_after = jnp.maximum(east_here, 0.0)
                for c in range(parts):
                    value = here[c]
                    total = centre * value + shifted(plus * value, minus * value)
                    if i > 0:
                        total = total + west[c]
                    if i + 1 < rows:
                        west[c] = leave_west * value
                        here[c] = read(c, i + 1)
                        total = total + east_after * here[c]
                    if k < STEPS - 1:
                        field[k, c, i] = total
                    elif i < STEPS:
                        ends_ref[c, i, at, :] = total
                    elif i >= rows - STEPS:
                        ends_ref[c, i - rows + 2 * STEPS, at, :] = total
                    else:
                        middle_ref[c, i - STEPS, at, :] = total

        def columns(i, carry):
            for c in range(parts):
                value = state_ref[0, c, i, at, :]
                first, last = value[:, :LANES], value[:, width - LANES:]
                for slot in range(STEPS - 1):
                    first = first + field[slot, c, i, :, :LANES]
                    last = last + field[slot, c, i, :, width - LANES:]
                column_ref[c, 0, i, at, :] = first
                column_ref[c, 1, i, at, :] = last
            return carry

        lax.fori_loop(0, rows, columns, 0, unroll=2)

    level_halves(levels, half)


def mix(targets, weights, cells, total):
    for target, weight in zip(targets, weights):
        total = total + jnp.where(as_column(target) == cells, as_column(weight), 0.0)
    return total


def ghost_base_kernel(
    cell_ref, offset_ref, weight_ref, owner_ref, column_ref, north_ref, pack_ref,
    mixing_ref, partial_ref, owner_out, pack_out,
):
    owner_out[...] = owner_ref[...]
    pack_out[...] = pack_ref[...]
    parts, _, rows, levels, _ = column_ref.shape
    slots = mixing_ref.shape[-1]
    width = north_ref.shape[-1]
    points = range(offset_ref.shape[0])
    cells = lax.broadcasted_iota(jnp.int32, (rows, slots), 1)
    for c in range(parts):
        for s in range(2):
            mixing_ref[c, s] = mix(
                [cell_ref[c, s:s + 1, :] + offset_ref[point, c, s:s + 1, :] for point in points],
                [weight_ref[point, c, s:s + 1, :] for point in points],
                cells, jnp.zeros((rows, slots), jnp.float32),
            )

    for c in range(parts):
        total = jnp.zeros((levels, slots), jnp.float32)
        for i in range(rows):
            south = jnp.maximum(north_ref[0, i, :, :1], 0.0) * column_ref[c, 0, i, :, :1]
            north = jnp.maximum(-north_ref[0, i, :, width - 1:], 0.0) * column_ref[c, 1, i, :, LANES - 1:]
            total = total + south * mixing_ref[c, 0, i:i + 1, :]
            total = total + north * mixing_ref[c, 1, i:i + 1, :]
        partial_ref[c] = total


def ghost_kernel(north_ref, other_ref, column_ref, mixing_ref, partial_ref, sum_ref, near_mixing):
    parts, levels, slots = partial_ref.shape
    rows = mixing_ref.shape[2]
    width = north_ref.shape[-1]
    flip = 1 - parity()
    cells = lax.broadcasted_iota(jnp.int32, (rows, slots), 1).astype(jnp.float32)
    points = (WEIGHTS - TARGETS) // LANES * 4
    for c in range(parts):
        for s in range(2):
            at = [(point * parts + c) * 2 + s for point in range(points)]
            near_mixing[c, s] = mix(
                [other_ref[EXTRA, n:n + 1, TARGETS:TARGETS + rows] for n in at],
                [other_ref[EXTRA, n:n + 1, WEIGHTS:WEIGHTS + rows] for n in at],
                cells, jnp.zeros((rows, slots), jnp.float32),
            )
    for c in range(parts):
        total = partial_ref[c]
        for r in range(STEPS - 1):
            i = r + flip * (rows - 1 - 2 * r)
            south = jnp.maximum(north_ref[0, i, :, :1], 0.0) * column_ref[c, 0, r, :, :1]
            north = jnp.maximum(-north_ref[0, i, :, width - 1:], 0.0) * column_ref[c, 1, r, :, LANES - 1:]
            total = total + south * mixing_ref[c, 0, pl.ds(i, 1), :]
            total = total + north * mixing_ref[c, 1, pl.ds(i, 1), :]
            i = r + (1 - flip) * (rows - 1 - 2 * r)
            if r == 0:
                first_rate = other_ref[FLUX_ROWS + 1, :, :LANES]
                last_rate = other_ref[FLUX_ROWS + 1, :, width - LANES:]
            else:
                lanes = (2 * r - 2) * LANES
                first_rate = other_ref[EXTRA, :, lanes:lanes + LANES]
                last_rate = other_ref[EXTRA, :, lanes + LANES:lanes + 2 * LANES]
            south = jnp.maximum(first_rate[:, :1], 0.0) * column_ref[c, 0, STEPS - 1 + r, :, :1]
            north = jnp.maximum(-last_rate[:, LANES - 1:], 0.0) * column_ref[c, 1, STEPS - 1 + r, :, LANES - 1:]
            total = total + south * near_mixing[c, 0, pl.ds(i, 1), :]
            total = total + north * near_mixing[c, 1, pl.ds(i, 1), :]
        sum_ref[c] = jnp.where(has_neighbour(flip), total, partial_ref[c])


def mend_side(flip, east_ref, north_ref, mine_ref, other_ref, store, store_column):
    levels, width = mine_ref.shape[1:]
    rows = east_ref.shape[1]
    sign = sign_of(flip)
    place = lambda r: flip * (rows - STEPS) + r + flip * (STEPS - 1 - 2 * r)

    def half(at):
        own = [Row(east_ref[0, place(r), at, :] * sign, north_ref[0, place(r), at, :]) for r in range(STEPS - 1)]
        near = Row(other_ref[FLUX_ROWS, at, :] * sign, other_ref[FLUX_ROWS + 1, at, :])
        far = Row(other_ref[FLUX_ROWS + 2, at, :] * sign)
        for c in range(FLUX_ROWS // STEPS):
            mine = lambda k: mine_ref[2 * k + c, at, :]
            theirs = lambda k: other_ref[2 * k + c, at, :]
            a0 = theirs(0)
            n1 = mine(0)
            b0 = own[0].stay(a0) + near.inward * n1 + theirs(1)
            b1 = own[0].inward * a0
            bn1 = near.stay(n1) + own[0].outward * a0 + mine(1)
            bn2 = near.outward * n1
            c0 = own[0].stay(b0) + near.inward * bn1 + own[1].outward * b1 + theirs(2)
            c1 = own[1].stay(b1) + own[0].inward * b0
            c2 = own[1].inward * b1
            cn1 = near.stay(bn1) + own[0].outward * b0 + far.inward * bn2 + mine(2)
            d0 = own[0].stay(c0) + near.inward * cn1 + own[1].outward * c1 + theirs(3)
            d1 = own[1].stay(c1) + own[0].inward * c0 + own[2].outward * c2
            d2 = own[2].stay(c2) + own[1].inward * c1
            d3 = own[2].inward * c2
            for r, value in enumerate((d0, d1, d2, d3)):
                store(c, r, at, value)
            if store_column is not None:
                tiles = (slice(0, LANES), slice(width - LANES, width))
                for s, lanes in enumerate(tiles):
                    tile = lambda value: value[:, lanes]
                    rate = other_ref[EXTRA, at, s * LANES:(s + 1) * LANES]
                    stays = 1.0 - jnp.abs(other_ref[FLUX_ROWS + 2, at, lanes]) - jnp.abs(rate)
                    drift = jnp.maximum(rate if s == 0 else -rate, 0.0) * tile(bn2)
                    cn2 = stays * tile(bn2) + pltpu.roll(drift, LANES - 1 if s == 0 else 1, 1)
                    cn2 = cn2 + tile(near.outward) * tile(bn1)
                    cn3 = tile(far.outward) * tile(bn2)
                    sums = (
                        tile(a0) + tile(b0) + tile(c0), tile(b1) + tile(c1), tile(c2),
                        tile(n1) + tile(bn1) + tile(cn1), tile(bn2) + cn2, cn3,
                    )
                    for r, value in enumerate(sums):
                        store_column(c, s, r, at, value)

    level_halves(levels, half)


def copy_end(flip, ends_ref, out_ref):
    for c in range(out_ref.shape[0]):
        for r in range(STEPS):
            out_ref[c, r] = ends_ref[c, flip * STEPS + r]


def mend_a_kernel(east_ref, north_ref, mine_ref, other_ref, ends_ref, base_ref, out_ref, column_ref):
    flip = 1 - parity()
    turn = lambda r: r + flip * (STEPS - 1 - 2 * r)

    def store(c, r, at, value):
        out_ref[c, turn(r), at, :] = ends_ref[c, flip * STEPS + turn(r), at, :] + value

    def store_column(c, s, r, at, value):
        column_ref[c, s, r, at, :] = value

    @pl.when(has_neighbour(flip))
    def _():
        mend_side(flip, east_ref, north_ref, mine_ref, other_ref, store, store_column)

    @pl.when(jnp.logical_not(has_neighbour(flip)))
    def _():
        column_ref[...] = jnp.zeros_like(column_ref)
        copy_end(flip, ends_ref, out_ref)


def mend_b_kernel(east_ref, north_ref, mine_ref, other_ref, ends_ref, _, __, out_ref):
    flip = parity()
    turn = lambda r: r + flip * (STEPS - 1 - 2 * r)

    def store(c, r, at, value):
        out_ref[c, turn(r), at, :] = ends_ref[c, flip * STEPS + turn(r), at, :] + value

    @pl.when(has_neighbour(flip))
    def _():
        mend_side(flip, east_ref, north_ref, mine_ref, other_ref, store, None)

    @pl.when(jnp.logical_not(has_neighbour(flip)))
    def _():
        copy_end(flip, ends_ref, out_ref)


def subtract_rows(state_ref, out_hbm, buffer, sems, jobs):
    copies = []
    is_last = lax.axis_index("sub") == lax.axis_size("sub") - 1
    for start, other in jobs:
        for c in range(other.shape[0]):
            count = other.shape[1]
            for r in range(count):
                buffer[c, start + r] = state_ref[0, c, start + r] - jnp.where(is_last, 0.0, other[c, r])
            at = pl.ds(start, count)
            copy = pltpu.make_async_copy(buffer.at[c, at], out_hbm.at[0, c, at], sems.at[len(copies)])
            copy.start()
            copies.append(copy)
    return copies


def begin_kernel(state_ref, middle_ref, a_ref, out_hbm, buffer, sems):
    start = parity() * (state_ref.shape[2] - STEPS)
    for copy in subtract_rows(state_ref, out_hbm, buffer, sems, ((STEPS, middle_ref), (start, a_ref))):
        copy.wait()


def end_kernel(begun_hbm, state_ref, b_ref, out_hbm, buffer, sems):
    start = (1 - parity()) * (state_ref.shape[2] - STEPS)
    for copy in subtract_rows(state_ref, out_hbm, buffer, sems, ((start, b_ref),)):
        copy.wait()


def pick_kernel(_, owner_ref, total_ref, came_ref, gradient_ref):
    parts = gradient_ref.shape[0]
    share, mine = gradient_ref.shape[1:]
    start = lax.axis_index("hor") * mine
    chosen = []
    for c in range(parts):
        total = total_ref[c] + came_ref[c]
        block = total[:share]
        for s in range(1, total.shape[0] // share):
            block = jnp.where(lax.axis_index("sub") == s, total[s * share:(s + 1) * share], block)
        chosen.append(block)
    chosen = jnp.concatenate(chosen, 0)
    column = lax.broadcasted_iota(jnp.int32, (parts * share, mine), 1)
    picked = jnp.zeros((parts * share, mine), jnp.float32)
    for q in range(mine):
        value = jnp.sum(jnp.where(owner_ref[...] == start + q, chosen, 0.0), axis=1, keepdims=True)
        picked = jnp.where(column == q, value, picked)
    for c in range(parts):
        gradient_ref[c] = picked[c * share:(c + 1) * share]


BRIEF = pl.CostEstimate(flops=1, bytes_accessed=1, transcendentals=0)
PARAMS = pltpu.CompilerParams(vmem_limit_bytes=24 * 1024 * 1024)


def local(
    adjoint_state,
    courant_east,
    courant_north,
    parent_cell,
    stencil_offset,
    stencil_weight,
    owner_slot,
):
    _, parts, rows, levels, width = adjoint_state.shape
    slots = owner_slot.shape[0]
    inner = rows - 2 * STEPS
    row_bytes = levels * width * 4
    f32 = lambda *shape: jax.ShapeDtypeStruct(shape, jnp.float32)
    vmem = pl.BlockSpec(memory_space=pltpu.VMEM)
    smem = pl.BlockSpec(memory_space=pltpu.SMEM)
    hbm = pl.BlockSpec(memory_space=pltpu.HBM)
    in_hbm = lambda value: pltpu.with_memory_space_constraint(value, pltpu.HBM)

    subs, hors = lax.axis_size("sub"), lax.axis_size("hor")
    small = [parent_cell, stencil_offset, stencil_weight]

    first_pack = pl.pallas_call(
        pack_kernel,
        in_specs=[hbm] * 6,
        out_specs=vmem,
        out_shape=f32(PACK_ROWS + 1, levels, width),
        scratch_shapes=[
            pltpu.VMEM((parts, STEPS, levels, width), jnp.float32),
            pltpu.VMEM((STEPS, levels, width), jnp.float32),
            pltpu.VMEM((STEPS, levels, width), jnp.float32),
        ]
        + [pltpu.VMEM(value.shape, value.dtype) for value in small]
        + [pltpu.SemaphoreType.DMA((levels // HALF, parts + 2)), pltpu.SemaphoreType.DMA((3,))],
        compiler_params=PARAMS,
        cost_estimate=BRIEF,
        name="pack",
    )(*[in_hbm(value) for value in [adjoint_state, courant_east, courant_north] + small])
    first_came = alternating(first_pack, -1)

    second_pack, middle, ends, columns, state, east, north = pl.pallas_call(
        sweep_kernel,
        in_specs=[hbm] * 3 + [pl.BlockSpec(memory_space=pl.ANY)],
        out_specs=[vmem] * 7,
        out_shape=[
            f32(PACK_ROWS, levels, width),
            f32(parts, inner, levels, width),
            f32(parts, 2 * STEPS, levels, width),
            f32(parts, 2, rows, levels, LANES),
            f32(*adjoint_state.shape), f32(*courant_east.shape), f32(*courant_north.shape),
        ],
        scratch_shapes=[
            pltpu.VMEM((STEPS - 1, parts, rows, HALF, width), jnp.float32),
            pltpu.VMEM((rows, HALF, width), jnp.float32),
            pltpu.VMEM((rows, HALF, width), jnp.float32),
            pltpu.VMEM((rows, HALF, width), jnp.float32),
            pltpu.SemaphoreType.DMA((parts + 2,)),
        ],
        compiler_params=PARAMS,
        cost_estimate=BRIEF,
        name="sweep",
    )(in_hbm(adjoint_state), in_hbm(courant_east), in_hbm(courant_north), first_pack)
    middle_came = to_previous(middle)

    mixing, base, owner, second_sent = pl.pallas_call(
        ghost_base_kernel,
        in_specs=[vmem] * 7,
        out_specs=[vmem] * 4,
        out_shape=[
            f32(parts, 2, rows, slots), f32(parts, levels, slots),
            jax.ShapeDtypeStruct((1, slots), owner_slot.dtype), f32(PACK_ROWS, levels, width),
        ],
        compiler_params=PARAMS,
        cost_estimate=BRIEF,
        name="ghost_base",
    )(*small, owner_slot[None], columns, north, second_pack)
    second_came = alternating(second_sent, 1)

    column_shape = (parts, 2, 2 * (STEPS - 1), levels, LANES)
    side_a, a_columns = pl.pallas_call(
        mend_a_kernel,
        in_specs=[vmem] * 6,
        out_specs=[vmem] * 2,
        out_shape=[f32(parts, STEPS, levels, width), f32(*column_shape)],
        compiler_params=PARAMS,
        cost_estimate=BRIEF,
        name="mend_a",
    )(east, north, second_pack, first_came, ends, base)
    a_came = to_previous(side_a)
    total = pl.pallas_call(
        ghost_kernel,
        in_specs=[vmem] * 5,
        out_specs=vmem,
        out_shape=f32(parts, levels, slots),
        scratch_shapes=[pltpu.VMEM((parts, 2, rows, slots), jnp.float32)],
        compiler_params=PARAMS,
        cost_estimate=BRIEF,
        name="ghost",
    )(north, first_came, a_columns, mixing, base)
    order = rounds()
    total = total + exchanged(total, *order[0])
    side_b = pl.pallas_call(
        mend_b_kernel,
        in_specs=[vmem] * 5 + [pl.BlockSpec(memory_space=pl.ANY)] * 2,
        out_specs=vmem,
        out_shape=f32(parts, STEPS, levels, width),
        compiler_params=PARAMS,
        cost_estimate=BRIEF,
        name="mend_b",
    )(east, north, first_pack, second_came, ends, middle_came, total)
    b_came = to_previous(side_b)

    for each in order[1:-1]:
        total = total + exchanged(total, *each)
    came = exchanged(total, *order[-1])

    result = f32(*adjoint_state.shape)
    buffer = pltpu.VMEM((parts, rows, levels, width), jnp.float32)
    begun = pl.pallas_call(
        begin_kernel,
        in_specs=[vmem] * 3,
        out_specs=hbm,
        out_shape=result,
        scratch_shapes=[buffer, pltpu.SemaphoreType.DMA((2 * parts,))],
        compiler_params=PARAMS,
        cost_estimate=BRIEF,
        name="begin",
    )(state, middle_came, a_came)
    adjoint_result = pl.pallas_call(
        end_kernel,
        in_specs=[hbm] + [vmem] * 2,
        out_specs=hbm,
        out_shape=result,
        scratch_shapes=[buffer, pltpu.SemaphoreType.DMA((parts,))],
        input_output_aliases={0: 0},
        compiler_params=PARAMS,
        cost_estimate=BRIEF,
        name="end",
    )(begun, state, b_came)
    boundary_gradient = pl.pallas_call(
        pick_kernel,
        in_specs=[hbm] + [vmem] * 3,
        out_specs=vmem,
        out_shape=f32(parts, levels // subs, slots // hors),
        compiler_params=PARAMS,
        cost_estimate=BRIEF,
        name="pick",
    )(in_hbm(adjoint_result), owner, total, came)
    return (adjoint_result, boundary_gradient)


def solution(mesh):
    in_specs = (
        P(("ens", "sub"), None, "hor", None, None),
        P(("ens", "sub"), "hor", None, None),
        P(("ens", "sub"), "hor", None, None),
        P(None, None, "hor"),
        P(None, None, None, "hor"),
        P(None, None, None, "hor"),
        P(),
    )
    out_specs = (P(("ens", "sub"), None, "hor", None, None), P("ens", "sub", "hor"))
    return jax.shard_map(local, mesh=mesh, in_specs=in_specs, out_specs=out_specs, check_vma=False)
```

```python
import functools

import jax
import jax.numpy as jnp
from jax import lax
from jax.experimental import pallas as pl
from jax.experimental.pallas import tpu as pltpu
from jax.sharding import PartitionSpec as P

STEPS = 4
HALF = 8
FLUX_ROWS = 2 * STEPS
PACK_ROWS = FLUX_ROWS + 3
LANES = 128
EXTRA = PACK_ROWS
TARGETS = 4 * LANES
WEIGHTS = 5 * LANES


def to_previous(value):
    peers = lax.axis_size("sub")
    return lax.ppermute(value, "sub", [(i, (i - 1) % peers) for i in range(peers)])


def alternating(value, sign):
    subs, hors = lax.axis_size("sub"), lax.axis_size("hor")
    assert subs % 2 == 0
    pairs = []
    for s in range(subs):
        step = sign if s % 2 == 0 else -sign
        for h in range(hors):
            inside = 0 <= h + step < hors
            pairs.append((s * hors + h, s * hors + h + step if inside else (s ^ 1) * hors + h))
    return lax.ppermute(value, ("sub", "hor"), pairs)


def has_neighbour(flip):
    hor = lax.axis_index("hor")
    return jnp.where(flip == 1, hor < lax.axis_size("hor") - 1, hor > 0)


def rounds():
    subs, hors = lax.axis_size("sub"), lax.axis_size("hor")
    assert not subs & (subs - 1) and not hors & (hors - 1)
    order = [("sub", range(min(subs, 4) - 1, 0, -1))]
    order += [("sub", [1 << n]) for n in range(2, subs.bit_length() - 1)]
    return order + [("hor", [1 << n]) for n in range(hors.bit_length() - 1)]


def exchanged(value, axis, distances):
    size = lax.axis_size(axis)
    return sum(lax.ppermute(value, axis, [(i, i ^ distance) for i in range(size)]) for distance in distances)


def parity():
    return lax.rem(lax.axis_index("sub"), 2)


def sign_of(flip):
    return jnp.where(flip == 1, jnp.float32(-1.0), jnp.float32(1.0))


def north_rates(north_rate):
    width = north_rate.shape[-1]
    column = lax.broadcasted_iota(jnp.int32, north_rate.shape, len(north_rate.shape) - 1)
    plus = jnp.where(column == 0, 0.0, jnp.maximum(north_rate, 0.0))
    minus = jnp.where(column == width - 1, 0.0, jnp.maximum(-north_rate, 0.0))
    return plus, minus


def shifted(flux_plus, flux_minus):
    width = flux_plus.shape[-1]
    axis = len(flux_plus.shape) - 1
    return pltpu.roll(flux_plus, width - 1, axis) + pltpu.roll(flux_minus, 1, axis)


class Row:
    def __init__(self, east_rate, north_rate=None):
        self.outward = jnp.maximum(east_rate, 0.0)
        self.inward = jnp.maximum(-east_rate, 0.0)
        if north_rate is not None:
            self.centre = 1.0 - jnp.abs(east_rate) - jnp.abs(north_rate)
            self.plus, self.minus = north_rates(north_rate)

    def stay(self, value):
        return self.centre * value + shifted(self.plus * value, self.minus * value)


def level_halves(levels, body):
    def step(h, carry):
        body(pl.ds(pl.multiple_of(h * HALF, HALF), HALF))
        return carry

    lax.fori_loop(0, levels // HALF, step, 0)


def pack_kernel(
    state_hbm, east_hbm, north_hbm, cell_hbm, offset_hbm, weight_hbm,
    pack_ref, state_ref, east_ref, north_ref, cell_ref, offset_ref, weight_ref, sems, small_sems,
):
    parts, rows, levels, width = state_hbm.shape[1:]
    flip = parity()
    sign = sign_of(flip)
    at_end = pl.ds(flip * (rows - STEPS), STEPS)
    place = lambda r: r + flip * (STEPS - 1 - 2 * r)
    halves = levels // HALF
    copies = []
    for h in range(halves):
        at = pl.ds(h * HALF, HALF)
        sem = sems.at[h]
        batch = [
            pltpu.make_async_copy(state_hbm.at[0, c, at_end, at], state_ref.at[c, :, at], sem.at[c])
            for c in range(parts)
        ]
        batch.append(pltpu.make_async_copy(east_hbm.at[0, at_end, at], east_ref.at[:, at], sem.at[parts]))
        batch.append(pltpu.make_async_copy(north_hbm.at[0, at_end, at], north_ref.at[:, at], sem.at[parts + 1]))
        copies.append(batch)
        for copy in batch:
            copy.start()
    small = [
        pltpu.make_async_copy(source, target, small_sems.at[n])
        for n, (source, target) in enumerate(
            ((cell_hbm, cell_ref), (offset_hbm, offset_ref), (weight_hbm, weight_ref))
        )
    ]
    for copy in small:
        copy.start()

    def half(at):
        row = [Row(east_ref[place(r), at, :] * sign, north_ref[place(r), at, :]) for r in range(STEPS)]
        pack_ref[FLUX_ROWS, at, :] = east_ref[place(0), at, :]
        pack_ref[FLUX_ROWS + 1, at, :] = north_ref[place(0), at, :]
        pack_ref[FLUX_ROWS + 2, at, :] = east_ref[place(1), at, :]
        for r in (1, 2):
            lanes = (2 * r - 2) * LANES
            pack_ref[EXTRA, at, lanes:lanes + LANES] = north_ref[place(r), at, :LANES]
            pack_ref[EXTRA, at, lanes + LANES:lanes + 2 * LANES] = north_ref[place(r), at, width - LANES:]
        for c in range(parts):
            field = [state_ref[c, place(r), at, :] for r in range(STEPS)]
            for k in range(STEPS):
                pack_ref[2 * k + c, at, :] = row[0].outward * field[0]
                after = []
                for r in range(STEPS - 1 - k):
                    value = row[r].stay(field[r]) + row[r + 1].outward * field[r + 1]
                    if r > 0:
                        value = value + row[r - 1].inward * field[r - 1]
                    after.append(value)
                field = after

    for h in range(halves):
        for copy in copies[h]:
            copy.wait()
        half(pl.ds(h * HALF, HALF))

    for copy in small:
        copy.wait()
    n = 0
    for point in range(offset_ref.shape[0]):
        for c in range(parts):
            target = (cell_ref[c] + offset_ref[point, c]).astype(jnp.float32)
            pack_ref[EXTRA, n:n + 2, TARGETS:TARGETS + rows] = target
            pack_ref[EXTRA, n:n + 2, WEIGHTS:WEIGHTS + rows] = weight_ref[point, c]
            n += 2


def as_column(row):
    count = row.shape[1]
    here = lax.broadcasted_iota(jnp.int32, (count, count), 0)
    there = lax.broadcasted_iota(jnp.int32, (count, count), 1)
    return jnp.sum(jnp.where(here == there, row, 0), axis=1, keepdims=True)


def sweep_kernel(
    state_hbm, east_hbm, north_hbm, _,
    pack_ref, middle_ref, ends_ref, column_ref, state_ref, east_ref, north_ref,
    field, plus_ref, minus_ref, centre_ref, sems,
):
    copies = [
        pltpu.make_async_copy(source, target, sems.at[n])
        for n, (source, target) in enumerate(
            ((east_hbm, east_ref), (north_hbm, north_ref))
            + tuple((state_hbm.at[0, c], state_ref.at[0, c]) for c in range(state_hbm.shape[1]))
        )
    ]
    for copy in copies:
        copy.start()
    for copy in copies:
        copy.wait()
    parts, rows, levels, width = state_ref.shape[1:]
    flip = 1 - parity()
    sign = sign_of(flip)
    end_row = flip * (rows - 1)
    next_row = end_row + 1 - 2 * flip

    def half(at):
        pack_ref[FLUX_ROWS, at, :] = east_ref[0, end_row, at, :]
        pack_ref[FLUX_ROWS + 1, at, :] = north_ref[0, end_row, at, :]
        pack_ref[FLUX_ROWS + 2, at, :] = east_ref[0, next_row, at, :]

        for k in range(STEPS):
            if k == 0:
                read = lambda c, i: state_ref[0, c, i, at, :]
            else:
                read = lambda c, i, slot=k - 1: field[slot, c, i]
            leaving = jnp.maximum(east_ref[0, end_row, at, :] * sign, 0.0)
            for c in range(parts):
                pack_ref[2 * k + c, at, :] = leaving * read(c, end_row)
            west = [None] * parts
            here = [read(c, 0) for c in range(parts)]
            east_here = east_ref[0, 0, at, :]
            for i in range(rows):
                leave_west = jnp.maximum(-east_here, 0.0)
                if k == 0:
                    north_rate = north_ref[0, i, at, :]
                    centre = 1.0 - jnp.abs(east_here) - jnp.abs(north_rate)
                    plus, minus = north_rates(north_rate)
                    centre_ref[i], plus_ref[i], minus_ref[i] = centre, plus, minus
                else:
                    centre, plus, minus = centre_ref[i], plus_ref[i], minus_ref[i]
                if i + 1 < rows:
                    east_here = east_ref[0, i + 1, at, :]
                    east_after = jnp.maximum(east_here, 0.0)
                for c in range(parts):
                    value = here[c]
                    total = centre * value + shifted(plus * value, minus * value)
                    if i > 0:
                        total = total + west[c]
                    if i + 1 < rows:
                        west[c] = leave_west * value
                        here[c] = read(c, i + 1)
                        total = total + east_after * here[c]
                    if k < STEPS - 1:
                        field[k, c, i] = total
                    elif i < STEPS:
                        ends_ref[c, i, at, :] = total
                    elif i >= rows - STEPS:
                        ends_ref[c, i - rows + 2 * STEPS, at, :] = total
                    else:
                        middle_ref[c, i - STEPS, at, :] = total

        def columns(i, carry):
            for c in range(parts):
                value = state_ref[0, c, i, at, :]
                first, last = value[:, :LANES], value[:, width - LANES:]
                for slot in range(STEPS - 1):
                    first = first + field[slot, c, i, :, :LANES]
                    last = last + field[slot, c, i, :, width - LANES:]
                column_ref[c, 0, i, at, :] = first
                column_ref[c, 1, i, at, :] = last
            return carry

        lax.fori_loop(0, rows, columns, 0, unroll=2)

    level_halves(levels, half)


def mix(targets, weights, cells, total):
    for target, weight in zip(targets, weights):
        total = total + jnp.where(as_column(target) == cells, as_column(weight), 0.0)
    return total


def ghost_base_kernel(
    cell_ref, offset_ref, weight_ref, owner_ref, column_ref, north_ref, pack_ref,
    mixing_ref, partial_ref, owner_out, pack_out,
):
    owner_out[...] = owner_ref[...]
    pack_out[...] = pack_ref[...]
    parts, _, rows, levels, _ = column_ref.shape
    slots = mixing_ref.shape[-1]
    width = north_ref.shape[-1]
    points = range(offset_ref.shape[0])
    cells = lax.broadcasted_iota(jnp.int32, (rows, slots), 1)
    for c in range(parts):
        for s in range(2):
            mixing_ref[c, s] = mix(
                [cell_ref[c, s:s + 1, :] + offset_ref[point, c, s:s + 1, :] for point in points],
                [weight_ref[point, c, s:s + 1, :] for point in points],
                cells, jnp.zeros((rows, slots), jnp.float32),
            )

    for c in range(parts):
        total = jnp.zeros((levels, slots), jnp.float32)
        for i in range(rows):
            south = jnp.maximum(north_ref[0, i, :, :1], 0.0) * column_ref[c, 0, i, :, :1]
            north = jnp.maximum(-north_ref[0, i, :, width - 1:], 0.0) * column_ref[c, 1, i, :, LANES - 1:]
            total = total + south * mixing_ref[c, 0, i:i + 1, :]
            total = total + north * mixing_ref[c, 1, i:i + 1, :]
        partial_ref[c] = total


def ghost_kernel(north_ref, other_ref, column_ref, mixing_ref, partial_ref, sum_ref, near_mixing):
    parts, levels, slots = partial_ref.shape
    rows = mixing_ref.shape[2]
    width = north_ref.shape[-1]
    flip = 1 - parity()
    cells = lax.broadcasted_iota(jnp.int32, (rows, slots), 1).astype(jnp.float32)
    points = (WEIGHTS - TARGETS) // LANES * 4
    for c in range(parts):
        for s in range(2):
            at = [(point * parts + c) * 2 + s for point in range(points)]
            near_mixing[c, s] = mix(
                [other_ref[EXTRA, n:n + 1, TARGETS:TARGETS + rows] for n in at],
                [other_ref[EXTRA, n:n + 1, WEIGHTS:WEIGHTS + rows] for n in at],
                cells, jnp.zeros((rows, slots), jnp.float32),
            )
    for c in range(parts):
        total = partial_ref[c]
        for r in range(STEPS - 1):
            i = r + flip * (rows - 1 - 2 * r)
            south = jnp.maximum(north_ref[0, i, :, :1], 0.0) * column_ref[c, 0, r, :, :1]
            north = jnp.maximum(-north_ref[0, i, :, width - 1:], 0.0) * column_ref[c, 1, r, :, LANES - 1:]
            total = total + south * mixing_ref[c, 0, pl.ds(i, 1), :]
            total = total + north * mixing_ref[c, 1, pl.ds(i, 1), :]
            i = r + (1 - flip) * (rows - 1 - 2 * r)
            if r == 0:
                first_rate = other_ref[FLUX_ROWS + 1, :, :LANES]
                last_rate = other_ref[FLUX_ROWS + 1, :, width - LANES:]
            else:
                lanes = (2 * r - 2) * LANES
                first_rate = other_ref[EXTRA, :, lanes:lanes + LANES]
                last_rate = other_ref[EXTRA, :, lanes + LANES:lanes + 2 * LANES]
            south = jnp.maximum(first_rate[:, :1], 0.0) * column_ref[c, 0, STEPS - 1 + r, :, :1]
            north = jnp.maximum(-last_rate[:, LANES - 1:], 0.0) * column_ref[c, 1, STEPS - 1 + r, :, LANES - 1:]
            total = total + south * near_mixing[c, 0, pl.ds(i, 1), :]
            total = total + north * near_mixing[c, 1, pl.ds(i, 1), :]
        sum_ref[c] = jnp.where(has_neighbour(flip), total, partial_ref[c])


def mend_side(flip, east_ref, north_ref, mine_ref, other_ref, store, store_column):
    levels, width = mine_ref.shape[1:]
    rows = east_ref.shape[1]
    sign = sign_of(flip)
    place = lambda r: flip * (rows - STEPS) + r + flip * (STEPS - 1 - 2 * r)

    def half(at):
        own = [Row(east_ref[0, place(r), at, :] * sign, north_ref[0, place(r), at, :]) for r in range(STEPS - 1)]
        near = Row(other_ref[FLUX_ROWS, at, :] * sign, other_ref[FLUX_ROWS + 1, at, :])
        far = Row(other_ref[FLUX_ROWS + 2, at, :] * sign)
        for c in range(FLUX_ROWS // STEPS):
            mine = lambda k: mine_ref[2 * k + c, at, :]
            theirs = lambda k: other_ref[2 * k + c, at, :]
            a0 = theirs(0)
            n1 = mine(0)
            b0 = own[0].stay(a0) + near.inward * n1 + theirs(1)
            b1 = own[0].inward * a0
            bn1 = near.stay(n1) + own[0].outward * a0 + mine(1)
            bn2 = near.outward * n1
            c0 = own[0].stay(b0) + near.inward * bn1 + own[1].outward * b1 + theirs(2)
            c1 = own[1].stay(b1) + own[0].inward * b0
            c2 = own[1].inward * b1
            cn1 = near.stay(bn1) + own[0].outward * b0 + far.inward * bn2 + mine(2)
            d0 = own[0].stay(c0) + near.inward * cn1 + own[1].outward * c1 + theirs(3)
            d1 = own[1].stay(c1) + own[0].inward * c0 + own[2].outward * c2
            d2 = own[2].stay(c2) + own[1].inward * c1
            d3 = own[2].inward * c2
            for r, value in enumerate((d0, d1, d2, d3)):
                store(c, r, at, value)
            if store_column is not None:
                tiles = (slice(0, LANES), slice(width - LANES, width))
                for s, lanes in enumerate(tiles):
                    tile = lambda value: value[:, lanes]
                    rate = other_ref[EXTRA, at, s * LANES:(s + 1) * LANES]
                    stays = 1.0 - jnp.abs(other_ref[FLUX_ROWS + 2, at, lanes]) - jnp.abs(rate)
                    drift = jnp.maximum(rate if s == 0 else -rate, 0.0) * tile(bn2)
                    cn2 = stays * tile(bn2) + pltpu.roll(drift, LANES - 1 if s == 0 else 1, 1)
                    cn2 = cn2 + tile(near.outward) * tile(bn1)
                    cn3 = tile(far.outward) * tile(bn2)
                    sums = (
                        tile(a0) + tile(b0) + tile(c0), tile(b1) + tile(c1), tile(c2),
                        tile(n1) + tile(bn1) + tile(cn1), tile(bn2) + cn2, cn3,
                    )
                    for r, value in enumerate(sums):
                        store_column(c, s, r, at, value)

    level_halves(levels, half)


def copy_end(flip, ends_ref, out_ref):
    for c in range(out_ref.shape[0]):
        for r in range(STEPS):
            out_ref[c, r] = ends_ref[c, flip * STEPS + r]


def mend_a_kernel(east_ref, north_ref, mine_ref, other_ref, ends_ref, base_ref, out_ref, column_ref):
    flip = 1 - parity()
    turn = lambda r: r + flip * (STEPS - 1 - 2 * r)

    def store(c, r, at, value):
        out_ref[c, turn(r), at, :] = ends_ref[c, flip * STEPS + turn(r), at, :] + value

    def store_column(c, s, r, at, value):
        column_ref[c, s, r, at, :] = value

    @pl.when(has_neighbour(flip))
    def _():
        mend_side(flip, east_ref, north_ref, mine_ref, other_ref, store, store_column)

    @pl.when(jnp.logical_not(has_neighbour(flip)))
    def _():
        column_ref[...] = jnp.zeros_like(column_ref)
        copy_end(flip, ends_ref, out_ref)


def mend_b_kernel(east_ref, north_ref, mine_ref, other_ref, ends_ref, _, __, out_ref):
    flip = parity()
    turn = lambda r: r + flip * (STEPS - 1 - 2 * r)

    def store(c, r, at, value):
        out_ref[c, turn(r), at, :] = ends_ref[c, flip * STEPS + turn(r), at, :] + value

    @pl.when(has_neighbour(flip))
    def _():
        mend_side(flip, east_ref, north_ref, mine_ref, other_ref, store, None)

    @pl.when(jnp.logical_not(has_neighbour(flip)))
    def _():
        copy_end(flip, ends_ref, out_ref)


def subtract_rows(state_ref, out_hbm, buffer, sems, jobs):
    copies = []
    is_last = lax.axis_index("sub") == lax.axis_size("sub") - 1
    for start, other in jobs:
        for c in range(other.shape[0]):
            count = other.shape[1]
            for r in range(count):
                buffer[c, start + r] = state_ref[0, c, start + r] - jnp.where(is_last, 0.0, other[c, r])
            at = pl.ds(start, count)
            copy = pltpu.make_async_copy(buffer.at[c, at], out_hbm.at[0, c, at], sems.at[len(copies)])
            copy.start()
            copies.append(copy)
    return copies


def begin_kernel(state_ref, middle_ref, a_ref, total_ref, out_hbm, total_out, buffer, sems):
    total_out[...] = total_ref[...]
    start = parity() * (state_ref.shape[2] - STEPS)
    for copy in subtract_rows(state_ref, out_hbm, buffer, sems, ((STEPS, middle_ref), (start, a_ref))):
        copy.wait()


def end_kernel(begun_hbm, state_ref, b_ref, out_hbm, buffer, sems):
    start = (1 - parity()) * (state_ref.shape[2] - STEPS)
    for copy in subtract_rows(state_ref, out_hbm, buffer, sems, ((start, b_ref),)):
        copy.wait()


def pick_kernel(_, owner_ref, total_ref, came_ref, gradient_ref):
    parts = gradient_ref.shape[0]
    share, mine = gradient_ref.shape[1:]
    start = lax.axis_index("hor") * mine
    chosen = []
    for c in range(parts):
        total = total_ref[c] + came_ref[c]
        block = total[:share]
        for s in range(1, total.shape[0] // share):
            block = jnp.where(lax.axis_index("sub") == s, total[s * share:(s + 1) * share], block)
        chosen.append(block)
    chosen = jnp.concatenate(chosen, 0)
    column = lax.broadcasted_iota(jnp.int32, (parts * share, mine), 1)
    picked = jnp.zeros((parts * share, mine), jnp.float32)
    for q in range(mine):
        value = jnp.sum(jnp.where(owner_ref[...] == start + q, chosen, 0.0), axis=1, keepdims=True)
        picked = jnp.where(column == q, value, picked)
    for c in range(parts):
        gradient_ref[c] = picked[c * share:(c + 1) * share]


BRIEF = pl.CostEstimate(flops=1, bytes_accessed=1, transcendentals=0)
PARAMS = pltpu.CompilerParams(vmem_limit_bytes=24 * 1024 * 1024)


def local(
    adjoint_state,
    courant_east,
    courant_north,
    parent_cell,
    stencil_offset,
    stencil_weight,
    owner_slot,
):
    _, parts, rows, levels, width = adjoint_state.shape
    slots = owner_slot.shape[0]
    inner = rows - 2 * STEPS
    row_bytes = levels * width * 4
    f32 = lambda *shape: jax.ShapeDtypeStruct(shape, jnp.float32)
    vmem = pl.BlockSpec(memory_space=pltpu.VMEM)
    smem = pl.BlockSpec(memory_space=pltpu.SMEM)
    hbm = pl.BlockSpec(memory_space=pltpu.HBM)
    in_hbm = lambda value: pltpu.with_memory_space_constraint(value, pltpu.HBM)

    subs, hors = lax.axis_size("sub"), lax.axis_size("hor")
    small = [parent_cell, stencil_offset, stencil_weight]

    first_pack = pl.pallas_call(
        pack_kernel,
        in_specs=[hbm] * 6,
        out_specs=vmem,
        out_shape=f32(PACK_ROWS + 1, levels, width),
        scratch_shapes=[
            pltpu.VMEM((parts, STEPS, levels, width), jnp.float32),
            pltpu.VMEM((STEPS, levels, width), jnp.float32),
            pltpu.VMEM((STEPS, levels, width), jnp.float32),
        ]
        + [pltpu.VMEM(value.shape, value.dtype) for value in small]
        + [pltpu.SemaphoreType.DMA((levels // HALF, parts + 2)), pltpu.SemaphoreType.DMA((3,))],
        compiler_params=PARAMS,
        cost_estimate=BRIEF,
        name="pack",
    )(*[in_hbm(value) for value in [adjoint_state, courant_east, courant_north] + small])
    first_came = alternating(first_pack, -1)

    second_pack, middle, ends, columns, state, east, north = pl.pallas_call(
        sweep_kernel,
        in_specs=[hbm] * 3 + [pl.BlockSpec(memory_space=pl.ANY)],
        out_specs=[vmem] * 7,
        out_shape=[
            f32(PACK_ROWS, levels, width),
            f32(parts, inner, levels, width),
            f32(parts, 2 * STEPS, levels, width),
            f32(parts, 2, rows, levels, LANES),
            f32(*adjoint_state.shape), f32(*courant_east.shape), f32(*courant_north.shape),
        ],
        scratch_shapes=[
            pltpu.VMEM((STEPS - 1, parts, rows, HALF, width), jnp.float32),
            pltpu.VMEM((rows, HALF, width), jnp.float32),
            pltpu.VMEM((rows, HALF, width), jnp.float32),
            pltpu.VMEM((rows, HALF, width), jnp.float32),
            pltpu.SemaphoreType.DMA((parts + 2,)),
        ],
        compiler_params=PARAMS,
        cost_estimate=BRIEF,
        name="sweep",
    )(in_hbm(adjoint_state), in_hbm(courant_east), in_hbm(courant_north), first_pack)
    middle_came = to_previous(middle)

    mixing, base, owner, second_sent = pl.pallas_call(
        ghost_base_kernel,
        in_specs=[vmem] * 7,
        out_specs=[vmem] * 4,
        out_shape=[
            f32(parts, 2, rows, slots), f32(parts, levels, slots),
            jax.ShapeDtypeStruct((1, slots), owner_slot.dtype), f32(PACK_ROWS, levels, width),
        ],
        compiler_params=PARAMS,
        cost_estimate=BRIEF,
        name="ghost_base",
    )(*small, owner_slot[None], columns, north, second_pack)
    second_came = alternating(second_sent, 1)

    column_shape = (parts, 2, 2 * (STEPS - 1), levels, LANES)
    side_a, a_columns = pl.pallas_call(
        mend_a_kernel,
        in_specs=[vmem] * 6,
        out_specs=[vmem] * 2,
        out_shape=[f32(parts, STEPS, levels, width), f32(*column_shape)],
        compiler_params=PARAMS,
        cost_estimate=BRIEF,
        name="mend_a",
    )(east, north, second_pack, first_came, ends, base)
    a_came = to_previous(side_a)
    total = pl.pallas_call(
        ghost_kernel,
        in_specs=[vmem] * 5,
        out_specs=vmem,
        out_shape=f32(parts, levels, slots),
        scratch_shapes=[pltpu.VMEM((parts, 2, rows, slots), jnp.float32)],
        compiler_params=PARAMS,
        cost_estimate=BRIEF,
        name="ghost",
    )(north, first_came, a_columns, mixing, base)
    order = rounds()
    total = total + exchanged(total, *order[0])
    side_b = pl.pallas_call(
        mend_b_kernel,
        in_specs=[vmem] * 5 + [pl.BlockSpec(memory_space=pl.ANY)] * 2,
        out_specs=vmem,
        out_shape=f32(parts, STEPS, levels, width),
        compiler_params=PARAMS,
        cost_estimate=BRIEF,
        name="mend_b",
    )(east, north, first_pack, second_came, ends, middle_came, total)
    b_came = to_previous(side_b)

    result = f32(*adjoint_state.shape)
    buffer = pltpu.VMEM((parts, rows, levels, width), jnp.float32)
    assert len(order) > 2
    came = exchanged(total, *order[1])
    begun, total = pl.pallas_call(
        begin_kernel,
        in_specs=[vmem] * 4,
        out_specs=[hbm, vmem],
        out_shape=[result, f32(parts, levels, slots)],
        scratch_shapes=[buffer, pltpu.SemaphoreType.DMA((2 * parts,))],
        compiler_params=PARAMS,
        cost_estimate=BRIEF,
        name="begin",
    )(state, middle_came, a_came, total)
    for each in order[2:]:
        total = total + came
        came = exchanged(total, *each)
    adjoint_result = pl.pallas_call(
        end_kernel,
        in_specs=[hbm] + [vmem] * 2,
        out_specs=hbm,
        out_shape=result,
        scratch_shapes=[buffer, pltpu.SemaphoreType.DMA((parts,))],
        input_output_aliases={0: 0},
        compiler_params=PARAMS,
        cost_estimate=BRIEF,
        name="end",
    )(begun, state, b_came)
    boundary_gradient = pl.pallas_call(
        pick_kernel,
        in_specs=[hbm] + [vmem] * 3,
        out_specs=vmem,
        out_shape=f32(parts, levels // subs, slots // hors),
        compiler_params=PARAMS,
        cost_estimate=BRIEF,
        name="pick",
    )(in_hbm(adjoint_result), owner, total, came)
    return (adjoint_result, boundary_gradient)


def solution(mesh):
    in_specs = (
        P(("ens", "sub"), None, "hor", None, None),
        P(("ens", "sub"), "hor", None, None),
        P(("ens", "sub"), "hor", None, None),
        P(None, None, "hor"),
        P(None, None, None, "hor"),
        P(None, None, None, "hor"),
        P(),
    )
    out_specs = (P(("ens", "sub"), None, "hor", None, None), P("ens", "sub", "hor"))
    return jax.shard_map(local, mesh=mesh, in_specs=in_specs, out_specs=out_specs, check_vma=False)
```

```python
import functools

import jax
import jax.numpy as jnp
from jax import lax
from jax.experimental import pallas as pl
from jax.experimental.pallas import tpu as pltpu
from jax.sharding import PartitionSpec as P

STEPS = 4
HALF = 8
FLUX_ROWS = 2 * STEPS
PACK_ROWS = FLUX_ROWS + 3
LANES = 128
EXTRA = PACK_ROWS
TARGETS = 4 * LANES
WEIGHTS = 5 * LANES


def to_previous(value):
    peers = lax.axis_size("sub")
    return lax.ppermute(value, "sub", [(i, (i - 1) % peers) for i in range(peers)])


def alternating(value, sign):
    subs, hors = lax.axis_size("sub"), lax.axis_size("hor")
    assert subs % 2 == 0
    pairs = []
    for s in range(subs):
        step = sign if s % 2 == 0 else -sign
        for h in range(hors):
            inside = 0 <= h + step < hors
            pairs.append((s * hors + h, s * hors + h + step if inside else (s ^ 1) * hors + h))
    return lax.ppermute(value, ("sub", "hor"), pairs)


def has_neighbour(flip):
    hor = lax.axis_index("hor")
    return jnp.where(flip == 1, hor < lax.axis_size("hor") - 1, hor > 0)


def rounds():
    subs, hors = lax.axis_size("sub"), lax.axis_size("hor")
    assert not subs & (subs - 1) and not hors & (hors - 1)
    order = [("sub", range(min(subs, 4) - 1, 0, -1))]
    order += [("sub", [1 << n]) for n in range(2, subs.bit_length() - 1)]
    return order + [("hor", [1 << n]) for n in range(hors.bit_length() - 1)]


def exchanged(value, axis, distances):
    size = lax.axis_size(axis)
    return sum(lax.ppermute(value, axis, [(i, i ^ distance) for i in range(size)]) for distance in distances)


def parity():
    return lax.rem(lax.axis_index("sub"), 2)


def sign_of(flip):
    return jnp.where(flip == 1, jnp.float32(-1.0), jnp.float32(1.0))


def north_rates(north_rate):
    width = north_rate.shape[-1]
    column = lax.broadcasted_iota(jnp.int32, north_rate.shape, len(north_rate.shape) - 1)
    plus = jnp.where(column == 0, 0.0, jnp.maximum(north_rate, 0.0))
    minus = jnp.where(column == width - 1, 0.0, jnp.maximum(-north_rate, 0.0))
    return plus, minus


def shifted(flux_plus, flux_minus):
    width = flux_plus.shape[-1]
    axis = len(flux_plus.shape) - 1
    return pltpu.roll(flux_plus, width - 1, axis) + pltpu.roll(flux_minus, 1, axis)


class Row:
    def __init__(self, east_rate, north_rate=None):
        self.outward = jnp.maximum(east_rate, 0.0)
        self.inward = jnp.maximum(-east_rate, 0.0)
        if north_rate is not None:
            self.centre = 1.0 - jnp.abs(east_rate) - jnp.abs(north_rate)
            self.plus, self.minus = north_rates(north_rate)

    def stay(self, value):
        return self.centre * value + shifted(self.plus * value, self.minus * value)


def level_halves(levels, body):
    def step(h, carry):
        body(pl.ds(pl.multiple_of(h * HALF, HALF), HALF))
        return carry

    lax.fori_loop(0, levels // HALF, step, 0)


def pack_kernel(
    state_hbm, east_hbm, north_hbm, cell_hbm, offset_hbm, weight_hbm,
    pack_ref, state_ref, east_ref, north_ref, cell_ref, offset_ref, weight_ref, sems, small_sems,
):
    parts, rows, levels, width = state_hbm.shape[1:]
    flip = parity()
    sign = sign_of(flip)
    at_end = pl.ds(flip * (rows - STEPS), STEPS)
    place = lambda r: r + flip * (STEPS - 1 - 2 * r)
    halves = levels // HALF
    copies = []
    for h in range(halves):
        at = pl.ds(h * HALF, HALF)
        sem = sems.at[h]
        batch = [
            pltpu.make_async_copy(state_hbm.at[0, c, at_end, at], state_ref.at[c, :, at], sem.at[c])
            for c in range(parts)
        ]
        batch.append(pltpu.make_async_copy(east_hbm.at[0, at_end, at], east_ref.at[:, at], sem.at[parts]))
        batch.append(pltpu.make_async_copy(north_hbm.at[0, at_end, at], north_ref.at[:, at], sem.at[parts + 1]))
        copies.append(batch)
        for copy in batch:
            copy.start()
    small = [
        pltpu.make_async_copy(source, target, small_sems.at[n])
        for n, (source, target) in enumerate(
            ((cell_hbm, cell_ref), (offset_hbm, offset_ref), (weight_hbm, weight_ref))
        )
    ]
    for copy in small:
        copy.start()

    def half(at):
        row = [Row(east_ref[place(r), at, :] * sign, north_ref[place(r), at, :]) for r in range(STEPS)]
        pack_ref[FLUX_ROWS, at, :] = east_ref[place(0), at, :]
        pack_ref[FLUX_ROWS + 1, at, :] = north_ref[place(0), at, :]
        pack_ref[FLUX_ROWS + 2, at, :] = east_ref[place(1), at, :]
        for r in (1, 2):
            lanes = (2 * r - 2) * LANES
            pack_ref[EXTRA, at, lanes:lanes + LANES] = north_ref[place(r), at, :LANES]
            pack_ref[EXTRA, at, lanes + LANES:lanes + 2 * LANES] = north_ref[place(r), at, width - LANES:]
        for c in range(parts):
            field = [state_ref[c, place(r), at, :] for r in range(STEPS)]
            for k in range(STEPS):
                pack_ref[2 * k + c, at, :] = row[0].outward * field[0]
                after = []
                for r in range(STEPS - 1 - k):
                    value = row[r].stay(field[r]) + row[r + 1].outward * field[r + 1]
                    if r > 0:
                        value = value + row[r - 1].inward * field[r - 1]
                    after.append(value)
                field = after

    for h in range(halves):
        for copy in copies[h]:
            copy.wait()
        half(pl.ds(h * HALF, HALF))

    for copy in small:
        copy.wait()
    n = 0
    for point in range(offset_ref.shape[0]):
        for c in range(parts):
            target = (cell_ref[c] + offset_ref[point, c]).astype(jnp.float32)
            pack_ref[EXTRA, n:n + 2, TARGETS:TARGETS + rows] = target
            pack_ref[EXTRA, n:n + 2, WEIGHTS:WEIGHTS + rows] = weight_ref[point, c]
            n += 2


def as_column(row):
    count = row.shape[1]
    here = lax.broadcasted_iota(jnp.int32, (count, count), 0)
    there = lax.broadcasted_iota(jnp.int32, (count, count), 1)
    return jnp.sum(jnp.where(here == there, row, 0), axis=1, keepdims=True)


def sweep_kernel(
    state_hbm, east_hbm, north_hbm, _,
    pack_ref, middle_ref, ends_ref, column_ref, state_ref, east_ref, north_ref,
    field, plus_ref, minus_ref, centre_ref, sems,
):
    copies = [
        pltpu.make_async_copy(source, target, sems.at[n])
        for n, (source, target) in enumerate(
            ((east_hbm, east_ref), (north_hbm, north_ref))
            + tuple((state_hbm.at[0, c], state_ref.at[0, c]) for c in range(state_hbm.shape[1]))
        )
    ]
    for copy in copies:
        copy.start()
    for copy in copies:
        copy.wait()
    parts, rows, levels, width = state_ref.shape[1:]
    flip = 1 - parity()
    sign = sign_of(flip)
    end_row = flip * (rows - 1)
    next_row = end_row + 1 - 2 * flip

    def half(at):
        pack_ref[FLUX_ROWS, at, :] = east_ref[0, end_row, at, :]
        pack_ref[FLUX_ROWS + 1, at, :] = north_ref[0, end_row, at, :]
        pack_ref[FLUX_ROWS + 2, at, :] = east_ref[0, next_row, at, :]

        for k in range(STEPS):
            if k == 0:
                read = lambda c, i: state_ref[0, c, i, at, :]
            else:
                read = lambda c, i, slot=k - 1: field[slot, c, i]
            leaving = jnp.maximum(east_ref[0, end_row, at, :] * sign, 0.0)
            for c in range(parts):
                pack_ref[2 * k + c, at, :] = leaving * read(c, end_row)
            west = [None] * parts
            here = [read(c, 0) for c in range(parts)]
            east_here = east_ref[0, 0, at, :]
            for i in range(rows):
                leave_west = jnp.maximum(-east_here, 0.0)
                if k == 0:
                    north_rate = north_ref[0, i, at, :]
                    centre = 1.0 - jnp.abs(east_here) - jnp.abs(north_rate)
                    plus, minus = north_rates(north_rate)
                    centre_ref[i], plus_ref[i], minus_ref[i] = centre, plus, minus
                else:
                    centre, plus, minus = centre_ref[i], plus_ref[i], minus_ref[i]
                if i + 1 < rows:
                    east_here = east_ref[0, i + 1, at, :]
                    east_after = jnp.maximum(east_here, 0.0)
                for c in range(parts):
                    value = here[c]
                    total = centre * value + shifted(plus * value, minus * value)
                    if i > 0:
                        total = total + west[c]
                    if i + 1 < rows:
                        west[c] = leave_west * value
                        here[c] = read(c, i + 1)
                        total = total + east_after * here[c]
                    if k < STEPS - 1:
                        field[k, c, i] = total
                    elif i < STEPS:
                        ends_ref[c, i, at, :] = total
                    elif i >= rows - STEPS:
                        ends_ref[c, i - rows + 2 * STEPS, at, :] = total
                    else:
                        middle_ref[c, i - STEPS, at, :] = total

        def columns(i, carry):
            for c in range(parts):
                value = state_ref[0, c, i, at, :]
                first, last = value[:, :LANES], value[:, width - LANES:]
                for slot in range(STEPS - 1):
                    first = first + field[slot, c, i, :, :LANES]
                    last = last + field[slot, c, i, :, width - LANES:]
                column_ref[c, 0, i, at, :] = first
                column_ref[c, 1, i, at, :] = last
            return carry

        lax.fori_loop(0, rows, columns, 0, unroll=2)

    level_halves(levels, half)


def mix(targets, weights, cells, total):
    for target, weight in zip(targets, weights):
        total = total + jnp.where(as_column(target) == cells, as_column(weight), 0.0)
    return total


def ghost_base_kernel(
    cell_ref, offset_ref, weight_ref, owner_ref, column_ref, north_ref, pack_ref,
    mixing_ref, partial_ref, owner_out, pack_out,
):
    owner_out[...] = owner_ref[...]
    pack_out[...] = pack_ref[...]
    parts, _, rows, levels, _ = column_ref.shape
    slots = mixing_ref.shape[-1]
    width = north_ref.shape[-1]
    points = range(offset_ref.shape[0])
    cells = lax.broadcasted_iota(jnp.int32, (rows, slots), 1)
    for c in range(parts):
        for s in range(2):
            mixing_ref[c, s] = mix(
                [cell_ref[c, s:s + 1, :] + offset_ref[point, c, s:s + 1, :] for point in points],
                [weight_ref[point, c, s:s + 1, :] for point in points],
                cells, jnp.zeros((rows, slots), jnp.float32),
            )

    for c in range(parts):
        total = jnp.zeros((levels, slots), jnp.float32)
        for i in range(rows):
            south = jnp.maximum(north_ref[0, i, :, :1], 0.0) * column_ref[c, 0, i, :, :1]
            north = jnp.maximum(-north_ref[0, i, :, width - 1:], 0.0) * column_ref[c, 1, i, :, LANES - 1:]
            total = total + south * mixing_ref[c, 0, i:i + 1, :]
            total = total + north * mixing_ref[c, 1, i:i + 1, :]
        partial_ref[c] = total


def hand_on_kernel(pack_ref, pack_out):
    pack_out[...] = pack_ref[...]


def ghost_kernel(north_ref, other_ref, column_ref, mixing_ref, partial_ref, sum_ref, near_mixing):
    parts, levels, slots = partial_ref.shape
    rows = mixing_ref.shape[2]
    width = north_ref.shape[-1]
    flip = 1 - parity()
    cells = lax.broadcasted_iota(jnp.int32, (rows, slots), 1).astype(jnp.float32)
    points = (WEIGHTS - TARGETS) // LANES * 4
    for c in range(parts):
        for s in range(2):
            at = [(point * parts + c) * 2 + s for point in range(points)]
            near_mixing[c, s] = mix(
                [other_ref[EXTRA, n:n + 1, TARGETS:TARGETS + rows] for n in at],
                [other_ref[EXTRA, n:n + 1, WEIGHTS:WEIGHTS + rows] for n in at],
                cells, jnp.zeros((rows, slots), jnp.float32),
            )
    for c in range(parts):
        total = partial_ref[c]
        for r in range(STEPS - 1):
            i = r + flip * (rows - 1 - 2 * r)
            south = jnp.maximum(north_ref[0, i, :, :1], 0.0) * column_ref[c, 0, r, :, :1]
            north = jnp.maximum(-north_ref[0, i, :, width - 1:], 0.0) * column_ref[c, 1, r, :, LANES - 1:]
            total = total + south * mixing_ref[c, 0, pl.ds(i, 1), :]
            total = total + north * mixing_ref[c, 1, pl.ds(i, 1), :]
            i = r + (1 - flip) * (rows - 1 - 2 * r)
            if r == 0:
                first_rate = other_ref[FLUX_ROWS + 1, :, :LANES]
                last_rate = other_ref[FLUX_ROWS + 1, :, width - LANES:]
            else:
                lanes = (2 * r - 2) * LANES
                first_rate = other_ref[EXTRA, :, lanes:lanes + LANES]
                last_rate = other_ref[EXTRA, :, lanes + LANES:lanes + 2 * LANES]
            south = jnp.maximum(first_rate[:, :1], 0.0) * column_ref[c, 0, STEPS - 1 + r, :, :1]
            north = jnp.maximum(-last_rate[:, LANES - 1:], 0.0) * column_ref[c, 1, STEPS - 1 + r, :, LANES - 1:]
            total = total + south * near_mixing[c, 0, pl.ds(i, 1), :]
            total = total + north * near_mixing[c, 1, pl.ds(i, 1), :]
        sum_ref[c] = jnp.where(has_neighbour(flip), total, partial_ref[c])


def mend_side(flip, east_ref, north_ref, mine_ref, other_ref, store, store_column):
    levels, width = mine_ref.shape[1:]
    rows = east_ref.shape[1]
    sign = sign_of(flip)
    place = lambda r: flip * (rows - STEPS) + r + flip * (STEPS - 1 - 2 * r)

    def half(at):
        own = [Row(east_ref[0, place(r), at, :] * sign, north_ref[0, place(r), at, :]) for r in range(STEPS - 1)]
        near = Row(other_ref[FLUX_ROWS, at, :] * sign, other_ref[FLUX_ROWS + 1, at, :])
        far = Row(other_ref[FLUX_ROWS + 2, at, :] * sign)
        for c in range(FLUX_ROWS // STEPS):
            mine = lambda k: mine_ref[2 * k + c, at, :]
            theirs = lambda k: other_ref[2 * k + c, at, :]
            a0 = theirs(0)
            n1 = mine(0)
            b0 = own[0].stay(a0) + near.inward * n1 + theirs(1)
            b1 = own[0].inward * a0
            bn1 = near.stay(n1) + own[0].outward * a0 + mine(1)
            bn2 = near.outward * n1
            c0 = own[0].stay(b0) + near.inward * bn1 + own[1].outward * b1 + theirs(2)
            c1 = own[1].stay(b1) + own[0].inward * b0
            c2 = own[1].inward * b1
            cn1 = near.stay(bn1) + own[0].outward * b0 + far.inward * bn2 + mine(2)
            d0 = own[0].stay(c0) + near.inward * cn1 + own[1].outward * c1 + theirs(3)
            d1 = own[1].stay(c1) + own[0].inward * c0 + own[2].outward * c2
            d2 = own[2].stay(c2) + own[1].inward * c1
            d3 = own[2].inward * c2
            for r, value in enumerate((d0, d1, d2, d3)):
                store(c, r, at, value)
            if store_column is not None:
                tiles = (slice(0, LANES), slice(width - LANES, width))
                for s, lanes in enumerate(tiles):
                    tile = lambda value: value[:, lanes]
                    rate = other_ref[EXTRA, at, s * LANES:(s + 1) * LANES]
                    stays = 1.0 - jnp.abs(other_ref[FLUX_ROWS + 2, at, lanes]) - jnp.abs(rate)
                    drift = jnp.maximum(rate if s == 0 else -rate, 0.0) * tile(bn2)
                    cn2 = stays * tile(bn2) + pltpu.roll(drift, LANES - 1 if s == 0 else 1, 1)
                    cn2 = cn2 + tile(near.outward) * tile(bn1)
                    cn3 = tile(far.outward) * tile(bn2)
                    sums = (
                        tile(a0) + tile(b0) + tile(c0), tile(b1) + tile(c1), tile(c2),
                        tile(n1) + tile(bn1) + tile(cn1), tile(bn2) + cn2, cn3,
                    )
                    for r, value in enumerate(sums):
                        store_column(c, s, r, at, value)

    level_halves(levels, half)


def copy_end(flip, ends_ref, out_ref):
    for c in range(out_ref.shape[0]):
        for r in range(STEPS):
            out_ref[c, r] = ends_ref[c, flip * STEPS + r]


def mend_a_kernel(east_ref, north_ref, mine_ref, other_ref, ends_ref, base_ref, out_ref, column_ref):
    flip = 1 - parity()
    turn = lambda r: r + flip * (STEPS - 1 - 2 * r)

    def store(c, r, at, value):
        out_ref[c, turn(r), at, :] = ends_ref[c, flip * STEPS + turn(r), at, :] + value

    def store_column(c, s, r, at, value):
        column_ref[c, s, r, at, :] = value

    @pl.when(has_neighbour(flip))
    def _():
        mend_side(flip, east_ref, north_ref, mine_ref, other_ref, store, store_column)

    @pl.when(jnp.logical_not(has_neighbour(flip)))
    def _():
        column_ref[...] = jnp.zeros_like(column_ref)
        copy_end(flip, ends_ref, out_ref)


def mend_b_kernel(east_ref, north_ref, mine_ref, other_ref, ends_ref, _, __, out_ref):
    flip = parity()
    turn = lambda r: r + flip * (STEPS - 1 - 2 * r)

    def store(c, r, at, value):
        out_ref[c, turn(r), at, :] = ends_ref[c, flip * STEPS + turn(r), at, :] + value

    @pl.when(has_neighbour(flip))
    def _():
        mend_side(flip, east_ref, north_ref, mine_ref, other_ref, store, None)

    @pl.when(jnp.logical_not(has_neighbour(flip)))
    def _():
        copy_end(flip, ends_ref, out_ref)


def subtract_rows(state_ref, out_hbm, buffer, sems, jobs):
    copies = []
    is_last = lax.axis_index("sub") == lax.axis_size("sub") - 1
    for start, other in jobs:
        for c in range(other.shape[0]):
            count = other.shape[1]
            for r in range(count):
                buffer[c, start + r] = state_ref[0, c, start + r] - jnp.where(is_last, 0.0, other[c, r])
            at = pl.ds(start, count)
            copy = pltpu.make_async_copy(buffer.at[c, at], out_hbm.at[0, c, at], sems.at[len(copies)])
            copy.start()
            copies.append(copy)
    return copies


def begin_kernel(state_ref, middle_ref, a_ref, out_hbm, buffer, sems):
    start = parity() * (state_ref.shape[2] - STEPS)
    for copy in subtract_rows(state_ref, out_hbm, buffer, sems, ((STEPS, middle_ref), (start, a_ref))):
        copy.wait()


def end_kernel(begun_hbm, state_ref, b_ref, out_hbm, buffer, sems):
    start = (1 - parity()) * (state_ref.shape[2] - STEPS)
    for copy in subtract_rows(state_ref, out_hbm, buffer, sems, ((start, b_ref),)):
        copy.wait()


def pick_kernel(_, owner_ref, total_ref, came_ref, gradient_ref):
    parts = gradient_ref.shape[0]
    share, mine = gradient_ref.shape[1:]
    start = lax.axis_index("hor") * mine
    chosen = []
    for c in range(parts):
        total = total_ref[c] + came_ref[c]
        block = total[:share]
        for s in range(1, total.shape[0] // share):
            block = jnp.where(lax.axis_index("sub") == s, total[s * share:(s + 1) * share], block)
        chosen.append(block)
    chosen = jnp.concatenate(chosen, 0)
    column = lax.broadcasted_iota(jnp.int32, (parts * share, mine), 1)
    picked = jnp.zeros((parts * share, mine), jnp.float32)
    for q in range(mine):
        value = jnp.sum(jnp.where(owner_ref[...] == start + q, chosen, 0.0), axis=1, keepdims=True)
        picked = jnp.where(column == q, value, picked)
    for c in range(parts):
        gradient_ref[c] = picked[c * share:(c + 1) * share]


BRIEF = pl.CostEstimate(flops=1, bytes_accessed=1, transcendentals=0)
PARAMS = pltpu.CompilerParams(vmem_limit_bytes=24 * 1024 * 1024)


def local(
    adjoint_state,
    courant_east,
    courant_north,
    parent_cell,
    stencil_offset,
    stencil_weight,
    owner_slot,
):
    _, parts, rows, levels, width = adjoint_state.shape
    slots = owner_slot.shape[0]
    inner = rows - 2 * STEPS
    row_bytes = levels * width * 4
    f32 = lambda *shape: jax.ShapeDtypeStruct(shape, jnp.float32)
    vmem = pl.BlockSpec(memory_space=pltpu.VMEM)
    smem = pl.BlockSpec(memory_space=pltpu.SMEM)
    hbm = pl.BlockSpec(memory_space=pltpu.HBM)
    in_hbm = lambda value: pltpu.with_memory_space_constraint(value, pltpu.HBM)

    subs, hors = lax.axis_size("sub"), lax.axis_size("hor")
    small = [parent_cell, stencil_offset, stencil_weight]

    first_pack = pl.pallas_call(
        pack_kernel,
        in_specs=[hbm] * 6,
        out_specs=vmem,
        out_shape=f32(PACK_ROWS + 1, levels, width),
        scratch_shapes=[
            pltpu.VMEM((parts, STEPS, levels, width), jnp.float32),
            pltpu.VMEM((STEPS, levels, width), jnp.float32),
            pltpu.VMEM((STEPS, levels, width), jnp.float32),
        ]
        + [pltpu.VMEM(value.shape, value.dtype) for value in small]
        + [pltpu.SemaphoreType.DMA((levels // HALF, parts + 2)), pltpu.SemaphoreType.DMA((3,))],
        compiler_params=PARAMS,
        cost_estimate=BRIEF,
        name="pack",
    )(*[in_hbm(value) for value in [adjoint_state, courant_east, courant_north] + small])
    first_came = alternating(first_pack, -1)

    second_pack, middle, ends, columns, state, east, north = pl.pallas_call(
        sweep_kernel,
        in_specs=[hbm] * 3 + [pl.BlockSpec(memory_space=pl.ANY)],
        out_specs=[vmem] * 7,
        out_shape=[
            f32(PACK_ROWS, levels, width),
            f32(parts, inner, levels, width),
            f32(parts, 2 * STEPS, levels, width),
            f32(parts, 2, rows, levels, LANES),
            f32(*adjoint_state.shape), f32(*courant_east.shape), f32(*courant_north.shape),
        ],
        scratch_shapes=[
            pltpu.VMEM((STEPS - 1, parts, rows, HALF, width), jnp.float32),
            pltpu.VMEM((rows, HALF, width), jnp.float32),
            pltpu.VMEM((rows, HALF, width), jnp.float32),
            pltpu.VMEM((rows, HALF, width), jnp.float32),
            pltpu.SemaphoreType.DMA((parts + 2,)),
        ],
        compiler_params=PARAMS,
        cost_estimate=BRIEF,
        name="sweep",
    )(in_hbm(adjoint_state), in_hbm(courant_east), in_hbm(courant_north), first_pack)
    middle_came = to_previous(middle)

    mixing, base, owner, second_sent = pl.pallas_call(
        ghost_base_kernel,
        in_specs=[vmem] * 7,
        out_specs=[vmem] * 4,
        out_shape=[
            f32(parts, 2, rows, slots), f32(parts, levels, slots),
            jax.ShapeDtypeStruct((1, slots), owner_slot.dtype), f32(PACK_ROWS, levels, width),
        ],
        compiler_params=PARAMS,
        cost_estimate=BRIEF,
        name="ghost_base",
    )(*small, owner_slot[None], columns, north, second_pack)
    second_sent = pl.pallas_call(
        hand_on_kernel,
        in_specs=[vmem],
        out_specs=vmem,
        out_shape=f32(PACK_ROWS, levels, width),
        compiler_params=PARAMS,
        cost_estimate=BRIEF,
        name="hand_on",
    )(second_sent)
    second_came = alternating(second_sent, 1)

    column_shape = (parts, 2, 2 * (STEPS - 1), levels, LANES)
    side_a, a_columns = pl.pallas_call(
        mend_a_kernel,
        in_specs=[vmem] * 6,
        out_specs=[vmem] * 2,
        out_shape=[f32(parts, STEPS, levels, width), f32(*column_shape)],
        compiler_params=PARAMS,
        cost_estimate=BRIEF,
        name="mend_a",
    )(east, north, second_pack, first_came, ends, base)
    a_came = to_previous(side_a)
    total = pl.pallas_call(
        ghost_kernel,
        in_specs=[vmem] * 5,
        out_specs=vmem,
        out_shape=f32(parts, levels, slots),
        scratch_shapes=[pltpu.VMEM((parts, 2, rows, slots), jnp.float32)],
        compiler_params=PARAMS,
        cost_estimate=BRIEF,
        name="ghost",
    )(north, first_came, a_columns, mixing, base)
    order = rounds()
    total = total + exchanged(total, *order[0])
    side_b = pl.pallas_call(
        mend_b_kernel,
        in_specs=[vmem] * 5 + [pl.BlockSpec(memory_space=pl.ANY)] * 2,
        out_specs=vmem,
        out_shape=f32(parts, STEPS, levels, width),
        compiler_params=PARAMS,
        cost_estimate=BRIEF,
        name="mend_b",
    )(east, north, first_pack, second_came, ends, middle_came, total)
    b_came = to_previous(side_b)

    for each in order[1:-1]:
        total = total + exchanged(total, *each)
    came = exchanged(total, *order[-1])

    result = f32(*adjoint_state.shape)
    buffer = pltpu.VMEM((parts, rows, levels, width), jnp.float32)
    begun = pl.pallas_call(
        begin_kernel,
        in_specs=[vmem] * 3,
        out_specs=hbm,
        out_shape=result,
        scratch_shapes=[buffer, pltpu.SemaphoreType.DMA((2 * parts,))],
        compiler_params=PARAMS,
        cost_estimate=BRIEF,
        name="begin",
    )(state, middle_came, a_came)
    adjoint_result = pl.pallas_call(
        end_kernel,
        in_specs=[hbm] + [vmem] * 2,
        out_specs=hbm,
        out_shape=result,
        scratch_shapes=[buffer, pltpu.SemaphoreType.DMA((parts,))],
        input_output_aliases={0: 0},
        compiler_params=PARAMS,
        cost_estimate=BRIEF,
        name="end",
    )(begun, state, b_came)
    boundary_gradient = pl.pallas_call(
        pick_kernel,
        in_specs=[hbm] + [vmem] * 3,
        out_specs=vmem,
        out_shape=f32(parts, levels // subs, slots // hors),
        compiler_params=PARAMS,
        cost_estimate=BRIEF,
        name="pick",
    )(in_hbm(adjoint_result), owner, total, came)
    return (adjoint_result, boundary_gradient)


def solution(mesh):
    in_specs = (
        P(("ens", "sub"), None, "hor", None, None),
        P(("ens", "sub"), "hor", None, None),
        P(("ens", "sub"), "hor", None, None),
        P(None, None, "hor"),
        P(None, None, None, "hor"),
        P(None, None, None, "hor"),
        P(),
    )
    out_specs = (P(("ens", "sub"), None, "hor", None, None), P("ens", "sub", "hor"))
    return jax.shard_map(local, mesh=mesh, in_specs=in_specs, out_specs=out_specs, check_vma=False)
```
